32 devices in a mesh: branch: 2 (over core), tp: 4 (over y, x), seq: 4 (over z).
Axes of the slice: x: 2, y: 2, z: 4, core: 2. Of those that a mesh axis runs over, the one named last changes fastest.
Arguments:
- block_input: bfloat16 [8, 2048, 2048], P('seq', 'tp'), may hold values from -6 to 6
- first_norm_gain: bfloat16 [2048], replicated, may hold values from 0.25 to 1.75
- first_norm_bias: bfloat16 [2048], replicated, may hold values from -1.5 to 1.5
- second_norm_gain: bfloat16 [2048], replicated, may hold values from 0.25 to 1.75
- second_norm_bias: bfloat16 [2048], replicated, may hold values from -1.5 to 1.5
- query_key_value: bfloat16 [2048, 6144], P(('branch', 'seq'), 'tp'), may hold values from -0.125 to 0.125
- query_key_value_bias: bfloat16 [6144], P('tp'), may hold values from -1.5 to 1.5
- attention_dense: bfloat16 [2048, 2048], P('tp', ('branch', 'seq')), may hold values from -0.375 to 0.375
- attention_dense_bias: bfloat16 [2048], replicated, may hold values from -1.5 to 1.5
- expand_weight: bfloat16 [2048, 8192], P(('branch', 'seq'), 'tp'), may hold values from -0.125 to 0.125
- expand_bias: bfloat16 [8192], P('tp'), may hold values from -2.5 to 2.5
- contract_weight: bfloat16 [8192, 2048], P('tp', ('branch', 'seq')), may hold values from -0.09375 to 0.09375
- contract_bias: bfloat16 [2048], replicated, may hold values from -1.5 to 1.5
- document_starts: int32 [8, 8], P('seq'), may hold values from 0 to 2048, as said below
- output_grad: bfloat16 [8, 2048, 2048], P('seq', 'tp'), may hold values from -6 to 6
Outputs:
- block_output: bfloat16 [8, 2048, 2048], P('seq', 'tp')
- input_grad: bfloat16 [8, 2048, 2048], P('seq', 'tp')
- first_gain_grad: float32 [2048], replicated
- first_bias_grad: float32 [2048], replicated
- second_gain_grad: float32 [2048], replicated
- second_bias_grad: float32 [2048], replicated
- query_key_value_grad: float32 [2048, 6144], P(('branch', 'seq'), 'tp')
- query_key_value_bias_grad: float32 [6144], P('tp')
- dense_grad: float32 [2048, 2048], P('tp', ('branch', 'seq'))
- dense_bias_grad: float32 [2048], replicated
- expand_grad: float32 [2048, 8192], P(('branch', 'seq'), 'tp')
- expand_bias_grad: float32 [8192], P('tp')
- contract_grad: float32 [8192, 2048], P('tp', ('branch', 'seq'))
- contract_bias_grad: float32 [2048], replicated
The draws below stay inside these ranges and needn't reach their ends.
Inputs may be any that keep to these rules, and one draw needn't show every extreme that they name: `document_starts`: each row lists where the documents of one packed sequence begin: it starts with 0, rises strictly, and the entries after its last document are 2048. Among the 2 rows of each index of seq, one (drawn) has a document that begins before position 512 and ends after position 1536; the others hold 2 to 8 documents.
All inputs are finite; a program needn't handle non-finite values.
Results may differ from the reference program's by a relative error of at most 0.01.
Values may be sent and summed in bfloat16 or wider, within the bound.
No kernel may reach another device: no remote copies, remote signals or barrier semaphores. Data moves between devices by JAX's collectives and lax.ppermute only.
A program may use at most 704 MiB of HBM per device.

```python
import math
import jax
import jax.numpy as jnp
from jax import lax

D = 2048
H = 16
HD = 128
ROT = 32
FF = 8192
LEN = 2048
MAXDOC = 8
SEQ_DEV = 2
SEQS = 8
TILE = 512


def draw_document_starts(key, part):
    key = jax.random.fold_in(key, 11)
    key_cuts, key_count, key_whole, key_head, key_tail = jax.random.split(key, 5)

    def one_row(row_key):
        shuffled = jax.random.permutation(row_key, LEN - 1) + 1
        return jnp.sort(shuffled[:MAXDOC - 1])
    cuts = jax.vmap(one_row)(jax.random.split(key_cuts, SEQS)).astype(jnp.int32)
    counts = jax.random.randint(key_count, (SEQS, 1), 1, MAXDOC)
    used = jnp.arange(MAXDOC - 1)[None, :] < counts
    whole_slot = jax.random.randint(key_whole, (SEQS // SEQ_DEV, 1), 0, SEQ_DEV)
    slot_of_row = jnp.arange(SEQS).reshape(SEQS // SEQ_DEV, SEQ_DEV) % SEQ_DEV
    spanning_row = (slot_of_row == whole_slot).reshape(SEQS, 1)
    head_cut = jax.random.randint(key_head, (SEQS, 1), 1, TILE)
    tail_cut = jax.random.randint(key_tail, (SEQS, 1), LEN - TILE + 1, LEN + 1)
    padding = jnp.full((SEQS, MAXDOC - 3), LEN, jnp.int32)
    spanning = jnp.concatenate([head_cut, tail_cut, padding], axis=1).astype(jnp.int32)
    drawn = jnp.where(used, cuts, LEN).astype(jnp.int32)
    chosen = jnp.where(spanning_row, spanning, drawn)
    return jnp.concatenate([jnp.zeros((SEQS, 1), jnp.int32), chosen], axis=1)


def raised(array, key, source, target, shards_of, factor):
    def block_of(position):
        return (jnp.arange(array.shape[position]) // (array.shape[position] // shards_of)).reshape((-1,) + (1,) * (array.ndim - 1 - position))

    near = jax.random.permutation(key, shards_of)[block_of(target)]
    far = (block_of(target) + shards_of // 2) % shards_of
    return jnp.where((block_of(source) == near) | (block_of(source) == far), factor * array, array)


def levels(stream_key, dims, cuts, smallest, largest):
    loudness, own = 1.0, jax.random.fold_in(stream_key, 6)
    for axis_at, parts in cuts:
        heights = jnp.exp(jax.random.uniform(jax.random.fold_in(own, axis_at), (parts,), jnp.float32, smallest / len(cuts), largest / len(cuts)))
        loudness = loudness * jnp.repeat(heights, dims[axis_at] // parts).reshape([-1 if axis == axis_at else 1 for axis in range(len(dims))])
    return loudness


def gaussian(own_key, shape, spread, limit, pieces=(), held_as=jnp.bfloat16):
    gain = levels(own_key, shape, pieces, -0.22, 0.18) if pieces else 1.0
    array = jax.random.normal(own_key, shape, jnp.float32) * spread * gain
    return jnp.minimum(jnp.maximum(array, -limit), limit).astype(held_as)


def noise_with(key, shape, deviation, limit, pieces, heavy, held_as=jnp.bfloat16):
    entries = deviation * jax.random.normal(key, shape, jnp.float32)
    if pieces:
        entries = entries * levels(key, shape, pieces, -0.22, 0.18)
    return jnp.clip(raised(entries, jax.random.fold_in(key, 3), *heavy), -limit, limit).astype(held_as)


def setup_inputs(seed: int = 0) -> dict:
    key_list = jax.random.split(jax.random.key(seed), 16)
    block_input = gaussian(key_list[0], (SEQS, LEN, D), 1.0, 6.0, ((0, 4), (1, 4)))
    first_norm_gain = jnp.clip(1.0 + 0.15 * jax.random.normal(key_list[1], (D,), jnp.float32), 0.25, 1.75).astype(jnp.bfloat16)
    first_norm_bias = gaussian(key_list[2], (D,), 0.3, 1.5)
    second_norm_gain = jnp.clip(1.0 + 0.15 * jax.random.normal(key_list[3], (D,), jnp.float32), 0.25, 1.75).astype(jnp.bfloat16)
    second_norm_bias = gaussian(key_list[4], (D,), 0.3, 1.5)
    query_key_value = gaussian(key_list[5], (D, 3 * D), D ** -0.5, 0.125, ((0, 8), (1, 4)))
    query_key_value_bias = gaussian(key_list[6], (3 * D,), 0.3, 1.5, ((0, 4),))
    attention_dense = gaussian(key_list[7], (D, D), (D // 8) ** -0.5, 0.375, ((0, 4), (1, 8)))
    attention_dense_bias = gaussian(key_list[8], (D,), 0.3, 1.5)
    expand_weight = gaussian(key_list[9], (D, FF), D ** -0.5, 0.125, ((0, 8), (1, 4)))
    expand_bias = gaussian(key_list[10], (FF,), 0.5, 2.5, ((0, 4),))
    contract_weight = gaussian(key_list[11], (FF, D), (FF // 2) ** -0.5, 0.09375, ((0, 4), (1, 8)))
    contract_bias = gaussian(key_list[12], (D,), 0.3, 1.5)
    document_starts = draw_document_starts(jax.random.fold_in(key_list[15], 71), 0)
    output_grad = noise_with(key_list[14], (SEQS, LEN, D), 1.0, 6.0, ((0, 4), (1, 4)), (0, 2, 4, 2.0))
    return {"block_input": block_input, "first_norm_gain": first_norm_gain, "first_norm_bias": first_norm_bias, "second_norm_gain": second_norm_gain, "second_norm_bias": second_norm_bias, "query_key_value": query_key_value, "query_key_value_bias": query_key_value_bias, "attention_dense": attention_dense, "attention_dense_bias": attention_dense_bias, "expand_weight": expand_weight, "expand_bias": expand_bias, "contract_weight": contract_weight, "contract_bias": contract_bias, "document_starts": document_starts, "output_grad": output_grad}


EPSILON = 1e-05
NEGATIVE = -1e+30
ROPE_BASE = 10000.0
HIGHEST = lax.Precision.HIGHEST

@jax.custom_vjp
def low(v):
    return lax.optimization_barrier(v.astype(jnp.bfloat16)).astype(jnp.float32)

@jax.custom_vjp
def low_back(v):
    return v

def low_keep(v):
    return (low(v), None)

def low_pass(kept, grad):
    return (grad,)

def back_keep(v):
    return (v, None)

def back_low(kept, grad):
    return (low(grad),)
low.defvjp(low_keep, low_pass)
low_back.defvjp(back_keep, back_low)

def product(left, right):
    return jnp.dot(left, right, precision=HIGHEST, preferred_element_type=jnp.float32)

def layer_norm(values, gain_row, shift_row):
    average = lax.optimization_barrier(jnp.mean(values, axis=-1, keepdims=True))
    centred = values - average
    variance = lax.optimization_barrier(jnp.mean(centred * centred, axis=-1, keepdims=True))
    return centred * lax.rsqrt(variance + EPSILON) * gain_row + shift_row

def doc_layout(starts, length):
    places = jnp.arange(length, dtype=jnp.int32)
    started = starts[..., None, :] <= places[:, None]
    doc_ids = lax.optimization_barrier(jnp.sum(started.astype(jnp.int32), axis=-1)) - 1
    begin_at = lax.optimization_barrier(jnp.max(jnp.where(started, starts[..., None, :], 0), axis=-1))
    return (doc_ids, places - begin_at)

def rotary_tables(relative):
    half_rot = ROT // 2
    exponent = jnp.arange(half_rot, dtype=jnp.float32) * (2.0 / ROT)
    frequency = ROPE_BASE ** (-exponent)
    angles = relative.astype(jnp.float32)[..., None] * frequency
    return (jnp.cos(angles), jnp.sin(angles))

def rotate(vectors, cosine_table, sine_table):
    half_rot = cosine_table.shape[-1]
    leading = vectors[..., :half_rot]
    second = vectors[..., half_rot:2 * half_rot]
    return jnp.concatenate([leading * cosine_table - second * sine_table, second * cosine_table + leading * sine_table, vectors[..., 2 * half_rot:]], axis=-1)

def attend(queries, keys, values, doc_ids):
    head_count, length, head_width = queries.shape
    block_rows = min(512, length)
    block_count = length // block_rows
    scaling = 1.0 / math.sqrt(head_width)
    places = jnp.arange(length, dtype=jnp.int32)

    def one_block(block_args):
        query_block, query_places, query_docs = block_args
        scores = low_back(jnp.einsum('hqd,hkd->hqk', query_block, keys, precision=HIGHEST)) * scaling
        allowed = (query_places[:, None] >= places[None, :]) & (query_docs[:, None] == doc_ids[None, :])
        scores = jnp.where(allowed[None], scores, NEGATIVE)
        row_max = lax.optimization_barrier(jnp.max(scores, axis=-1, keepdims=True))
        exponent = jnp.exp(scores - row_max)
        weights = exponent / lax.optimization_barrier(jnp.sum(exponent, axis=-1, keepdims=True))
        return jnp.einsum('hqk,hkd->hqd', low(weights), values, precision=HIGHEST)
    query_blocks = queries.reshape(head_count, block_count, block_rows, head_width).transpose(1, 0, 2, 3)
    outputs = lax.map(jax.checkpoint(one_block), (query_blocks, places.reshape(block_count, block_rows), doc_ids.reshape(block_count, block_rows)))
    return outputs.transpose(1, 0, 2, 3).reshape(head_count, length, head_width)

def sequence_block(tokens, starts, params):
    gain_one, shift_one, gain_two, shift_two, joined_weight, joined_bias, dense_weight, dense_bias, expand_matrix, expand_shift, contract_matrix, contract_shift = params
    length = tokens.shape[0]
    doc_ids, relative = doc_layout(starts, length)
    cosine_table, sine_table = rotary_tables(relative)
    first_normed = low(layer_norm(tokens, gain_one, shift_one))
    joined = low_back(product(first_normed, joined_weight) + joined_bias)
    joined = joined.reshape(length, H, 3, HD).transpose(2, 1, 0, 3)
    queries = low(rotate(joined[0], cosine_table, sine_table))
    keys = low(rotate(joined[1], cosine_table, sine_table))
    values = low(joined[2])
    attended = attend(queries, keys, values, doc_ids)
    attended = low(low_back(attended.transpose(1, 0, 2).reshape(length, H * HD)))
    attention_out = product(attended, dense_weight) + dense_bias
    second_normed = low(layer_norm(tokens, gain_two, shift_two))
    pre_act = low_back(product(second_normed, expand_matrix) + expand_shift)
    activated = low(jax.nn.gelu(pre_act, approximate=False))
    mlp_out = product(activated, contract_matrix) + contract_shift
    return tokens + attention_out + mlp_out

def reference(block_input, first_norm_gain, first_norm_bias, second_norm_gain, second_norm_bias, query_key_value, query_key_value_bias, attention_dense, attention_dense_bias, expand_weight, expand_bias, contract_weight, contract_bias, document_starts, output_grad):
    weights = tuple((weight_item.astype(jnp.float32) for weight_item in (first_norm_gain, first_norm_bias, second_norm_gain, second_norm_bias, query_key_value, query_key_value_bias, attention_dense, attention_dense_bias, expand_weight, expand_bias, contract_weight, contract_bias)))

    def forward(inputs, *params):

        def one_sequence(carried, seq_pair):
            return (carried, sequence_block(seq_pair[0], seq_pair[1], params))
        unused, outputs = lax.scan(one_sequence, jnp.zeros((), jnp.float32), (inputs, document_starts))
        return outputs
    result, pullback = jax.vjp(forward, block_input.astype(jnp.float32), *weights)
    gradients = pullback(output_grad.astype(jnp.float32))
    return (result.astype(jnp.bfloat16), gradients[0].astype(jnp.bfloat16), gradients[1], gradients[2], gradients[3], gradients[4], gradients[5], gradients[6], gradients[7], gradients[8], gradients[9], gradients[10], gradients[11], gradients[12])
```

```python
from functools import partial
import math

import jax
import jax.numpy as jnp
from jax import lax
from jax.experimental import pallas as pl
from jax.experimental.pallas import tpu as pltpu
from jax.sharding import PartitionSpec as P

HD = 128
ROT = 32


EPSILON = 1e-05
NEGATIVE = -1e30
ROPE_BASE = 10000.0
LOG2E = math.log2(math.e)
F32 = jnp.float32
BF16 = jnp.bfloat16
CONTRACT_LAST = (((1,), (1,)), ((), ()))
CONTRACT_FIRST = (((0,), (0,)), ((), ()))
VMEM_BYTES = 56 * 1024 * 1024
ANY = pl.BlockSpec(memory_space=pl.ANY)


def params(steps):
    return pltpu.CompilerParams(
        dimension_semantics=("arbitrary",) * steps, vmem_limit_bytes=VMEM_BYTES
    )


def cost(flops, moved, transcendentals=0):
    return pl.CostEstimate(
        flops=int(flops), bytes_accessed=int(moved), transcendentals=int(transcendentals)
    )


def swap(value, axis, bit):
    size = lax.axis_size(axis)
    return lax.ppermute(value, axis, [(i, i ^ bit) for i in range(size)])


def onward(value, axis):
    size = lax.axis_size(axis)
    return lax.ppermute(value, axis, [(i, (i + 1) % size) for i in range(size)])


def after(value, other):
    return lax.optimization_barrier((value, other))[0]


def bit_orders(size):
    bits = [1 << k for k in range(size.bit_length() - 1)]
    return (bits, bits[::-1])


def last_bit(number, order):
    return [bit for bit in order if number & bit][-1]


def gather_tiles(own):
    size = lax.axis_size("tp")
    half = own.shape[0] // 2
    orders = bit_orders(size)
    whole = {0: own}
    halves = {}

    def part(j, q):
        return whole[j][q * half : (q + 1) * half] if j in whole else halves[j][q]

    for j in sorted(range(1, size), key=lambda j: bin(j).count("1")):
        steps = [(bit, j ^ bit) for bit in (last_bit(j, order) for order in orders)]
        if steps[0] == steps[1] and steps[0][1] in whole:
            whole[j] = swap(whole[steps[0][1]], "tp", steps[0][0])
        else:
            halves[j] = [swap(part(source, q), "tp", bit) for q, (bit, source) in enumerate(steps)]
    return whole, halves


def both_cores(whole, halves):
    entries = {}
    for j in list(whole) + list(halves):
        if j in whole:
            other = swap(whole[j], "branch", 1) if j else None
            entries[j] = [(whole[j], 0), (whole[j], 1), (other, 0), (other, 1)]
        else:
            others = [swap(item, "branch", 1) for item in halves[j]]
            entries[j] = [(item, 0) for item in halves[j]] + [(item, 0) for item in others]
    return entries


def reduce_tiles(pieces):
    size = lax.axis_size("tp")
    half = pieces[0].shape[0] // 2
    results = []
    for q, order in enumerate(bit_orders(size)):
        arrived = {j: [] for j in range(size)}
        for j in sorted(range(size), key=lambda j: -bin(j).count("1")):
            total = pieces[j][q * half : (q + 1) * half]
            if arrived[j] or j == 0:
                total = total.astype(F32)
                for item in arrived[j]:
                    total = total + item.astype(F32)
            if j == 0:
                results.append(total)
            else:
                bit = last_bit(j, order)
                arrived[j ^ bit].append(swap(total.astype(BF16), "tp", bit))
    return results


def ring_gather(piece, place, buffer):
    size = lax.axis_size("seq")
    me = lax.axis_index("seq")
    current = piece
    buffer = place(buffer, current, me)
    for step in range(1, size):
        current = onward(current, "seq")
        buffer = place(buffer, current, (me - step) % size)
    return buffer, current


def ring_scatter(block):
    size = lax.axis_size("seq")
    me = lax.axis_index("seq")
    total = block((me - 1) % size)
    for step in range(1, size):
        arrived = onward(total.astype(BF16), "seq")
        total = arrived.astype(F32) + block((me - 1 - step) % size).astype(F32)
    return total


def all_sum(value, axis):
    size = lax.axis_size(axis)
    bit = 1
    while bit < size:
        value = value + swap(value, axis, bit)
        bit *= 2
    return value


def rope(vectors, cosine, sine_up, sine_down):
    return (
        vectors * cosine
        + pltpu.roll(vectors, ROT // 2, 1) * sine_up
        + pltpu.roll(vectors, HD - ROT // 2, 1) * sine_down
    )


def norm_project_kernel(
    x0, x1, x2, x3, gain1, shift1, gain2, shift2, weight, bias, cosine, sine_up, sine_down, *rest
):
    normal, first, second, queries, keys, values, scratch = rest[-7:]
    step = pl.program_id(0)
    for number, x_ref in enumerate((x0, x1, x2, x3)):

        @pl.when(step == number)
        def _(x_ref=x_ref):
            scratch[...] = x_ref[...].astype(F32)

    x = scratch[...]
    centred = x - jnp.mean(x, axis=-1, keepdims=True)
    variance = jnp.mean(centred * centred, axis=-1, keepdims=True)
    n = centred * lax.rsqrt(variance + EPSILON)
    normal[...] = n.astype(BF16)
    second[...] = (n * gain2[...] + shift2[...]).astype(BF16)
    one = (n * gain1[...] + shift1[...]).astype(BF16)
    first[...] = one
    joined = jnp.dot(one, weight[...], preferred_element_type=F32) + bias[...]
    tables = (cosine[...], sine_up[...], sine_down[...])
    for head in range(queries.shape[0]):
        at = head * 3 * HD
        queries[head, 0, 0] = rope(joined[:, at : at + HD], *tables).astype(BF16)
        keys[head, 0, 0] = rope(joined[:, at + HD : at + 2 * HD], *tables).astype(BF16)
        values[head, 0, 0] = joined[:, at + 2 * HD : at + 3 * HD].astype(BF16)


def norm_project(j, entries, rows_in_all, gains, weight, bias, tables, held):
    rows = entries[1][0].shape[0] * (1 if entries[1][1] == 0 else 1)
    model_width, joined_cols = weight.shape
    heads = joined_cols // (3 * HD)
    size = lax.axis_size("tp")
    tile = rows_in_all // (2 * size)
    half = tile // 2
    steps = 4

    def fixed(block, *at):
        return pl.BlockSpec(block, lambda i: at)

    x_specs = [fixed((half, model_width), part, 0) for _, part in entries]
    row = fixed((1, model_width), 0, 0)
    table = pl.BlockSpec((half, HD), lambda i: (j * 4 + i, 0))
    wide = pl.BlockSpec((half, model_width), lambda i: (j * 4 + i, 0))
    narrow = pl.BlockSpec((heads, 1, 1, half, HD), lambda i: (0, j, i // 2, i % 2, 0))
    operands = [item for item, _ in entries] + list(gains) + [weight, bias] + list(tables)
    in_specs = (
        x_specs
        + [row] * 4
        + [fixed((model_width, joined_cols), 0, 0), fixed((1, joined_cols), 0, 0)]
        + [table] * 3
    )
    aliases = {}
    if held is not None:
        aliases = {len(operands) + k: k for k in range(6)}
        operands += list(held)
        in_specs += [ANY] * 6
    wide_shape = jax.ShapeDtypeStruct((rows_in_all, model_width), BF16)
    narrow_shape = jax.ShapeDtypeStruct((heads, size, 2, tile, HD), BF16)
    return pl.pallas_call(
        norm_project_kernel,
        grid=(steps,),
        in_specs=in_specs,
        out_specs=[wide] * 3 + [narrow] * 3,
        out_shape=[wide_shape] * 3 + [narrow_shape] * 3,
        scratch_shapes=[pltpu.VMEM((half, model_width), F32)],
        input_output_aliases=aliases,
        compiler_params=params(1),
        cost_estimate=cost(
            2 * 2 * tile * model_width * joined_cols, 2 * tile * model_width * 8 + weight.size * 2
        ),
        name="norm_project",
    )(*operands)


def attend_kernel(meta, q_ref, k_ref, v_ref, begin_ref, out_ref, lse_ref):
    seq_at, block = pl.program_id(1), pl.program_id(2)
    rows, blocks = q_ref.shape[-2], k_ref.shape[1]
    here = meta[0]
    low = meta[1 + seq_at * blocks + block]
    query = q_ref[0, 0, 0]
    begin = begin_ref[...]
    query_places = block * rows + lax.broadcasted_iota(jnp.int32, (rows, 1), 0)
    factor = LOG2E / math.sqrt(HD)

    def step(number, carry):
        top, total, mixed = carry
        key = k_ref[0, number ^ here, 0]
        value = v_ref[0, number ^ here, 0]
        scores = (
            lax.dot_general(query, key, CONTRACT_LAST, preferred_element_type=F32) * factor
        )
        key_places = number * rows + lax.broadcasted_iota(jnp.int32, (1, rows), 1)
        allowed = (key_places >= begin) & (key_places <= query_places)
        scores = jnp.where(allowed, scores, NEGATIVE)
        new_top = jnp.maximum(top, jnp.max(scores, axis=-1, keepdims=True))
        weights = jnp.exp2(scores - new_top)
        shrink = jnp.exp2(top - new_top)
        total = total * shrink + jnp.sum(weights, axis=-1, keepdims=True)
        mixed = mixed * shrink + jnp.dot(
            weights.astype(BF16), value, preferred_element_type=F32
        )
        return new_top, total, mixed

    top, total, mixed = lax.fori_loop(
        low,
        block + 1,
        step,
        (
            jnp.full((rows, 1), NEGATIVE, F32),
            jnp.zeros((rows, 1), F32),
            jnp.zeros((rows, HD), F32),
        ),
    )
    out_ref[...] = (mixed / total).astype(BF16)[None, None]
    log_sum = top + jnp.log(total) * LOG2E
    lse_ref[...] = jnp.broadcast_to(log_sum, (rows, HD)).T[:1][None, None, None]


def attend(meta, queries, keys, values, begin_column):
    heads, blocks, seqs, rows, _ = queries.shape

    def here(meta, i):
        return i ^ meta[0]

    one = pl.BlockSpec((1, 1, 1, rows, HD), lambda h, s, i, meta: (h, here(meta, i), s, 0, 0))
    full = pl.BlockSpec((1, blocks, 1, rows, HD), lambda h, s, i, meta: (h, 0, s, 0, 0))
    pairs = heads * seqs * blocks * (blocks + 1) // 2
    return pl.pallas_call(
        attend_kernel,
        grid_spec=pltpu.PrefetchScalarGridSpec(
            num_scalar_prefetch=1,
            grid=(heads, seqs, blocks),
            in_specs=[
                one,
                full,
                full,
                pl.BlockSpec((rows, 1), lambda h, s, i, meta: (here(meta, i) * seqs + s, 0)),
            ],
            out_specs=[
                pl.BlockSpec((1, 1, rows, HD), lambda h, s, i, meta: (here(meta, i), s, 0, h)),
                pl.BlockSpec(
                    (1, 1, 1, 1, rows), lambda h, s, i, meta: (h, here(meta, i), s, 0, 0)
                ),
            ],
        ),
        out_shape=[
            jax.ShapeDtypeStruct((blocks, seqs, rows, heads * HD), BF16),
            jax.ShapeDtypeStruct((heads, blocks, seqs, 1, rows), F32),
        ],
        compiler_params=params(3),
        cost_estimate=cost(
            pairs * 8 * rows * rows * HD, 4 * queries.size * 2, 4 * pairs * rows * rows
        ),
        name="attend",
    )(meta, queries, keys, values, begin_column)


def attend_back_kernel(
    meta,
    q_ref,
    k_ref,
    v_ref,
    grad_ref,
    out_ref,
    lse_ref,
    begin_ref,
    cosine,
    sine_up,
    sine_down,
    joined_ref,
    sum_ref,
    query_grad,
    delta,
):
    seq_at, block = pl.program_id(1), pl.program_id(2)
    blocks, rows = q_ref.shape[1], q_ref.shape[-2]
    here = meta[0]
    high = meta[1 + (2 + seq_at) * blocks + block]
    scaling = 1.0 / math.sqrt(HD)

    @pl.when(block == 0)
    def _():
        query_grad[...] = jnp.zeros_like(query_grad)

        def inner(j, carry):
            product = grad_ref[j, 0].astype(F32) * out_ref[j, 0].astype(F32)
            delta[j] = jnp.sum(product.T, axis=0, keepdims=True)
            return carry

        lax.fori_loop(0, blocks, inner, 0)

    own = block ^ here
    key = k_ref[0, own, 0]
    value = v_ref[0, own, 0]
    key_places = block * rows + lax.broadcasted_iota(jnp.int32, (rows, 1), 0)

    def step(number, carry):
        key_grad, value_grad = carry
        at = number ^ here
        query = q_ref[0, at, 0]
        grad = grad_ref[at, 0]
        scores = lax.dot_general(key, query, CONTRACT_LAST, preferred_element_type=F32)
        scores = scores * (scaling * LOG2E) - lse_ref[0, at, 0]
        query_places = number * rows + lax.broadcasted_iota(jnp.int32, (1, rows), 1)
        allowed = (key_places >= begin_ref[at, 0]) & (key_places <= query_places)
        weights = jnp.where(allowed, jnp.exp2(scores), 0.0)
        weight_grad = lax.dot_general(value, grad, CONTRACT_LAST, preferred_element_type=F32)
        score_grad = (weights * (weight_grad - delta[at]) * scaling).astype(BF16)
        value_grad = value_grad + jnp.dot(
            weights.astype(BF16), grad, preferred_element_type=F32
        )
        key_grad = key_grad + jnp.dot(score_grad, query, preferred_element_type=F32)
        query_grad[at] = query_grad[at] + lax.dot_general(
            score_grad, key, CONTRACT_FIRST, preferred_element_type=F32
        )
        return key_grad, value_grad

    empty = jnp.zeros((rows, HD), F32)
    key_grad, value_grad = lax.fori_loop(block, high + 1, step, (empty, empty))
    tables = (cosine[own, 0], -sine_up[own, 0], -sine_down[own, 0])
    joined_ref[own, 0, :, HD : 2 * HD] = rope(key_grad, *tables).astype(BF16)
    joined_ref[own, 0, :, 2 * HD :] = value_grad.astype(BF16)

    @pl.when(block == blocks - 1)
    def _():
        def inner(j, carry):
            tables = (cosine[j, 0], -sine_up[j, 0], -sine_down[j, 0])
            joined_ref[j, 0, :, :HD] = rope(query_grad[j], *tables).astype(BF16)
            return carry + jnp.sum(joined_ref[j, 0].astype(F32), axis=0, keepdims=True)

        sum_ref[0, 0] = lax.fori_loop(0, blocks, inner, jnp.zeros((1, 3 * HD), F32))


def attend_back(meta, queries, keys, values, grad, out, log_sums, begin_row, tables):
    heads, blocks, seqs, rows, _ = queries.shape
    head_spec = pl.BlockSpec((1, blocks, 1, rows, HD), lambda h, s, i, meta: (h, 0, s, 0, 0))
    side = pl.BlockSpec((blocks, 1, rows, HD), lambda h, s, i, meta: (0, s, 0, h))
    table = pl.BlockSpec((blocks, 1, rows, HD), lambda h, s, i, meta: (0, s, 0, 0))
    tables = [item.reshape(blocks, seqs, rows, HD) for item in tables]
    pairs = heads * seqs * blocks * (blocks + 1) // 2
    return pl.pallas_call(
        attend_back_kernel,
        grid_spec=pltpu.PrefetchScalarGridSpec(
            num_scalar_prefetch=1,
            grid=(heads, seqs, blocks),
            in_specs=[
                head_spec,
                head_spec,
                head_spec,
                side,
                side,
                pl.BlockSpec((1, blocks, 1, 1, rows), lambda h, s, i, meta: (h, 0, s, 0, 0)),
                pl.BlockSpec((blocks, 1, 1, rows), lambda h, s, i, meta: (0, s, 0, 0)),
                table,
                table,
                table,
            ],
            out_specs=[
                pl.BlockSpec((blocks, 1, rows, 3 * HD), lambda h, s, i, meta: (0, s, 0, h)),
                pl.BlockSpec((1, 1, 1, 3 * HD), lambda h, s, i, meta: (h, s, 0, 0)),
            ],
            scratch_shapes=[
                pltpu.VMEM((blocks, rows, HD), F32),
                pltpu.VMEM((blocks, 1, rows), F32),
            ],
        ),
        out_shape=[
            jax.ShapeDtypeStruct((blocks, seqs, rows, heads * 3 * HD), BF16),
            jax.ShapeDtypeStruct((heads, seqs, 1, 3 * HD), F32),
        ],
        compiler_params=params(3),
        cost_estimate=cost(
            pairs * 20 * rows * rows * HD, 12 * queries.size * 2, 4 * pairs * rows * rows
        ),
        name="attend_back",
    )(meta, queries, keys, values, grad, out, log_sums, begin_row, *tables)


def expand_kernel(rows_ref, weight, bias, activated, slope):
    cols = weight.shape[1]
    chunk = min(256, cols)
    left = rows_ref[...]
    for at in range(0, cols, chunk):
        pre = (
            jnp.dot(left, weight[:, at : at + chunk], preferred_element_type=F32)
            + bias[:, at : at + chunk]
        )
        share = 0.5 + 0.5 * lax.erf(pre * math.sqrt(0.5))
        density = jnp.exp2(pre * pre * (-0.5 * LOG2E)) * (1.0 / math.sqrt(2.0 * math.pi))
        activated[:, at : at + chunk] = (pre * share).astype(BF16)
        slope[:, at : at + chunk] = (share + pre * density).astype(BF16)


def expand(normed, weight, bias):
    rows, model_width = normed.shape
    cols = weight.shape[1]
    tile = 256
    out = pl.BlockSpec((tile, cols), lambda i: (i, 0))
    return pl.pallas_call(
        expand_kernel,
        grid=(rows // tile,),
        in_specs=[
            pl.BlockSpec((tile, model_width), lambda i: (i, 0)),
            pl.BlockSpec((model_width, cols), lambda i: (0, 0)),
            pl.BlockSpec((1, cols), lambda i: (0, 0)),
        ],
        out_specs=[out, out],
        out_shape=[jax.ShapeDtypeStruct((rows, cols), BF16)] * 2,
        compiler_params=params(1),
        cost_estimate=cost(
            2 * rows * model_width * cols,
            2 * (rows * model_width + weight.size + 2 * rows * cols),
            2 * rows * cols,
        ),
        name="expand",
    )(normed, weight, bias)


def output_kernel(att_ref, act_ref, dense, contract, keep, send):
    step = pl.program_id(0)
    total = jnp.dot(att_ref[...], dense[...], preferred_element_type=F32) + jnp.dot(
        act_ref[...], contract[...], preferred_element_type=F32
    )
    total = total.astype(BF16)
    half = pl.num_programs(0) // 2

    @pl.when(step < half)
    def _():
        keep[...] = total

    @pl.when(step >= half)
    def _():
        send[...] = total


def kept_and_sent(tile, steps, width):
    half = steps // 2
    return [
        pl.BlockSpec((tile, width), lambda i: (jnp.minimum(i, half - 1), 0)),
        pl.BlockSpec((tile, width), lambda i: (jnp.maximum(i - half, 0), 0)),
    ]


def output_piece(j, attended, activated, dense, contract):
    rows = attended.shape[0] // lax.axis_size("tp")
    width = dense.shape[1]
    tile = rows // 4
    shape = jax.ShapeDtypeStruct((rows // 2, width), BF16)
    return pl.pallas_call(
        output_kernel,
        grid=(4,),
        in_specs=[
            pl.BlockSpec((tile, attended.shape[1]), lambda i: (j * 4 + i, 0)),
            pl.BlockSpec((tile, activated.shape[1]), lambda i: (j * 4 + i, 0)),
            pl.BlockSpec(dense.shape, lambda i: (0, 0)),
            pl.BlockSpec(contract.shape, lambda i: (0, 0)),
        ],
        out_specs=kept_and_sent(tile, 4, width),
        out_shape=[shape, shape],
        compiler_params=params(1),
        cost_estimate=cost(
            2 * rows * width * (dense.shape[0] + contract.shape[0]),
            2 * (dense.size + contract.size + rows * (width + attended.shape[1] + activated.shape[1])),
        ),
        name="output_piece",
    )(attended, activated, dense, contract)


def pre_grad_kernel(grad_ref, slope, contract, out, sums):
    @pl.when(pl.program_id(0) == 0)
    def _():
        sums[...] = jnp.zeros_like(sums)

    left = grad_ref[...]
    cols = contract.shape[0]
    chunk = min(256, cols)
    for at in range(0, cols, chunk):
        part = lax.dot_general(
            left, contract[at : at + chunk, :], CONTRACT_LAST, preferred_element_type=F32
        )
        part = (part * slope[:, at : at + chunk].astype(F32)).astype(BF16)
        out[:, at : at + chunk] = part
        sums[:, at : at + chunk] += jnp.sum(part.astype(F32), axis=0, keepdims=True)


def pre_grad_of(grad, slope, contract):
    rows, width = grad.shape
    cols = contract.shape[0]
    tile = 256
    return pl.pallas_call(
        pre_grad_kernel,
        grid=(rows // tile,),
        in_specs=[
            pl.BlockSpec((tile, width), lambda i: (i, 0)),
            pl.BlockSpec((tile, cols), lambda i: (i, 0)),
            pl.BlockSpec((cols, width), lambda i: (0, 0)),
        ],
        out_specs=[
            pl.BlockSpec((tile, cols), lambda i: (i, 0)),
            pl.BlockSpec((1, cols), lambda i: (0, 0)),
        ],
        out_shape=[
            jax.ShapeDtypeStruct((rows, cols), BF16),
            jax.ShapeDtypeStruct((1, cols), F32),
        ],
        compiler_params=params(1),
        cost_estimate=cost(
            2 * rows * width * cols, 2 * (rows * width + contract.size + 2 * rows * cols)
        ),
        name="pre_grad",
    )(grad, slope, contract)


def normed_grad_kernel(joined, pre, normal, joined_weight, expand_weight, gain1, gain2, keep, send, sums):
    step = pl.program_id(0)
    half = pl.num_programs(0) // 2

    @pl.when(step == 0)
    def _():
        sums[...] = jnp.zeros_like(sums)

    width = joined_weight.shape[0]
    chunk = min(512, width)
    for at in range(0, width, chunk):
        cols = slice(at, at + chunk)
        first = lax.dot_general(
            joined[...], joined_weight[cols, :], CONTRACT_LAST, preferred_element_type=F32
        )
        second = lax.dot_general(
            pre[...], expand_weight[cols, :], CONTRACT_LAST, preferred_element_type=F32
        )
        n = normal[:, cols].astype(F32)
        sums[0:1, cols] += jnp.sum(first * n, axis=0, keepdims=True)
        sums[1:2, cols] += jnp.sum(first, axis=0, keepdims=True)
        sums[2:3, cols] += jnp.sum(second * n, axis=0, keepdims=True)
        sums[3:4, cols] += jnp.sum(second, axis=0, keepdims=True)
        total = (first * gain1[:, cols] + second * gain2[:, cols]).astype(BF16)

        @pl.when(step < half)
        def _(total=total, cols=cols):
            keep[:, cols] = total

        @pl.when(step >= half)
        def _(total=total, cols=cols):
            send[:, cols] = total


def normed_grad_piece(j, joined, pre, normal, joined_weight, expand_weight, gain1, gain2):
    rows = joined.shape[0] // lax.axis_size("tp")
    width = joined_weight.shape[0]
    tile = rows // 4
    shape = jax.ShapeDtypeStruct((rows // 2, width), BF16)
    return pl.pallas_call(
        normed_grad_kernel,
        grid=(4,),
        in_specs=[
            pl.BlockSpec((tile, joined.shape[1]), lambda i: (j * 4 + i, 0)),
            pl.BlockSpec((tile, pre.shape[1]), lambda i: (j * 4 + i, 0)),
            pl.BlockSpec((tile, width), lambda i: (j * 4 + i, 0)),
            pl.BlockSpec(joined_weight.shape, lambda i: (0, 0)),
            pl.BlockSpec(expand_weight.shape, lambda i: (0, 0)),
            pl.BlockSpec((1, width), lambda i: (0, 0)),
            pl.BlockSpec((1, width), lambda i: (0, 0)),
        ],
        out_specs=kept_and_sent(tile, 4, width) + [pl.BlockSpec((8, width), lambda i: (0, 0))],
        out_shape=[shape, shape, jax.ShapeDtypeStruct((8, width), F32)],
        compiler_params=params(1),
        cost_estimate=cost(
            2 * rows * width * (joined.shape[1] + pre.shape[1]),
            2 * (joined_weight.size + expand_weight.size)
            + 2 * rows * (2 * width + joined.shape[1] + pre.shape[1]),
        ),
        name="normed_grad_piece",
    )(joined, pre, normal, joined_weight, expand_weight, gain1, gain2)


def per_device(
    block_input,
    first_norm_gain,
    first_norm_bias,
    second_norm_gain,
    second_norm_bias,
    query_key_value,
    query_key_value_bias,
    attention_dense,
    attention_dense_bias,
    expand_weight,
    expand_bias,
    contract_weight,
    contract_bias,
    document_starts,
    output_grad,
):
    seqs, tile, model_width = block_input.shape
    tiles = lax.axis_size("tp")
    groups = lax.axis_size("seq")
    core = lax.axis_index("branch")
    here = lax.axis_index("tp")
    first_core = core == 0
    length = tile * tiles
    rows_in_all = length * seqs
    share = query_key_value.shape[0]

    def by_core(mine, others):
        return jnp.where(first_core, mine, others), jnp.where(first_core, others, mine)

    def halves_of(value, axis):
        size = value.shape[axis] // 2
        return (
            lax.dynamic_slice_in_dim(value, core * size, size, axis),
            lax.dynamic_slice_in_dim(value, (1 - core) * size, size, axis),
        )

    starts = jnp.stack(
        [
            lax.dynamic_index_in_dim(document_starts, core, 0, False),
            lax.dynamic_index_in_dim(document_starts, 1 - core, 0, False),
        ]
    )
    places = (
        (jnp.arange(tiles, dtype=jnp.int32) ^ here)[:, None] * tile
        + jnp.arange(tile, dtype=jnp.int32)[None, :]
    )[:, None, :]
    started = starts[None, :, None, :] <= places[..., None]
    begin_at = jnp.max(jnp.where(started, starts[None, :, None, :], 0), axis=-1)
    relative = (places - begin_at).astype(F32).reshape(rows_in_all, 1)
    exponent = jnp.arange(ROT // 2, dtype=F32) * (2.0 / ROT)
    angles = relative * (ROPE_BASE ** (-exponent))
    cosines, sines = jnp.cos(angles), jnp.sin(angles)
    rest = jnp.zeros((rows_in_all, HD - ROT), F32)
    nothing = jnp.zeros_like(sines)
    tables = (
        jnp.concatenate([cosines, cosines, rest + 1.0], axis=1),
        jnp.concatenate([nothing, sines, rest], axis=1),
        jnp.concatenate([-sines, nothing, rest], axis=1),
    )
    numbers = jnp.arange(tiles, dtype=jnp.int32)
    edges = numbers[None, :] * tile
    edge_begin = jnp.max(
        jnp.where(starts[:, None, :] <= edges[..., None], starts[:, None, :], 0), axis=-1
    )
    lows = edge_begin // tile
    highs = jnp.sum((lows[:, None, :] <= numbers[None, :, None]).astype(jnp.int32), axis=-1) - 1
    meta = jnp.concatenate(
        [here[None].astype(jnp.int32), lows.reshape(-1), highs.reshape(-1)]
    ).astype(jnp.int32)

    def row_piece(weight):
        mine, others = halves_of(weight, 1)
        return jnp.stack(by_core(mine, swap(others, "branch", 1)))

    def gather_rows(piece):
        buffer = jnp.zeros((2, groups) + piece.shape[1:], BF16)

        def place(buffer, item, at):
            return lax.dynamic_update_slice_in_dim(buffer, item[:, None], at, 1)

        buffer, last = ring_gather(piece, place, buffer)
        return buffer.reshape(-1, piece.shape[-1]), last

    def column_piece(weight):
        mine, others = halves_of(weight, 0)
        return jnp.stack(by_core(mine, swap(others, "branch", 1)))

    def gather_columns(piece):
        buffer = jnp.zeros((piece.shape[1], model_width), BF16)

        def place(buffer, item, at):
            for c in range(2):
                buffer = lax.dynamic_update_slice_in_dim(
                    buffer, item[c], (c * groups + at) * share, 1
                )
            return buffer

        return ring_gather(piece, place, buffer)

    joined_weight, last = gather_rows(row_piece(query_key_value))
    dense_full, last = gather_columns(after(column_piece(attention_dense), last))
    expand_full, last = gather_rows(after(row_piece(expand_weight), last))
    contract_full, last = gather_columns(after(column_piece(contract_weight), last))
    joined_bias = halves_of(query_key_value_bias, 0)[0].astype(F32)[None]
    hidden_bias = halves_of(expand_bias, 0)[0].astype(F32)[None]

    def own_and_other(value):
        return (
            lax.dynamic_index_in_dim(value, core, 0, False),
            lax.dynamic_index_in_dim(value, 1 - core, 0, False),
        )

    input_own, input_other = own_and_other(block_input)
    grad_own, grad_other = own_and_other(output_grad)
    whole, halves = gather_tiles(input_own)
    entries = both_cores(whole, halves)
    entries[0][2:] = [(input_other, 0), (input_other, 1)]
    last_input = [item for j in sorted(halves) for item in halves[j]] or [whole[tiles - 1]]
    whole, halves = gather_tiles(after(grad_own, tuple(last_input)))
    grad_entries = both_cores(whole, halves)
    grad_entries[0] = [(grad_own, 0), (grad_own, 1), (grad_other, 0), (grad_other, 1)]
    half = tile // 2
    grad_rows = jnp.concatenate(
        [
            item[part * half : (part + 1) * half]
            for j in range(tiles)
            for item, part in grad_entries[j]
        ]
    )

    gain1 = first_norm_gain.astype(F32)[None]
    gain2 = second_norm_gain.astype(F32)[None]
    gains = (
        gain1,
        first_norm_bias.astype(F32)[None],
        gain2,
        second_norm_bias.astype(F32)[None],
    )
    held = None
    for j in range(tiles):
        held = norm_project(
            j, entries[j], rows_in_all, gains, joined_weight, joined_bias, tables, held
        )
    normal, first_normed, second_normed, queries, keys, values = held
    attended, log_sums = attend(
        meta, queries, keys, values, begin_at.reshape(rows_in_all, 1)
    )
    attended_flat = attended.reshape(rows_in_all, -1)
    activated, slope = expand(second_normed, expand_full, hidden_bias)

    def reduced(pieces):
        summed = {}
        for j in sorted(pieces, key=lambda j: -bin(j).count("1")):
            keep, send = pieces[j]
            summed[j] = (keep.astype(F32) + swap(send, "branch", 1).astype(F32)).astype(BF16)
        return jnp.concatenate(reduce_tiles(summed))

    order = sorted(range(tiles), key=lambda j: -bin(j).count("1"))
    branch_sum = reduced(
        {j: output_piece(j, attended_flat, activated, dense_full, contract_full) for j in order}
    )
    output_own = (
        input_own.astype(F32)
        + branch_sum
        + attention_dense_bias.astype(F32)
        + contract_bias.astype(F32)
    ).astype(BF16)
    block_output = jnp.stack(by_core(output_own, swap(output_own, "branch", 1)))

    def weight_grad(left, right):
        return lax.dot_general(left, right, CONTRACT_FIRST, preferred_element_type=F32).astype(BF16)

    def scatter_rows(part):
        blocks = part.reshape(2, groups, share, part.shape[1])

        def block(at):
            return lax.dynamic_index_in_dim(blocks, at, 1, False)

        total = ring_scatter(block)
        mine, others = halves_of(total, 0)
        return jnp.concatenate(by_core(mine[0], swap(others[0], "branch", 1)), axis=1)

    def scatter_columns(part):
        def block(at):
            return jnp.stack(
                [
                    lax.dynamic_slice_in_dim(part, (c * groups + at) * share, share, 1)
                    for c in range(2)
                ]
            )

        total = ring_scatter(block)
        mine, others = halves_of(total, 0)
        return jnp.concatenate(by_core(mine[0], swap(others[0], "branch", 1)), axis=0)

    contract_grad = scatter_columns(weight_grad(activated, grad_rows))
    dense_grad = scatter_columns(weight_grad(attended_flat, grad_rows))
    attended_grad = lax.dot_general(
        grad_rows, dense_full, CONTRACT_LAST, preferred_element_type=F32
    ).astype(BF16)
    joined_grad, joined_sums = attend_back(
        meta,
        queries,
        keys,
        values,
        attended_grad.reshape(attended.shape),
        attended,
        log_sums,
        begin_at[:, :, None, :],
        tables,
    )
    joined_grad = joined_grad.reshape(rows_in_all, -1)
    pre_grad, pre_sums = pre_grad_of(grad_rows, slope, contract_full)
    expand_grad = scatter_rows(weight_grad(second_normed, pre_grad))
    query_key_value_grad = scatter_rows(weight_grad(first_normed, joined_grad))
    normed_pieces = {}
    sums = jnp.zeros((8, model_width), F32)
    for j in order:
        keep, send, part = normed_grad_piece(
            j, joined_grad, pre_grad, normal, joined_weight, expand_full, gain1, gain2
        )
        normed_pieces[j] = (keep, send)
        sums = sums + part
    term_sum = reduced(normed_pieces)
    x = input_own.astype(F32)
    centred = x - jnp.mean(x, axis=-1, keepdims=True)
    rate = lax.rsqrt(jnp.mean(centred * centred, axis=-1, keepdims=True) + EPSILON)
    n = centred * rate
    terms = rate * (
        term_sum
        - jnp.mean(term_sum, axis=-1, keepdims=True)
        - n * jnp.mean(term_sum * n, axis=-1, keepdims=True)
    )
    grad_own_wide = grad_own.astype(F32)
    input_grad_own = (grad_own_wide + terms).astype(BF16)
    input_grad = jnp.stack(by_core(input_grad_own, swap(input_grad_own, "branch", 1)))

    joined_part = jnp.sum(joined_sums, axis=1).reshape(-1)
    hidden_part = pre_sums[0]
    small = jnp.concatenate(
        [
            sums[:4].reshape(-1),
            jnp.sum(grad_own_wide, axis=0),
            joined_part,
            hidden_part,
        ]
    )
    small = all_sum(small, "seq")
    everywhere = 5 * model_width
    per_core = small[everywhere:]
    both = jnp.stack(by_core(per_core, swap(per_core, "branch", 1)))
    query_key_value_bias_grad = both[:, : joined_part.shape[0]].reshape(-1)
    expand_bias_grad = both[:, joined_part.shape[0] :].reshape(-1)
    shared = all_sum(all_sum(small[:everywhere], "tp"), "branch").reshape(5, model_width)
    return (
        block_output,
        input_grad,
        shared[0],
        shared[1],
        shared[2],
        shared[3],
        query_key_value_grad,
        query_key_value_bias_grad,
        dense_grad,
        shared[4],
        expand_grad,
        expand_bias_grad,
        contract_grad,
        shared[4],
    )


def solution(mesh):
    in_specs = (
        P("seq", "tp", None),
        P(),
        P(),
        P(),
        P(),
        P(("branch", "seq"), "tp"),
        P("tp"),
        P("tp", ("branch", "seq")),
        P(),
        P(("branch", "seq"), "tp"),
        P("tp"),
        P("tp", ("branch", "seq")),
        P(),
        P("seq", None),
        P("seq", "tp", None),
    )
    out_specs = (
        P("seq", "tp", None),
        P("seq", "tp", None),
        P(),
        P(),
        P(),
        P(),
        P(("branch", "seq"), "tp"),
        P("tp"),
        P("tp", ("branch", "seq")),
        P(),
        P(("branch", "seq"), "tp"),
        P("tp"),
        P("tp", ("branch", "seq")),
        P(),
    )
    return jax.shard_map(
        per_device, mesh=mesh, in_specs=in_specs, out_specs=out_specs, check_vma=False
    )
```

```python
from functools import partial
import math

import jax
import jax.numpy as jnp
from jax import lax
from jax.experimental import pallas as pl
from jax.experimental.pallas import tpu as pltpu
from jax.sharding import PartitionSpec as P

HD = 128
ROT = 32


EPSILON = 1e-05
NEGATIVE = -1e30
ROPE_BASE = 10000.0
LOG2E = math.log2(math.e)
F32 = jnp.float32
BF16 = jnp.bfloat16
CONTRACT_LAST = (((1,), (1,)), ((), ()))
CONTRACT_FIRST = (((0,), (0,)), ((), ()))
VMEM_BYTES = 56 * 1024 * 1024
ANY = pl.BlockSpec(memory_space=pl.ANY)
HINT = 0.02


def cost(flops, moved, transcendentals=0):
    return pl.CostEstimate(
        flops=1 + int(flops * HINT), bytes_accessed=1 + int(moved * HINT), transcendentals=0
    )


def launch(
    kernel,
    operands,
    in_specs,
    grid,
    out_specs,
    out_shape,
    name,
    cost_estimate,
    prefetch=(),
    held=(),
    tokens=(),
    scratch_shapes=(),
):
    lead = len(prefetch) + len(operands)
    extra = len(held) + len(tokens)

    def body(*refs):
        kernel(*refs[:lead], *refs[lead + extra :])

    return pl.pallas_call(
        body,
        grid_spec=pltpu.PrefetchScalarGridSpec(
            num_scalar_prefetch=len(prefetch),
            grid=grid,
            in_specs=list(in_specs) + [ANY] * extra,
            out_specs=out_specs,
            scratch_shapes=list(scratch_shapes),
        ),
        out_shape=out_shape,
        input_output_aliases={lead + k: k for k in range(len(held))},
        compiler_params=pltpu.CompilerParams(
            dimension_semantics=("arbitrary",) * len(grid), vmem_limit_bytes=VMEM_BYTES
        ),
        cost_estimate=cost_estimate,
        name=name,
    )(*prefetch, *operands, *held, *tokens)


def hold(value, *tokens):
    def nothing(out):
        pass

    return launch(
        nothing,
        [],
        [],
        (1,),
        ANY,
        jax.ShapeDtypeStruct(value.shape, value.dtype),
        "hold",
        cost(1, 1),
        held=[value],
        tokens=tokens,
    )


def swap(value, axis, bit):
    size = lax.axis_size(axis)
    return lax.ppermute(value, axis, [(i, i ^ bit) for i in range(size)])


def onward(value, axis):
    size = lax.axis_size(axis)
    return lax.ppermute(value, axis, [(i, (i + 1) % size) for i in range(size)])


def bit_orders(size):
    bits = [1 << k for k in range(size.bit_length() - 1)]
    return (bits, bits[::-1])


def last_bit(number, order):
    return [bit for bit in order if number & bit][-1]


def gather_near(own, number):
    size = lax.axis_size("tp")
    bits = [1 << k for k in range(size.bit_length() - 1)]
    return {
        (bit, (n + number) % 2): swap(own[(n + number) % 2], "tp", bit)
        for n, bit in enumerate(bits)
    }


def hold_all(items, *tokens):
    return {key: hold(item, *tokens) for key, item in items.items()}


def in_pieces(first, second):
    items = {**first, **second}
    return {j: [items[j, 0], items[j, 1]] for j in sorted({j for j, _ in items})}


def gather_far(near):
    size = lax.axis_size("tp")
    pieces = dict(near)
    far = {}
    for j in sorted(range(1, size), key=lambda j: bin(j).count("1")):
        if j not in near:
            bits = [last_bit(j, order) for order in bit_orders(size)]
            far[j] = [swap(pieces[j ^ bit][q], "tp", bit) for q, bit in enumerate(bits)]
            pieces[j] = far[j]
    return far


def with_other_core(items):
    return items + [swap(item, "branch", 1) for item in items]


def add_up(items):
    total = items[0].astype(F32)
    for item in items[1:]:
        total = total + item.astype(F32)
    return total


class TileSum:
    def __init__(self):
        self.orders = bit_orders(lax.axis_size("tp"))
        size = lax.axis_size("tp")
        self.waiting = [(q, j) for j in range(1, size) for q in range(2)]
        self.expected = {(q, j): 0 for j in range(size) for q in range(2)}
        for q, j in self.waiting:
            self.expected[q, j ^ last_bit(j, self.orders[q])] += 1
        self.waiting.sort(key=lambda at: (-bin(at[1]).count("1"), not self.expected[at]))
        self.pieces = {}
        self.arrived = {}
        self.moving = []

    def part(self, q, j):
        half = self.pieces[j].shape[0] // 2
        return self.pieces[j][q * half : (q + 1) * half]

    def send(self, most=None):
        ready = [
            (q, j)
            for q, j in self.waiting
            if j in self.pieces and len(self.arrived.get((q, j), [])) == self.expected[q, j]
        ][:most]
        operands = []
        for q, j in ready:
            if (q, j) not in self.waiting:
                continue
            bit = last_bit(j, self.orders[q])
            both = (1 - q, j) in ready and last_bit(j, self.orders[1 - q]) == bit
            if both:
                operand = self.pieces[j]
                half = operand.shape[0] // 2
                for side in range(2):
                    if self.arrived.get((side, j)):
                        total = add_up([self.part(side, j)] + self.taken(side, j)).astype(BF16)
                        operand = lax.dynamic_update_slice_in_dim(operand, total, side * half, 0)
            else:
                operand = add_up([self.part(q, j)] + self.taken(q, j)).astype(BF16)
            sides = [0, 1] if both else [q]
            for side in sides:
                self.waiting.remove((side, j))
            self.moving.append((sides, j ^ bit, swap(operand, "tp", bit)))
            operands.append(operand)
        return operands

    def taken(self, q, j):
        half = self.pieces[j].shape[0] // 2
        return [
            item[at * half : (at + 1) * half] for item, at in self.arrived.get((q, j), [])
        ]

    def land(self, *tokens):
        items = []
        for sides, j, item in self.moving:
            item = hold(item, *tokens) if tokens else item
            items.append(item)
            for at, side in enumerate(sides):
                self.arrived.setdefault((side, j), []).append((item, at))
        self.moving = []
        return items

    def terms(self):
        return [[(self.pieces[0], 0), (self.pieces[0], 1)]] + [
            list(pair) for pair in zip(self.arrived[0, 0], self.arrived[1, 0])
        ]


def all_sum(value, axis):
    size = lax.axis_size(axis)
    bit = 1
    while bit < size:
        value = value + swap(value, axis, bit)
        bit *= 2
    return value


def rope(vectors, cosine, sine_up, sine_down):
    return (
        vectors * cosine
        + pltpu.roll(vectors, ROT // 2, 1) * sine_up
        + pltpu.roll(vectors, HD - ROT // 2, 1) * sine_down
    )


class Documents:
    def __init__(self, place, starts, seq_at, rows):
        self.row = place[1] ^ seq_at
        self.starts = starts
        self.rows = rows

    def begin(self, places):
        begin = jnp.zeros_like(places)
        for number in range(self.starts.shape[1]):
            start = self.starts[self.row, number]
            begin = jnp.where(places >= start, start, begin)
        return begin

    def first_key_block(self, block):
        return lax.div(self.begin(block * self.rows), jnp.int32(self.rows))

    def last_query_block(self, block, blocks):
        last = block
        for number in range(1, blocks):
            after = jnp.minimum(block + number, blocks - 1)
            last = jnp.where(self.first_key_block(after) <= block, jnp.maximum(last, after), last)
        return last


def table_kernel(place, starts, cosine, sine_up, sine_down):
    rows = cosine.shape[0]
    blocks = lax.axis_size("tp")
    step = pl.program_id(0)
    block, seq_at = lax.rem(step, blocks) ^ place[0], lax.div(step, blocks)
    places = block * rows + lax.broadcasted_iota(jnp.int32, (rows, 1), 0)
    begin = Documents(place, starts, seq_at, rows).begin(places)
    lane = lax.broadcasted_iota(jnp.int32, (1, HD), 1)
    half = ROT // 2
    number = jnp.where(lane < half, lane, lane - half).astype(F32)
    frequency = jnp.exp2(number * (-2.0 / ROT * math.log2(ROPE_BASE)))
    angles = (places - begin).astype(F32) * jnp.where(lane < ROT, frequency, 0.0)
    cosine[...] = jnp.cos(angles)
    sines = jnp.sin(angles)
    sine_up[...] = jnp.where((lane >= half) & (lane < ROT), sines, 0.0)
    sine_down[...] = jnp.where(lane < half, -sines, 0.0)


def rotary_tables(place, starts, rows, tokens):
    steps = 2 * lax.axis_size("tp")
    tile = rows // steps
    out = pl.BlockSpec((tile, HD), lambda i, *_: (i, 0))
    return launch(
        table_kernel,
        [],
        [],
        (steps,),
        [out] * 3,
        [jax.ShapeDtypeStruct((rows, HD), F32)] * 3,
        "rotary_tables",
        cost(rows * HD * 100, rows * HD * 48),
        prefetch=[place, starts],
        tokens=tokens,
    )


def place_kernel(x0, x1, x2, x3, out):
    step = pl.program_id(0)
    for number, x_ref in enumerate((x0, x1, x2, x3)):

        @pl.when(step == number)
        def _(x_ref=x_ref):
            out[...] = x_ref[...]


def half_of_piece(j):
    size = lax.axis_size("tp")
    return lambda i: ((lax.div(i, 2) * size + j) * 2 + lax.rem(i, 2), 0)


def place_piece(j, halves, rows_in_all, held, tokens=()):
    half, model_width = halves[0].shape
    return launch(
        place_kernel,
        halves,
        [whole_spec(halves[0])] * 4,
        (4,),
        pl.BlockSpec((half, model_width), half_of_piece(j)),
        jax.ShapeDtypeStruct((rows_in_all, model_width), BF16),
        "place_piece",
        cost(1, 4 * half * model_width * 4),
        held=held,
        tokens=tokens,
    )


def norm_kernel(x0, x1, x2, x3, gain1, shift1, gain2, shift2, *rest):
    normal, first, second, mark, scratch = rest[-5:]
    step = pl.program_id(0)
    mark[...] = jnp.zeros_like(mark)
    for number, x_ref in enumerate((x0, x1, x2, x3)):

        @pl.when(step == number)
        def _(x_ref=x_ref):
            scratch[...] = x_ref[...].astype(F32)

    x = scratch[...]
    centred = x - jnp.mean(x, axis=-1, keepdims=True)
    variance = jnp.mean(centred * centred, axis=-1, keepdims=True)
    n = centred * lax.rsqrt(variance + EPSILON)
    normal[...] = n.astype(BF16)
    first[...] = (n * gain1[...] + shift1[...]).astype(BF16)
    second[...] = (n * gain2[...] + shift2[...]).astype(BF16)


def norm_piece(j, halves, rows_in_all, gains, held, tokens):
    half, model_width = halves[0].shape
    wide = pl.BlockSpec((half, model_width), half_of_piece(j))
    return launch(
        norm_kernel,
        halves + list(gains),
        [whole_spec(item) for item in halves + list(gains)],
        (4,),
        [wide] * 3 + [pl.BlockSpec((8, HD), lambda i: (0, 0))],
        [jax.ShapeDtypeStruct((rows_in_all, model_width), BF16)] * 3
        + [jax.ShapeDtypeStruct((8, HD), F32)],
        "norm_piece",
        cost(4 * half * model_width * 16, 4 * half * model_width * 16),
        held=held,
        tokens=tokens,
        scratch_shapes=[pltpu.VMEM((half, model_width), F32)],
    )


def chunks_of(weight):
    groups, cores = weight.shape[:2]
    return [(z, c, c * groups + z) for c in range(cores) for z in range(groups)]


def row_product(left, weight, share):
    total = None
    for z, c, at in chunks_of(weight):
        part = jnp.dot(
            left[:, at * share : (at + 1) * share], weight[z, c], preferred_element_type=F32
        )
        total = part if total is None else total + part
    return total


def column_back(left, weight, share):
    total = None
    for z, c, at in chunks_of(weight):
        part = lax.dot_general(
            left[:, at * share : (at + 1) * share],
            weight[z, c],
            CONTRACT_LAST,
            preferred_element_type=F32,
        )
        total = part if total is None else total + part
    return total


def whole_spec(array, prefetched=0):
    rank = array.ndim
    return pl.BlockSpec(array.shape, lambda *at: (0,) * rank)


def project_kernel(normed, weight, bias, cosine, sine_up, sine_down, queries, keys, values):
    joined = row_product(normed, weight, weight.shape[2]) + bias[...]
    tables = (cosine[...], sine_up[...], sine_down[...])
    for head in range(queries.shape[0]):
        at = head * 3 * HD
        queries[head, 0, 0] = rope(joined[:, at : at + HD], *tables).astype(BF16)
        keys[head, 0, 0] = rope(joined[:, at + HD : at + 2 * HD], *tables).astype(BF16)
        values[head, 0, 0] = joined[:, at + 2 * HD : at + 3 * HD].astype(BF16)


def project(first, last, normed, weight, bias, tables, held):
    rows, model_width = normed.shape
    joined_cols = weight.shape[3]
    heads = joined_cols // (3 * HD)
    size = lax.axis_size("tp")
    tile = rows // (2 * size)
    table = pl.BlockSpec((tile, HD), lambda s, i: (s * size + first + i, 0))
    share = (last - first) / size
    return launch(
        project_kernel,
        [normed, weight, bias] + list(tables),
        [
            pl.BlockSpec((tile, model_width), lambda s, i: (s * size + first + i, 0)),
            whole_spec(weight),
            whole_spec(bias),
            table,
            table,
            table,
        ],
        (2, last - first),
        [pl.BlockSpec((heads, 1, 1, tile, HD), lambda s, i: (0, s, first + i, 0, 0))] * 3,
        [jax.ShapeDtypeStruct((heads, 2, size, tile, HD), BF16)] * 3,
        "project",
        cost(
            2 * rows * share * model_width * joined_cols,
            2 * (rows * share * (model_width + joined_cols) + weight.size),
        ),
        held=held,
    )


def attend_kernel(place, starts, q_ref, k_ref, v_ref, out_ref, send_ref, lse_ref):
    block = pl.program_id(1)
    heads, rows = q_ref.shape[0], q_ref.shape[-2]
    here = place[0]
    documents = Documents(place, starts, pl.program_id(0), rows)
    low = documents.first_key_block(block)
    query_places = block * rows + lax.broadcasted_iota(jnp.int32, (rows, 1), 0)
    begin = documents.begin(query_places)
    factor = LOG2E / math.sqrt(HD)

    def step(number, carry):
        key_places = number * rows + lax.broadcasted_iota(jnp.int32, (1, rows), 1)
        allowed = (key_places >= begin) & (key_places <= query_places)
        results = []
        for head in range(heads):
            top, total, mixed = carry[head]
            key = k_ref[head, 0, number ^ here]
            value = v_ref[head, 0, number ^ here]
            scores = lax.dot_general(
                q_ref[head, 0, 0], key, CONTRACT_LAST, preferred_element_type=F32
            )
            scores = jnp.where(allowed, scores * factor, NEGATIVE)
            new_top = jnp.maximum(top, jnp.max(scores, axis=-1, keepdims=True))
            weights = jnp.exp2(scores - new_top)
            shrink = jnp.exp2(top - new_top)
            total = total * shrink + jnp.sum(weights, axis=-1, keepdims=True)
            mixed = mixed * shrink + jnp.dot(
                weights.astype(BF16), value, preferred_element_type=F32
            )
            results.append((new_top, total, mixed))
        return tuple(results)

    empty = (
        jnp.full((rows, 1), NEGATIVE, F32),
        jnp.zeros((rows, 1), F32),
        jnp.zeros((rows, HD), F32),
    )
    results = lax.fori_loop(low, block + 1, step, (empty,) * heads)
    for head, (top, total, mixed) in enumerate(results):
        result = (mixed / total).astype(BF16)
        out_ref[0, 0, :, head * HD : (head + 1) * HD] = result
        send_ref[0, :, head * HD : (head + 1) * HD] = result
        log_sum = top + jnp.log(total) * LOG2E
        lse_ref[head, 0, 0] = jnp.broadcast_to(log_sum, (rows, HD)).T[:1]


def attend(place, starts, queries, keys, values, tokens):
    heads, seqs, blocks, rows, _ = queries.shape
    one = pl.BlockSpec(
        (heads, 1, 1, rows, HD), lambda s, i, place, starts: (0, s, i ^ place[0], 0, 0)
    )
    full = pl.BlockSpec((heads, 1, blocks, rows, HD), lambda s, i, *_: (0, s, 0, 0, 0))
    pairs = heads * seqs * blocks * (blocks + 1) // 2
    return launch(
        attend_kernel,
        [queries, keys, values],
        [one, full, full],
        (seqs, blocks),
        [
            pl.BlockSpec(
                (1, 1, rows, heads * HD), lambda s, i, place, starts: (s, i ^ place[0], 0, 0)
            ),
            pl.BlockSpec(
                (1, rows, heads * HD), lambda s, i, place, starts: ((s * i) ^ place[0], 0, 0)
            ),
            pl.BlockSpec(
                (heads, 1, 1, 1, rows), lambda s, i, place, starts: (0, s, i ^ place[0], 0, 0)
            ),
        ],
        [
            jax.ShapeDtypeStruct((seqs, blocks, rows, heads * HD), BF16),
            jax.ShapeDtypeStruct((blocks, rows, heads * HD), BF16),
            jax.ShapeDtypeStruct((heads, seqs, blocks, 1, rows), F32),
        ],
        "attend",
        cost(pairs * 30 * rows * rows * HD, 4 * queries.size * 2),
        prefetch=[place, starts],
        tokens=tokens,
    )


def attend_back_kernel(
    place,
    starts,
    q_ref,
    k_ref,
    v_ref,
    grad_ref,
    out_ref,
    lse_ref,
    cosine,
    sine_up,
    sine_down,
    joined_ref,
    send_ref,
    sum_ref,
    query_grad,
    delta,
):
    block = pl.program_id(1)
    heads, blocks, rows = q_ref.shape[0], q_ref.shape[2], q_ref.shape[-2]
    here = place[0]
    documents = Documents(place, starts, pl.program_id(0), rows)
    high = documents.last_query_block(block, blocks)
    scaling = 1.0 / math.sqrt(HD)

    @pl.when(block == 0)
    def _():
        query_grad[...] = jnp.zeros_like(query_grad)

        def inner(j, carry):
            for head in range(heads):
                cols = slice(head * HD, (head + 1) * HD)
                product = grad_ref[0, j, :, cols].astype(F32) * out_ref[0, j, :, cols].astype(F32)
                delta[head, j] = jnp.sum(product.T, axis=0, keepdims=True)
            return carry

        lax.fori_loop(0, blocks, inner, 0)

    own = block ^ here
    key_places = block * rows + lax.broadcasted_iota(jnp.int32, (rows, 1), 0)

    def step(number, carry):
        at = number ^ here
        query_places = number * rows + lax.broadcasted_iota(jnp.int32, (1, rows), 1)
        allowed = (key_places >= documents.begin(query_places)) & (key_places <= query_places)
        results = []
        for head in range(heads):
            key_grad, value_grad = carry[head]
            key = k_ref[head, 0, own]
            value = v_ref[head, 0, own]
            query = q_ref[head, 0, at]
            grad = grad_ref[0, at, :, head * HD : (head + 1) * HD]
            scores = lax.dot_general(key, query, CONTRACT_LAST, preferred_element_type=F32)
            scores = scores * (scaling * LOG2E) - lse_ref[head, 0, at]
            weights = jnp.where(allowed, jnp.exp2(scores), 0.0)
            weight_grad = lax.dot_general(value, grad, CONTRACT_LAST, preferred_element_type=F32)
            score_grad = (weights * (weight_grad - delta[head, at]) * scaling).astype(BF16)
            value_grad = value_grad + jnp.dot(
                weights.astype(BF16), grad, preferred_element_type=F32
            )
            key_grad = key_grad + jnp.dot(score_grad, query, preferred_element_type=F32)
            query_grad[head, at] = query_grad[head, at] + lax.dot_general(
                score_grad, key, CONTRACT_FIRST, preferred_element_type=F32
            )
            results.append((key_grad, value_grad))
        return tuple(results)

    empty = jnp.zeros((rows, HD), F32)
    results = lax.fori_loop(block, high + 1, step, ((empty, empty),) * heads)
    tables = (cosine[0, own], -sine_up[0, own], -sine_down[0, own])
    for head, (key_grad, value_grad) in enumerate(results):
        at = head * 3 * HD
        joined_ref[0, own, :, at + HD : at + 2 * HD] = rope(key_grad, *tables).astype(BF16)
        joined_ref[0, own, :, at + 2 * HD : at + 3 * HD] = value_grad.astype(BF16)

    @pl.when(block == blocks - 1)
    def _():
        def inner(j, carry):
            tables = (cosine[0, j], -sine_up[0, j], -sine_down[0, j])
            for head in range(heads):
                at = head * 3 * HD
                joined_ref[0, j, :, at : at + HD] = rope(query_grad[head, j], *tables).astype(BF16)
            send_ref[j] = joined_ref[0, j]
            return carry + jnp.sum(joined_ref[0, j].astype(F32), axis=0, keepdims=True)

        sum_ref[0] = lax.fori_loop(0, blocks, inner, jnp.zeros((1, heads * 3 * HD), F32))


def attend_back(place, starts, queries, keys, values, grad, out, log_sums, tables, tokens):
    heads, seqs, blocks, rows, _ = queries.shape
    joined_cols = heads * 3 * HD
    head_spec = pl.BlockSpec((heads, 1, blocks, rows, HD), lambda s, i, *_: (0, s, 0, 0, 0))
    side = pl.BlockSpec((1, blocks, rows, heads * HD), lambda s, i, *_: (s, 0, 0, 0))
    table = pl.BlockSpec((1, blocks, rows, HD), lambda s, i, *_: (s, 0, 0, 0))
    pairs = heads * seqs * blocks * (blocks + 1) // 2
    return launch(
        attend_back_kernel,
        [queries, keys, values, grad, out, log_sums]
        + [item.reshape(seqs, blocks, rows, HD) for item in tables],
        [
            head_spec,
            head_spec,
            head_spec,
            side,
            side,
            pl.BlockSpec((heads, 1, blocks, 1, rows), lambda s, i, *_: (0, s, 0, 0, 0)),
            table,
            table,
            table,
        ],
        (seqs, blocks),
        [
            pl.BlockSpec((1, blocks, rows, joined_cols), lambda s, i, *_: (s, 0, 0, 0)),
            pl.BlockSpec((blocks, rows, joined_cols), lambda s, i, *_: (0, 0, 0)),
            pl.BlockSpec((1, 1, joined_cols), lambda s, i, *_: (s, 0, 0)),
        ],
        [
            jax.ShapeDtypeStruct((seqs, blocks, rows, joined_cols), BF16),
            jax.ShapeDtypeStruct((blocks, rows, joined_cols), BF16),
            jax.ShapeDtypeStruct((seqs, 1, joined_cols), F32),
        ],
        "attend_back",
        cost(pairs * 50 * rows * rows * HD, 12 * queries.size * 2),
        prefetch=[place, starts],
        tokens=tokens,
        scratch_shapes=[
            pltpu.VMEM((heads, blocks, rows, HD), F32),
            pltpu.VMEM((heads, blocks, 1, rows), F32),
        ],
    )


def expand_kernel(normed, weight, bias, activated, send, slope):
    pre = row_product(normed, weight, weight.shape[2]) + bias[...]
    share = 0.5 + 0.5 * lax.erf(pre * math.sqrt(0.5))
    density = jnp.exp2(pre * pre * (-0.5 * LOG2E)) * (1.0 / math.sqrt(2.0 * math.pi))
    result = (pre * share).astype(BF16)
    activated[...] = result
    send[...] = result
    slope[...] = (share + pre * density).astype(BF16)


def later_half(tile, width, steps):
    half = steps // 2
    return pl.BlockSpec((tile, width), lambda i: (jnp.maximum(i - half, 0), 0))


def expand(normed, weight, bias, tokens):
    rows, model_width = normed.shape
    cols = weight.shape[3]
    tile = 512
    steps = rows // tile
    out = pl.BlockSpec((tile, cols), lambda i: (i, 0))
    shape = jax.ShapeDtypeStruct((rows, cols), BF16)
    return launch(
        expand_kernel,
        [normed, weight, bias],
        [pl.BlockSpec((tile, model_width), lambda i: (i, 0)), whole_spec(weight), whole_spec(bias)],
        (steps,),
        [out, later_half(tile, cols, steps), out],
        [shape, jax.ShapeDtypeStruct((rows // 2, cols), BF16), shape],
        "expand",
        cost(
            2 * rows * model_width * cols,
            2 * (rows * model_width + weight.size + 2 * rows * cols),
        ),
        tokens=tokens,
    )


def output_kernel(att, att_other, act, act_other, dense, dense_other, contract, contract_other, out):
    share = dense.shape[3]
    for n in range(dense.shape[0]):
        total = jnp.dot(att[...], dense[n, 0], preferred_element_type=F32)
        for left, right in (
            (att_other, dense_other),
            (act, contract),
            (act_other, contract_other),
        ):
            total = total + jnp.dot(left[...], right[n, 0], preferred_element_type=F32)
        out[:, n * share : (n + 1) * share] = total.astype(BF16)


def by_columns(weight):
    groups = weight.shape[0] // 2
    return pl.BlockSpec(
        (2, 1) + weight.shape[2:], lambda i: (lax.rem(i, groups), lax.div(i, groups), 0, 0)
    )


def output_piece(j, pieces, attended, activated, dense, contract, tokens):
    tile = attended[1].shape[0] // pieces
    groups, cores, _, share = dense[0].shape
    steps, share = groups * cores // 2, 2 * share
    lefts = [*attended, *activated]
    rights = [*dense, *contract]
    return launch(
        output_kernel,
        lefts + rights,
        [pl.BlockSpec((tile, item.shape[1]), lambda i: (j, 0)) for item in lefts]
        + [by_columns(item) for item in rights],
        (steps,),
        pl.BlockSpec((tile, share), lambda i: (0, i)),
        jax.ShapeDtypeStruct((tile, steps * share), BF16),
        "output_piece",
        cost(4 * tile * sum(item.size for item in rights), 4 * sum(item.size for item in rights)),
        tokens=tokens,
    )


def dense_back_kernel(grad_ref, att_ref, dense, out, blocks, total):
    step = pl.program_id(0)
    share = dense.shape[3]

    @pl.when(step == 0)
    def _():
        total[...] = jnp.zeros_like(total)

    out[...] = column_back(grad_ref, dense, share).astype(BF16)
    total[...] += lax.dot_general(
        att_ref[...], grad_ref[...], CONTRACT_FIRST, preferred_element_type=F32
    )

    @pl.when(step == pl.num_programs(0) - 1)
    def _():
        for z, c, at in chunks_of(dense):
            blocks[z, c] = total[:, at * share : (at + 1) * share].T.astype(BF16)


def dense_back(grad, attended, dense, tokens):
    rows, width = grad.shape
    groups, cores, cols, share = dense.shape
    turned = jax.ShapeDtypeStruct((groups, cores, share, cols), BF16)
    tile = 512
    return launch(
        dense_back_kernel,
        [grad, attended, dense],
        [
            pl.BlockSpec((tile, width), lambda i: (i, 0)),
            pl.BlockSpec((tile, cols), lambda i: (i, 0)),
            whole_spec(dense),
        ],
        (rows // tile,),
        [pl.BlockSpec((tile, cols), lambda i: (i, 0)), whole_spec(turned)],
        [jax.ShapeDtypeStruct((rows, cols), BF16), turned],
        "dense_back",
        cost(4 * rows * dense.size, 2 * (rows * (width + cols) + dense.size)),
        tokens=tokens,
        scratch_shapes=[pltpu.VMEM((cols, width), F32)],
    )


def pre_grad_kernel(grad_ref, slope, contract, out, send, sums):
    @pl.when(pl.program_id(0) == 0)
    def _():
        sums[...] = jnp.zeros_like(sums)

    part = column_back(grad_ref, contract, contract.shape[3]) * slope[...].astype(F32)
    part = part.astype(BF16)
    out[...] = part
    send[...] = part
    sums[...] += jnp.sum(part.astype(F32), axis=0, keepdims=True)


def pre_grad_of(grad, slope, contract, tokens):
    rows, width = grad.shape
    cols = contract.shape[2]
    tile = 512
    steps = rows // tile
    return launch(
        pre_grad_kernel,
        [grad, slope, contract],
        [
            pl.BlockSpec((tile, width), lambda i: (i, 0)),
            pl.BlockSpec((tile, cols), lambda i: (i, 0)),
            whole_spec(contract),
        ],
        (steps,),
        [
            pl.BlockSpec((tile, cols), lambda i: (i, 0)),
            later_half(tile, cols, steps),
            pl.BlockSpec((1, cols), lambda i: (0, 0)),
        ],
        [
            jax.ShapeDtypeStruct((rows, cols), BF16),
            jax.ShapeDtypeStruct((rows // 2, cols), BF16),
            jax.ShapeDtypeStruct((1, cols), F32),
        ],
        "pre_grad",
        cost(2 * rows * contract.size, 2 * (rows * width + contract.size + 2 * rows * cols)),
        tokens=tokens,
    )


def normed_grad_kernel(
    joined,
    joined_other,
    pre,
    pre_other,
    joined_weight,
    joined_weight_other,
    expand_weight,
    expand_weight_other,
    normal,
    gain1,
    gain2,
    out,
    sums,
):
    share = joined_weight.shape[2]
    for number in range(joined_weight.shape[0]):

        def back(left, weight):
            return lax.dot_general(
                left[...], weight[number, 0], CONTRACT_LAST, preferred_element_type=F32
            )

        cols = slice(number * share, (number + 1) * share)
        first = back(joined, joined_weight) + back(joined_other, joined_weight_other)
        second = back(pre, expand_weight) + back(pre_other, expand_weight_other)
        n = normal[:, cols].astype(F32)
        sums[0:1, cols] = jnp.sum(first * n, axis=0, keepdims=True)
        sums[1:2, cols] = jnp.sum(first, axis=0, keepdims=True)
        sums[2:3, cols] = jnp.sum(second * n, axis=0, keepdims=True)
        sums[3:4, cols] = jnp.sum(second, axis=0, keepdims=True)
        out[:, cols] = (first * gain1[:, cols] + second * gain2[:, cols]).astype(BF16)


def normed_grad_piece(
    j, pieces, joined, pre, joined_weight, expand_weight, normal, gain1, gain2, tokens
):
    tile = joined[1].shape[0] // pieces
    groups, cores, share, _ = joined_weight[0].shape
    steps, share = groups * cores // 2, 2 * share
    lefts = [*joined, *pre]
    rights = [*joined_weight, *expand_weight]
    row = pl.BlockSpec((1, share), lambda i: (0, i))
    return launch(
        normed_grad_kernel,
        lefts + rights + [normal, gain1, gain2],
        [pl.BlockSpec((tile, item.shape[1]), lambda i: (j, 0)) for item in lefts]
        + [by_columns(item) for item in rights]
        + [pl.BlockSpec((tile, share), lambda i: (j, i)), row, row],
        (steps,),
        [
            pl.BlockSpec((tile, share), lambda i: (0, i)),
            pl.BlockSpec((8, share), lambda i: (0, i)),
        ],
        [
            jax.ShapeDtypeStruct((tile, steps * share), BF16),
            jax.ShapeDtypeStruct((8, steps * share), F32),
        ],
        "normed_grad_piece",
        cost(4 * tile * sum(item.size for item in rights), 4 * sum(item.size for item in rights)),
        tokens=tokens,
    )


def rows_at(half, width, here):
    if here:
        return pl.BlockSpec((1, half, width), lambda i, place: (place[1], i, 0))
    return pl.BlockSpec((1, half, width), lambda i, place: (1 - place[1], i, 0))


def finish_tile(body, name, place, operands, whole, tile, width, tokens=()):
    half = tile // 2
    listed, specs, picks = [], [], []
    for pair in operands:
        if pair[0][0] is pair[1][0] and (pair[0][1], pair[1][1]) == (0, 1):
            picks.append((len(listed), False))
            listed.append(pair[0][0])
            specs.append(pl.BlockSpec((half, width), lambda i, place: (i, 0)))
        else:
            picks.append((len(listed), True))
            for item, at in pair:
                listed.append(item)
                specs.append(pl.BlockSpec((half, width), lambda i, place, at=at: (at, 0)))
    count = len(listed)

    def kernel(place, *refs):
        both, own = refs[count + len(whole) :]
        first = pl.program_id(0) == 0
        values = [
            jnp.where(first, refs[at][...], refs[at + 1][...]) if pair else refs[at][...]
            for at, pair in picks
        ]
        result = body(values, refs[count : count + len(whole)]).astype(BF16)
        both[0] = result
        own[...] = result

    return launch(
        kernel,
        listed + list(whole),
        specs + [pl.BlockSpec(item.shape, lambda i, place: (0, 0)) for item in whole],
        (2,),
        [rows_at(half, width, True), pl.BlockSpec((half, width), lambda i, place: (i, 0))],
        [
            jax.ShapeDtypeStruct((2, tile, width), BF16),
            jax.ShapeDtypeStruct((tile, width), BF16),
        ],
        name,
        cost(20 * tile * width, 20 * tile * width),
        prefetch=[place],
        tokens=tokens,
    )


def both_halves(item):
    return [(item, 0), (item, 1)]


def fill_other(place, both, other):
    tile, width = other.shape

    def kernel(place, value, out):
        out[0] = value[...]

    return launch(
        kernel,
        [other],
        [pl.BlockSpec((tile // 2, width), lambda i, place: (i, 0))],
        (2,),
        rows_at(tile // 2, width, False),
        jax.ShapeDtypeStruct(both.shape, BF16),
        "fill_other",
        cost(1, 4 * tile * width),
        prefetch=[place],
        held=[both],
    )


def per_device(
    block_input,
    first_norm_gain,
    first_norm_bias,
    second_norm_gain,
    second_norm_bias,
    query_key_value,
    query_key_value_bias,
    attention_dense,
    attention_dense_bias,
    expand_weight,
    expand_bias,
    contract_weight,
    contract_bias,
    document_starts,
    output_grad,
):
    seqs, tile, model_width = block_input.shape
    tiles = lax.axis_size("tp")
    groups = lax.axis_size("seq")
    core = lax.axis_index("branch")
    here = lax.axis_index("tp")
    first_core = core == 0
    length = tile * tiles
    rows_in_all = length * seqs
    share = query_key_value.shape[0]

    def by_core(mine, others):
        return jnp.where(first_core, mine, others), jnp.where(first_core, others, mine)

    def halves_of(value, axis):
        size = value.shape[axis] // 2
        return (
            lax.dynamic_slice_in_dim(value, core * size, size, axis),
            lax.dynamic_slice_in_dim(value, (1 - core) * size, size, axis),
        )

    place = jnp.stack([here, core]).astype(jnp.int32)

    def core_halves(weight, axis):
        mine, others = halves_of(weight, axis)
        return jnp.stack(by_core(mine, swap(others, "branch", 1)))

    def gather_seq(piece):
        return lax.all_gather(piece, "seq", axis=0)

    weight_pieces = [
        core_halves(query_key_value, 1),
        core_halves(expand_weight, 1),
        core_halves(attention_dense, 0),
        core_halves(contract_weight, 0),
    ]
    joined_weight, expand_full, dense_full, contract_full = map(gather_seq, weight_pieces)
    joined_bias = halves_of(query_key_value_bias, 0)[0].astype(F32)[None]
    hidden_bias = halves_of(expand_bias, 0)[0].astype(F32)[None]

    def own_and_other(value):
        return (
            lax.dynamic_index_in_dim(value, core, 0, False),
            lax.dynamic_index_in_dim(value, 1 - core, 0, False),
        )

    def in_halves(value):
        return [value[: tile // 2], value[tile // 2 :]]

    input_own, input_other = own_and_other(block_input)
    grad_own, grad_other = own_and_other(output_grad)
    gain1 = first_norm_gain.astype(F32)[None]
    gain2 = second_norm_gain.astype(F32)[None]
    gains = (
        gain1,
        first_norm_bias.astype(F32)[None],
        gain2,
        second_norm_bias.astype(F32)[None],
    )
    input_halves = in_halves(input_own)
    near = {**gather_near(input_halves, 0), **gather_near(input_halves, 1)}
    grad_halves = in_halves(grad_own)
    grad_rows = place_piece(
        0, grad_halves + in_halves(grad_other), rows_in_all, (), weight_pieces
    )
    tables = rotary_tables(place, document_starts, rows_in_all, [*weight_pieces, grad_rows])
    *normed, mark = norm_piece(
        0, input_halves + in_halves(input_other), rows_in_all, gains, (), [tables[0]]
    )
    near = in_pieces(hold_all(near, mark), {})
    far = gather_far(near)
    for j in sorted(near):
        *normed, mark = norm_piece(j, with_other_core(near[j]), rows_in_all, gains, normed, [])
    heads_held = ()
    far_from = tiles
    if tiles == 4:
        heads_held = project(0, 3, normed[1], joined_weight, joined_bias, tables, ())
        far_from = 3
    for j in sorted(far):
        last_items = [hold(item, mark) for item in far[j]]
        *normed, mark = norm_piece(
            j, with_other_core(last_items), rows_in_all, gains, normed, heads_held[:1]
        )
    heads_held = project(
        far_from % tiles, tiles, normed[1], joined_weight, joined_bias, tables, heads_held
    )
    normal, first_normed, second_normed = normed
    queries, keys, values = heads_held

    first = gather_near([hold(item, *last_items) for item in grad_halves], 0)
    first = hold_all(first, queries)
    second = gather_near([hold(item, *first.values()) for item in grad_halves], 1)
    attended, attended_send, log_sums = attend(
        place, document_starts, queries, keys, values, [*first.values()]
    )
    attended_flat = attended.reshape(rows_in_all, -1)
    near = in_pieces(first, hold_all(second, log_sums))
    far = gather_far(near)
    activated, activated_send, slope = expand(
        second_normed, expand_full, hidden_bias, [item for j in near for item in near[j]]
    )
    near = {
        j: items + [hold(swap(item, "branch", 1), slope) for item in items]
        for j, items in near.items()
    }
    far = {j: [hold(item, slope) for item in items] for j, items in far.items()}
    arrived = [item for items in [*near.values(), *far.values()] for item in items]
    for j in sorted(near):
        grad_rows = place_piece(j, near[j], rows_in_all, [grad_rows], [slope])
    for j in sorted(far):
        items = with_other_core(far[j])
        grad_rows = place_piece(j, items, rows_in_all, [grad_rows], [slope])

    def weight_grad(left, right):
        return lax.dot_general(left, right, CONTRACT_FIRST, preferred_element_type=F32).astype(BF16)

    def in_order(part):
        return part.reshape(2, groups, share, part.shape[1]).transpose(1, 0, 2, 3)

    def scatter(blocks):
        return lax.psum_scatter(blocks, "seq", scatter_dimension=0, tiled=False)

    def finish(total, axis, *tokens):
        total = hold(total, *tokens)
        mine = jnp.where(first_core, total[0], total[1])
        others = swap(jnp.where(first_core, total[1], total[0]), "branch", 1)
        return jnp.concatenate(by_core(mine.astype(F32), others.astype(F32)), axis=axis)

    def exchanged(own, send, *tokens):
        send = send.reshape(-1, send.shape[-1])
        return own.reshape(-1, own.shape[-1]), swap(hold(send, *tokens) if tokens else send, "branch", 1)

    def with_other_weight(weight):
        return weight, swap(weight, "branch", 1)

    attended_pair = exchanged(attended, attended_send, *arrived)
    activated_pair = exchanged(activated, activated_send, *arrived)
    contract_blocks = in_order(weight_grad(grad_rows, activated))
    contract_total = scatter(contract_blocks)
    pre_grad, pre_send, pre_sums = pre_grad_of(
        grad_rows, slope, contract_full, [contract_blocks, attended_pair[1], activated_pair[1]]
    )
    pre_pair = exchanged(pre_grad, pre_send)
    contract_pair = with_other_weight(contract_full)
    expand_blocks = in_order(weight_grad(second_normed, pre_grad))
    expand_total = scatter(expand_blocks)
    attended_grad, dense_blocks = dense_back(
        grad_rows, attended_flat, dense_full, [expand_blocks, pre_pair[1], contract_pair[1]]
    )
    dense_pair = with_other_weight(dense_full)
    order = [tiles - 1] + list(range(1, tiles - 1)) + [0]
    outputs = TileSum()
    mark = attended_grad
    operands = []
    for j in order:
        mark = outputs.pieces[j] = output_piece(
            j,
            tiles,
            attended_pair,
            activated_pair,
            dense_pair,
            contract_pair,
            [mark, *operands],
        )
        operands = outputs.send() if j == order[0] else []
    landed = outputs.land(mark)
    operands = outputs.send()
    joined_grad, joined_send, joined_sums = attend_back(
        place,
        document_starts,
        queries,
        keys,
        values,
        attended_grad.reshape(attended.shape),
        attended,
        log_sums,
        tables,
        [*landed, *operands],
    )
    landed = outputs.land(joined_sums)
    joined_pair = exchanged(joined_grad, joined_send, *landed)
    joined_weight_pair = with_other_weight(joined_weight)
    expand_weight_pair = with_other_weight(expand_full)
    joined_grad = joined_pair[0]
    joined_blocks = jnp.concatenate(
        [in_order(weight_grad(hold(first_normed, *landed), joined_grad)), dense_blocks], axis=3
    )
    joined_total = scatter(joined_blocks)
    while outputs.waiting:
        outputs.send()
        outputs.land()

    inputs = TileSum()
    sums = jnp.zeros((8, model_width), F32)
    mark = joined_blocks
    landed = []
    for j in order:
        inputs.pieces[j], part = normed_grad_piece(
            j,
            tiles,
            joined_pair,
            pre_pair,
            joined_weight_pair,
            expand_weight_pair,
            normal,
            gain1,
            gain2,
            [mark] + landed,
        )
        sums = sums + part
        mark = part
        landed = inputs.land(mark) + inputs.send()
    tail = [mark]

    biases = (
        attention_dense_bias.astype(F32)[None],
        contract_bias.astype(F32)[None],
    )

    def output_body(values, whole):
        return add_up(values) + whole[0][...] + whole[1][...]

    output_both, output_own = finish_tile(
        output_body,
        "finish_output",
        place,
        [both_halves(input_own)] + outputs.terms(),
        biases,
        tile,
        model_width,
        tail,
    )
    block_output = fill_other(place, output_both, swap(output_own, "branch", 1))

    joined_bias_part = jnp.sum(joined_sums, axis=0).reshape(-1)
    hidden_bias_part = pre_sums[0]
    small = jnp.concatenate(
        [
            sums[:4].reshape(-1),
            jnp.sum(grad_own.astype(F32), axis=0),
            joined_bias_part,
            hidden_bias_part,
        ]
    )
    everywhere = 5 * model_width
    small = all_sum(hold(small, output_own), "seq")
    per_core = small[everywhere:]
    both = jnp.stack(by_core(per_core, swap(per_core, "branch", 1)))
    query_key_value_bias_grad = both[:, : joined_bias_part.shape[0]].reshape(-1)
    expand_bias_grad = both[:, joined_bias_part.shape[0] :].reshape(-1)
    shared = all_sum(all_sum(small[:everywhere], "tp"), "branch").reshape(5, model_width)
    expand_grad = finish(expand_total, 1, output_own)
    contract_grad = finish(contract_total, 1, output_own).T
    while inputs.waiting:
        inputs.land()
        inputs.send()
    inputs.land(shared, block_output, expand_grad, contract_grad)

    def input_body(values, whole):
        x, grad = values[0].astype(F32), values[1].astype(F32)
        total = add_up(values[2:])
        centred = x - jnp.mean(x, axis=-1, keepdims=True)
        rate = lax.rsqrt(jnp.mean(centred * centred, axis=-1, keepdims=True) + EPSILON)
        n = centred * rate
        middle = jnp.mean(total, axis=-1, keepdims=True)
        along = jnp.mean(total * n, axis=-1, keepdims=True)
        return grad + rate * (total - middle - n * along)

    input_both, input_grad_own = finish_tile(
        input_body,
        "finish_input",
        place,
        [both_halves(input_own), both_halves(grad_own)] + inputs.terms(),
        (),
        tile,
        model_width,
    )
    input_grad = fill_other(place, input_both, swap(input_grad_own, "branch", 1))
    joined_grads = finish(joined_total, 1, input_grad_own)
    half_cols = joined_grads.shape[1] // 2
    cols = joined_weight.shape[3]
    query_key_value_grad = jnp.concatenate(
        [joined_grads[:, at : at + cols] for at in (0, half_cols)], axis=1
    )
    dense_grad = jnp.concatenate(
        [joined_grads[:, at + cols : at + half_cols].T for at in (0, half_cols)], axis=0
    )
    return (
        block_output,
        input_grad,
        shared[0],
        shared[1],
        shared[2],
        shared[3],
        query_key_value_grad,
        query_key_value_bias_grad,
        dense_grad,
        shared[4],
        expand_grad,
        expand_bias_grad,
        contract_grad,
        shared[4],
    )


def solution(mesh):
    in_specs = (
        P("seq", "tp", None),
        P(),
        P(),
        P(),
        P(),
        P(("branch", "seq"), "tp"),
        P("tp"),
        P("tp", ("branch", "seq")),
        P(),
        P(("branch", "seq"), "tp"),
        P("tp"),
        P("tp", ("branch", "seq")),
        P(),
        P("seq", None),
        P("seq", "tp", None),
    )
    out_specs = (
        P("seq", "tp", None),
        P("seq", "tp", None),
        P(),
        P(),
        P(),
        P(),
        P(("branch", "seq"), "tp"),
        P("tp"),
        P("tp", ("branch", "seq")),
        P(),
        P(("branch", "seq"), "tp"),
        P("tp"),
        P("tp", ("branch", "seq")),
        P(),
    )
    return jax.shard_map(
        per_device, mesh=mesh, in_specs=in_specs, out_specs=out_specs, check_vma=False
    )
```

```python
from functools import partial
import math

import jax
import jax.numpy as jnp
from jax import lax
from jax.experimental import pallas as pl
from jax.experimental.pallas import tpu as pltpu
from jax.sharding import PartitionSpec as P

HD = 128
ROT = 32


EPSILON = 1e-05
NEGATIVE = -1e30
ROPE_BASE = 10000.0
LOG2E = math.log2(math.e)
F32 = jnp.float32
BF16 = jnp.bfloat16
CONTRACT_LAST = (((1,), (1,)), ((), ()))
CONTRACT_FIRST = (((0,), (0,)), ((), ()))
VMEM_BYTES = 56 * 1024 * 1024
ANY = pl.BlockSpec(memory_space=pl.ANY)
HINT = 0.02


def cost(flops, moved, transcendentals=0):
    return pl.CostEstimate(
        flops=1 + int(flops * HINT), bytes_accessed=1 + int(moved * HINT), transcendentals=0
    )


def launch(
    kernel,
    operands,
    in_specs,
    grid,
    out_specs,
    out_shape,
    name,
    cost_estimate,
    prefetch=(),
    held=(),
    tokens=(),
    scratch_shapes=(),
):
    lead = len(prefetch) + len(operands)
    extra = len(held) + len(tokens)

    def body(*refs):
        kernel(*refs[:lead], *refs[lead + extra :])

    return pl.pallas_call(
        body,
        grid_spec=pltpu.PrefetchScalarGridSpec(
            num_scalar_prefetch=len(prefetch),
            grid=grid,
            in_specs=list(in_specs) + [ANY] * extra,
            out_specs=out_specs,
            scratch_shapes=list(scratch_shapes),
        ),
        out_shape=out_shape,
        input_output_aliases={lead + k: k for k in range(len(held))},
        compiler_params=pltpu.CompilerParams(
            dimension_semantics=("arbitrary",) * len(grid), vmem_limit_bytes=VMEM_BYTES
        ),
        cost_estimate=cost_estimate,
        name=name,
    )(*prefetch, *operands, *held, *tokens)


def hold(value, *tokens):
    def nothing(out):
        pass

    return launch(
        nothing,
        [],
        [],
        (1,),
        ANY,
        jax.ShapeDtypeStruct(value.shape, value.dtype),
        "hold",
        cost(1, 1),
        held=[value],
        tokens=tokens,
    )


def swap(value, axis, bit):
    size = lax.axis_size(axis)
    return lax.ppermute(value, axis, [(i, i ^ bit) for i in range(size)])


def onward(value, axis):
    size = lax.axis_size(axis)
    return lax.ppermute(value, axis, [(i, (i + 1) % size) for i in range(size)])


def bit_orders(size):
    bits = [1 << k for k in range(size.bit_length() - 1)]
    return (bits, bits[::-1])


def last_bit(number, order):
    return [bit for bit in order if number & bit][-1]


def gather_near(own, number):
    size = lax.axis_size("tp")
    bits = [1 << k for k in range(size.bit_length() - 1)]
    return {
        (bit, (n + number) % 2): swap(own[(n + number) % 2], "tp", bit)
        for n, bit in enumerate(bits)
    }


def hold_all(items, *tokens):
    return {key: hold(item, *tokens) for key, item in items.items()}


def in_pieces(first, second):
    items = {**first, **second}
    return {j: [items[j, 0], items[j, 1]] for j in sorted({j for j, _ in items})}


def gather_far(near):
    size = lax.axis_size("tp")
    pieces = dict(near)
    far = {}
    for j in sorted(range(1, size), key=lambda j: bin(j).count("1")):
        if j not in near:
            bits = [last_bit(j, order) for order in bit_orders(size)]
            far[j] = [swap(pieces[j ^ bit][q], "tp", bit) for q, bit in enumerate(bits)]
            pieces[j] = far[j]
    return far


def with_other_core(items):
    return items + [swap(item, "branch", 1) for item in items]


def add_up(items):
    total = items[0].astype(F32)
    for item in items[1:]:
        total = total + item.astype(F32)
    return total


class TileSum:
    def __init__(self):
        self.orders = bit_orders(lax.axis_size("tp"))
        size = lax.axis_size("tp")
        self.waiting = [(q, j) for j in range(1, size) for q in range(2)]
        self.expected = {(q, j): 0 for j in range(size) for q in range(2)}
        for q, j in self.waiting:
            self.expected[q, j ^ last_bit(j, self.orders[q])] += 1
        self.waiting.sort(key=lambda at: (-bin(at[1]).count("1"), not self.expected[at]))
        self.pieces = {}
        self.arrived = {}
        self.moving = []

    def part(self, q, j):
        half = self.pieces[j].shape[0] // 2
        return self.pieces[j][q * half : (q + 1) * half]

    def send(self, most=None):
        ready = [
            (q, j)
            for q, j in self.waiting
            if j in self.pieces and len(self.arrived.get((q, j), [])) == self.expected[q, j]
        ][:most]
        operands = []
        for q, j in ready:
            if (q, j) not in self.waiting:
                continue
            bit = last_bit(j, self.orders[q])
            both = (1 - q, j) in ready and last_bit(j, self.orders[1 - q]) == bit
            if both:
                operand = self.pieces[j]
                half = operand.shape[0] // 2
                for side in range(2):
                    if self.arrived.get((side, j)):
                        total = add_up([self.part(side, j)] + self.taken(side, j)).astype(BF16)
                        operand = lax.dynamic_update_slice_in_dim(operand, total, side * half, 0)
            else:
                operand = add_up([self.part(q, j)] + self.taken(q, j)).astype(BF16)
            sides = [0, 1] if both else [q]
            for side in sides:
                self.waiting.remove((side, j))
            self.moving.append((sides, j ^ bit, swap(operand, "tp", bit)))
            operands.append(operand)
        return operands

    def taken(self, q, j):
        half = self.pieces[j].shape[0] // 2
        return [
            item[at * half : (at + 1) * half] for item, at in self.arrived.get((q, j), [])
        ]

    def land(self, *tokens):
        items = []
        for sides, j, item in self.moving:
            item = hold(item, *tokens) if tokens else item
            items.append(item)
            for at, side in enumerate(sides):
                self.arrived.setdefault((side, j), []).append((item, at))
        self.moving = []
        return items

    def terms(self):
        return [[(self.pieces[0], 0), (self.pieces[0], 1)]] + [
            list(pair) for pair in zip(self.arrived[0, 0], self.arrived[1, 0])
        ]


def all_sum(value, axis):
    size = lax.axis_size(axis)
    bit = 1
    while bit < size:
        value = value + swap(value, axis, bit)
        bit *= 2
    return value


def rope(vectors, cosine, sine_up, sine_down):
    return (
        vectors * cosine
        + pltpu.roll(vectors, ROT // 2, 1) * sine_up
        + pltpu.roll(vectors, HD - ROT // 2, 1) * sine_down
    )


class Documents:
    def __init__(self, place, starts, seq_at, rows):
        self.row = place[1] ^ seq_at
        self.starts = starts
        self.rows = rows

    def begin(self, places):
        begin = jnp.zeros_like(places)
        for number in range(self.starts.shape[1]):
            start = self.starts[self.row, number]
            begin = jnp.where(places >= start, start, begin)
        return begin

    def first_key_block(self, block):
        return lax.div(self.begin(block * self.rows), jnp.int32(self.rows))

    def last_query_block(self, block, blocks):
        last = block
        for number in range(1, blocks):
            after = jnp.minimum(block + number, blocks - 1)
            last = jnp.where(self.first_key_block(after) <= block, jnp.maximum(last, after), last)
        return last


def table_kernel(place, starts, cosine, sine_up, sine_down):
    rows = cosine.shape[0]
    blocks = lax.axis_size("tp")
    step = pl.program_id(0)
    block, seq_at = lax.rem(step, blocks) ^ place[0], lax.div(step, blocks)
    places = block * rows + lax.broadcasted_iota(jnp.int32, (rows, 1), 0)
    begin = Documents(place, starts, seq_at, rows).begin(places)
    lane = lax.broadcasted_iota(jnp.int32, (1, HD), 1)
    half = ROT // 2
    number = jnp.where(lane < half, lane, lane - half).astype(F32)
    frequency = jnp.exp2(number * (-2.0 / ROT * math.log2(ROPE_BASE)))
    angles = (places - begin).astype(F32) * jnp.where(lane < ROT, frequency, 0.0)
    cosine[...] = jnp.cos(angles)
    sines = jnp.sin(angles)
    sine_up[...] = jnp.where((lane >= half) & (lane < ROT), sines, 0.0)
    sine_down[...] = jnp.where(lane < half, -sines, 0.0)


def rotary_tables(place, starts, rows, tokens):
    steps = 2 * lax.axis_size("tp")
    tile = rows // steps
    out = pl.BlockSpec((tile, HD), lambda i, *_: (i, 0))
    return launch(
        table_kernel,
        [],
        [],
        (steps,),
        [out] * 3,
        [jax.ShapeDtypeStruct((rows, HD), F32)] * 3,
        "rotary_tables",
        cost(rows * HD * 100, rows * HD * 48),
        prefetch=[place, starts],
        tokens=tokens,
    )


def half_of_piece(j):
    size = lax.axis_size("tp")
    return lambda i, *_: ((lax.div(i, 2) * size + j) * 2 + lax.rem(i, 2), 0)


def own_tile_specs(tile):
    _, rows, width = tile.shape

    def spec(h, q):
        return pl.BlockSpec((1, rows // 2, width), lambda i, place: (place[1] ^ h, q, 0))

    return [spec(h, q) for h in range(2) for q in range(2)]


def own_halves(place, tile, tokens=()):
    _, rows, width = tile.shape

    def kernel(place, first, second, out_first, out_second):
        out_first[...] = first[0]
        out_second[...] = second[0]

    shape = jax.ShapeDtypeStruct((rows // 2, width), BF16)
    return launch(
        kernel,
        [tile, tile],
        own_tile_specs(tile)[:2],
        (1,),
        [whole_spec(shape)] * 2,
        [shape, shape],
        "own_halves",
        cost(1, 4 * rows * width),
        prefetch=[place],
        tokens=tokens,
    )


def place_kernel(place, x0, x1, x2, x3, out):
    step = pl.program_id(0)
    for number, x_ref in enumerate((x0, x1, x2, x3)):

        @pl.when(step == number)
        def _(x_ref=x_ref):
            out[...] = x_ref[...].reshape(out.shape)


def place_piece(j, place, halves, rows_in_all, held, tokens=()):
    if j == 0:
        specs = own_tile_specs(halves)
        half, model_width = halves.shape[1] // 2, halves.shape[2]
        halves = [halves] * 4
    else:
        half, model_width = halves[0].shape
        specs = [whole_spec(item) for item in halves]
    return launch(
        place_kernel,
        halves,
        specs,
        (4,),
        pl.BlockSpec((half, model_width), half_of_piece(j)),
        jax.ShapeDtypeStruct((rows_in_all, model_width), BF16),
        "place_piece",
        cost(1, 4 * half * model_width * 4),
        prefetch=[place],
        held=held,
        tokens=tokens,
    )


def norm_kernel(place, x0, x1, x2, x3, gain1, shift1, gain2, shift2, *rest):
    normal, first, second, mark, scratch = rest[-5:]
    step = pl.program_id(0)
    mark[...] = jnp.zeros_like(mark)
    for number, x_ref in enumerate((x0, x1, x2, x3)):

        @pl.when(step == number)
        def _(x_ref=x_ref):
            scratch[...] = (x_ref[0] if len(x_ref.shape) == 3 else x_ref[...]).astype(F32)

    x = scratch[...]
    centred = x - jnp.mean(x, axis=-1, keepdims=True)
    variance = jnp.mean(centred * centred, axis=-1, keepdims=True)
    n = centred * lax.rsqrt(variance + EPSILON)
    normal[...] = n.astype(BF16)
    first[...] = (n * gain1[...] + shift1[...]).astype(BF16)
    second[...] = (n * gain2[...] + shift2[...]).astype(BF16)


def norm_piece(j, place, halves, rows_in_all, gains, held, tokens):
    if j == 0:
        specs = own_tile_specs(halves)
        half, model_width = halves.shape[1] // 2, halves.shape[2]
        halves = [halves] * 4
    else:
        half, model_width = halves[0].shape
        specs = [whole_spec(item) for item in halves]
    wide = pl.BlockSpec((half, model_width), half_of_piece(j))
    return launch(
        norm_kernel,
        halves + list(gains),
        specs + [whole_spec(item) for item in gains],
        (4,),
        [wide] * 3 + [pl.BlockSpec((8, HD), lambda i, *_: (0, 0))],
        [jax.ShapeDtypeStruct((rows_in_all, model_width), BF16)] * 3
        + [jax.ShapeDtypeStruct((8, HD), F32)],
        "norm_piece",
        cost(4 * half * model_width * 16, 4 * half * model_width * 16),
        prefetch=[place],
        held=held,
        tokens=tokens,
        scratch_shapes=[pltpu.VMEM((half, model_width), F32)],
    )


def chunks_of(weight):
    groups, cores = weight.shape[:2]
    return [(z, c, c * groups + z) for c in range(cores) for z in range(groups)]


def row_product(left, weight, share):
    total = None
    for z, c, at in chunks_of(weight):
        part = jnp.dot(
            left[:, at * share : (at + 1) * share], weight[z, c], preferred_element_type=F32
        )
        total = part if total is None else total + part
    return total


def column_back(left, weight, share):
    total = None
    for z, c, at in chunks_of(weight):
        part = lax.dot_general(
            left[:, at * share : (at + 1) * share],
            weight[z, c],
            CONTRACT_LAST,
            preferred_element_type=F32,
        )
        total = part if total is None else total + part
    return total


def whole_spec(array, prefetched=0):
    rank = array.ndim
    return pl.BlockSpec(array.shape, lambda *at: (0,) * rank)


def project_kernel(normed, weight, bias, cosine, sine_up, sine_down, queries, keys, values):
    joined = row_product(normed, weight, weight.shape[2]) + bias[...]
    tables = (cosine[...], sine_up[...], sine_down[...])
    for head in range(queries.shape[0]):
        at = head * 3 * HD
        queries[head, 0, 0] = rope(joined[:, at : at + HD], *tables).astype(BF16)
        keys[head, 0, 0] = rope(joined[:, at + HD : at + 2 * HD], *tables).astype(BF16)
        values[head, 0, 0] = joined[:, at + 2 * HD : at + 3 * HD].astype(BF16)


def project(first, last, normed, weight, bias, tables, held):
    rows, model_width = normed.shape
    joined_cols = weight.shape[3]
    heads = joined_cols // (3 * HD)
    size = lax.axis_size("tp")
    tile = rows // (2 * size)
    table = pl.BlockSpec((tile, HD), lambda s, i: (s * size + first + i, 0))
    share = (last - first) / size
    return launch(
        project_kernel,
        [normed, weight, bias] + list(tables),
        [
            pl.BlockSpec((tile, model_width), lambda s, i: (s * size + first + i, 0)),
            whole_spec(weight),
            whole_spec(bias),
            table,
            table,
            table,
        ],
        (2, last - first),
        [pl.BlockSpec((heads, 1, 1, tile, HD), lambda s, i: (0, s, first + i, 0, 0))] * 3,
        [jax.ShapeDtypeStruct((heads, 2, size, tile, HD), BF16)] * 3,
        "project",
        cost(
            2 * rows * share * model_width * joined_cols,
            2 * (rows * share * (model_width + joined_cols) + weight.size),
        ),
        held=held,
    )


def attend_kernel(place, starts, q_ref, k_ref, v_ref, out_ref, send_ref, lse_ref):
    block = pl.program_id(1)
    heads, rows = q_ref.shape[0], q_ref.shape[-2]
    here = place[0]
    documents = Documents(place, starts, pl.program_id(0), rows)
    low = documents.first_key_block(block)
    query_places = block * rows + lax.broadcasted_iota(jnp.int32, (rows, 1), 0)
    begin = documents.begin(query_places)
    factor = LOG2E / math.sqrt(HD)

    def step(number, carry):
        key_places = number * rows + lax.broadcasted_iota(jnp.int32, (1, rows), 1)
        allowed = (key_places >= begin) & (key_places <= query_places)
        results = []
        for head in range(heads):
            top, total, mixed = carry[head]
            key = k_ref[head, 0, number ^ here]
            value = v_ref[head, 0, number ^ here]
            scores = lax.dot_general(
                q_ref[head, 0, 0], key, CONTRACT_LAST, preferred_element_type=F32
            )
            scores = jnp.where(allowed, scores * factor, NEGATIVE)
            new_top = jnp.maximum(top, jnp.max(scores, axis=-1, keepdims=True))
            weights = jnp.exp2(scores - new_top)
            shrink = jnp.exp2(top - new_top)
            total = total * shrink + jnp.sum(weights, axis=-1, keepdims=True)
            mixed = mixed * shrink + jnp.dot(
                weights.astype(BF16), value, preferred_element_type=F32
            )
            results.append((new_top, total, mixed))
        return tuple(results)

    empty = (
        jnp.full((rows, 1), NEGATIVE, F32),
        jnp.zeros((rows, 1), F32),
        jnp.zeros((rows, HD), F32),
    )
    results = lax.fori_loop(low, block + 1, step, (empty,) * heads)
    for head, (top, total, mixed) in enumerate(results):
        result = (mixed / total).astype(BF16)
        out_ref[0, 0, :, head * HD : (head + 1) * HD] = result
        send_ref[0, :, head * HD : (head + 1) * HD] = result
        log_sum = top + jnp.log(total) * LOG2E
        lse_ref[head, 0, 0] = jnp.broadcast_to(log_sum, (rows, HD)).T[:1]


def attend(place, starts, queries, keys, values, tokens):
    heads, seqs, blocks, rows, _ = queries.shape
    one = pl.BlockSpec(
        (heads, 1, 1, rows, HD), lambda s, i, place, starts: (0, s, i ^ place[0], 0, 0)
    )
    full = pl.BlockSpec((heads, 1, blocks, rows, HD), lambda s, i, *_: (0, s, 0, 0, 0))
    pairs = heads * seqs * blocks * (blocks + 1) // 2
    return launch(
        attend_kernel,
        [queries, keys, values],
        [one, full, full],
        (seqs, blocks),
        [
            pl.BlockSpec(
                (1, 1, rows, heads * HD), lambda s, i, place, starts: (s, i ^ place[0], 0, 0)
            ),
            pl.BlockSpec(
                (1, rows, heads * HD), lambda s, i, place, starts: ((s * i) ^ place[0], 0, 0)
            ),
            pl.BlockSpec(
                (heads, 1, 1, 1, rows), lambda s, i, place, starts: (0, s, i ^ place[0], 0, 0)
            ),
        ],
        [
            jax.ShapeDtypeStruct((seqs, blocks, rows, heads * HD), BF16),
            jax.ShapeDtypeStruct((blocks, rows, heads * HD), BF16),
            jax.ShapeDtypeStruct((heads, seqs, blocks, 1, rows), F32),
        ],
        "attend",
        cost(pairs * 30 * rows * rows * HD, 4 * queries.size * 2),
        prefetch=[place, starts],
        tokens=tokens,
    )


def attend_back_kernel(
    place,
    starts,
    q_ref,
    k_ref,
    v_ref,
    grad_ref,
    out_ref,
    lse_ref,
    cosine,
    sine_up,
    sine_down,
    joined_ref,
    send_ref,
    sum_ref,
    query_grad,
    delta,
):
    block = pl.program_id(1)
    heads, blocks, rows = q_ref.shape[0], q_ref.shape[2], q_ref.shape[-2]
    here = place[0]
    documents = Documents(place, starts, pl.program_id(0), rows)
    high = documents.last_query_block(block, blocks)
    scaling = 1.0 / math.sqrt(HD)

    @pl.when(block == 0)
    def _():
        query_grad[...] = jnp.zeros_like(query_grad)

        def inner(j, carry):
            for head in range(heads):
                cols = slice(head * HD, (head + 1) * HD)
                product = grad_ref[0, j, :, cols].astype(F32) * out_ref[0, j, :, cols].astype(F32)
                delta[head, j] = jnp.sum(product.T, axis=0, keepdims=True)
            return carry

        lax.fori_loop(0, blocks, inner, 0)

    own = block ^ here
    key_places = block * rows + lax.broadcasted_iota(jnp.int32, (rows, 1), 0)

    def step(number, carry):
        at = number ^ here
        query_places = number * rows + lax.broadcasted_iota(jnp.int32, (1, rows), 1)
        allowed = (key_places >= documents.begin(query_places)) & (key_places <= query_places)
        results = []
        for head in range(heads):
            key_grad, value_grad = carry[head]
            key = k_ref[head, 0, own]
            value = v_ref[head, 0, own]
            query = q_ref[head, 0, at]
            grad = grad_ref[0, at, :, head * HD : (head + 1) * HD]
            scores = lax.dot_general(key, query, CONTRACT_LAST, preferred_element_type=F32)
            scores = scores * (scaling * LOG2E) - lse_ref[head, 0, at]
            weights = jnp.where(allowed, jnp.exp2(scores), 0.0)
            weight_grad = lax.dot_general(value, grad, CONTRACT_LAST, preferred_element_type=F32)
            score_grad = (weights * (weight_grad - delta[head, at]) * scaling).astype(BF16)
            value_grad = value_grad + jnp.dot(
                weights.astype(BF16), grad, preferred_element_type=F32
            )
            key_grad = key_grad + jnp.dot(score_grad, query, preferred_element_type=F32)
            query_grad[head, at] = query_grad[head, at] + lax.dot_general(
                score_grad, key, CONTRACT_FIRST, preferred_element_type=F32
            )
            results.append((key_grad, value_grad))
        return tuple(results)

    empty = jnp.zeros((rows, HD), F32)
    results = lax.fori_loop(block, high + 1, step, ((empty, empty),) * heads)
    tables = (cosine[0, own], -sine_up[0, own], -sine_down[0, own])
    for head, (key_grad, value_grad) in enumerate(results):
        at = head * 3 * HD
        joined_ref[0, own, :, at + HD : at + 2 * HD] = rope(key_grad, *tables).astype(BF16)
        joined_ref[0, own, :, at + 2 * HD : at + 3 * HD] = value_grad.astype(BF16)

    @pl.when(block == blocks - 1)
    def _():
        def inner(j, carry):
            tables = (cosine[0, j], -sine_up[0, j], -sine_down[0, j])
            for head in range(heads):
                at = head * 3 * HD
                joined_ref[0, j, :, at : at + HD] = rope(query_grad[head, j], *tables).astype(BF16)
            send_ref[j] = joined_ref[0, j]
            return carry + jnp.sum(joined_ref[0, j].astype(F32), axis=0, keepdims=True)

        sum_ref[0] = lax.fori_loop(0, blocks, inner, jnp.zeros((1, heads * 3 * HD), F32))


def attend_back(place, starts, queries, keys, values, grad, out, log_sums, tables, tokens):
    heads, seqs, blocks, rows, _ = queries.shape
    joined_cols = heads * 3 * HD
    head_spec = pl.BlockSpec((heads, 1, blocks, rows, HD), lambda s, i, *_: (0, s, 0, 0, 0))
    side = pl.BlockSpec((1, blocks, rows, heads * HD), lambda s, i, *_: (s, 0, 0, 0))
    table = pl.BlockSpec((1, blocks, rows, HD), lambda s, i, *_: (s, 0, 0, 0))
    pairs = heads * seqs * blocks * (blocks + 1) // 2
    return launch(
        attend_back_kernel,
        [queries, keys, values, grad, out, log_sums]
        + [item.reshape(seqs, blocks, rows, HD) for item in tables],
        [
            head_spec,
            head_spec,
            head_spec,
            side,
            side,
            pl.BlockSpec((heads, 1, blocks, 1, rows), lambda s, i, *_: (0, s, 0, 0, 0)),
            table,
            table,
            table,
        ],
        (seqs, blocks),
        [
            pl.BlockSpec((1, blocks, rows, joined_cols), lambda s, i, *_: (s, 0, 0, 0)),
            pl.BlockSpec((blocks, rows, joined_cols), lambda s, i, *_: (0, 0, 0)),
            pl.BlockSpec((1, 1, joined_cols), lambda s, i, *_: (s, 0, 0)),
        ],
        [
            jax.ShapeDtypeStruct((seqs, blocks, rows, joined_cols), BF16),
            jax.ShapeDtypeStruct((blocks, rows, joined_cols), BF16),
            jax.ShapeDtypeStruct((seqs, 1, joined_cols), F32),
        ],
        "attend_back",
        cost(pairs * 50 * rows * rows * HD, 12 * queries.size * 2),
        prefetch=[place, starts],
        tokens=tokens,
        scratch_shapes=[
            pltpu.VMEM((heads, blocks, rows, HD), F32),
            pltpu.VMEM((heads, blocks, 1, rows), F32),
        ],
    )


def expand_kernel(normed, weight, bias, activated, send, slope):
    pre = row_product(normed, weight, weight.shape[2]) + bias[...]
    share = 0.5 + 0.5 * lax.erf(pre * math.sqrt(0.5))
    density = jnp.exp2(pre * pre * (-0.5 * LOG2E)) * (1.0 / math.sqrt(2.0 * math.pi))
    result = (pre * share).astype(BF16)
    activated[...] = result
    send[...] = result
    slope[...] = (share + pre * density).astype(BF16)


def later_half(tile, width, steps):
    half = steps // 2
    return pl.BlockSpec((tile, width), lambda i: (jnp.maximum(i - half, 0), 0))


def expand(normed, weight, bias, tokens):
    rows, model_width = normed.shape
    cols = weight.shape[3]
    tile = 512
    steps = rows // tile
    out = pl.BlockSpec((tile, cols), lambda i: (i, 0))
    shape = jax.ShapeDtypeStruct((rows, cols), BF16)
    return launch(
        expand_kernel,
        [normed, weight, bias],
        [pl.BlockSpec((tile, model_width), lambda i: (i, 0)), whole_spec(weight), whole_spec(bias)],
        (steps,),
        [out, later_half(tile, cols, steps), out],
        [shape, jax.ShapeDtypeStruct((rows // 2, cols), BF16), shape],
        "expand",
        cost(
            2 * rows * model_width * cols,
            2 * (rows * model_width + weight.size + 2 * rows * cols),
        ),
        tokens=tokens,
    )


def output_kernel(att, att_other, act, act_other, dense, dense_other, contract, contract_other, out):
    share = dense.shape[3]
    for n in range(dense.shape[0]):
        total = jnp.dot(att[...], dense[n, 0], preferred_element_type=F32)
        for left, right in (
            (att_other, dense_other),
            (act, contract),
            (act_other, contract_other),
        ):
            total = total + jnp.dot(left[...], right[n, 0], preferred_element_type=F32)
        out[:, n * share : (n + 1) * share] = total.astype(BF16)


def by_columns(weight):
    groups = weight.shape[0] // 2
    return pl.BlockSpec(
        (2, 1) + weight.shape[2:], lambda i: (lax.rem(i, groups), lax.div(i, groups), 0, 0)
    )


def output_piece(j, pieces, attended, activated, dense, contract, tokens):
    tile = attended[1].shape[0] // pieces
    groups, cores, _, share = dense[0].shape
    steps, share = groups * cores // 2, 2 * share
    lefts = [*attended, *activated]
    rights = [*dense, *contract]
    return launch(
        output_kernel,
        lefts + rights,
        [pl.BlockSpec((tile, item.shape[1]), lambda i: (j, 0)) for item in lefts]
        + [by_columns(item) for item in rights],
        (steps,),
        pl.BlockSpec((tile, share), lambda i: (0, i)),
        jax.ShapeDtypeStruct((tile, steps * share), BF16),
        "output_piece",
        cost(4 * tile * sum(item.size for item in rights), 4 * sum(item.size for item in rights)),
        tokens=tokens,
    )


def dense_back_kernel(grad_ref, att_ref, dense, out, blocks, total):
    step = pl.program_id(0)
    share = dense.shape[3]

    @pl.when(step == 0)
    def _():
        total[...] = jnp.zeros_like(total)

    out[...] = column_back(grad_ref, dense, share).astype(BF16)
    total[...] += lax.dot_general(
        att_ref[...], grad_ref[...], CONTRACT_FIRST, preferred_element_type=F32
    )

    @pl.when(step == pl.num_programs(0) - 1)
    def _():
        for z, c, at in chunks_of(dense):
            blocks[z, c] = total[:, at * share : (at + 1) * share].T.astype(BF16)


def dense_back(grad, attended, dense, tokens):
    rows, width = grad.shape
    groups, cores, cols, share = dense.shape
    turned = jax.ShapeDtypeStruct((groups, cores, share, cols), BF16)
    tile = 512
    return launch(
        dense_back_kernel,
        [grad, attended, dense],
        [
            pl.BlockSpec((tile, width), lambda i: (i, 0)),
            pl.BlockSpec((tile, cols), lambda i: (i, 0)),
            whole_spec(dense),
        ],
        (rows // tile,),
        [pl.BlockSpec((tile, cols), lambda i: (i, 0)), whole_spec(turned)],
        [jax.ShapeDtypeStruct((rows, cols), BF16), turned],
        "dense_back",
        cost(4 * rows * dense.size, 2 * (rows * (width + cols) + dense.size)),
        tokens=tokens,
        scratch_shapes=[pltpu.VMEM((cols, width), F32)],
    )


def pre_grad_kernel(grad_ref, slope, contract, out, send, sums):
    @pl.when(pl.program_id(0) == 0)
    def _():
        sums[...] = jnp.zeros_like(sums)

    part = column_back(grad_ref, contract, contract.shape[3]) * slope[...].astype(F32)
    part = part.astype(BF16)
    out[...] = part
    send[...] = part
    sums[...] += jnp.sum(part.astype(F32), axis=0, keepdims=True)


def pre_grad_of(grad, slope, contract, tokens):
    rows, width = grad.shape
    cols = contract.shape[2]
    tile = 512
    steps = rows // tile
    return launch(
        pre_grad_kernel,
        [grad, slope, contract],
        [
            pl.BlockSpec((tile, width), lambda i: (i, 0)),
            pl.BlockSpec((tile, cols), lambda i: (i, 0)),
            whole_spec(contract),
        ],
        (steps,),
        [
            pl.BlockSpec((tile, cols), lambda i: (i, 0)),
            later_half(tile, cols, steps),
            pl.BlockSpec((1, cols), lambda i: (0, 0)),
        ],
        [
            jax.ShapeDtypeStruct((rows, cols), BF16),
            jax.ShapeDtypeStruct((rows // 2, cols), BF16),
            jax.ShapeDtypeStruct((1, cols), F32),
        ],
        "pre_grad",
        cost(2 * rows * contract.size, 2 * (rows * width + contract.size + 2 * rows * cols)),
        tokens=tokens,
    )


def normed_grad_kernel(
    joined,
    joined_other,
    pre,
    pre_other,
    joined_weight,
    joined_weight_other,
    expand_weight,
    expand_weight_other,
    normal,
    gain1,
    gain2,
    out,
    sums,
):
    share = joined_weight.shape[2]
    for number in range(joined_weight.shape[0]):

        def back(left, weight):
            return lax.dot_general(
                left[...], weight[number, 0], CONTRACT_LAST, preferred_element_type=F32
            )

        cols = slice(number * share, (number + 1) * share)
        first = back(joined, joined_weight) + back(joined_other, joined_weight_other)
        second = back(pre, expand_weight) + back(pre_other, expand_weight_other)
        n = normal[:, cols].astype(F32)
        sums[0:1, cols] = jnp.sum(first * n, axis=0, keepdims=True)
        sums[1:2, cols] = jnp.sum(first, axis=0, keepdims=True)
        sums[2:3, cols] = jnp.sum(second * n, axis=0, keepdims=True)
        sums[3:4, cols] = jnp.sum(second, axis=0, keepdims=True)
        out[:, cols] = (first * gain1[:, cols] + second * gain2[:, cols]).astype(BF16)


def normed_grad_piece(
    j, pieces, joined, pre, joined_weight, expand_weight, normal, gain1, gain2, tokens
):
    tile = joined[1].shape[0] // pieces
    groups, cores, share, _ = joined_weight[0].shape
    steps, share = groups * cores // 2, 2 * share
    lefts = [*joined, *pre]
    rights = [*joined_weight, *expand_weight]
    row = pl.BlockSpec((1, share), lambda i: (0, i))
    return launch(
        normed_grad_kernel,
        lefts + rights + [normal, gain1, gain2],
        [pl.BlockSpec((tile, item.shape[1]), lambda i: (j, 0)) for item in lefts]
        + [by_columns(item) for item in rights]
        + [pl.BlockSpec((tile, share), lambda i: (j, i)), row, row],
        (steps,),
        [
            pl.BlockSpec((tile, share), lambda i: (0, i)),
            pl.BlockSpec((8, share), lambda i: (0, i)),
        ],
        [
            jax.ShapeDtypeStruct((tile, steps * share), BF16),
            jax.ShapeDtypeStruct((8, steps * share), F32),
        ],
        "normed_grad_piece",
        cost(4 * tile * sum(item.size for item in rights), 4 * sum(item.size for item in rights)),
        tokens=tokens,
    )


def rows_at(half, width, here):
    if here:
        return pl.BlockSpec((1, half, width), lambda i, place: (place[1], i, 0))
    return pl.BlockSpec((1, half, width), lambda i, place: (1 - place[1], i, 0))


def finish_tile(body, name, place, operands, whole, tile, width, tokens=()):
    half = tile // 2
    listed, specs, picks = [], [], []
    for pair in operands:
        if not isinstance(pair, list):
            picks.append((len(listed), False))
            listed.append(pair)
            specs.append(pl.BlockSpec((1, half, width), lambda i, place: (place[1], i, 0)))
        elif pair[0][0] is pair[1][0] and (pair[0][1], pair[1][1]) == (0, 1):
            picks.append((len(listed), False))
            listed.append(pair[0][0])
            specs.append(pl.BlockSpec((half, width), lambda i, place: (i, 0)))
        else:
            picks.append((len(listed), True))
            for item, at in pair:
                listed.append(item)
                specs.append(pl.BlockSpec((half, width), lambda i, place, at=at: (at, 0)))
    count = len(listed)

    def kernel(place, *refs):
        both, own = refs[count + len(whole) :]
        first = pl.program_id(0) == 0
        values = [
            jnp.where(first, refs[at][...], refs[at + 1][...])
            if pair
            else refs[at][...].reshape(half, width)
            for at, pair in picks
        ]
        result = body(values, refs[count : count + len(whole)]).astype(BF16)
        both[0] = result
        own[...] = result

    return launch(
        kernel,
        listed + list(whole),
        specs + [pl.BlockSpec(item.shape, lambda i, place: (0, 0)) for item in whole],
        (2,),
        [rows_at(half, width, True), pl.BlockSpec((half, width), lambda i, place: (i, 0))],
        [
            jax.ShapeDtypeStruct((2, tile, width), BF16),
            jax.ShapeDtypeStruct((tile, width), BF16),
        ],
        name,
        cost(20 * tile * width, 20 * tile * width),
        prefetch=[place],
        tokens=tokens,
    )


def finish_weight(place, total, straight, tokens):
    _, rows, cols = total.shape

    def pick(place, value, out):
        out[...] = value[0]

    other = launch(
        pick,
        [total],
        [pl.BlockSpec((1, rows, cols), lambda i, place: (1 - place[1], 0, 0))],
        (1,),
        pl.BlockSpec((rows, cols), lambda i, place: (0, 0)),
        jax.ShapeDtypeStruct((rows, cols), BF16),
        "pick_other",
        cost(1, 4 * rows * cols),
        prefetch=[place],
        tokens=tokens,
    )
    other = swap(other, "branch", 1)
    turned = cols - straight

    def join(place, mine, others, *outs):
        value = jnp.where(pl.program_id(0) == 0, mine[0], others[...]).astype(F32)
        if straight:
            outs[0][...] = value[:, :straight]
        if turned:
            outs[-1][...] = value[:, straight:].T

    specs, shapes = [], []
    if straight:
        specs.append(pl.BlockSpec((rows, straight), lambda i, place: (0, place[1] ^ i)))
        shapes.append(jax.ShapeDtypeStruct((rows, 2 * straight), F32))
    if turned:
        specs.append(pl.BlockSpec((turned, rows), lambda i, place: (place[1] ^ i, 0)))
        shapes.append(jax.ShapeDtypeStruct((2 * turned, rows), F32))
    return launch(
        join,
        [total, other],
        [
            pl.BlockSpec((1, rows, cols), lambda i, place: (place[1], 0, 0)),
            pl.BlockSpec((rows, cols), lambda i, place: (0, 0)),
        ],
        (2,),
        specs,
        shapes,
        "finish_weight",
        cost(1, 16 * rows * cols),
        prefetch=[place],
    )


def fill_other(place, both, other):
    tile, width = other.shape

    def kernel(place, value, out):
        out[0] = value[...]

    return launch(
        kernel,
        [other],
        [pl.BlockSpec((tile // 2, width), lambda i, place: (i, 0))],
        (2,),
        rows_at(tile // 2, width, False),
        jax.ShapeDtypeStruct(both.shape, BF16),
        "fill_other",
        cost(1, 4 * tile * width),
        prefetch=[place],
        held=[both],
    )


def per_device(
    block_input,
    first_norm_gain,
    first_norm_bias,
    second_norm_gain,
    second_norm_bias,
    query_key_value,
    query_key_value_bias,
    attention_dense,
    attention_dense_bias,
    expand_weight,
    expand_bias,
    contract_weight,
    contract_bias,
    document_starts,
    output_grad,
):
    seqs, tile, model_width = block_input.shape
    tiles = lax.axis_size("tp")
    groups = lax.axis_size("seq")
    core = lax.axis_index("branch")
    here = lax.axis_index("tp")
    first_core = core == 0
    length = tile * tiles
    rows_in_all = length * seqs
    share = query_key_value.shape[0]

    def by_core(mine, others):
        return jnp.where(first_core, mine, others), jnp.where(first_core, others, mine)

    def halves_of(value, axis):
        size = value.shape[axis] // 2
        return (
            lax.dynamic_slice_in_dim(value, core * size, size, axis),
            lax.dynamic_slice_in_dim(value, (1 - core) * size, size, axis),
        )

    place = jnp.stack([here, core]).astype(jnp.int32)

    input_halves = own_halves(place, block_input)
    near = {**gather_near(input_halves, 0), **gather_near(input_halves, 1)}

    def core_halves(weight, axis):
        mine, others = halves_of(weight, axis)
        return jnp.stack(by_core(mine, swap(others, "branch", 1)))

    def gather_seq(piece):
        return lax.all_gather(piece, "seq", axis=0)

    weight_pieces = [
        core_halves(query_key_value, 1),
        core_halves(expand_weight, 1),
        core_halves(attention_dense, 0),
        core_halves(contract_weight, 0),
    ]
    joined_weight, expand_full, dense_full, contract_full = map(gather_seq, weight_pieces)
    joined_bias = halves_of(query_key_value_bias, 0)[0].astype(F32)[None]
    hidden_bias = halves_of(expand_bias, 0)[0].astype(F32)[None]

    gain1 = first_norm_gain.astype(F32)[None]
    gain2 = second_norm_gain.astype(F32)[None]
    gains = (
        gain1,
        first_norm_bias.astype(F32)[None],
        gain2,
        second_norm_bias.astype(F32)[None],
    )
    tables = rotary_tables(place, document_starts, rows_in_all, weight_pieces)
    grad_halves = own_halves(place, output_grad, [tables[0]])
    grad_rows = place_piece(0, place, output_grad, rows_in_all, (), grad_halves)
    *normed, mark = norm_piece(
        0, place, block_input, rows_in_all, gains, (), [tables[0], grad_rows]
    )
    near = in_pieces(hold_all(near, mark), {})
    far = gather_far(near)
    for j in sorted(near):
        *normed, mark = norm_piece(
            j, place, with_other_core(near[j]), rows_in_all, gains, normed, []
        )
    heads_held = ()
    far_from = tiles
    if tiles == 4:
        heads_held = project(0, 3, normed[1], joined_weight, joined_bias, tables, ())
        far_from = 3
    for j in sorted(far):
        last_items = [hold(item, mark) for item in far[j]]
        *normed, mark = norm_piece(
            j, place, with_other_core(last_items), rows_in_all, gains, normed, heads_held[:1]
        )
    heads_held = project(
        far_from % tiles, tiles, normed[1], joined_weight, joined_bias, tables, heads_held
    )
    normal, first_normed, second_normed = normed
    queries, keys, values = heads_held

    first = gather_near([hold(item, *last_items) for item in grad_halves], 0)
    first = hold_all(first, queries)
    second = gather_near([hold(item, *first.values()) for item in grad_halves], 1)
    attended, attended_send, log_sums = attend(
        place, document_starts, queries, keys, values, [*first.values()]
    )
    attended_flat = attended.reshape(rows_in_all, -1)
    near = in_pieces(first, hold_all(second, log_sums))
    far = gather_far(near)
    activated, activated_send, slope = expand(
        second_normed, expand_full, hidden_bias, [item for j in near for item in near[j]]
    )
    near = {
        j: items + [hold(swap(item, "branch", 1), slope) for item in items]
        for j, items in near.items()
    }
    far = {j: [hold(item, slope) for item in items] for j, items in far.items()}
    arrived = [item for items in [*near.values(), *far.values()] for item in items]
    far = {j: with_other_core(items) for j, items in far.items()}
    for j, items in {**near, **far}.items():
        grad_rows = place_piece(j, place, items, rows_in_all, [grad_rows], [slope])

    def weight_grad(left, right):
        return lax.dot_general(left, right, CONTRACT_FIRST, preferred_element_type=F32).astype(BF16)

    def in_order(part):
        return part.reshape(2, groups, share, part.shape[1]).transpose(1, 0, 2, 3)

    def scatter(blocks):
        return lax.psum_scatter(blocks, "seq", scatter_dimension=0, tiled=False)

    def exchanged(own, send, *tokens):
        send = send.reshape(-1, send.shape[-1])
        return own.reshape(-1, own.shape[-1]), swap(hold(send, *tokens) if tokens else send, "branch", 1)

    def with_other_weight(weight):
        return weight, swap(weight, "branch", 1)

    attended_pair = exchanged(attended, attended_send, *arrived)
    activated_pair = exchanged(activated, activated_send, *arrived)
    contract_blocks = in_order(weight_grad(grad_rows, activated))
    contract_total = scatter(contract_blocks)
    contract_full = hold(contract_full, contract_blocks)
    pre_grad, pre_send, pre_sums = pre_grad_of(
        grad_rows, slope, contract_full, [contract_blocks]
    )
    pre_pair = exchanged(pre_grad, pre_send)
    contract_pair = with_other_weight(contract_full)
    expand_blocks = in_order(weight_grad(second_normed, pre_grad))
    expand_total = scatter(expand_blocks)
    attended_grad, dense_blocks = dense_back(
        grad_rows, attended_flat, dense_full, [expand_blocks]
    )
    dense_pair = with_other_weight(dense_full)
    order = [tiles - 1] + list(range(1, tiles - 1)) + [0]
    outputs = TileSum()
    mark = attended_grad
    operands = []
    for j in order:
        mark = outputs.pieces[j] = output_piece(
            j,
            tiles,
            attended_pair,
            activated_pair,
            dense_pair,
            contract_pair,
            [mark, *operands],
        )
        operands = outputs.send() if j == order[0] else []
    landed = outputs.land(mark)
    operands = outputs.send()
    joined_grad, joined_send, joined_sums = attend_back(
        place,
        document_starts,
        queries,
        keys,
        values,
        attended_grad.reshape(attended.shape),
        attended,
        log_sums,
        tables,
        [*landed, *operands],
    )
    landed = outputs.land(joined_sums)
    joined_pair = exchanged(joined_grad, joined_send, *landed)
    joined_weight_pair = with_other_weight(joined_weight)
    expand_weight_pair = with_other_weight(expand_full)
    joined_grad = joined_pair[0]
    while outputs.waiting:
        outputs.send()
        outputs.land()

    biases = (
        attention_dense_bias.astype(F32)[None],
        contract_bias.astype(F32)[None],
    )

    def output_body(values, whole):
        return add_up(values) + whole[0][...] + whole[1][...]

    def finish_others(mark):
        output_both, output_own = finish_tile(
            output_body,
            "finish_output",
            place,
            [block_input] + outputs.terms(),
            biases,
            tile,
            model_width,
            [mark],
        )
        (contract_grad,) = finish_weight(place, contract_total, 0, [mark])
        (expand_grad,) = finish_weight(place, expand_total, expand_total.shape[2], [mark])
        block_output = fill_other(place, output_both, swap(output_own, "branch", 1))
        return block_output, contract_grad, expand_grad

    inputs = TileSum()
    sums = jnp.zeros((8, model_width), F32)
    mark = joined_sums
    wait = [*landed]
    for number, j in enumerate(order):
        inputs.pieces[j], part = normed_grad_piece(
            j,
            tiles,
            joined_pair,
            pre_pair,
            joined_weight_pair,
            expand_weight_pair,
            normal,
            gain1,
            gain2,
            [mark, *wait],
        )
        sums = sums + part
        mark = part
        wait = []
        if number == 0:
            started = inputs.send()
            part = weight_grad(hold(first_normed, mark, *started), joined_grad)
            wait = inputs.land(part)
            joined_blocks = jnp.concatenate([in_order(hold(part, *wait)), dense_blocks], axis=3)
            joined_total = scatter(joined_blocks)
            mark = joined_blocks
        elif j == 0:
            inputs.land(mark)
        wait = wait + inputs.send()

    joined_bias_part = jnp.sum(joined_sums, axis=0).reshape(-1)
    hidden_bias_part = pre_sums[0]
    grad_own = lax.dynamic_index_in_dim(output_grad, core, 0, False)
    block_output, contract_grad, expand_grad = finish_others(mark)
    small = jnp.concatenate(
        [
            sums[:4].reshape(-1),
            jnp.sum(grad_own.astype(F32), axis=0),
            joined_bias_part,
            hidden_bias_part,
        ]
    )
    everywhere = 5 * model_width
    small = all_sum(hold(small, mark), "seq")
    per_core = small[everywhere:]
    both = jnp.stack(by_core(per_core, swap(per_core, "branch", 1)))
    query_key_value_bias_grad = both[:, : joined_bias_part.shape[0]].reshape(-1)
    expand_bias_grad = both[:, joined_bias_part.shape[0] :].reshape(-1)
    shared = all_sum(all_sum(small[:everywhere], "tp"), "branch").reshape(5, model_width)
    while inputs.waiting:
        inputs.land()
        inputs.send()
    inputs.land()

    def input_body(values, whole):
        x, grad = values[0].astype(F32), values[1].astype(F32)
        total = add_up(values[2:])
        centred = x - jnp.mean(x, axis=-1, keepdims=True)
        rate = lax.rsqrt(jnp.mean(centred * centred, axis=-1, keepdims=True) + EPSILON)
        n = centred * rate
        middle = jnp.mean(total, axis=-1, keepdims=True)
        along = jnp.mean(total * n, axis=-1, keepdims=True)
        return grad + rate * (total - middle - n * along)

    input_both, input_grad_own = finish_tile(
        input_body,
        "finish_input",
        place,
        [block_input, output_grad] + inputs.terms(),
        (),
        tile,
        model_width,
        [shared, block_output, contract_grad, expand_grad],
    )
    input_grad = fill_other(place, input_both, swap(input_grad_own, "branch", 1))
    query_key_value_grad, dense_grad = finish_weight(
        place, joined_total, joined_weight.shape[3], [input_grad_own]
    )
    return (
        block_output,
        input_grad,
        shared[0],
        shared[1],
        shared[2],
        shared[3],
        query_key_value_grad,
        query_key_value_bias_grad,
        dense_grad,
        shared[4],
        expand_grad,
        expand_bias_grad,
        contract_grad,
        shared[4],
    )


def solution(mesh):
    in_specs = (
        P("seq", "tp", None),
        P(),
        P(),
        P(),
        P(),
        P(("branch", "seq"), "tp"),
        P("tp"),
        P("tp", ("branch", "seq")),
        P(),
        P(("branch", "seq"), "tp"),
        P("tp"),
        P("tp", ("branch", "seq")),
        P(),
        P("seq", None),
        P("seq", "tp", None),
    )
    out_specs = (
        P("seq", "tp", None),
        P("seq", "tp", None),
        P(),
        P(),
        P(),
        P(),
        P(("branch", "seq"), "tp"),
        P("tp"),
        P("tp", ("branch", "seq")),
        P(),
        P(("branch", "seq"), "tp"),
        P("tp"),
        P("tp", ("branch", "seq")),
        P(),
    )
    return jax.shard_map(
        per_device, mesh=mesh, in_specs=in_specs, out_specs=out_specs, check_vma=False
    )
```

```python
from functools import partial
import math

import jax
import jax.numpy as jnp
from jax import lax
from jax.experimental import pallas as pl
from jax.experimental.pallas import tpu as pltpu
from jax.sharding import PartitionSpec as P

HD = 128
ROT = 32


EPSILON = 1e-05
NEGATIVE = -1e30
ROPE_BASE = 10000.0
LOG2E = math.log2(math.e)
F32 = jnp.float32
BF16 = jnp.bfloat16
CONTRACT_LAST = (((1,), (1,)), ((), ()))
CONTRACT_FIRST = (((0,), (0,)), ((), ()))
VMEM_BYTES = 56 * 1024 * 1024
ANY = pl.BlockSpec(memory_space=pl.ANY)
HINT = 0.02


def cost(flops, moved, transcendentals=0):
    return pl.CostEstimate(
        flops=1 + int(flops * HINT), bytes_accessed=1 + int(moved * HINT), transcendentals=0
    )


def launch(
    kernel,
    operands,
    in_specs,
    grid,
    out_specs,
    out_shape,
    name,
    cost_estimate,
    prefetch=(),
    held=(),
    tokens=(),
    scratch_shapes=(),
):
    lead = len(prefetch) + len(operands)
    extra = len(held) + len(tokens)

    def body(*refs):
        kernel(*refs[:lead], *refs[lead + extra :])

    return pl.pallas_call(
        body,
        grid_spec=pltpu.PrefetchScalarGridSpec(
            num_scalar_prefetch=len(prefetch),
            grid=grid,
            in_specs=list(in_specs) + [ANY] * extra,
            out_specs=out_specs,
            scratch_shapes=list(scratch_shapes),
        ),
        out_shape=out_shape,
        input_output_aliases={lead + k: k for k in range(len(held))},
        compiler_params=pltpu.CompilerParams(
            dimension_semantics=("arbitrary",) * len(grid), vmem_limit_bytes=VMEM_BYTES
        ),
        cost_estimate=cost_estimate,
        name=name,
    )(*prefetch, *operands, *held, *tokens)


def hold(value, *tokens):
    def nothing(out):
        pass

    return launch(
        nothing,
        [],
        [],
        (1,),
        ANY,
        jax.ShapeDtypeStruct(value.shape, value.dtype),
        "hold",
        cost(1, 1),
        held=[value],
        tokens=tokens,
    )


def swap(value, axis, bit):
    size = lax.axis_size(axis)
    return lax.ppermute(value, axis, [(i, i ^ bit) for i in range(size)])


def onward(value, axis):
    size = lax.axis_size(axis)
    return lax.ppermute(value, axis, [(i, (i + 1) % size) for i in range(size)])


def bit_orders(size):
    bits = [1 << k for k in range(size.bit_length() - 1)]
    return (bits, bits[::-1])


def last_bit(number, order):
    return [bit for bit in order if number & bit][-1]


def gather_near(own, number):
    size = lax.axis_size("tp")
    bits = [1 << k for k in range(size.bit_length() - 1)]
    return {
        (bit, (n + number) % 2): swap(own[(n + number) % 2], "tp", bit)
        for n, bit in enumerate(bits)
    }


def hold_all(items, *tokens):
    return {key: hold(item, *tokens) for key, item in items.items()}


def in_pieces(first, second):
    items = {**first, **second}
    return {j: [items[j, 0], items[j, 1]] for j in sorted({j for j, _ in items})}


def gather_far(near):
    size = lax.axis_size("tp")
    pieces = dict(near)
    far = {}
    for j in sorted(range(1, size), key=lambda j: bin(j).count("1")):
        if j not in near:
            bits = [last_bit(j, order) for order in bit_orders(size)]
            far[j] = [swap(pieces[j ^ bit][q], "tp", bit) for q, bit in enumerate(bits)]
            pieces[j] = far[j]
    return far


def with_other_core(items):
    return items + [swap(item, "branch", 1) for item in items]


def add_up(items):
    total = items[0].astype(F32)
    for item in items[1:]:
        total = total + item.astype(F32)
    return total


class TileSum:
    def __init__(self):
        size = lax.axis_size("tp")
        self.orders = bit_orders(size)
        self.waiting = [(q, j) for j in range(1, size) for q in range(2)]
        self.expected = {(q, j): 0 for j in range(size) for q in range(2)}
        for q, j in self.waiting:
            self.expected[q, j ^ last_bit(j, self.orders[q])] += 1
        self.waiting.sort(key=lambda at: (-bin(at[1]).count("1"), at[1]))
        self.pieces = {}
        self.arrived = {}
        self.moving = []

    def splits(self, j):
        return j > 0 and len({last_bit(j, order) for order in self.orders}) > 1

    def extras(self, j):
        return [(q, item) for q in range(2) for item in self.arrived.get((q, j), [])]

    def complete(self, j):
        return all(len(self.arrived.get((q, j), [])) == self.expected[q, j] for q in range(2))

    def send(self, *tokens):
        operands = []
        for q, j in list(self.waiting):
            if j not in self.pieces or (q, j) not in self.waiting:
                continue
            bit = last_bit(j, self.orders[q])
            if self.splits(j):
                sides, operand = [q], self.pieces[j][q]
            else:
                sides, operand = [0, 1], self.pieces[j]
            for side in sides:
                self.waiting.remove((side, j))
            if tokens:
                operand = hold(operand, *tokens)
            self.moving.append((sides, j ^ bit, swap(operand, "tp", bit)))
            operands.append(operand)
        return operands

    def land(self, *tokens):
        items = []
        for sides, j, item in self.moving:
            item = hold(item, *tokens) if tokens else item
            items.append(item)
            if j == 0:
                self.arrived.setdefault(0, []).append(item)
                continue
            half = item.shape[0] // 2
            for side in sides:
                part = item[side * half : (side + 1) * half] if len(sides) > 1 else item
                self.arrived.setdefault((side, j), []).append(part)
        self.moving = []
        return items

    def terms(self):
        return [[(item, 0), (item, 1)] for item in [self.pieces[0]] + self.arrived[0]]


def finish_piece(total, column, extras, outs):
    half = total.shape[0] // 2
    width = total.shape[1]
    cols = slice(column, column + width)
    parts = [total[:half], total[half:]]
    for q, ref in extras:
        parts[q] = parts[q] + ref[:, cols].astype(F32)
    for q in range(2):
        if len(outs) > 1:
            outs[q][:, cols] = parts[q].astype(BF16)
        else:
            outs[0][q * half : (q + 1) * half, cols] = parts[q].astype(BF16)


def piece_specs(tile, share, steps, split):
    rows, count = (tile // 2, 2) if split else (tile, 1)
    return (
        [pl.BlockSpec((rows, share), lambda i: (0, i))] * count,
        [jax.ShapeDtypeStruct((rows, steps * share), BF16)] * count,
    )


def all_sum(value, axis):
    size = lax.axis_size(axis)
    bit = 1
    while bit < size:
        value = value + swap(value, axis, bit)
        bit *= 2
    return value


def rope(vectors, cosine, sine_up, sine_down):
    return (
        vectors * cosine
        + pltpu.roll(vectors, ROT // 2, 1) * sine_up
        + pltpu.roll(vectors, HD - ROT // 2, 1) * sine_down
    )


class Documents:
    def __init__(self, place, starts, seq_at, rows):
        self.row = place[1] ^ seq_at
        self.starts = starts
        self.rows = rows

    def begin(self, places):
        begin = jnp.zeros_like(places)
        for number in range(self.starts.shape[1]):
            start = self.starts[self.row, number]
            begin = jnp.where(places >= start, start, begin)
        return begin

    def first_key_block(self, block):
        return lax.div(self.begin(block * self.rows), jnp.int32(self.rows))

    def last_query_block(self, block, blocks):
        last = block
        for number in range(1, blocks):
            after = jnp.minimum(block + number, blocks - 1)
            last = jnp.where(self.first_key_block(after) <= block, jnp.maximum(last, after), last)
        return last


def table_kernel(place, starts, cosine, sine_up, sine_down):
    rows = cosine.shape[0]
    blocks = lax.axis_size("tp")
    step = pl.program_id(0)
    block, seq_at = lax.rem(step, blocks) ^ place[0], lax.div(step, blocks)
    places = block * rows + lax.broadcasted_iota(jnp.int32, (rows, 1), 0)
    begin = Documents(place, starts, seq_at, rows).begin(places)
    lane = lax.broadcasted_iota(jnp.int32, (1, HD), 1)
    half = ROT // 2
    number = jnp.where(lane < half, lane, lane - half).astype(F32)
    frequency = jnp.exp2(number * (-2.0 / ROT * math.log2(ROPE_BASE)))
    angles = (places - begin).astype(F32) * jnp.where(lane < ROT, frequency, 0.0)
    cosine[...] = jnp.cos(angles)
    sines = jnp.sin(angles)
    sine_up[...] = jnp.where((lane >= half) & (lane < ROT), sines, 0.0)
    sine_down[...] = jnp.where(lane < half, -sines, 0.0)


def rotary_tables(place, starts, rows, tokens):
    steps = 2 * lax.axis_size("tp")
    tile = rows // steps
    out = pl.BlockSpec((tile, HD), lambda i, *_: (i, 0))
    return launch(
        table_kernel,
        [],
        [],
        (steps,),
        [out] * 3,
        [jax.ShapeDtypeStruct((rows, HD), F32)] * 3,
        "rotary_tables",
        cost(rows * HD * 100, rows * HD * 48),
        prefetch=[place, starts],
        tokens=tokens,
    )


def half_of_piece(j):
    size = lax.axis_size("tp")
    return lambda i, *_: ((lax.div(i, 2) * size + j) * 2 + lax.rem(i, 2), 0)


def own_tile_specs(tile):
    _, rows, width = tile.shape

    def spec(h, q):
        return pl.BlockSpec((1, rows // 2, width), lambda i, place: (place[1] ^ h, q, 0))

    return [spec(h, q) for h in range(2) for q in range(2)]


def own_halves(place, tile, tokens=()):
    _, rows, width = tile.shape

    def kernel(place, first, second, out_first, out_second):
        out_first[...] = first[0]
        out_second[...] = second[0]

    shape = jax.ShapeDtypeStruct((rows // 2, width), BF16)
    return launch(
        kernel,
        [tile, tile],
        own_tile_specs(tile)[:2],
        (1,),
        [whole_spec(shape)] * 2,
        [shape, shape],
        "own_halves",
        cost(1, 4 * rows * width),
        prefetch=[place],
        tokens=tokens,
    )


def place_kernel(place, x0, x1, x2, x3, out):
    step = pl.program_id(0)
    for number, x_ref in enumerate((x0, x1, x2, x3)):

        @pl.when(step == number)
        def _(x_ref=x_ref):
            out[...] = x_ref[...].reshape(out.shape)


def place_piece(j, place, halves, rows_in_all, held, tokens=()):
    if j == 0:
        specs = own_tile_specs(halves)
        half, model_width = halves.shape[1] // 2, halves.shape[2]
        halves = [halves] * 4
    else:
        half, model_width = halves[0].shape
        specs = [whole_spec(item) for item in halves]
    return launch(
        place_kernel,
        halves,
        specs,
        (4,),
        pl.BlockSpec((half, model_width), half_of_piece(j)),
        jax.ShapeDtypeStruct((rows_in_all, model_width), BF16),
        "place_piece",
        cost(1, 4 * half * model_width * 4),
        prefetch=[place],
        held=held,
        tokens=tokens,
    )


def norm_kernel(place, x0, x1, x2, x3, gain1, shift1, gain2, shift2, *rest):
    normal, first, second, mark, scratch = rest[-5:]
    step = pl.program_id(0)
    mark[...] = jnp.zeros_like(mark)
    for number, x_ref in enumerate((x0, x1, x2, x3)):

        @pl.when(step == number)
        def _(x_ref=x_ref):
            scratch[...] = (x_ref[0] if len(x_ref.shape) == 3 else x_ref[...]).astype(F32)

    x = scratch[...]
    centred = x - jnp.mean(x, axis=-1, keepdims=True)
    variance = jnp.mean(centred * centred, axis=-1, keepdims=True)
    n = centred * lax.rsqrt(variance + EPSILON)
    normal[...] = n.astype(BF16)
    first[...] = (n * gain1[...] + shift1[...]).astype(BF16)
    second[...] = (n * gain2[...] + shift2[...]).astype(BF16)


def norm_piece(j, place, halves, rows_in_all, gains, held, tokens):
    if j == 0:
        specs = own_tile_specs(halves)
        half, model_width = halves.shape[1] // 2, halves.shape[2]
        halves = [halves] * 4
    else:
        half, model_width = halves[0].shape
        specs = [whole_spec(item) for item in halves]
    wide = pl.BlockSpec((half, model_width), half_of_piece(j))
    return launch(
        norm_kernel,
        halves + list(gains),
        specs + [whole_spec(item) for item in gains],
        (4,),
        [wide] * 3 + [pl.BlockSpec((8, HD), lambda i, *_: (0, 0))],
        [jax.ShapeDtypeStruct((rows_in_all, model_width), BF16)] * 3
        + [jax.ShapeDtypeStruct((8, HD), F32)],
        "norm_piece",
        cost(4 * half * model_width * 16, 4 * half * model_width * 16),
        prefetch=[place],
        held=held,
        tokens=tokens,
        scratch_shapes=[pltpu.VMEM((half, model_width), F32)],
    )


def chunks_of(weight):
    groups, cores = weight.shape[:2]
    return [(z, c, c * groups + z) for c in range(cores) for z in range(groups)]


def row_product(left, weight, share):
    total = None
    for z, c, at in chunks_of(weight):
        part = jnp.dot(
            left[:, at * share : (at + 1) * share], weight[z, c], preferred_element_type=F32
        )
        total = part if total is None else total + part
    return total


def column_back(left, weight, share):
    total = None
    for z, c, at in chunks_of(weight):
        part = lax.dot_general(
            left[:, at * share : (at + 1) * share],
            weight[z, c],
            CONTRACT_LAST,
            preferred_element_type=F32,
        )
        total = part if total is None else total + part
    return total


def whole_spec(array, prefetched=0):
    rank = array.ndim
    return pl.BlockSpec(array.shape, lambda *at: (0,) * rank)


def project_kernel(normed, weight, bias, cosine, sine_up, sine_down, queries, keys, values):
    joined = row_product(normed, weight, weight.shape[2]) + bias[...]
    tables = (cosine[...], sine_up[...], sine_down[...])
    for head in range(queries.shape[0]):
        at = head * 3 * HD
        queries[head, 0, 0] = rope(joined[:, at : at + HD], *tables).astype(BF16)
        keys[head, 0, 0] = rope(joined[:, at + HD : at + 2 * HD], *tables).astype(BF16)
        values[head, 0, 0] = joined[:, at + 2 * HD : at + 3 * HD].astype(BF16)


def project(first, last, normed, weight, bias, tables, held):
    rows, model_width = normed.shape
    joined_cols = weight.shape[3]
    heads = joined_cols // (3 * HD)
    size = lax.axis_size("tp")
    tile = rows // (2 * size)
    table = pl.BlockSpec((tile, HD), lambda s, i: (s * size + first + i, 0))
    share = (last - first) / size
    return launch(
        project_kernel,
        [normed, weight, bias] + list(tables),
        [
            pl.BlockSpec((tile, model_width), lambda s, i: (s * size + first + i, 0)),
            whole_spec(weight),
            whole_spec(bias),
            table,
            table,
            table,
        ],
        (2, last - first),
        [pl.BlockSpec((heads, 1, 1, tile, HD), lambda s, i: (0, s, first + i, 0, 0))] * 3,
        [jax.ShapeDtypeStruct((heads, 2, size, tile, HD), BF16)] * 3,
        "project",
        cost(
            2 * rows * share * model_width * joined_cols,
            2 * (rows * share * (model_width + joined_cols) + weight.size),
        ),
        held=held,
    )


def attend_kernel(place, starts, q_ref, k_ref, v_ref, out_ref, send_ref, lse_ref):
    block = pl.program_id(1)
    heads, rows = q_ref.shape[0], q_ref.shape[-2]
    here = place[0]
    documents = Documents(place, starts, pl.program_id(0), rows)
    low = documents.first_key_block(block)
    query_places = block * rows + lax.broadcasted_iota(jnp.int32, (rows, 1), 0)
    begin = documents.begin(query_places)
    factor = LOG2E / math.sqrt(HD)

    def step(number, carry):
        key_places = number * rows + lax.broadcasted_iota(jnp.int32, (1, rows), 1)
        allowed = (key_places >= begin) & (key_places <= query_places)
        results = []
        for head in range(heads):
            top, total, mixed = carry[head]
            key = k_ref[head, 0, number ^ here]
            value = v_ref[head, 0, number ^ here]
            scores = lax.dot_general(
                q_ref[head, 0, 0], key, CONTRACT_LAST, preferred_element_type=F32
            )
            scores = jnp.where(allowed, scores * factor, NEGATIVE)
            new_top = jnp.maximum(top, jnp.max(scores, axis=-1, keepdims=True))
            weights = jnp.exp2(scores - new_top)
            shrink = jnp.exp2(top - new_top)
            total = total * shrink + jnp.sum(weights, axis=-1, keepdims=True)
            mixed = mixed * shrink + jnp.dot(
                weights.astype(BF16), value, preferred_element_type=F32
            )
            results.append((new_top, total, mixed))
        return tuple(results)

    empty = (
        jnp.full((rows, 1), NEGATIVE, F32),
        jnp.zeros((rows, 1), F32),
        jnp.zeros((rows, HD), F32),
    )
    results = lax.fori_loop(low, block + 1, step, (empty,) * heads)
    for head, (top, total, mixed) in enumerate(results):
        result = (mixed / total).astype(BF16)
        out_ref[0, 0, :, head * HD : (head + 1) * HD] = result
        send_ref[0, :, head * HD : (head + 1) * HD] = result
        log_sum = top + jnp.log(total) * LOG2E
        lse_ref[head, 0, 0] = jnp.broadcast_to(log_sum, (rows, HD)).T[:1]


def attend(place, starts, queries, keys, values, tokens):
    heads, seqs, blocks, rows, _ = queries.shape
    one = pl.BlockSpec(
        (heads, 1, 1, rows, HD), lambda s, i, place, starts: (0, s, i ^ place[0], 0, 0)
    )
    full = pl.BlockSpec((heads, 1, blocks, rows, HD), lambda s, i, *_: (0, s, 0, 0, 0))
    pairs = heads * seqs * blocks * (blocks + 1) // 2
    return launch(
        attend_kernel,
        [queries, keys, values],
        [one, full, full],
        (seqs, blocks),
        [
            pl.BlockSpec(
                (1, 1, rows, heads * HD), lambda s, i, place, starts: (s, i ^ place[0], 0, 0)
            ),
            pl.BlockSpec(
                (1, rows, heads * HD), lambda s, i, place, starts: ((s * i) ^ place[0], 0, 0)
            ),
            pl.BlockSpec(
                (heads, 1, 1, 1, rows), lambda s, i, place, starts: (0, s, i ^ place[0], 0, 0)
            ),
        ],
        [
            jax.ShapeDtypeStruct((seqs, blocks, rows, heads * HD), BF16),
            jax.ShapeDtypeStruct((blocks, rows, heads * HD), BF16),
            jax.ShapeDtypeStruct((heads, seqs, blocks, 1, rows), F32),
        ],
        "attend",
        cost(pairs * 30 * rows * rows * HD, 4 * queries.size * 2),
        prefetch=[place, starts],
        tokens=tokens,
    )


def attend_back_kernel(
    place,
    starts,
    q_ref,
    k_ref,
    v_ref,
    grad_ref,
    out_ref,
    lse_ref,
    cosine,
    sine_up,
    sine_down,
    joined_ref,
    send_ref,
    sum_ref,
    query_grad,
    delta,
):
    block = pl.program_id(1)
    heads, blocks, rows = q_ref.shape[0], q_ref.shape[2], q_ref.shape[-2]
    here = place[0]
    documents = Documents(place, starts, pl.program_id(0), rows)
    high = documents.last_query_block(block, blocks)
    scaling = 1.0 / math.sqrt(HD)

    @pl.when(block == 0)
    def _():
        query_grad[...] = jnp.zeros_like(query_grad)

        def inner(j, carry):
            for head in range(heads):
                cols = slice(head * HD, (head + 1) * HD)
                product = grad_ref[0, j, :, cols].astype(F32) * out_ref[0, j, :, cols].astype(F32)
                delta[head, j] = jnp.sum(product.T, axis=0, keepdims=True)
            return carry

        lax.fori_loop(0, blocks, inner, 0)

    own = block ^ here
    key_places = block * rows + lax.broadcasted_iota(jnp.int32, (rows, 1), 0)

    def step(number, carry):
        at = number ^ here
        query_places = number * rows + lax.broadcasted_iota(jnp.int32, (1, rows), 1)
        allowed = (key_places >= documents.begin(query_places)) & (key_places <= query_places)
        results = []
        for head in range(heads):
            key_grad, value_grad = carry[head]
            key = k_ref[head, 0, own]
            value = v_ref[head, 0, own]
            query = q_ref[head, 0, at]
            grad = grad_ref[0, at, :, head * HD : (head + 1) * HD]
            scores = lax.dot_general(key, query, CONTRACT_LAST, preferred_element_type=F32)
            scores = scores * (scaling * LOG2E) - lse_ref[head, 0, at]
            weights = jnp.where(allowed, jnp.exp2(scores), 0.0)
            weight_grad = lax.dot_general(value, grad, CONTRACT_LAST, preferred_element_type=F32)
            score_grad = (weights * (weight_grad - delta[head, at]) * scaling).astype(BF16)
            value_grad = value_grad + jnp.dot(
                weights.astype(BF16), grad, preferred_element_type=F32
            )
            key_grad = key_grad + jnp.dot(score_grad, query, preferred_element_type=F32)
            query_grad[head, at] = query_grad[head, at] + lax.dot_general(
                score_grad, key, CONTRACT_FIRST, preferred_element_type=F32
            )
            results.append((key_grad, value_grad))
        return tuple(results)

    empty = jnp.zeros((rows, HD), F32)
    results = lax.fori_loop(block, high + 1, step, ((empty, empty),) * heads)
    tables = (cosine[0, own], -sine_up[0, own], -sine_down[0, own])
    for head, (key_grad, value_grad) in enumerate(results):
        at = head * 3 * HD
        joined_ref[0, own, :, at + HD : at + 2 * HD] = rope(key_grad, *tables).astype(BF16)
        joined_ref[0, own, :, at + 2 * HD : at + 3 * HD] = value_grad.astype(BF16)

    @pl.when(block == blocks - 1)
    def _():
        def inner(j, carry):
            tables = (cosine[0, j], -sine_up[0, j], -sine_down[0, j])
            for head in range(heads):
                at = head * 3 * HD
                joined_ref[0, j, :, at : at + HD] = rope(query_grad[head, j], *tables).astype(BF16)
            send_ref[j] = joined_ref[0, j]
            return carry + jnp.sum(joined_ref[0, j].astype(F32), axis=0, keepdims=True)

        sum_ref[0] = lax.fori_loop(0, blocks, inner, jnp.zeros((1, heads * 3 * HD), F32))


def attend_back(place, starts, queries, keys, values, grad, out, log_sums, tables, tokens):
    heads, seqs, blocks, rows, _ = queries.shape
    joined_cols = heads * 3 * HD
    head_spec = pl.BlockSpec((heads, 1, blocks, rows, HD), lambda s, i, *_: (0, s, 0, 0, 0))
    side = pl.BlockSpec((1, blocks, rows, heads * HD), lambda s, i, *_: (s, 0, 0, 0))
    table = pl.BlockSpec((1, blocks, rows, HD), lambda s, i, *_: (s, 0, 0, 0))
    pairs = heads * seqs * blocks * (blocks + 1) // 2
    return launch(
        attend_back_kernel,
        [queries, keys, values, grad, out, log_sums]
        + [item.reshape(seqs, blocks, rows, HD) for item in tables],
        [
            head_spec,
            head_spec,
            head_spec,
            side,
            side,
            pl.BlockSpec((heads, 1, blocks, 1, rows), lambda s, i, *_: (0, s, 0, 0, 0)),
            table,
            table,
            table,
        ],
        (seqs, blocks),
        [
            pl.BlockSpec((1, blocks, rows, joined_cols), lambda s, i, *_: (s, 0, 0, 0)),
            pl.BlockSpec((blocks, rows, joined_cols), lambda s, i, *_: (0, 0, 0)),
            pl.BlockSpec((1, 1, joined_cols), lambda s, i, *_: (s, 0, 0)),
        ],
        [
            jax.ShapeDtypeStruct((seqs, blocks, rows, joined_cols), BF16),
            jax.ShapeDtypeStruct((blocks, rows, joined_cols), BF16),
            jax.ShapeDtypeStruct((seqs, 1, joined_cols), F32),
        ],
        "attend_back",
        cost(pairs * 50 * rows * rows * HD, 12 * queries.size * 2),
        prefetch=[place, starts],
        tokens=tokens,
        scratch_shapes=[
            pltpu.VMEM((heads, blocks, rows, HD), F32),
            pltpu.VMEM((heads, blocks, 1, rows), F32),
        ],
    )


def expand_kernel(normed, weight, bias, activated, send, slope):
    pre = row_product(normed, weight, weight.shape[2]) + bias[...]
    share = 0.5 + 0.5 * lax.erf(pre * math.sqrt(0.5))
    density = jnp.exp2(pre * pre * (-0.5 * LOG2E)) * (1.0 / math.sqrt(2.0 * math.pi))
    result = (pre * share).astype(BF16)
    activated[...] = result
    send[...] = result
    slope[...] = (share + pre * density).astype(BF16)


def later_half(tile, width, steps):
    half = steps // 2
    return pl.BlockSpec((tile, width), lambda i: (jnp.maximum(i - half, 0), 0))


def expand(normed, weight, bias, tokens):
    rows, model_width = normed.shape
    cols = weight.shape[3]
    tile = 512
    steps = rows // tile
    out = pl.BlockSpec((tile, cols), lambda i: (i, 0))
    shape = jax.ShapeDtypeStruct((rows, cols), BF16)
    return launch(
        expand_kernel,
        [normed, weight, bias],
        [pl.BlockSpec((tile, model_width), lambda i: (i, 0)), whole_spec(weight), whole_spec(bias)],
        (steps,),
        [out, later_half(tile, cols, steps), out],
        [shape, jax.ShapeDtypeStruct((rows // 2, cols), BF16), shape],
        "expand",
        cost(
            2 * rows * model_width * cols,
            2 * (rows * model_width + weight.size + 2 * rows * cols),
        ),
        tokens=tokens,
    )


def by_columns(weight):
    groups = weight.shape[0] // 2
    return pl.BlockSpec(
        (2, 1) + weight.shape[2:], lambda i: (lax.rem(i, groups), lax.div(i, groups), 0, 0)
    )


def output_piece(j, pieces, attended, activated, dense, contract, sums, tokens):
    tile = attended[1].shape[0] // pieces
    groups, cores, _, share = dense[0].shape
    steps = groups * cores // 2
    lefts = [*attended, *activated]
    rights = [*dense, *contract]
    extras = sums.extras(j)

    def kernel(*refs):
        outs = refs[8 + len(extras) :]
        arrived = [(q, ref) for (q, _), ref in zip(extras, refs[8:])]
        for n in range(2):
            total = None
            for left, right in zip(refs[:4], refs[4:8]):
                part = jnp.dot(left[...], right[n, 0], preferred_element_type=F32)
                total = part if total is None else total + part
            finish_piece(total, n * share, arrived, outs)

    specs, shapes = piece_specs(tile, 2 * share, steps, sums.splits(j))
    result = launch(
        kernel,
        lefts + rights + [item for _, item in extras],
        [pl.BlockSpec((tile, item.shape[1]), lambda i: (j, 0)) for item in lefts]
        + [by_columns(item) for item in rights]
        + [pl.BlockSpec((tile // 2, 2 * share), lambda i: (0, i))] * len(extras),
        (steps,),
        specs,
        shapes,
        "output_piece",
        cost(4 * tile * sum(item.size for item in rights), 4 * sum(item.size for item in rights)),
        tokens=tokens,
    )
    sums.pieces[j] = result if sums.splits(j) else result[0]
    return result[0]


def dense_back_kernel(grad_ref, att_ref, dense, out, blocks, total):
    step = pl.program_id(0)
    share = dense.shape[3]

    @pl.when(step == 0)
    def _():
        total[...] = jnp.zeros_like(total)

    out[...] = column_back(grad_ref, dense, share).astype(BF16)
    total[...] += lax.dot_general(
        att_ref[...], grad_ref[...], CONTRACT_FIRST, preferred_element_type=F32
    )

    @pl.when(step == pl.num_programs(0) - 1)
    def _():
        for z, c, at in chunks_of(dense):
            blocks[z, c] = total[:, at * share : (at + 1) * share].T.astype(BF16)


def dense_back(grad, attended, dense, tokens):
    rows, width = grad.shape
    groups, cores, cols, share = dense.shape
    turned = jax.ShapeDtypeStruct((groups, cores, share, cols), BF16)
    tile = 512
    return launch(
        dense_back_kernel,
        [grad, attended, dense],
        [
            pl.BlockSpec((tile, width), lambda i: (i, 0)),
            pl.BlockSpec((tile, cols), lambda i: (i, 0)),
            whole_spec(dense),
        ],
        (rows // tile,),
        [pl.BlockSpec((tile, cols), lambda i: (i, 0)), whole_spec(turned)],
        [jax.ShapeDtypeStruct((rows, cols), BF16), turned],
        "dense_back",
        cost(4 * rows * dense.size, 2 * (rows * (width + cols) + dense.size)),
        tokens=tokens,
        scratch_shapes=[pltpu.VMEM((cols, width), F32)],
    )


def pre_grad_kernel(grad_ref, slope, contract, out, send, sums):
    @pl.when(pl.program_id(0) == 0)
    def _():
        sums[...] = jnp.zeros_like(sums)

    part = column_back(grad_ref, contract, contract.shape[3]) * slope[...].astype(F32)
    part = part.astype(BF16)
    out[...] = part
    send[...] = part
    sums[...] += jnp.sum(part.astype(F32), axis=0, keepdims=True)


def pre_grad_of(grad, slope, contract, tokens):
    rows, width = grad.shape
    cols = contract.shape[2]
    tile = 512
    steps = rows // tile
    return launch(
        pre_grad_kernel,
        [grad, slope, contract],
        [
            pl.BlockSpec((tile, width), lambda i: (i, 0)),
            pl.BlockSpec((tile, cols), lambda i: (i, 0)),
            whole_spec(contract),
        ],
        (steps,),
        [
            pl.BlockSpec((tile, cols), lambda i: (i, 0)),
            later_half(tile, cols, steps),
            pl.BlockSpec((1, cols), lambda i: (0, 0)),
        ],
        [
            jax.ShapeDtypeStruct((rows, cols), BF16),
            jax.ShapeDtypeStruct((rows // 2, cols), BF16),
            jax.ShapeDtypeStruct((1, cols), F32),
        ],
        "pre_grad",
        cost(2 * rows * contract.size, 2 * (rows * width + contract.size + 2 * rows * cols)),
        tokens=tokens,
    )


def normed_grad_piece(
    j, pieces, joined, pre, joined_weight, expand_weight, normal, gain1, gain2, sums, tokens
):
    tile = joined[1].shape[0] // pieces
    groups, cores, share, _ = joined_weight[0].shape
    steps = groups * cores // 2
    lefts = [*joined, *pre]
    rights = [*joined_weight, *expand_weight]
    extras = sums.extras(j)

    def kernel(*refs):
        normal, gain1, gain2 = refs[8:11]
        arrived = [(q, ref) for (q, _), ref in zip(extras, refs[11:])]
        *outs, along = refs[11 + len(extras) :]
        for n in range(2):

            def back(at):
                return lax.dot_general(
                    refs[at][...], refs[at + 4][n, 0], CONTRACT_LAST, preferred_element_type=F32
                )

            cols = slice(n * share, (n + 1) * share)
            first, second = back(0) + back(1), back(2) + back(3)
            rows = normal[:, cols].astype(F32)
            along[0:1, cols] = jnp.sum(first * rows, axis=0, keepdims=True)
            along[1:2, cols] = jnp.sum(first, axis=0, keepdims=True)
            along[2:3, cols] = jnp.sum(second * rows, axis=0, keepdims=True)
            along[3:4, cols] = jnp.sum(second, axis=0, keepdims=True)
            finish_piece(
                first * gain1[:, cols] + second * gain2[:, cols], n * share, arrived, outs
            )

    row = pl.BlockSpec((1, 2 * share), lambda i: (0, i))
    specs, shapes = piece_specs(tile, 2 * share, steps, sums.splits(j))
    *result, along = launch(
        kernel,
        lefts + rights + [normal, gain1, gain2] + [item for _, item in extras],
        [pl.BlockSpec((tile, item.shape[1]), lambda i: (j, 0)) for item in lefts]
        + [by_columns(item) for item in rights]
        + [pl.BlockSpec((tile, 2 * share), lambda i: (j, i)), row, row]
        + [pl.BlockSpec((tile // 2, 2 * share), lambda i: (0, i))] * len(extras),
        (steps,),
        specs + [pl.BlockSpec((8, 2 * share), lambda i: (0, i))],
        shapes + [jax.ShapeDtypeStruct((8, steps * 2 * share), F32)],
        "normed_grad_piece",
        cost(4 * tile * sum(item.size for item in rights), 4 * sum(item.size for item in rights)),
        tokens=tokens,
    )
    sums.pieces[j] = result if sums.splits(j) else result[0]
    return along


def rows_at(half, width, here):
    if here:
        return pl.BlockSpec((1, half, width), lambda i, place: (place[1], i, 0))
    return pl.BlockSpec((1, half, width), lambda i, place: (1 - place[1], i, 0))


def finish_tile(body, name, place, operands, whole, tile, width, tokens=()):
    half = tile // 2
    listed, specs, picks = [], [], []
    for pair in operands:
        if not isinstance(pair, list):
            picks.append((len(listed), False))
            listed.append(pair)
            specs.append(pl.BlockSpec((1, half, width), lambda i, place: (place[1], i, 0)))
        elif pair[0][0] is pair[1][0] and (pair[0][1], pair[1][1]) == (0, 1):
            picks.append((len(listed), False))
            listed.append(pair[0][0])
            specs.append(pl.BlockSpec((half, width), lambda i, place: (i, 0)))
        else:
            picks.append((len(listed), True))
            for item, at in pair:
                listed.append(item)
                specs.append(pl.BlockSpec((half, width), lambda i, place, at=at: (at, 0)))
    count = len(listed)

    def kernel(place, *refs):
        both, own = refs[count + len(whole) :]
        first = pl.program_id(0) == 0
        values = [
            jnp.where(first, refs[at][...], refs[at + 1][...])
            if pair
            else refs[at][...].reshape(half, width)
            for at, pair in picks
        ]
        result = body(values, refs[count : count + len(whole)]).astype(BF16)
        both[0] = result
        own[...] = result

    return launch(
        kernel,
        listed + list(whole),
        specs + [pl.BlockSpec(item.shape, lambda i, place: (0, 0)) for item in whole],
        (2,),
        [rows_at(half, width, True), pl.BlockSpec((half, width), lambda i, place: (i, 0))],
        [
            jax.ShapeDtypeStruct((2, tile, width), BF16),
            jax.ShapeDtypeStruct((tile, width), BF16),
        ],
        name,
        cost(20 * tile * width, 20 * tile * width),
        prefetch=[place],
        tokens=tokens,
    )


def pick_other(place, total, tokens):
    _, rows, cols = total.shape

    def pick(place, value, out):
        out[...] = value[0]

    other = launch(
        pick,
        [total],
        [pl.BlockSpec((1, rows, cols), lambda i, place: (1 - place[1], 0, 0))],
        (1,),
        pl.BlockSpec((rows, cols), lambda i, place: (0, 0)),
        jax.ShapeDtypeStruct((rows, cols), BF16),
        "pick_other",
        cost(1, 4 * rows * cols),
        prefetch=[place],
        tokens=tokens,
    )
    return swap(other, "branch", 1)


def join_cores(place, total, other, straight, tokens):
    _, rows, cols = total.shape
    turned = cols - straight

    def join(place, mine, others, *outs):
        value = jnp.where(pl.program_id(0) == 0, mine[0], others[...]).astype(F32)
        if straight:
            outs[0][...] = value[:, :straight]
        if turned:
            outs[-1][...] = value[:, straight:].T

    specs, shapes = [], []
    if straight:
        specs.append(pl.BlockSpec((rows, straight), lambda i, place: (0, place[1] ^ i)))
        shapes.append(jax.ShapeDtypeStruct((rows, 2 * straight), F32))
    if turned:
        specs.append(pl.BlockSpec((turned, rows), lambda i, place: (place[1] ^ i, 0)))
        shapes.append(jax.ShapeDtypeStruct((2 * turned, rows), F32))
    return launch(
        join,
        [total, other],
        [
            pl.BlockSpec((1, rows, cols), lambda i, place: (place[1], 0, 0)),
            pl.BlockSpec((rows, cols), lambda i, place: (0, 0)),
        ],
        (2,),
        specs,
        shapes,
        "finish_weight",
        cost(1, 16 * rows * cols),
        prefetch=[place],
        tokens=tokens,
    )


def fill_other(place, both, other, tokens=()):
    tile, width = other.shape

    def kernel(place, value, out):
        out[0] = value[...]

    return launch(
        kernel,
        [other],
        [pl.BlockSpec((tile // 2, width), lambda i, place: (i, 0))],
        (2,),
        rows_at(tile // 2, width, False),
        jax.ShapeDtypeStruct(both.shape, BF16),
        "fill_other",
        cost(1, 4 * tile * width),
        prefetch=[place],
        tokens=tokens,
        held=[both],
    )


def per_device(
    block_input,
    first_norm_gain,
    first_norm_bias,
    second_norm_gain,
    second_norm_bias,
    query_key_value,
    query_key_value_bias,
    attention_dense,
    attention_dense_bias,
    expand_weight,
    expand_bias,
    contract_weight,
    contract_bias,
    document_starts,
    output_grad,
):
    seqs, tile, model_width = block_input.shape
    tiles = lax.axis_size("tp")
    groups = lax.axis_size("seq")
    core = lax.axis_index("branch")
    here = lax.axis_index("tp")
    first_core = core == 0
    length = tile * tiles
    rows_in_all = length * seqs
    share = query_key_value.shape[0]

    def by_core(mine, others):
        return jnp.where(first_core, mine, others), jnp.where(first_core, others, mine)

    def halves_of(value, axis):
        size = value.shape[axis] // 2
        return (
            lax.dynamic_slice_in_dim(value, core * size, size, axis),
            lax.dynamic_slice_in_dim(value, (1 - core) * size, size, axis),
        )

    place = jnp.stack([here, core]).astype(jnp.int32)

    input_halves = own_halves(place, block_input)
    near = {**gather_near(input_halves, 0), **gather_near(input_halves, 1)}

    def core_halves(weight, axis):
        mine, others = halves_of(weight, axis)
        return jnp.stack(by_core(mine, swap(others, "branch", 1)))

    def gather_seq(piece):
        return lax.all_gather(piece, "seq", axis=0)

    weight_pieces = [
        core_halves(query_key_value, 1),
        core_halves(expand_weight, 1),
        core_halves(attention_dense, 0),
        core_halves(contract_weight, 0),
    ]
    joined_weight, expand_full, dense_full, contract_full = map(gather_seq, weight_pieces)
    joined_bias = halves_of(query_key_value_bias, 0)[0].astype(F32)[None]
    hidden_bias = halves_of(expand_bias, 0)[0].astype(F32)[None]

    gain1 = first_norm_gain.astype(F32)[None]
    gain2 = second_norm_gain.astype(F32)[None]
    gains = (
        gain1,
        first_norm_bias.astype(F32)[None],
        gain2,
        second_norm_bias.astype(F32)[None],
    )
    tables = rotary_tables(place, document_starts, rows_in_all, weight_pieces)
    grad_halves = own_halves(place, output_grad, [tables[0]])
    grad_rows = place_piece(0, place, output_grad, rows_in_all, (), grad_halves)
    *normed, mark = norm_piece(
        0, place, block_input, rows_in_all, gains, (), [tables[0], grad_rows]
    )
    near = in_pieces(hold_all(near, mark), {})
    far = gather_far(near)
    for j in sorted(near):
        *normed, mark = norm_piece(
            j, place, with_other_core(near[j]), rows_in_all, gains, normed, []
        )
    heads_held = ()
    far_from = tiles
    if tiles == 4:
        heads_held = project(0, 3, normed[1], joined_weight, joined_bias, tables, ())
        far_from = 3
    for j in sorted(far):
        last_items = [hold(item, mark) for item in far[j]]
        *normed, mark = norm_piece(
            j, place, with_other_core(last_items), rows_in_all, gains, normed, heads_held[:1]
        )
    heads_held = project(
        far_from % tiles, tiles, normed[1], joined_weight, joined_bias, tables, heads_held
    )
    normal, first_normed, second_normed = normed
    queries, keys, values = heads_held

    first = gather_near([hold(item, *last_items) for item in grad_halves], 0)
    first = hold_all(first, queries)
    second = gather_near([hold(item, *first.values()) for item in grad_halves], 1)
    attended, attended_send, log_sums = attend(
        place, document_starts, queries, keys, values, [*first.values()]
    )
    attended_flat = attended.reshape(rows_in_all, -1)
    near = in_pieces(first, hold_all(second, log_sums))
    far = gather_far(near)
    activated, activated_send, slope = expand(
        second_normed, expand_full, hidden_bias, [item for j in near for item in near[j]]
    )
    near = {
        j: items + [hold(swap(item, "branch", 1), slope) for item in items]
        for j, items in near.items()
    }
    far = {j: [hold(item, slope) for item in items] for j, items in far.items()}
    arrived = [item for items in [*near.values(), *far.values()] for item in items]
    far = {j: with_other_core(items) for j, items in far.items()}
    for j, items in {**near, **far}.items():
        grad_rows = place_piece(j, place, items, rows_in_all, [grad_rows], [slope])

    def weight_grad(left, right):
        return lax.dot_general(left, right, CONTRACT_FIRST, preferred_element_type=F32).astype(BF16)

    def in_order(part):
        return part.reshape(2, groups, share, part.shape[1]).transpose(1, 0, 2, 3)

    def scatter(blocks):
        return lax.psum_scatter(blocks, "seq", scatter_dimension=0, tiled=False)

    def exchanged(own, send, *tokens):
        send = send.reshape(-1, send.shape[-1])
        return own.reshape(-1, own.shape[-1]), swap(hold(send, *tokens) if tokens else send, "branch", 1)

    def with_other_weight(weight):
        return weight, swap(weight, "branch", 1)

    attended_pair = exchanged(attended, attended_send, *arrived)
    activated_pair = exchanged(activated, activated_send, *arrived)
    contract_blocks = in_order(weight_grad(grad_rows, activated))
    contract_total = scatter(contract_blocks)
    contract_full = hold(contract_full, contract_blocks)
    pre_grad, pre_send, pre_sums = pre_grad_of(
        grad_rows, slope, contract_full, [contract_blocks]
    )
    pre_pair = exchanged(pre_grad, pre_send)
    contract_pair = with_other_weight(contract_full)
    expand_blocks = in_order(weight_grad(second_normed, pre_grad))
    expand_total = scatter(expand_blocks)
    dense_pair = with_other_weight(dense_full)
    order = sorted(range(1, tiles), key=lambda j: (-bin(j).count("1"), j))
    outputs = TileSum()

    def output(j, *tokens):
        return output_piece(
            j, tiles, attended_pair, activated_pair, dense_pair, contract_pair, outputs, tokens
        )

    mark = expand_blocks
    operands = []
    for number, j in enumerate(order):
        if number and bin(order[number - 1]).count("1") > bin(j).count("1"):
            if not outputs.pieces.get(0) is None:
                operands += outputs.land(mark)
            else:
                attended_grad, dense_blocks = dense_back(
                    grad_rows, attended_flat, dense_full, [mark, *operands]
                )
                mark = output(0, attended_grad)
                operands = outputs.land(mark)
        mark = output(j, mark, *operands)
        operands = outputs.send() if outputs.complete(j) else []
    operands += outputs.send()
    landed = []
    joined_grad, joined_send, joined_sums = attend_back(
        place,
        document_starts,
        queries,
        keys,
        values,
        attended_grad.reshape(attended.shape),
        attended,
        log_sums,
        tables,
        [mark, *operands],
    )
    landed = outputs.land(joined_sums)
    joined_pair = exchanged(joined_grad, joined_send, *landed)
    joined_weight_pair = with_other_weight(joined_weight)
    expand_weight_pair = with_other_weight(expand_full)
    joined_grad = joined_pair[0]
    inputs = TileSum()
    sums = jnp.zeros((8, model_width), F32)
    mark = joined_sums
    wait = landed
    joined_blocks = None
    for number, j in enumerate(order + [0]):
        if number and j and bin(order[number - 1]).count("1") > bin(j).count("1"):
            if joined_blocks is None:
                part = weight_grad(hold(first_normed, mark, *wait), joined_grad)
                wait = inputs.land(part)
                joined_blocks = jnp.concatenate(
                    [in_order(hold(part, *wait)), dense_blocks], axis=3
                )
                joined_total = scatter(joined_blocks)
                mark = joined_blocks
            else:
                wait = inputs.land(mark)
        part = normed_grad_piece(
            j,
            tiles,
            joined_pair,
            pre_pair,
            joined_weight_pair,
            expand_weight_pair,
            normal,
            gain1,
            gain2,
            inputs,
            [mark, *wait],
        )
        sums = sums + part
        mark = part
        wait = inputs.send()
    landed = inputs.land(mark)

    biases = (
        attention_dense_bias.astype(F32)[None],
        contract_bias.astype(F32)[None],
    )

    def output_body(values, whole):
        return add_up(values) + whole[0][...] + whole[1][...]

    def all_sum_beside(value, axis, others):
        size = lax.axis_size(axis)
        bit = 1
        while bit < size:
            arrived = swap(value, axis, bit)
            if others:
                arrived = hold(arrived, *others.pop(0)())
            value = value + arrived
            bit *= 2
        return value

    kept = {}

    def first_beside():
        kept["both"], kept["own"] = finish_tile(
            output_body,
            "finish_output",
            place,
            [block_input] + outputs.terms(),
            biases,
            tile,
            model_width,
            [mark],
        )
        return [kept["own"]]

    def second_beside():
        kept["contract"] = pick_other(place, contract_total, [kept["own"]])
        kept["expand"] = pick_other(place, expand_total, [kept["contract"]])
        return [kept["expand"]]

    def third_beside():
        (kept["contract_grad"],) = join_cores(
            place, contract_total, kept["contract"], 0, [kept["expand"]]
        )
        return [kept["contract_grad"], *landed]

    def fourth_beside():
        (kept["expand_grad"],) = join_cores(
            place,
            expand_total,
            kept["expand"],
            expand_total.shape[2],
            [kept["contract_grad"]],
        )
        return [kept["expand_grad"]]

    def fifth_beside():
        kept["output"] = fill_other(
            place, kept["both"], swap(kept["own"], "branch", 1), [kept["expand_grad"]]
        )
        return [kept["output"]]

    others = [first_beside, second_beside, third_beside, fourth_beside, fifth_beside]
    joined_bias_part = jnp.sum(joined_sums, axis=0).reshape(-1)
    hidden_bias_part = pre_sums[0]
    grad_own = lax.dynamic_index_in_dim(output_grad, core, 0, False)
    small = jnp.concatenate(
        [
            sums[:4].reshape(-1),
            jnp.sum(grad_own.astype(F32), axis=0),
            joined_bias_part,
            hidden_bias_part,
        ]
    )
    everywhere = 5 * model_width
    small = all_sum_beside(hold(small, mark), "seq", others)
    per_core = small[everywhere:]
    both = jnp.stack(by_core(per_core, swap(per_core, "branch", 1)))
    query_key_value_bias_grad = both[:, : joined_bias_part.shape[0]].reshape(-1)
    expand_bias_grad = both[:, joined_bias_part.shape[0] :].reshape(-1)
    shared = all_sum_beside(small[:everywhere], "tp", others)
    shared = all_sum_beside(shared, "branch", others).reshape(5, model_width)
    while others:
        others.pop(0)()
    block_output, contract_grad = kept["output"], kept["contract_grad"]
    expand_grad = kept["expand_grad"]
    joined_other = pick_other(place, joined_total, [shared, block_output])

    def input_body(values, whole):
        x, grad = values[0].astype(F32), values[1].astype(F32)
        total = add_up(values[2:])
        centred = x - jnp.mean(x, axis=-1, keepdims=True)
        rate = lax.rsqrt(jnp.mean(centred * centred, axis=-1, keepdims=True) + EPSILON)
        n = centred * rate
        middle = jnp.mean(total, axis=-1, keepdims=True)
        along = jnp.mean(total * n, axis=-1, keepdims=True)
        return grad + rate * (total - middle - n * along)

    input_both, input_grad_own = finish_tile(
        input_body,
        "finish_input",
        place,
        [block_input, output_grad] + inputs.terms(),
        (),
        tile,
        model_width,
        [joined_other],
    )
    query_key_value_grad, dense_grad = join_cores(
        place, joined_total, joined_other, joined_weight.shape[3], [input_grad_own]
    )
    input_grad = fill_other(
        place, input_both, swap(input_grad_own, "branch", 1), [query_key_value_grad]
    )
    return (
        block_output,
        input_grad,
        shared[0],
        shared[1],
        shared[2],
        shared[3],
        query_key_value_grad,
        query_key_value_bias_grad,
        dense_grad,
        shared[4],
        expand_grad,
        expand_bias_grad,
        contract_grad,
        shared[4],
    )


def solution(mesh):
    in_specs = (
        P("seq", "tp", None),
        P(),
        P(),
        P(),
        P(),
        P(("branch", "seq"), "tp"),
        P("tp"),
        P("tp", ("branch", "seq")),
        P(),
        P(("branch", "seq"), "tp"),
        P("tp"),
        P("tp", ("branch", "seq")),
        P(),
        P("seq", None),
        P("seq", "tp", None),
    )
    out_specs = (
        P("seq", "tp", None),
        P("seq", "tp", None),
        P(),
        P(),
        P(),
        P(),
        P(("branch", "seq"), "tp"),
        P("tp"),
        P("tp", ("branch", "seq")),
        P(),
        P(("branch", "seq"), "tp"),
        P("tp"),
        P("tp", ("branch", "seq")),
        P(),
    )
    return jax.shard_map(
        per_device, mesh=mesh, in_specs=in_specs, out_specs=out_specs, check_vma=False
    )
```

```python
from functools import partial
import math

import jax
import jax.numpy as jnp
from jax import lax
from jax.experimental import pallas as pl
from jax.experimental.pallas import tpu as pltpu
from jax.sharding import PartitionSpec as P

HD = 128
ROT = 32


EPSILON = 1e-05
NEGATIVE = -1e30
ROPE_BASE = 10000.0
LOG2E = math.log2(math.e)
F32 = jnp.float32
BF16 = jnp.bfloat16
CONTRACT_LAST = (((1,), (1,)), ((), ()))
CONTRACT_FIRST = (((0,), (0,)), ((), ()))
VMEM_BYTES = 56 * 1024 * 1024
ANY = pl.BlockSpec(memory_space=pl.ANY)
HINT = 0.02


def cost(flops, moved, transcendentals=0):
    return pl.CostEstimate(
        flops=1 + int(flops * HINT), bytes_accessed=1 + int(moved * HINT), transcendentals=0
    )


def launch(
    kernel,
    operands,
    in_specs,
    grid,
    out_specs,
    out_shape,
    name,
    cost_estimate,
    prefetch=(),
    held=(),
    tokens=(),
    scratch_shapes=(),
):
    lead = len(prefetch) + len(operands)
    extra = len(held) + len(tokens)

    def body(*refs):
        kernel(*refs[:lead], *refs[lead + extra :])

    return pl.pallas_call(
        body,
        grid_spec=pltpu.PrefetchScalarGridSpec(
            num_scalar_prefetch=len(prefetch),
            grid=grid,
            in_specs=list(in_specs) + [ANY] * extra,
            out_specs=out_specs,
            scratch_shapes=list(scratch_shapes),
        ),
        out_shape=out_shape,
        input_output_aliases={lead + k: k for k in range(len(held))},
        compiler_params=pltpu.CompilerParams(
            dimension_semantics=("arbitrary",) * len(grid), vmem_limit_bytes=VMEM_BYTES
        ),
        cost_estimate=cost_estimate,
        name=name,
    )(*prefetch, *operands, *held, *tokens)


def hold(value, *tokens):
    def nothing(out):
        pass

    return launch(
        nothing,
        [],
        [],
        (1,),
        ANY,
        jax.ShapeDtypeStruct(value.shape, value.dtype),
        "hold",
        cost(1, 1),
        held=[value],
        tokens=tokens,
    )


def swap(value, axis, bit):
    size = lax.axis_size(axis)
    return lax.ppermute(value, axis, [(i, i ^ bit) for i in range(size)])


def onward(value, axis):
    size = lax.axis_size(axis)
    return lax.ppermute(value, axis, [(i, (i + 1) % size) for i in range(size)])


def bit_orders(size):
    bits = [1 << k for k in range(size.bit_length() - 1)]
    return (bits, bits[::-1])


def last_bit(number, order):
    return [bit for bit in order if number & bit][-1]


def gather_near(own, number):
    size = lax.axis_size("tp")
    bits = [1 << k for k in range(size.bit_length() - 1)]
    return {
        (bit, (n + number) % 2): swap(own[(n + number) % 2], "tp", bit)
        for n, bit in enumerate(bits)
    }


def hold_all(items, *tokens):
    return {key: hold(item, *tokens) for key, item in items.items()}


def in_pieces(first, second):
    items = {**first, **second}
    return {j: [items[j, 0], items[j, 1]] for j in sorted({j for j, _ in items})}


def gather_far(near):
    size = lax.axis_size("tp")
    pieces = dict(near)
    far = {}
    for j in sorted(range(1, size), key=lambda j: bin(j).count("1")):
        if j not in near:
            bits = [last_bit(j, order) for order in bit_orders(size)]
            far[j] = [swap(pieces[j ^ bit][q], "tp", bit) for q, bit in enumerate(bits)]
            pieces[j] = far[j]
    return far


def with_other_core(items):
    return items + [swap(item, "branch", 1) for item in items]


def add_up(items):
    total = items[0].astype(F32)
    for item in items[1:]:
        total = total + item.astype(F32)
    return total


class TileSum:
    def __init__(self):
        size = lax.axis_size("tp")
        self.orders = bit_orders(size)
        self.waiting = [(q, j) for j in range(1, size) for q in range(2)]
        self.expected = {(q, j): 0 for j in range(size) for q in range(2)}
        for q, j in self.waiting:
            self.expected[q, j ^ last_bit(j, self.orders[q])] += 1
        self.waiting.sort(key=lambda at: (-bin(at[1]).count("1"), at[1]))
        self.pieces = {}
        self.arrived = {}
        self.moving = []

    def splits(self, j):
        return j > 0 and len({last_bit(j, order) for order in self.orders}) > 1

    def extras(self, j):
        return [(q, item) for q in range(2) for item in self.arrived.get((q, j), [])]

    def complete(self, j):
        return all(len(self.arrived.get((q, j), [])) == self.expected[q, j] for q in range(2))

    def send(self, *tokens):
        operands = []
        for q, j in list(self.waiting):
            if j not in self.pieces or (q, j) not in self.waiting:
                continue
            bit = last_bit(j, self.orders[q])
            if self.splits(j):
                sides, operand = [q], self.pieces[j][q]
            else:
                sides, operand = [0, 1], self.pieces[j]
            for side in sides:
                self.waiting.remove((side, j))
            if tokens:
                operand = hold(operand, *tokens)
            self.moving.append((sides, j ^ bit, swap(operand, "tp", bit)))
            operands.append(operand)
        return operands

    def land(self, *tokens):
        items = []
        for sides, j, item in self.moving:
            item = hold(item, *tokens) if tokens else item
            items.append(item)
            if j == 0:
                self.arrived.setdefault(0, []).append(item)
                continue
            half = item.shape[0] // 2
            for side in sides:
                part = item[side * half : (side + 1) * half] if len(sides) > 1 else item
                self.arrived.setdefault((side, j), []).append(part)
        self.moving = []
        return items

    def terms(self):
        return [[(item, 0), (item, 1)] for item in [self.pieces[0]] + self.arrived[0]]


def finish_piece(total, column, extras, outs):
    half = total.shape[0] // 2
    width = total.shape[1]
    cols = slice(column, column + width)
    parts = [total[:half], total[half:]]
    for q, ref in extras:
        parts[q] = parts[q] + ref[:, cols].astype(F32)
    for q in range(2):
        if len(outs) > 1:
            outs[q][:, cols] = parts[q].astype(BF16)
        else:
            outs[0][q * half : (q + 1) * half, cols] = parts[q].astype(BF16)


def piece_specs(tile, share, steps, split):
    rows, count = (tile // 2, 2) if split else (tile, 1)
    return (
        [pl.BlockSpec((rows, share), lambda i: (0, i))] * count,
        [jax.ShapeDtypeStruct((rows, steps * share), BF16)] * count,
    )


def all_sum(value, axis):
    size = lax.axis_size(axis)
    bit = 1
    while bit < size:
        value = value + swap(value, axis, bit)
        bit *= 2
    return value


def rope(vectors, cosine, sine_up, sine_down):
    return (
        vectors * cosine
        + pltpu.roll(vectors, ROT // 2, 1) * sine_up
        + pltpu.roll(vectors, HD - ROT // 2, 1) * sine_down
    )


class Documents:
    def __init__(self, place, starts, seq_at, rows):
        self.row = place[1] ^ seq_at
        self.starts = starts
        self.rows = rows

    def begin(self, places):
        begin = jnp.zeros_like(places)
        for number in range(self.starts.shape[1]):
            start = self.starts[self.row, number]
            begin = jnp.where(places >= start, start, begin)
        return begin

    def first_key_block(self, block):
        return lax.div(self.begin(block * self.rows), jnp.int32(self.rows))

    def last_query_block(self, block, blocks):
        last = block
        for number in range(1, blocks):
            after = jnp.minimum(block + number, blocks - 1)
            last = jnp.where(self.first_key_block(after) <= block, jnp.maximum(last, after), last)
        return last


def table_kernel(place, starts, cosine, sine_up, sine_down):
    rows = cosine.shape[0]
    blocks = lax.axis_size("tp")
    step = pl.program_id(0)
    block, seq_at = lax.rem(step, blocks) ^ place[0], lax.div(step, blocks)
    places = block * rows + lax.broadcasted_iota(jnp.int32, (rows, 1), 0)
    begin = Documents(place, starts, seq_at, rows).begin(places)
    lane = lax.broadcasted_iota(jnp.int32, (1, HD), 1)
    half = ROT // 2
    number = jnp.where(lane < half, lane, lane - half).astype(F32)
    frequency = jnp.exp2(number * (-2.0 / ROT * math.log2(ROPE_BASE)))
    angles = (places - begin).astype(F32) * jnp.where(lane < ROT, frequency, 0.0)
    cosine[...] = jnp.cos(angles)
    sines = jnp.sin(angles)
    sine_up[...] = jnp.where((lane >= half) & (lane < ROT), sines, 0.0)
    sine_down[...] = jnp.where(lane < half, -sines, 0.0)


def rotary_tables(place, starts, rows, tokens):
    steps = 2 * lax.axis_size("tp")
    tile = rows // steps
    out = pl.BlockSpec((tile, HD), lambda i, *_: (i, 0))
    return launch(
        table_kernel,
        [],
        [],
        (steps,),
        [out] * 3,
        [jax.ShapeDtypeStruct((rows, HD), F32)] * 3,
        "rotary_tables",
        cost(rows * HD * 100, rows * HD * 48),
        prefetch=[place, starts],
        tokens=tokens,
    )


def half_of_piece(j):
    size = lax.axis_size("tp")
    return lambda i, *_: ((lax.div(i, 2) * size + j) * 2 + lax.rem(i, 2), 0)


def own_tile_specs(tile):
    _, rows, width = tile.shape

    def spec(h, q):
        return pl.BlockSpec((1, rows // 2, width), lambda i, place: (place[1] ^ h, q, 0))

    return [spec(h, q) for h in range(2) for q in range(2)]


def own_halves(place, tile, tokens=()):
    _, rows, width = tile.shape

    def kernel(place, first, second, out_first, out_second):
        out_first[...] = first[0]
        out_second[...] = second[0]

    shape = jax.ShapeDtypeStruct((rows // 2, width), BF16)
    return launch(
        kernel,
        [tile, tile],
        own_tile_specs(tile)[:2],
        (1,),
        [whole_spec(shape)] * 2,
        [shape, shape],
        "own_halves",
        cost(1, 4 * rows * width),
        prefetch=[place],
        tokens=tokens,
    )


def place_kernel(place, x0, x1, x2, x3, out):
    step = pl.program_id(0)
    for number, x_ref in enumerate((x0, x1, x2, x3)):

        @pl.when(step == number)
        def _(x_ref=x_ref):
            out[...] = x_ref[...].reshape(out.shape)


def place_piece(j, place, halves, rows_in_all, held, tokens=()):
    if j == 0:
        specs = own_tile_specs(halves)
        half, model_width = halves.shape[1] // 2, halves.shape[2]
        halves = [halves] * 4
    else:
        half, model_width = halves[0].shape
        specs = [whole_spec(item) for item in halves]
    return launch(
        place_kernel,
        halves,
        specs,
        (4,),
        pl.BlockSpec((half, model_width), half_of_piece(j)),
        jax.ShapeDtypeStruct((rows_in_all, model_width), BF16),
        "place_piece",
        cost(1, 4 * half * model_width * 4),
        prefetch=[place],
        held=held,
        tokens=tokens,
    )


def norm_kernel(place, x0, x1, x2, x3, gain1, shift1, gain2, shift2, *rest):
    normal, first, second, mark, scratch = rest[-5:]
    step = pl.program_id(0)
    mark[...] = jnp.zeros_like(mark)
    for number, x_ref in enumerate((x0, x1, x2, x3)):

        @pl.when(step == number)
        def _(x_ref=x_ref):
            scratch[...] = (x_ref[0] if len(x_ref.shape) == 3 else x_ref[...]).astype(F32)

    x = scratch[...]
    centred = x - jnp.mean(x, axis=-1, keepdims=True)
    variance = jnp.mean(centred * centred, axis=-1, keepdims=True)
    n = centred * lax.rsqrt(variance + EPSILON)
    normal[...] = n.astype(BF16)
    first[...] = (n * gain1[...] + shift1[...]).astype(BF16)
    second[...] = (n * gain2[...] + shift2[...]).astype(BF16)


def norm_piece(j, place, halves, rows_in_all, gains, held, tokens):
    if j == 0:
        specs = own_tile_specs(halves)
        half, model_width = halves.shape[1] // 2, halves.shape[2]
        halves = [halves] * 4
    else:
        half, model_width = halves[0].shape
        specs = [whole_spec(item) for item in halves]
    wide = pl.BlockSpec((half, model_width), half_of_piece(j))
    return launch(
        norm_kernel,
        halves + list(gains),
        specs + [whole_spec(item) for item in gains],
        (4,),
        [wide] * 3 + [pl.BlockSpec((8, HD), lambda i, *_: (0, 0))],
        [jax.ShapeDtypeStruct((rows_in_all, model_width), BF16)] * 3
        + [jax.ShapeDtypeStruct((8, HD), F32)],
        "norm_piece",
        cost(4 * half * model_width * 16, 4 * half * model_width * 16),
        prefetch=[place],
        held=held,
        tokens=tokens,
        scratch_shapes=[pltpu.VMEM((half, model_width), F32)],
    )


def chunks_of(weight):
    groups, cores = weight.shape[:2]
    return [(z, c, c * groups + z) for c in range(cores) for z in range(groups)]


def row_product(left, weight, share):
    total = None
    for z, c, at in chunks_of(weight):
        part = jnp.dot(
            left[:, at * share : (at + 1) * share], weight[z, c], preferred_element_type=F32
        )
        total = part if total is None else total + part
    return total


def column_back(left, weight, share):
    total = None
    for z, c, at in chunks_of(weight):
        part = lax.dot_general(
            left[:, at * share : (at + 1) * share],
            weight[z, c],
            CONTRACT_LAST,
            preferred_element_type=F32,
        )
        total = part if total is None else total + part
    return total


def whole_spec(array, prefetched=0):
    rank = array.ndim
    return pl.BlockSpec(array.shape, lambda *at: (0,) * rank)


def project_kernel(normed, weight, bias, cosine, sine_up, sine_down, queries, keys, values):
    joined = row_product(normed, weight, weight.shape[2]) + bias[...]
    tables = (cosine[...], sine_up[...], sine_down[...])
    for head in range(queries.shape[0]):
        at = head * 3 * HD
        queries[head, 0, 0] = rope(joined[:, at : at + HD], *tables).astype(BF16)
        keys[head, 0, 0] = rope(joined[:, at + HD : at + 2 * HD], *tables).astype(BF16)
        values[head, 0, 0] = joined[:, at + 2 * HD : at + 3 * HD].astype(BF16)


def project(first, last, normed, weight, bias, tables, held):
    rows, model_width = normed.shape
    joined_cols = weight.shape[3]
    heads = joined_cols // (3 * HD)
    size = lax.axis_size("tp")
    tile = rows // (2 * size)
    table = pl.BlockSpec((tile, HD), lambda s, i: (s * size + first + i, 0))
    share = (last - first) / size
    return launch(
        project_kernel,
        [normed, weight, bias] + list(tables),
        [
            pl.BlockSpec((tile, model_width), lambda s, i: (s * size + first + i, 0)),
            whole_spec(weight),
            whole_spec(bias),
            table,
            table,
            table,
        ],
        (2, last - first),
        [pl.BlockSpec((heads, 1, 1, tile, HD), lambda s, i: (0, s, first + i, 0, 0))] * 3,
        [jax.ShapeDtypeStruct((heads, 2, size, tile, HD), BF16)] * 3,
        "project",
        cost(
            2 * rows * share * model_width * joined_cols,
            2 * (rows * share * (model_width + joined_cols) + weight.size),
        ),
        held=held,
    )


def attend_kernel(place, starts, q_ref, k_ref, v_ref, out_ref, send_ref, lse_ref):
    block = pl.program_id(1)
    heads, rows = q_ref.shape[0], q_ref.shape[-2]
    here = place[0]
    documents = Documents(place, starts, pl.program_id(0), rows)
    low = documents.first_key_block(block)
    query_places = block * rows + lax.broadcasted_iota(jnp.int32, (rows, 1), 0)
    begin = documents.begin(query_places)
    factor = LOG2E / math.sqrt(HD)

    def step(number, carry):
        key_places = number * rows + lax.broadcasted_iota(jnp.int32, (1, rows), 1)
        allowed = (key_places >= begin) & (key_places <= query_places)
        results = []
        for head in range(heads):
            top, total, mixed = carry[head]
            key = k_ref[head, 0, number ^ here]
            value = v_ref[head, 0, number ^ here]
            scores = lax.dot_general(
                q_ref[head, 0, 0], key, CONTRACT_LAST, preferred_element_type=F32
            )
            scores = jnp.where(allowed, scores * factor, NEGATIVE)
            new_top = jnp.maximum(top, jnp.max(scores, axis=-1, keepdims=True))
            weights = jnp.exp2(scores - new_top)
            shrink = jnp.exp2(top - new_top)
            total = total * shrink + jnp.sum(weights, axis=-1, keepdims=True)
            mixed = mixed * shrink + jnp.dot(
                weights.astype(BF16), value, preferred_element_type=F32
            )
            results.append((new_top, total, mixed))
        return tuple(results)

    empty = (
        jnp.full((rows, 1), NEGATIVE, F32),
        jnp.zeros((rows, 1), F32),
        jnp.zeros((rows, HD), F32),
    )
    results = lax.fori_loop(low, block + 1, step, (empty,) * heads)
    for head, (top, total, mixed) in enumerate(results):
        result = (mixed / total).astype(BF16)
        out_ref[0, 0, :, head * HD : (head + 1) * HD] = result
        send_ref[0, :, head * HD : (head + 1) * HD] = result
        log_sum = top + jnp.log(total) * LOG2E
        lse_ref[head, 0, 0] = jnp.broadcast_to(log_sum, (rows, HD)).T[:1]


def attend(place, starts, queries, keys, values, tokens):
    heads, seqs, blocks, rows, _ = queries.shape
    one = pl.BlockSpec(
        (heads, 1, 1, rows, HD), lambda s, i, place, starts: (0, s, i ^ place[0], 0, 0)
    )
    full = pl.BlockSpec((heads, 1, blocks, rows, HD), lambda s, i, *_: (0, s, 0, 0, 0))
    pairs = heads * seqs * blocks * (blocks + 1) // 2
    return launch(
        attend_kernel,
        [queries, keys, values],
        [one, full, full],
        (seqs, blocks),
        [
            pl.BlockSpec(
                (1, 1, rows, heads * HD), lambda s, i, place, starts: (s, i ^ place[0], 0, 0)
            ),
            pl.BlockSpec(
                (1, rows, heads * HD), lambda s, i, place, starts: ((s * i) ^ place[0], 0, 0)
            ),
            pl.BlockSpec(
                (heads, 1, 1, 1, rows), lambda s, i, place, starts: (0, s, i ^ place[0], 0, 0)
            ),
        ],
        [
            jax.ShapeDtypeStruct((seqs, blocks, rows, heads * HD), BF16),
            jax.ShapeDtypeStruct((blocks, rows, heads * HD), BF16),
            jax.ShapeDtypeStruct((heads, seqs, blocks, 1, rows), F32),
        ],
        "attend",
        cost(pairs * 30 * rows * rows * HD, 4 * queries.size * 2),
        prefetch=[place, starts],
        tokens=tokens,
    )


def attend_back_kernel(
    place,
    starts,
    q_ref,
    k_ref,
    v_ref,
    grad_ref,
    out_ref,
    lse_ref,
    cosine,
    sine_up,
    sine_down,
    joined_ref,
    send_ref,
    sum_ref,
    query_grad,
    delta,
):
    block = pl.program_id(1)
    heads, blocks, rows = q_ref.shape[0], q_ref.shape[2], q_ref.shape[-2]
    here = place[0]
    documents = Documents(place, starts, pl.program_id(0), rows)
    high = documents.last_query_block(block, blocks)
    scaling = 1.0 / math.sqrt(HD)

    @pl.when(block == 0)
    def _():
        query_grad[...] = jnp.zeros_like(query_grad)

        def inner(j, carry):
            for head in range(heads):
                cols = slice(head * HD, (head + 1) * HD)
                product = grad_ref[0, j, :, cols].astype(F32) * out_ref[0, j, :, cols].astype(F32)
                delta[head, j] = jnp.sum(product.T, axis=0, keepdims=True)
            return carry

        lax.fori_loop(0, blocks, inner, 0)

    own = block ^ here
    key_places = block * rows + lax.broadcasted_iota(jnp.int32, (rows, 1), 0)

    def step(number, carry):
        at = number ^ here
        query_places = number * rows + lax.broadcasted_iota(jnp.int32, (1, rows), 1)
        allowed = (key_places >= documents.begin(query_places)) & (key_places <= query_places)
        results = []
        for head in range(heads):
            key_grad, value_grad = carry[head]
            key = k_ref[head, 0, own]
            value = v_ref[head, 0, own]
            query = q_ref[head, 0, at]
            grad = grad_ref[0, at, :, head * HD : (head + 1) * HD]
            scores = lax.dot_general(key, query, CONTRACT_LAST, preferred_element_type=F32)
            scores = scores * (scaling * LOG2E) - lse_ref[head, 0, at]
            weights = jnp.where(allowed, jnp.exp2(scores), 0.0)
            weight_grad = lax.dot_general(value, grad, CONTRACT_LAST, preferred_element_type=F32)
            score_grad = (weights * (weight_grad - delta[head, at]) * scaling).astype(BF16)
            value_grad = value_grad + jnp.dot(
                weights.astype(BF16), grad, preferred_element_type=F32
            )
            key_grad = key_grad + jnp.dot(score_grad, query, preferred_element_type=F32)
            query_grad[head, at] = query_grad[head, at] + lax.dot_general(
                score_grad, key, CONTRACT_FIRST, preferred_element_type=F32
            )
            results.append((key_grad, value_grad))
        return tuple(results)

    empty = jnp.zeros((rows, HD), F32)
    results = lax.fori_loop(block, high + 1, step, ((empty, empty),) * heads)
    tables = (cosine[0, own], -sine_up[0, own], -sine_down[0, own])
    for head, (key_grad, value_grad) in enumerate(results):
        at = head * 3 * HD
        joined_ref[0, own, :, at + HD : at + 2 * HD] = rope(key_grad, *tables).astype(BF16)
        joined_ref[0, own, :, at + 2 * HD : at + 3 * HD] = value_grad.astype(BF16)

    @pl.when(block == blocks - 1)
    def _():
        def inner(j, carry):
            tables = (cosine[0, j], -sine_up[0, j], -sine_down[0, j])
            for head in range(heads):
                at = head * 3 * HD
                joined_ref[0, j, :, at : at + HD] = rope(query_grad[head, j], *tables).astype(BF16)
            send_ref[j] = joined_ref[0, j]
            return carry + jnp.sum(joined_ref[0, j].astype(F32), axis=0, keepdims=True)

        sum_ref[0] = lax.fori_loop(0, blocks, inner, jnp.zeros((1, heads * 3 * HD), F32))


def attend_back(place, starts, queries, keys, values, grad, out, log_sums, tables, tokens):
    heads, seqs, blocks, rows, _ = queries.shape
    joined_cols = heads * 3 * HD
    head_spec = pl.BlockSpec((heads, 1, blocks, rows, HD), lambda s, i, *_: (0, s, 0, 0, 0))
    side = pl.BlockSpec((1, blocks, rows, heads * HD), lambda s, i, *_: (s, 0, 0, 0))
    table = pl.BlockSpec((1, blocks, rows, HD), lambda s, i, *_: (s, 0, 0, 0))
    pairs = heads * seqs * blocks * (blocks + 1) // 2
    return launch(
        attend_back_kernel,
        [queries, keys, values, grad, out, log_sums]
        + [item.reshape(seqs, blocks, rows, HD) for item in tables],
        [
            head_spec,
            head_spec,
            head_spec,
            side,
            side,
            pl.BlockSpec((heads, 1, blocks, 1, rows), lambda s, i, *_: (0, s, 0, 0, 0)),
            table,
            table,
            table,
        ],
        (seqs, blocks),
        [
            pl.BlockSpec((1, blocks, rows, joined_cols), lambda s, i, *_: (s, 0, 0, 0)),
            pl.BlockSpec((blocks, rows, joined_cols), lambda s, i, *_: (0, 0, 0)),
            pl.BlockSpec((1, 1, joined_cols), lambda s, i, *_: (s, 0, 0)),
        ],
        [
            jax.ShapeDtypeStruct((seqs, blocks, rows, joined_cols), BF16),
            jax.ShapeDtypeStruct((blocks, rows, joined_cols), BF16),
            jax.ShapeDtypeStruct((seqs, 1, joined_cols), F32),
        ],
        "attend_back",
        cost(pairs * 50 * rows * rows * HD, 12 * queries.size * 2),
        prefetch=[place, starts],
        tokens=tokens,
        scratch_shapes=[
            pltpu.VMEM((heads, blocks, rows, HD), F32),
            pltpu.VMEM((heads, blocks, 1, rows), F32),
        ],
    )


def expand_kernel(normed, weight, bias, activated, send, slope):
    pre = row_product(normed, weight, weight.shape[2]) + bias[...]
    share = 0.5 + 0.5 * lax.erf(pre * math.sqrt(0.5))
    density = jnp.exp2(pre * pre * (-0.5 * LOG2E)) * (1.0 / math.sqrt(2.0 * math.pi))
    result = (pre * share).astype(BF16)
    activated[...] = result
    send[...] = result
    slope[...] = (share + pre * density).astype(BF16)


def later_half(tile, width, steps):
    half = steps // 2
    return pl.BlockSpec((tile, width), lambda i: (jnp.maximum(i - half, 0), 0))


def expand(normed, weight, bias, tokens):
    rows, model_width = normed.shape
    cols = weight.shape[3]
    tile = 512
    steps = rows // tile
    out = pl.BlockSpec((tile, cols), lambda i: (i, 0))
    shape = jax.ShapeDtypeStruct((rows, cols), BF16)
    return launch(
        expand_kernel,
        [normed, weight, bias],
        [pl.BlockSpec((tile, model_width), lambda i: (i, 0)), whole_spec(weight), whole_spec(bias)],
        (steps,),
        [out, later_half(tile, cols, steps), out],
        [shape, jax.ShapeDtypeStruct((rows // 2, cols), BF16), shape],
        "expand",
        cost(
            2 * rows * model_width * cols,
            2 * (rows * model_width + weight.size + 2 * rows * cols),
        ),
        tokens=tokens,
    )


def by_columns(weight):
    groups = weight.shape[0] // 2
    return pl.BlockSpec(
        (2, 1) + weight.shape[2:], lambda i: (lax.rem(i, groups), lax.div(i, groups), 0, 0)
    )


def output_piece(j, pieces, attended, activated, dense, contract, sums, tokens):
    tile = attended[1].shape[0] // pieces
    groups, cores, _, share = dense[0].shape
    steps = groups * cores // 2
    lefts = [*attended, *activated]
    rights = [*dense, *contract]
    extras = sums.extras(j)

    def kernel(*refs):
        outs = refs[8 + len(extras) :]
        arrived = [(q, ref) for (q, _), ref in zip(extras, refs[8:])]
        for n in range(2):
            total = None
            for left, right in zip(refs[:4], refs[4:8]):
                part = jnp.dot(left[...], right[n, 0], preferred_element_type=F32)
                total = part if total is None else total + part
            finish_piece(total, n * share, arrived, outs)

    specs, shapes = piece_specs(tile, 2 * share, steps, sums.splits(j))
    result = launch(
        kernel,
        lefts + rights + [item for _, item in extras],
        [pl.BlockSpec((tile, item.shape[1]), lambda i: (j, 0)) for item in lefts]
        + [by_columns(item) for item in rights]
        + [pl.BlockSpec((tile // 2, 2 * share), lambda i: (0, i))] * len(extras),
        (steps,),
        specs,
        shapes,
        "output_piece",
        cost(4 * tile * sum(item.size for item in rights), 4 * sum(item.size for item in rights)),
        tokens=tokens,
    )
    sums.pieces[j] = result if sums.splits(j) else result[0]
    return result[0]


def dense_back_kernel(grad_ref, att_ref, dense, out, blocks, total):
    step = pl.program_id(0)
    share = dense.shape[3]

    @pl.when(step == 0)
    def _():
        total[...] = jnp.zeros_like(total)

    out[...] = column_back(grad_ref, dense, share).astype(BF16)
    total[...] += lax.dot_general(
        att_ref[...], grad_ref[...], CONTRACT_FIRST, preferred_element_type=F32
    )

    @pl.when(step == pl.num_programs(0) - 1)
    def _():
        for z, c, at in chunks_of(dense):
            blocks[c, z] = total[:, at * share : (at + 1) * share].T.astype(BF16)


def dense_back(grad, attended, dense, tokens):
    rows, width = grad.shape
    groups, cores, cols, share = dense.shape
    turned = jax.ShapeDtypeStruct((cores, groups, share, cols), BF16)
    tile = 512
    return launch(
        dense_back_kernel,
        [grad, attended, dense],
        [
            pl.BlockSpec((tile, width), lambda i: (i, 0)),
            pl.BlockSpec((tile, cols), lambda i: (i, 0)),
            whole_spec(dense),
        ],
        (rows // tile,),
        [pl.BlockSpec((tile, cols), lambda i: (i, 0)), whole_spec(turned)],
        [jax.ShapeDtypeStruct((rows, cols), BF16), turned],
        "dense_back",
        cost(4 * rows * dense.size, 2 * (rows * (width + cols) + dense.size)),
        tokens=tokens,
        scratch_shapes=[pltpu.VMEM((cols, width), F32)],
    )


def pre_grad_kernel(grad_ref, slope, contract, out, send, sums):
    @pl.when(pl.program_id(0) == 0)
    def _():
        sums[...] = jnp.zeros_like(sums)

    part = column_back(grad_ref, contract, contract.shape[3]) * slope[...].astype(F32)
    part = part.astype(BF16)
    out[...] = part
    send[...] = part
    sums[...] += jnp.sum(part.astype(F32), axis=0, keepdims=True)


def pre_grad_of(grad, slope, contract, tokens):
    rows, width = grad.shape
    cols = contract.shape[2]
    tile = 512
    steps = rows // tile
    return launch(
        pre_grad_kernel,
        [grad, slope, contract],
        [
            pl.BlockSpec((tile, width), lambda i: (i, 0)),
            pl.BlockSpec((tile, cols), lambda i: (i, 0)),
            whole_spec(contract),
        ],
        (steps,),
        [
            pl.BlockSpec((tile, cols), lambda i: (i, 0)),
            later_half(tile, cols, steps),
            pl.BlockSpec((1, cols), lambda i: (0, 0)),
        ],
        [
            jax.ShapeDtypeStruct((rows, cols), BF16),
            jax.ShapeDtypeStruct((rows // 2, cols), BF16),
            jax.ShapeDtypeStruct((1, cols), F32),
        ],
        "pre_grad",
        cost(2 * rows * contract.size, 2 * (rows * width + contract.size + 2 * rows * cols)),
        tokens=tokens,
    )


def normed_grad_piece(
    j, pieces, joined, pre, joined_weight, expand_weight, normal, gain1, gain2, sums, tokens
):
    tile = joined[1].shape[0] // pieces
    groups, cores, share, _ = joined_weight[0].shape
    steps = groups * cores // 2
    lefts = [*joined, *pre]
    rights = [*joined_weight, *expand_weight]
    extras = sums.extras(j)

    def kernel(*refs):
        normal, gain1, gain2 = refs[8:11]
        arrived = [(q, ref) for (q, _), ref in zip(extras, refs[11:])]
        *outs, along = refs[11 + len(extras) :]
        for n in range(2):

            def back(at):
                return lax.dot_general(
                    refs[at][...], refs[at + 4][n, 0], CONTRACT_LAST, preferred_element_type=F32
                )

            cols = slice(n * share, (n + 1) * share)
            first, second = back(0) + back(1), back(2) + back(3)
            rows = normal[:, cols].astype(F32)
            along[0:1, cols] = jnp.sum(first * rows, axis=0, keepdims=True)
            along[1:2, cols] = jnp.sum(first, axis=0, keepdims=True)
            along[2:3, cols] = jnp.sum(second * rows, axis=0, keepdims=True)
            along[3:4, cols] = jnp.sum(second, axis=0, keepdims=True)
            finish_piece(
                first * gain1[:, cols] + second * gain2[:, cols], n * share, arrived, outs
            )

    row = pl.BlockSpec((1, 2 * share), lambda i: (0, i))
    specs, shapes = piece_specs(tile, 2 * share, steps, sums.splits(j))
    *result, along = launch(
        kernel,
        lefts + rights + [normal, gain1, gain2] + [item for _, item in extras],
        [pl.BlockSpec((tile, item.shape[1]), lambda i: (j, 0)) for item in lefts]
        + [by_columns(item) for item in rights]
        + [pl.BlockSpec((tile, 2 * share), lambda i: (j, i)), row, row]
        + [pl.BlockSpec((tile // 2, 2 * share), lambda i: (0, i))] * len(extras),
        (steps,),
        specs + [pl.BlockSpec((8, 2 * share), lambda i: (0, i))],
        shapes + [jax.ShapeDtypeStruct((8, steps * 2 * share), F32)],
        "normed_grad_piece",
        cost(4 * tile * sum(item.size for item in rights), 4 * sum(item.size for item in rights)),
        tokens=tokens,
    )
    sums.pieces[j] = result if sums.splits(j) else result[0]
    return along


def rows_at(half, width, here):
    if here:
        return pl.BlockSpec((1, half, width), lambda i, place: (place[1], i, 0))
    return pl.BlockSpec((1, half, width), lambda i, place: (1 - place[1], i, 0))


def finish_tile(body, name, place, operands, whole, tile, width, tokens=()):
    half = tile // 2
    listed, specs, picks = [], [], []
    for pair in operands:
        if not isinstance(pair, list):
            picks.append((len(listed), False))
            listed.append(pair)
            specs.append(pl.BlockSpec((1, half, width), lambda i, place: (place[1], i, 0)))
        elif pair[0][0] is pair[1][0] and (pair[0][1], pair[1][1]) == (0, 1):
            picks.append((len(listed), False))
            listed.append(pair[0][0])
            specs.append(pl.BlockSpec((half, width), lambda i, place: (i, 0)))
        else:
            picks.append((len(listed), True))
            for item, at in pair:
                listed.append(item)
                specs.append(pl.BlockSpec((half, width), lambda i, place, at=at: (at, 0)))
    count = len(listed)

    def kernel(place, *refs):
        both, own = refs[count + len(whole) :]
        first = pl.program_id(0) == 0
        values = [
            jnp.where(first, refs[at][...], refs[at + 1][...])
            if pair
            else refs[at][...].reshape(half, width)
            for at, pair in picks
        ]
        result = body(values, refs[count : count + len(whole)]).astype(BF16)
        both[0] = result
        own[...] = result

    return launch(
        kernel,
        listed + list(whole),
        specs + [pl.BlockSpec(item.shape, lambda i, place: (0, 0)) for item in whole],
        (2,),
        [rows_at(half, width, True), pl.BlockSpec((half, width), lambda i, place: (i, 0))],
        [
            jax.ShapeDtypeStruct((2, tile, width), BF16),
            jax.ShapeDtypeStruct((tile, width), BF16),
        ],
        name,
        cost(20 * tile * width, 20 * tile * width),
        prefetch=[place],
        tokens=tokens,
    )


def pick_other(place, total, tokens):
    _, rows, cols = total.shape

    def pick(place, value, out):
        out[...] = value[0]

    other = launch(
        pick,
        [total],
        [pl.BlockSpec((1, rows, cols), lambda i, place: (1 - place[1], 0, 0))],
        (1,),
        pl.BlockSpec((rows, cols), lambda i, place: (0, 0)),
        jax.ShapeDtypeStruct((rows, cols), BF16),
        "pick_other",
        cost(1, 4 * rows * cols),
        prefetch=[place],
        tokens=tokens,
    )
    return swap(other, "branch", 1)


def join_cores(place, total, other, straight, tokens):
    _, rows, cols = total.shape
    turned = cols - straight

    def join(place, mine, others, *outs):
        value = jnp.where(pl.program_id(0) == 0, mine[0], others[...]).astype(F32)
        if straight:
            outs[0][...] = value[:, :straight]
        if turned:
            outs[-1][...] = value[:, straight:].T

    specs, shapes = [], []
    if straight:
        specs.append(pl.BlockSpec((rows, straight), lambda i, place: (0, place[1] ^ i)))
        shapes.append(jax.ShapeDtypeStruct((rows, 2 * straight), F32))
    if turned:
        specs.append(pl.BlockSpec((turned, rows), lambda i, place: (place[1] ^ i, 0)))
        shapes.append(jax.ShapeDtypeStruct((2 * turned, rows), F32))
    return launch(
        join,
        [total, other],
        [
            pl.BlockSpec((1, rows, cols), lambda i, place: (place[1], 0, 0)),
            pl.BlockSpec((rows, cols), lambda i, place: (0, 0)),
        ],
        (2,),
        specs,
        shapes,
        "finish_weight",
        cost(1, 16 * rows * cols),
        prefetch=[place],
        tokens=tokens,
    )


def fill_other(place, both, other, tokens=()):
    tile, width = other.shape

    def kernel(place, value, out):
        out[0] = value[...]

    return launch(
        kernel,
        [other],
        [pl.BlockSpec((tile // 2, width), lambda i, place: (i, 0))],
        (2,),
        rows_at(tile // 2, width, False),
        jax.ShapeDtypeStruct(both.shape, BF16),
        "fill_other",
        cost(1, 4 * tile * width),
        prefetch=[place],
        tokens=tokens,
        held=[both],
    )


def per_device(
    block_input,
    first_norm_gain,
    first_norm_bias,
    second_norm_gain,
    second_norm_bias,
    query_key_value,
    query_key_value_bias,
    attention_dense,
    attention_dense_bias,
    expand_weight,
    expand_bias,
    contract_weight,
    contract_bias,
    document_starts,
    output_grad,
):
    seqs, tile, model_width = block_input.shape
    tiles = lax.axis_size("tp")
    groups = lax.axis_size("seq")
    core = lax.axis_index("branch")
    here = lax.axis_index("tp")
    first_core = core == 0
    length = tile * tiles
    rows_in_all = length * seqs
    share = query_key_value.shape[0]

    def by_core(mine, others):
        return jnp.where(first_core, mine, others), jnp.where(first_core, others, mine)

    def halves_of(value, axis):
        size = value.shape[axis] // 2
        return (
            lax.dynamic_slice_in_dim(value, core * size, size, axis),
            lax.dynamic_slice_in_dim(value, (1 - core) * size, size, axis),
        )

    place = jnp.stack([here, core]).astype(jnp.int32)

    input_halves = own_halves(place, block_input)
    near = {**gather_near(input_halves, 0), **gather_near(input_halves, 1)}

    def core_halves(weight, axis):
        mine, others = halves_of(weight, axis)
        return jnp.stack(by_core(mine, swap(others, "branch", 1)))

    def gather_seq(piece):
        return lax.all_gather(piece, "seq", axis=0)

    weight_pieces = [
        core_halves(query_key_value, 1),
        core_halves(expand_weight, 1),
        core_halves(attention_dense, 0),
        core_halves(contract_weight, 0),
    ]
    joined_weight, expand_full, dense_full, contract_full = map(gather_seq, weight_pieces)
    joined_bias = halves_of(query_key_value_bias, 0)[0].astype(F32)[None]
    hidden_bias = halves_of(expand_bias, 0)[0].astype(F32)[None]

    gain1 = first_norm_gain.astype(F32)[None]
    gain2 = second_norm_gain.astype(F32)[None]
    gains = (
        gain1,
        first_norm_bias.astype(F32)[None],
        gain2,
        second_norm_bias.astype(F32)[None],
    )
    tables = rotary_tables(place, document_starts, rows_in_all, weight_pieces)
    grad_halves = own_halves(place, output_grad, [tables[0]])
    grad_rows = place_piece(0, place, output_grad, rows_in_all, (), grad_halves)
    *normed, mark = norm_piece(
        0, place, block_input, rows_in_all, gains, (), [tables[0], grad_rows]
    )
    near = in_pieces(hold_all(near, mark), {})
    far = gather_far(near)
    for j in sorted(near):
        *normed, mark = norm_piece(
            j, place, with_other_core(near[j]), rows_in_all, gains, normed, []
        )
    heads_held = ()
    far_from = tiles
    if tiles == 4:
        heads_held = project(0, 3, normed[1], joined_weight, joined_bias, tables, ())
        far_from = 3
    for j in sorted(far):
        last_items = [hold(item, mark) for item in far[j]]
        *normed, mark = norm_piece(
            j, place, with_other_core(last_items), rows_in_all, gains, normed, heads_held[:1]
        )
    heads_held = project(
        far_from % tiles, tiles, normed[1], joined_weight, joined_bias, tables, heads_held
    )
    normal, first_normed, second_normed = normed
    queries, keys, values = heads_held

    first = gather_near([hold(item, *last_items) for item in grad_halves], 0)
    first = hold_all(first, queries)
    second = gather_near([hold(item, *first.values()) for item in grad_halves], 1)
    attended, attended_send, log_sums = attend(
        place, document_starts, queries, keys, values, [*first.values()]
    )
    attended_flat = attended.reshape(rows_in_all, -1)
    near = in_pieces(first, hold_all(second, log_sums))
    far = gather_far(near)
    activated, activated_send, slope = expand(
        second_normed, expand_full, hidden_bias, [item for j in near for item in near[j]]
    )
    near = {
        j: items + [hold(swap(item, "branch", 1), slope) for item in items]
        for j, items in near.items()
    }
    far = {j: [hold(item, slope) for item in items] for j, items in far.items()}
    arrived = [item for items in [*near.values(), *far.values()] for item in items]
    far = {j: with_other_core(items) for j, items in far.items()}
    for j, items in {**near, **far}.items():
        grad_rows = place_piece(j, place, items, rows_in_all, [grad_rows], [slope])

    def weight_grad(left, right):
        return lax.dot_general(left, right, CONTRACT_FIRST, preferred_element_type=F32).astype(BF16)

    def in_order(part):
        return part.reshape(2, groups, share, part.shape[1])

    def scatter(blocks):
        return lax.psum_scatter(blocks, "seq", scatter_dimension=1, tiled=False)

    def exchanged(own, send, *tokens):
        send = send.reshape(-1, send.shape[-1])
        return own.reshape(-1, own.shape[-1]), swap(hold(send, *tokens) if tokens else send, "branch", 1)

    def with_other_weight(weight):
        return weight, swap(weight, "branch", 1)

    contract_blocks = in_order(weight_grad(grad_rows, activated))
    contract_total = scatter(contract_blocks)
    contract_full = hold(contract_full, contract_blocks)
    pre_grad, pre_send, pre_sums = pre_grad_of(
        grad_rows, slope, contract_full, [contract_blocks]
    )
    pre_pair = exchanged(pre_grad, pre_send)
    dense_full = hold(dense_full, pre_sums)
    attended_pair = exchanged(attended, attended_send, pre_sums)
    activated_pair = exchanged(activated, activated_send, pre_sums)
    contract_pair = with_other_weight(hold(contract_full, pre_sums))
    expand_blocks = in_order(weight_grad(second_normed, pre_grad))
    expand_total = scatter(expand_blocks)
    dense_pair = with_other_weight(dense_full)
    order = sorted(range(1, tiles), key=lambda j: (-bin(j).count("1"), j))
    outputs = TileSum()

    def output(j, *tokens):
        return output_piece(
            j, tiles, attended_pair, activated_pair, dense_pair, contract_pair, outputs, tokens
        )

    mark = expand_blocks
    operands = []
    for number, j in enumerate(order):
        if number and bin(order[number - 1]).count("1") > bin(j).count("1"):
            if not outputs.pieces.get(0) is None:
                operands += outputs.land(mark)
            else:
                attended_grad, dense_blocks = dense_back(
                    grad_rows, attended_flat, dense_full, [mark, *operands]
                )
                mark = output(0, attended_grad)
                operands = outputs.land(mark)
        mark = output(j, mark, *operands)
        operands = outputs.send() if outputs.complete(j) else []
    operands += outputs.send()
    landed = []
    joined_grad, joined_send, joined_sums = attend_back(
        place,
        document_starts,
        queries,
        keys,
        values,
        attended_grad.reshape(attended.shape),
        attended,
        log_sums,
        tables,
        [mark, *operands],
    )
    landed = outputs.land(joined_sums)
    joined_pair = exchanged(joined_grad, joined_send, *landed)
    joined_weight_pair = with_other_weight(joined_weight)
    expand_weight_pair = with_other_weight(expand_full)
    joined_grad = joined_pair[0]
    inputs = TileSum()
    sums = jnp.zeros((8, model_width), F32)
    mark = joined_sums
    wait = landed
    joined_blocks = None
    for number, j in enumerate(order + [0]):
        if number and j and bin(order[number - 1]).count("1") > bin(j).count("1"):
            if joined_blocks is None:
                part = weight_grad(hold(first_normed, mark, *wait), joined_grad)
                wait = inputs.land(part)
                joined_blocks = jnp.concatenate(
                    [in_order(hold(part, *wait)), dense_blocks], axis=3
                )
                joined_total = scatter(joined_blocks)
                mark = joined_blocks
            else:
                wait = inputs.land(mark)
        part = normed_grad_piece(
            j,
            tiles,
            joined_pair,
            pre_pair,
            joined_weight_pair,
            expand_weight_pair,
            normal,
            gain1,
            gain2,
            inputs,
            [mark, *wait],
        )
        sums = sums + part
        mark = part
        wait = inputs.send()
    landed = inputs.land(mark)

    biases = (
        attention_dense_bias.astype(F32)[None],
        contract_bias.astype(F32)[None],
    )

    def output_body(values, whole):
        return add_up(values) + whole[0][...] + whole[1][...]

    def input_body(values, whole):
        x, grad = values[0].astype(F32), values[1].astype(F32)
        total = add_up(values[2:])
        centred = x - jnp.mean(x, axis=-1, keepdims=True)
        rate = lax.rsqrt(jnp.mean(centred * centred, axis=-1, keepdims=True) + EPSILON)
        n = centred * rate
        middle = jnp.mean(total, axis=-1, keepdims=True)
        along = jnp.mean(total * n, axis=-1, keepdims=True)
        return grad + rate * (total - middle - n * along)

    def all_sum_beside(value, axis, others):
        size = lax.axis_size(axis)
        bit = 1
        while bit < size:
            arrived = swap(value, axis, bit)
            if others:
                arrived = hold(arrived, *others.pop(0)(value))
            value = value + arrived
            bit *= 2
        return value

    kept = {}

    def first_beside(value):
        kept["both"], kept["own"] = finish_tile(
            output_body,
            "finish_output",
            place,
            [block_input] + outputs.terms(),
            biases,
            tile,
            model_width,
            [value],
        )
        return [kept["own"]]

    def second_beside(value):
        kept["contract"] = pick_other(place, contract_total, [value])
        return [kept["contract"]]

    def third_beside(value):
        kept["expand"] = pick_other(place, expand_total, [value, kept["contract"]])
        return [kept["expand"], *landed]

    def fourth_beside(value):
        kept["input_both"], kept["input_own"] = finish_tile(
            input_body,
            "finish_input",
            place,
            [block_input, output_grad] + inputs.terms(),
            (),
            tile,
            model_width,
            [value],
        )
        return [kept["input_own"]]

    def fifth_beside(value):
        (kept["contract_grad"],) = join_cores(place, contract_total, kept["contract"], 0, [value])
        (kept["expand_grad"],) = join_cores(
            place, expand_total, kept["expand"], expand_total.shape[2], [kept["contract_grad"]]
        )
        return [kept["expand_grad"]]

    others = [first_beside, second_beside, third_beside, fourth_beside, fifth_beside]
    joined_bias_part = jnp.sum(joined_sums, axis=0).reshape(-1)
    hidden_bias_part = pre_sums[0]
    grad_own = lax.dynamic_index_in_dim(output_grad, core, 0, False)
    small = jnp.concatenate(
        [
            sums[:4].reshape(-1),
            jnp.sum(grad_own.astype(F32), axis=0),
            joined_bias_part,
            hidden_bias_part,
        ]
    )
    everywhere = 5 * model_width
    small = all_sum_beside(hold(small, mark), "seq", others)
    per_core = small[everywhere:]
    both = jnp.stack(by_core(per_core, swap(per_core, "branch", 1)))
    query_key_value_bias_grad = both[:, : joined_bias_part.shape[0]].reshape(-1)
    expand_bias_grad = both[:, joined_bias_part.shape[0] :].reshape(-1)
    shared = all_sum_beside(small[:everywhere], "tp", others)
    shared = all_sum_beside(shared, "branch", others).reshape(5, model_width)
    while others:
        others.pop(0)(mark)
    contract_grad, expand_grad = kept["contract_grad"], kept["expand_grad"]
    block_output = fill_other(
        place, kept["both"], swap(kept["own"], "branch", 1), [expand_grad]
    )
    joined_other = pick_other(place, joined_total, [block_output])
    input_grad = fill_other(
        place, kept["input_both"], swap(kept["input_own"], "branch", 1), [joined_other]
    )
    query_key_value_grad, dense_grad = join_cores(
        place, joined_total, joined_other, joined_weight.shape[3], [input_grad]
    )
    return (
        block_output,
        input_grad,
        shared[0],
        shared[1],
        shared[2],
        shared[3],
        query_key_value_grad,
        query_key_value_bias_grad,
        dense_grad,
        shared[4],
        expand_grad,
        expand_bias_grad,
        contract_grad,
        shared[4],
    )


def solution(mesh):
    in_specs = (
        P("seq", "tp", None),
        P(),
        P(),
        P(),
        P(),
        P(("branch", "seq"), "tp"),
        P("tp"),
        P("tp", ("branch", "seq")),
        P(),
        P(("branch", "seq"), "tp"),
        P("tp"),
        P("tp", ("branch", "seq")),
        P(),
        P("seq", None),
        P("seq", "tp", None),
    )
    out_specs = (
        P("seq", "tp", None),
        P("seq", "tp", None),
        P(),
        P(),
        P(),
        P(),
        P(("branch", "seq"), "tp"),
        P("tp"),
        P("tp", ("branch", "seq")),
        P(),
        P(("branch", "seq"), "tp"),
        P("tp"),
        P("tp", ("branch", "seq")),
        P(),
    )
    return jax.shard_map(
        per_device, mesh=mesh, in_specs=in_specs, out_specs=out_specs, check_vma=False
    )
```

```python
from functools import partial
import math

import jax
import jax.numpy as jnp
from jax import lax
from jax.experimental import pallas as pl
from jax.experimental.pallas import tpu as pltpu
from jax.sharding import PartitionSpec as P

HD = 128
ROT = 32


EPSILON = 1e-05
NEGATIVE = -1e30
ROPE_BASE = 10000.0
LOG2E = math.log2(math.e)
F32 = jnp.float32
BF16 = jnp.bfloat16
CONTRACT_LAST = (((1,), (1,)), ((), ()))
CONTRACT_FIRST = (((0,), (0,)), ((), ()))
VMEM_BYTES = 56 * 1024 * 1024
ANY = pl.BlockSpec(memory_space=pl.ANY)
HINT = 0.02


def cost(flops, moved, transcendentals=0):
    return pl.CostEstimate(
        flops=1 + int(flops * HINT), bytes_accessed=1 + int(moved * HINT), transcendentals=0
    )


def launch(
    kernel,
    operands,
    in_specs,
    grid,
    out_specs,
    out_shape,
    name,
    cost_estimate,
    prefetch=(),
    held=(),
    tokens=(),
    scratch_shapes=(),
):
    lead = len(prefetch) + len(operands)
    extra = len(held) + len(tokens)

    def body(*refs):
        kernel(*refs[:lead], *refs[lead + extra :])

    return pl.pallas_call(
        body,
        grid_spec=pltpu.PrefetchScalarGridSpec(
            num_scalar_prefetch=len(prefetch),
            grid=grid,
            in_specs=list(in_specs) + [ANY] * extra,
            out_specs=out_specs,
            scratch_shapes=list(scratch_shapes),
        ),
        out_shape=out_shape,
        input_output_aliases={lead + k: k for k in range(len(held))},
        compiler_params=pltpu.CompilerParams(
            dimension_semantics=("arbitrary",) * len(grid), vmem_limit_bytes=VMEM_BYTES
        ),
        cost_estimate=cost_estimate,
        name=name,
    )(*prefetch, *operands, *held, *tokens)


def hold(value, *tokens):
    def nothing(out):
        pass

    return launch(
        nothing,
        [],
        [],
        (1,),
        ANY,
        jax.ShapeDtypeStruct(value.shape, value.dtype),
        "hold",
        cost(1, 1),
        held=[value],
        tokens=tokens,
    )


def swap(value, axis, bit):
    size = lax.axis_size(axis)
    return lax.ppermute(value, axis, [(i, i ^ bit) for i in range(size)])


def onward(value, axis):
    size = lax.axis_size(axis)
    return lax.ppermute(value, axis, [(i, (i + 1) % size) for i in range(size)])


def bit_orders(size):
    bits = [1 << k for k in range(size.bit_length() - 1)]
    return (bits, bits[::-1])


def last_bit(number, order):
    return [bit for bit in order if number & bit][-1]


def gather_near(own, number):
    size = lax.axis_size("tp")
    bits = [1 << k for k in range(size.bit_length() - 1)]
    return {
        (bit, (n + number) % 2): swap(own[(n + number) % 2], "tp", bit)
        for n, bit in enumerate(bits)
    }


def hold_all(items, *tokens):
    return {key: hold(item, *tokens) for key, item in items.items()}


def in_pieces(first, second):
    items = {**first, **second}
    return {j: [items[j, 0], items[j, 1]] for j in sorted({j for j, _ in items})}


def gather_far(near):
    size = lax.axis_size("tp")
    pieces = dict(near)
    far = {}
    for j in sorted(range(1, size), key=lambda j: bin(j).count("1")):
        if j not in near:
            bits = [last_bit(j, order) for order in bit_orders(size)]
            far[j] = [swap(pieces[j ^ bit][q], "tp", bit) for q, bit in enumerate(bits)]
            pieces[j] = far[j]
    return far


def with_other_core(items):
    return items + [swap(item, "branch", 1) for item in items]


def add_up(items):
    total = items[0].astype(F32)
    for item in items[1:]:
        total = total + item.astype(F32)
    return total


class TileSum:
    def __init__(self):
        size = lax.axis_size("tp")
        self.orders = bit_orders(size)
        self.waiting = [(q, j) for j in range(1, size) for q in range(2)]
        self.expected = {(q, j): 0 for j in range(size) for q in range(2)}
        for q, j in self.waiting:
            self.expected[q, j ^ last_bit(j, self.orders[q])] += 1
        self.waiting.sort(key=lambda at: (-bin(at[1]).count("1"), at[1]))
        self.pieces = {}
        self.arrived = {}
        self.moving = []

    def splits(self, j):
        return j > 0 and len({last_bit(j, order) for order in self.orders}) > 1

    def extras(self, j):
        return [(q, item) for q in range(2) for item in self.arrived.get((q, j), [])]

    def complete(self, j):
        return all(len(self.arrived.get((q, j), [])) == self.expected[q, j] for q in range(2))

    def send(self, *tokens):
        operands = []
        for q, j in list(self.waiting):
            if j not in self.pieces or (q, j) not in self.waiting:
                continue
            bit = last_bit(j, self.orders[q])
            if self.splits(j):
                sides, operand = [q], self.pieces[j][q]
            else:
                sides, operand = [0, 1], self.pieces[j]
            for side in sides:
                self.waiting.remove((side, j))
            if tokens:
                operand = hold(operand, *tokens)
            self.moving.append((sides, j ^ bit, swap(operand, "tp", bit)))
            operands.append(operand)
        return operands

    def land(self, *tokens):
        items = []
        for sides, j, item in self.moving:
            item = hold(item, *tokens) if tokens else item
            items.append(item)
            if j == 0:
                self.arrived.setdefault(0, []).append(item)
                continue
            half = item.shape[0] // 2
            for side in sides:
                part = item[side * half : (side + 1) * half] if len(sides) > 1 else item
                self.arrived.setdefault((side, j), []).append(part)
        self.moving = []
        return items

    def terms(self):
        return [[(item, 0), (item, 1)] for item in [self.pieces[0]] + self.arrived[0]]


def finish_piece(total, column, extras, outs):
    half = total.shape[0] // 2
    width = total.shape[1]
    cols = slice(column, column + width)
    parts = [total[:half], total[half:]]
    for q, ref in extras:
        parts[q] = parts[q] + ref[:, cols].astype(F32)
    for q in range(2):
        if len(outs) > 1:
            outs[q][:, cols] = parts[q].astype(BF16)
        else:
            outs[0][q * half : (q + 1) * half, cols] = parts[q].astype(BF16)


def piece_specs(tile, share, steps, split):
    rows, count = (tile // 2, 2) if split else (tile, 1)
    return (
        [pl.BlockSpec((rows, share), lambda i: (0, i))] * count,
        [jax.ShapeDtypeStruct((rows, steps * share), BF16)] * count,
    )


def all_sum(value, axis):
    size = lax.axis_size(axis)
    bit = 1
    while bit < size:
        value = value + swap(value, axis, bit)
        bit *= 2
    return value


def rope(vectors, cosine, sine_up, sine_down):
    return (
        vectors * cosine
        + pltpu.roll(vectors, ROT // 2, 1) * sine_up
        + pltpu.roll(vectors, HD - ROT // 2, 1) * sine_down
    )


class Documents:
    def __init__(self, place, starts, seq_at, rows):
        self.row = place[1] ^ seq_at
        self.starts = starts
        self.rows = rows

    def begin(self, places):
        begin = jnp.zeros_like(places)
        for number in range(self.starts.shape[1]):
            start = self.starts[self.row, number]
            begin = jnp.where(places >= start, start, begin)
        return begin

    def first_key_block(self, block):
        return lax.div(self.begin(block * self.rows), jnp.int32(self.rows))

    def first_whole_key_block(self, block):
        begin = self.begin((block + 1) * self.rows - 1)
        return lax.div(begin + (self.rows - 1), jnp.int32(self.rows))

    def last_whole_query_block(self, block, blocks):
        last = block
        for number in range(1, blocks):
            after = jnp.minimum(block + number, blocks - 1)
            whole = self.begin((after + 1) * self.rows - 1) <= block * self.rows
            last = jnp.where(whole, jnp.maximum(last, after), last)
        return last

    def last_query_block(self, block, blocks):
        last = block
        for number in range(1, blocks):
            after = jnp.minimum(block + number, blocks - 1)
            last = jnp.where(self.first_key_block(after) <= block, jnp.maximum(last, after), last)
        return last


def table_kernel(place, starts, cosine, sine_up, sine_down):
    rows = cosine.shape[0]
    blocks = lax.axis_size("tp")
    step = pl.program_id(0)
    block, seq_at = lax.rem(step, blocks) ^ place[0], lax.div(step, blocks)
    places = block * rows + lax.broadcasted_iota(jnp.int32, (rows, 1), 0)
    begin = Documents(place, starts, seq_at, rows).begin(places)
    lane = lax.broadcasted_iota(jnp.int32, (1, HD), 1)
    half = ROT // 2
    number = jnp.where(lane < half, lane, lane - half).astype(F32)
    frequency = jnp.exp2(number * (-2.0 / ROT * math.log2(ROPE_BASE)))
    angles = (places - begin).astype(F32) * jnp.where(lane < ROT, frequency, 0.0)
    cosine[...] = jnp.cos(angles)
    sines = jnp.sin(angles)
    sine_up[...] = jnp.where((lane >= half) & (lane < ROT), sines, 0.0)
    sine_down[...] = jnp.where(lane < half, -sines, 0.0)


def rotary_tables(place, starts, rows, tokens):
    steps = 2 * lax.axis_size("tp")
    tile = rows // steps
    out = pl.BlockSpec((tile, HD), lambda i, *_: (i, 0))
    return launch(
        table_kernel,
        [],
        [],
        (steps,),
        [out] * 3,
        [jax.ShapeDtypeStruct((rows, HD), F32)] * 3,
        "rotary_tables",
        cost(rows * HD * 100, rows * HD * 48),
        prefetch=[place, starts],
        tokens=tokens,
    )


def half_of_piece(j):
    size = lax.axis_size("tp")
    return lambda i, *_: ((lax.div(i, 2) * size + j) * 2 + lax.rem(i, 2), 0)


def own_tile_specs(tile):
    _, rows, width = tile.shape

    def spec(h, q):
        return pl.BlockSpec((1, rows // 2, width), lambda i, place: (place[1] ^ h, q, 0))

    return [spec(h, q) for h in range(2) for q in range(2)]


def own_halves(place, tile, tokens=()):
    _, rows, width = tile.shape

    def kernel(place, first, second, out_first, out_second):
        out_first[...] = first[0]
        out_second[...] = second[0]

    shape = jax.ShapeDtypeStruct((rows // 2, width), BF16)
    return launch(
        kernel,
        [tile, tile],
        own_tile_specs(tile)[:2],
        (1,),
        [whole_spec(shape)] * 2,
        [shape, shape],
        "own_halves",
        cost(1, 4 * rows * width),
        prefetch=[place],
        tokens=tokens,
    )


def place_kernel(place, x0, x1, x2, x3, out):
    step = pl.program_id(0)
    for number, x_ref in enumerate((x0, x1, x2, x3)):

        @pl.when(step == number)
        def _(x_ref=x_ref):
            out[...] = x_ref[...].reshape(out.shape)


def place_piece(j, place, halves, rows_in_all, held, tokens=()):
    if j == 0:
        specs = own_tile_specs(halves)
        half, model_width = halves.shape[1] // 2, halves.shape[2]
        halves = [halves] * 4
    else:
        half, model_width = halves[0].shape
        specs = [whole_spec(item) for item in halves]
    return launch(
        place_kernel,
        halves,
        specs,
        (4,),
        pl.BlockSpec((half, model_width), half_of_piece(j)),
        jax.ShapeDtypeStruct((rows_in_all, model_width), BF16),
        "place_piece",
        cost(1, 4 * half * model_width * 4),
        prefetch=[place],
        held=held,
        tokens=tokens,
    )


def norm_kernel(place, x0, x1, x2, x3, gain1, shift1, gain2, shift2, *rest):
    normal, first, second, mark, scratch = rest[-5:]
    step = pl.program_id(0)
    mark[...] = jnp.zeros_like(mark)
    for number, x_ref in enumerate((x0, x1, x2, x3)):

        @pl.when(step == number)
        def _(x_ref=x_ref):
            scratch[...] = (x_ref[0] if len(x_ref.shape) == 3 else x_ref[...]).astype(F32)

    x = scratch[...]
    centred = x - jnp.mean(x, axis=-1, keepdims=True)
    variance = jnp.mean(centred * centred, axis=-1, keepdims=True)
    n = centred * lax.rsqrt(variance + EPSILON)
    normal[...] = n.astype(BF16)
    first[...] = (n * gain1[...] + shift1[...]).astype(BF16)
    second[...] = (n * gain2[...] + shift2[...]).astype(BF16)


def norm_piece(j, place, halves, rows_in_all, gains, held, tokens):
    if j == 0:
        specs = own_tile_specs(halves)
        half, model_width = halves.shape[1] // 2, halves.shape[2]
        halves = [halves] * 4
    else:
        half, model_width = halves[0].shape
        specs = [whole_spec(item) for item in halves]
    wide = pl.BlockSpec((half, model_width), half_of_piece(j))
    return launch(
        norm_kernel,
        halves + list(gains),
        specs + [whole_spec(item) for item in gains],
        (4,),
        [wide] * 3 + [pl.BlockSpec((8, HD), lambda i, *_: (0, 0))],
        [jax.ShapeDtypeStruct((rows_in_all, model_width), BF16)] * 3
        + [jax.ShapeDtypeStruct((8, HD), F32)],
        "norm_piece",
        cost(4 * half * model_width * 16, 4 * half * model_width * 16),
        prefetch=[place],
        held=held,
        tokens=tokens,
        scratch_shapes=[pltpu.VMEM((half, model_width), F32)],
    )


def chunks_of(weight):
    groups, cores = weight.shape[:2]
    return [(z, c, c * groups + z) for c in range(cores) for z in range(groups)]


def row_product(left, weight, share):
    total = None
    for z, c, at in chunks_of(weight):
        part = jnp.dot(
            left[:, at * share : (at + 1) * share], weight[z, c], preferred_element_type=F32
        )
        total = part if total is None else total + part
    return total


def column_back(left, weight, share):
    total = None
    for z, c, at in chunks_of(weight):
        part = lax.dot_general(
            left[:, at * share : (at + 1) * share],
            weight[z, c],
            CONTRACT_LAST,
            preferred_element_type=F32,
        )
        total = part if total is None else total + part
    return total


def whole_spec(array, prefetched=0):
    rank = array.ndim
    return pl.BlockSpec(array.shape, lambda *at: (0,) * rank)


def project_kernel(normed, weight, bias, cosine, sine_up, sine_down, queries, keys, values):
    joined = row_product(normed, weight, weight.shape[2]) + bias[...]
    tables = (cosine[...], sine_up[...], sine_down[...])
    for head in range(queries.shape[0]):
        at = head * 3 * HD
        queries[head, 0, 0] = rope(joined[:, at : at + HD], *tables).astype(BF16)
        keys[head, 0, 0] = rope(joined[:, at + HD : at + 2 * HD], *tables).astype(BF16)
        values[head, 0, 0] = joined[:, at + 2 * HD : at + 3 * HD].astype(BF16)


def project(first, last, normed, weight, bias, tables, held):
    rows, model_width = normed.shape
    joined_cols = weight.shape[3]
    heads = joined_cols // (3 * HD)
    size = lax.axis_size("tp")
    tile = rows // (2 * size)
    table = pl.BlockSpec((tile, HD), lambda s, i: (s * size + first + i, 0))
    share = (last - first) / size
    return launch(
        project_kernel,
        [normed, weight, bias] + list(tables),
        [
            pl.BlockSpec((tile, model_width), lambda s, i: (s * size + first + i, 0)),
            whole_spec(weight),
            whole_spec(bias),
            table,
            table,
            table,
        ],
        (2, last - first),
        [pl.BlockSpec((heads, 1, 1, tile, HD), lambda s, i: (0, s, first + i, 0, 0))] * 3,
        [jax.ShapeDtypeStruct((heads, 2, size, tile, HD), BF16)] * 3,
        "project",
        cost(
            2 * rows * share * model_width * joined_cols,
            2 * (rows * share * (model_width + joined_cols) + weight.size),
        ),
        held=held,
    )


def attend_kernel(place, starts, q_ref, k_ref, v_ref, out_ref, send_ref, lse_ref):
    block = pl.program_id(1)
    heads, rows = q_ref.shape[0], q_ref.shape[-2]
    here = place[0]
    documents = Documents(place, starts, pl.program_id(0), rows)
    low = documents.first_key_block(block)
    query_places = block * rows + lax.broadcasted_iota(jnp.int32, (rows, 1), 0)
    begin = documents.begin(query_places)
    factor = LOG2E / math.sqrt(HD)

    def step(masked, number, carry):
        key_places = number * rows + lax.broadcasted_iota(jnp.int32, (1, rows), 1)
        if masked:
            allowed = (key_places >= begin) & (key_places <= query_places)
        results = []
        for head in range(heads):
            top, total, mixed = carry[head]
            key = k_ref[head, 0, number ^ here]
            value = v_ref[head, 0, number ^ here]
            scores = lax.dot_general(
                q_ref[head, 0, 0], key, CONTRACT_LAST, preferred_element_type=F32
            )
            if masked:
                scores = jnp.where(allowed, scores, NEGATIVE)
            new_top = jnp.maximum(top, jnp.max(scores, axis=-1, keepdims=True))
            weights = jnp.exp2((scores - new_top) * factor)
            shrink = jnp.exp2((top - new_top) * factor)
            total = total * shrink + jnp.sum(weights, axis=-1, keepdims=True)
            mixed = mixed * shrink + jnp.dot(
                weights.astype(BF16), value, preferred_element_type=F32
            )
            results.append((new_top, total, mixed))
        return tuple(results)

    empty = (
        jnp.full((rows, 1), NEGATIVE, F32),
        jnp.zeros((rows, 1), F32),
        jnp.zeros((rows, HD), F32),
    )
    whole = jnp.minimum(jnp.maximum(documents.first_whole_key_block(block), low), block)
    results = lax.fori_loop(low, whole, partial(step, True), (empty,) * heads)
    results = lax.fori_loop(whole, block, partial(step, False), results)
    results = step(True, block, results)
    for head, (top, total, mixed) in enumerate(results):
        result = (mixed / total).astype(BF16)
        out_ref[0, 0, :, head * HD : (head + 1) * HD] = result
        send_ref[0, :, head * HD : (head + 1) * HD] = result
        log_sum = top * factor + jnp.log(total) * LOG2E
        lse_ref[head, 0, 0] = jnp.broadcast_to(log_sum, (rows, HD)).T[:1]


def attend(place, starts, queries, keys, values, tokens):
    heads, seqs, blocks, rows, _ = queries.shape
    one = pl.BlockSpec(
        (heads, 1, 1, rows, HD), lambda s, i, place, starts: (0, s, i ^ place[0], 0, 0)
    )
    full = pl.BlockSpec((heads, 1, blocks, rows, HD), lambda s, i, *_: (0, s, 0, 0, 0))
    pairs = heads * seqs * blocks * (blocks + 1) // 2
    return launch(
        attend_kernel,
        [queries, keys, values],
        [one, full, full],
        (seqs, blocks),
        [
            pl.BlockSpec(
                (1, 1, rows, heads * HD), lambda s, i, place, starts: (s, i ^ place[0], 0, 0)
            ),
            pl.BlockSpec(
                (1, rows, heads * HD), lambda s, i, place, starts: ((s * i) ^ place[0], 0, 0)
            ),
            pl.BlockSpec(
                (heads, 1, 1, 1, rows), lambda s, i, place, starts: (0, s, i ^ place[0], 0, 0)
            ),
        ],
        [
            jax.ShapeDtypeStruct((seqs, blocks, rows, heads * HD), BF16),
            jax.ShapeDtypeStruct((blocks, rows, heads * HD), BF16),
            jax.ShapeDtypeStruct((heads, seqs, blocks, 1, rows), F32),
        ],
        "attend",
        cost(pairs * 30 * rows * rows * HD, 4 * queries.size * 2),
        prefetch=[place, starts],
        tokens=tokens,
    )


def attend_back_kernel(
    place,
    starts,
    q_ref,
    k_ref,
    v_ref,
    grad_ref,
    out_ref,
    lse_ref,
    cosine,
    sine_up,
    sine_down,
    joined_ref,
    send_ref,
    sum_ref,
    query_grad,
    delta,
):
    block = pl.program_id(1)
    heads, blocks, rows = q_ref.shape[0], q_ref.shape[2], q_ref.shape[-2]
    here = place[0]
    documents = Documents(place, starts, pl.program_id(0), rows)
    high = documents.last_query_block(block, blocks)
    scaling = 1.0 / math.sqrt(HD)

    @pl.when(block == 0)
    def _():
        query_grad[...] = jnp.zeros_like(query_grad)

        def inner(j, carry):
            for head in range(heads):
                cols = slice(head * HD, (head + 1) * HD)
                product = grad_ref[0, j, :, cols].astype(F32) * out_ref[0, j, :, cols].astype(F32)
                delta[head, j] = jnp.sum(product.T, axis=0, keepdims=True)
            return carry

        lax.fori_loop(0, blocks, inner, 0)

    own = block ^ here
    key_places = block * rows + lax.broadcasted_iota(jnp.int32, (rows, 1), 0)

    def step(masked, number, carry):
        at = number ^ here
        if masked:
            query_places = number * rows + lax.broadcasted_iota(jnp.int32, (1, rows), 1)
            allowed = (key_places >= documents.begin(query_places)) & (
                key_places <= query_places
            )
        results = []
        for head in range(heads):
            key_grad, value_grad = carry[head]
            key = k_ref[head, 0, own]
            value = v_ref[head, 0, own]
            query = q_ref[head, 0, at]
            grad = grad_ref[0, at, :, head * HD : (head + 1) * HD]
            scores = lax.dot_general(key, query, CONTRACT_LAST, preferred_element_type=F32)
            weights = jnp.exp2(scores * (scaling * LOG2E) - lse_ref[head, 0, at])
            if masked:
                weights = jnp.where(allowed, weights, 0.0)
            weight_grad = lax.dot_general(value, grad, CONTRACT_LAST, preferred_element_type=F32)
            score_grad = (weights * (weight_grad - delta[head, at]) * scaling).astype(BF16)
            value_grad = value_grad + jnp.dot(
                weights.astype(BF16), grad, preferred_element_type=F32
            )
            key_grad = key_grad + jnp.dot(score_grad, query, preferred_element_type=F32)
            query_grad[head, at] = query_grad[head, at] + lax.dot_general(
                score_grad, key, CONTRACT_FIRST, preferred_element_type=F32
            )
            results.append((key_grad, value_grad))
        return tuple(results)

    empty = jnp.zeros((rows, HD), F32)
    whole = documents.last_whole_query_block(block, blocks)
    results = step(True, block, ((empty, empty),) * heads)
    results = lax.fori_loop(block + 1, whole + 1, partial(step, False), results)
    results = lax.fori_loop(whole + 1, high + 1, partial(step, True), results)
    tables = (cosine[0, own], -sine_up[0, own], -sine_down[0, own])
    for head, (key_grad, value_grad) in enumerate(results):
        at = head * 3 * HD
        joined_ref[0, own, :, at + HD : at + 2 * HD] = rope(key_grad, *tables).astype(BF16)
        joined_ref[0, own, :, at + 2 * HD : at + 3 * HD] = value_grad.astype(BF16)

    @pl.when(block == blocks - 1)
    def _():
        def inner(j, carry):
            tables = (cosine[0, j], -sine_up[0, j], -sine_down[0, j])
            for head in range(heads):
                at = head * 3 * HD
                joined_ref[0, j, :, at : at + HD] = rope(query_grad[head, j], *tables).astype(BF16)
            send_ref[j] = joined_ref[0, j]
            return carry + jnp.sum(joined_ref[0, j].astype(F32), axis=0, keepdims=True)

        sum_ref[0] = lax.fori_loop(0, blocks, inner, jnp.zeros((1, heads * 3 * HD), F32))


def attend_back(place, starts, queries, keys, values, grad, out, log_sums, tables, tokens):
    heads, seqs, blocks, rows, _ = queries.shape
    joined_cols = heads * 3 * HD
    head_spec = pl.BlockSpec((heads, 1, blocks, rows, HD), lambda s, i, *_: (0, s, 0, 0, 0))
    side = pl.BlockSpec((1, blocks, rows, heads * HD), lambda s, i, *_: (s, 0, 0, 0))
    table = pl.BlockSpec((1, blocks, rows, HD), lambda s, i, *_: (s, 0, 0, 0))
    pairs = heads * seqs * blocks * (blocks + 1) // 2
    return launch(
        attend_back_kernel,
        [queries, keys, values, grad, out, log_sums]
        + [item.reshape(seqs, blocks, rows, HD) for item in tables],
        [
            head_spec,
            head_spec,
            head_spec,
            side,
            side,
            pl.BlockSpec((heads, 1, blocks, 1, rows), lambda s, i, *_: (0, s, 0, 0, 0)),
            table,
            table,
            table,
        ],
        (seqs, blocks),
        [
            pl.BlockSpec((1, blocks, rows, joined_cols), lambda s, i, *_: (s, 0, 0, 0)),
            pl.BlockSpec((blocks, rows, joined_cols), lambda s, i, *_: (0, 0, 0)),
            pl.BlockSpec((1, 1, joined_cols), lambda s, i, *_: (s, 0, 0)),
        ],
        [
            jax.ShapeDtypeStruct((seqs, blocks, rows, joined_cols), BF16),
            jax.ShapeDtypeStruct((blocks, rows, joined_cols), BF16),
            jax.ShapeDtypeStruct((seqs, 1, joined_cols), F32),
        ],
        "attend_back",
        cost(pairs * 50 * rows * rows * HD, 12 * queries.size * 2),
        prefetch=[place, starts],
        tokens=tokens,
        scratch_shapes=[
            pltpu.VMEM((heads, blocks, rows, HD), F32),
            pltpu.VMEM((heads, blocks, 1, rows), F32),
        ],
    )


def expand_kernel(normed, weight, bias, activated, send, slope):
    pre = row_product(normed, weight, weight.shape[2]) + bias[...]
    share = 0.5 + 0.5 * lax.erf(pre * math.sqrt(0.5))
    density = jnp.exp2(pre * pre * (-0.5 * LOG2E)) * (1.0 / math.sqrt(2.0 * math.pi))
    result = (pre * share).astype(BF16)
    activated[...] = result
    send[...] = result
    slope[...] = (share + pre * density).astype(BF16)


def later_half(tile, width, steps):
    half = steps // 2
    return pl.BlockSpec((tile, width), lambda i: (jnp.maximum(i - half, 0), 0))


def expand(normed, weight, bias, tokens):
    rows, model_width = normed.shape
    cols = weight.shape[3]
    tile = 512
    steps = rows // tile
    out = pl.BlockSpec((tile, cols), lambda i: (i, 0))
    shape = jax.ShapeDtypeStruct((rows, cols), BF16)
    return launch(
        expand_kernel,
        [normed, weight, bias],
        [pl.BlockSpec((tile, model_width), lambda i: (i, 0)), whole_spec(weight), whole_spec(bias)],
        (steps,),
        [out, later_half(tile, cols, steps), out],
        [shape, jax.ShapeDtypeStruct((rows // 2, cols), BF16), shape],
        "expand",
        cost(
            2 * rows * model_width * cols,
            2 * (rows * model_width + weight.size + 2 * rows * cols),
        ),
        tokens=tokens,
    )


def by_columns(weight):
    groups = weight.shape[0] // 2
    return pl.BlockSpec(
        (2, 1) + weight.shape[2:], lambda i: (lax.rem(i, groups), lax.div(i, groups), 0, 0)
    )


def output_piece(j, pieces, attended, activated, dense, contract, sums, tokens):
    tile = attended[1].shape[0] // pieces
    groups, cores, _, share = dense[0].shape
    steps = groups * cores // 2
    lefts = [*attended, *activated]
    rights = [*dense, *contract]
    extras = sums.extras(j)

    def kernel(*refs):
        outs = refs[8 + len(extras) :]
        arrived = [(q, ref) for (q, _), ref in zip(extras, refs[8:])]
        for n in range(2):
            total = None
            for left, right in zip(refs[:4], refs[4:8]):
                part = jnp.dot(left[...], right[n, 0], preferred_element_type=F32)
                total = part if total is None else total + part
            finish_piece(total, n * share, arrived, outs)

    specs, shapes = piece_specs(tile, 2 * share, steps, sums.splits(j))
    result = launch(
        kernel,
        lefts + rights + [item for _, item in extras],
        [pl.BlockSpec((tile, item.shape[1]), lambda i: (j, 0)) for item in lefts]
        + [by_columns(item) for item in rights]
        + [pl.BlockSpec((tile // 2, 2 * share), lambda i: (0, i))] * len(extras),
        (steps,),
        specs,
        shapes,
        "output_piece",
        cost(4 * tile * sum(item.size for item in rights), 4 * sum(item.size for item in rights)),
        tokens=tokens,
    )
    sums.pieces[j] = result if sums.splits(j) else result[0]
    return result[0]


def dense_back_kernel(grad_ref, att_ref, dense, out, blocks, total):
    step = pl.program_id(0)
    share = dense.shape[3]

    @pl.when(step == 0)
    def _():
        total[...] = jnp.zeros_like(total)

    out[...] = column_back(grad_ref, dense, share).astype(BF16)
    total[...] += lax.dot_general(
        att_ref[...], grad_ref[...], CONTRACT_FIRST, preferred_element_type=F32
    )

    @pl.when(step == pl.num_programs(0) - 1)
    def _():
        for z, c, at in chunks_of(dense):
            blocks[z, c] = total[:, at * share : (at + 1) * share].T.astype(BF16)


def dense_back(grad, attended, dense, tokens):
    rows, width = grad.shape
    groups, cores, cols, share = dense.shape
    turned = jax.ShapeDtypeStruct((groups, cores, share, cols), BF16)
    tile = 512
    return launch(
        dense_back_kernel,
        [grad, attended, dense],
        [
            pl.BlockSpec((tile, width), lambda i: (i, 0)),
            pl.BlockSpec((tile, cols), lambda i: (i, 0)),
            whole_spec(dense),
        ],
        (rows // tile,),
        [pl.BlockSpec((tile, cols), lambda i: (i, 0)), whole_spec(turned)],
        [jax.ShapeDtypeStruct((rows, cols), BF16), turned],
        "dense_back",
        cost(4 * rows * dense.size, 2 * (rows * (width + cols) + dense.size)),
        tokens=tokens,
        scratch_shapes=[pltpu.VMEM((cols, width), F32)],
    )


def pre_grad_kernel(grad_ref, slope, contract, out, send, sums):
    @pl.when(pl.program_id(0) == 0)
    def _():
        sums[...] = jnp.zeros_like(sums)

    part = column_back(grad_ref, contract, contract.shape[3]) * slope[...].astype(F32)
    part = part.astype(BF16)
    out[...] = part
    send[...] = part
    sums[...] += jnp.sum(part.astype(F32), axis=0, keepdims=True)


def pre_grad_of(grad, slope, contract, tokens):
    rows, width = grad.shape
    cols = contract.shape[2]
    tile = 512
    steps = rows // tile
    return launch(
        pre_grad_kernel,
        [grad, slope, contract],
        [
            pl.BlockSpec((tile, width), lambda i: (i, 0)),
            pl.BlockSpec((tile, cols), lambda i: (i, 0)),
            whole_spec(contract),
        ],
        (steps,),
        [
            pl.BlockSpec((tile, cols), lambda i: (i, 0)),
            later_half(tile, cols, steps),
            pl.BlockSpec((1, cols), lambda i: (0, 0)),
        ],
        [
            jax.ShapeDtypeStruct((rows, cols), BF16),
            jax.ShapeDtypeStruct((rows // 2, cols), BF16),
            jax.ShapeDtypeStruct((1, cols), F32),
        ],
        "pre_grad",
        cost(2 * rows * contract.size, 2 * (rows * width + contract.size + 2 * rows * cols)),
        tokens=tokens,
    )


def normed_grad_piece(
    j, pieces, joined, pre, joined_weight, expand_weight, normal, gain1, gain2, sums, tokens
):
    tile = joined[1].shape[0] // pieces
    groups, cores, share, _ = joined_weight[0].shape
    steps = groups * cores // 2
    lefts = [*joined, *pre]
    rights = [*joined_weight, *expand_weight]
    extras = sums.extras(j)

    def kernel(*refs):
        normal, gain1, gain2 = refs[8:11]
        arrived = [(q, ref) for (q, _), ref in zip(extras, refs[11:])]
        *outs, along = refs[11 + len(extras) :]
        for n in range(2):

            def back(at):
                return lax.dot_general(
                    refs[at][...], refs[at + 4][n, 0], CONTRACT_LAST, preferred_element_type=F32
                )

            cols = slice(n * share, (n + 1) * share)
            first, second = back(0) + back(1), back(2) + back(3)
            rows = normal[:, cols].astype(F32)
            along[0:1, cols] = jnp.sum(first * rows, axis=0, keepdims=True)
            along[1:2, cols] = jnp.sum(first, axis=0, keepdims=True)
            along[2:3, cols] = jnp.sum(second * rows, axis=0, keepdims=True)
            along[3:4, cols] = jnp.sum(second, axis=0, keepdims=True)
            finish_piece(
                first * gain1[:, cols] + second * gain2[:, cols], n * share, arrived, outs
            )

    row = pl.BlockSpec((1, 2 * share), lambda i: (0, i))
    specs, shapes = piece_specs(tile, 2 * share, steps, sums.splits(j))
    *result, along = launch(
        kernel,
        lefts + rights + [normal, gain1, gain2] + [item for _, item in extras],
        [pl.BlockSpec((tile, item.shape[1]), lambda i: (j, 0)) for item in lefts]
        + [by_columns(item) for item in rights]
        + [pl.BlockSpec((tile, 2 * share), lambda i: (j, i)), row, row]
        + [pl.BlockSpec((tile // 2, 2 * share), lambda i: (0, i))] * len(extras),
        (steps,),
        specs + [pl.BlockSpec((8, 2 * share), lambda i: (0, i))],
        shapes + [jax.ShapeDtypeStruct((8, steps * 2 * share), F32)],
        "normed_grad_piece",
        cost(4 * tile * sum(item.size for item in rights), 4 * sum(item.size for item in rights)),
        tokens=tokens,
    )
    sums.pieces[j] = result if sums.splits(j) else result[0]
    return along


def rows_at(half, width, here):
    if here:
        return pl.BlockSpec((1, half, width), lambda i, place: (place[1], i, 0))
    return pl.BlockSpec((1, half, width), lambda i, place: (1 - place[1], i, 0))


def finish_tile(body, name, place, operands, whole, tile, width, tokens=()):
    half = tile // 2
    listed, specs, picks = [], [], []
    for pair in operands:
        if not isinstance(pair, list):
            picks.append((len(listed), False))
            listed.append(pair)
            specs.append(pl.BlockSpec((1, half, width), lambda i, place: (place[1], i, 0)))
        elif pair[0][0] is pair[1][0] and (pair[0][1], pair[1][1]) == (0, 1):
            picks.append((len(listed), False))
            listed.append(pair[0][0])
            specs.append(pl.BlockSpec((half, width), lambda i, place: (i, 0)))
        else:
            picks.append((len(listed), True))
            for item, at in pair:
                listed.append(item)
                specs.append(pl.BlockSpec((half, width), lambda i, place, at=at: (at, 0)))
    count = len(listed)

    def kernel(place, *refs):
        both, own = refs[count + len(whole) :]
        first = pl.program_id(0) == 0
        values = [
            jnp.where(first, refs[at][...], refs[at + 1][...])
            if pair
            else refs[at][...].reshape(half, width)
            for at, pair in picks
        ]
        result = body(values, refs[count : count + len(whole)]).astype(BF16)
        both[0] = result
        own[...] = result

    return launch(
        kernel,
        listed + list(whole),
        specs + [pl.BlockSpec(item.shape, lambda i, place: (0, 0)) for item in whole],
        (2,),
        [rows_at(half, width, True), pl.BlockSpec((half, width), lambda i, place: (i, 0))],
        [
            jax.ShapeDtypeStruct((2, tile, width), BF16),
            jax.ShapeDtypeStruct((tile, width), BF16),
        ],
        name,
        cost(20 * tile * width, 20 * tile * width),
        prefetch=[place],
        tokens=tokens,
    )


def pick_other(place, total, tokens):
    _, rows, cols = total.shape

    def pick(place, value, out):
        out[...] = value[0]

    other = launch(
        pick,
        [total],
        [pl.BlockSpec((1, rows, cols), lambda i, place: (1 - place[1], 0, 0))],
        (1,),
        pl.BlockSpec((rows, cols), lambda i, place: (0, 0)),
        jax.ShapeDtypeStruct((rows, cols), BF16),
        "pick_other",
        cost(1, 4 * rows * cols),
        prefetch=[place],
        tokens=tokens,
    )
    return swap(other, "branch", 1)


def join_cores(place, total, other, straight, tokens):
    _, rows, cols = total.shape
    turned = cols - straight

    def join(place, mine, others, *outs):
        value = jnp.where(pl.program_id(0) == 0, mine[0], others[...]).astype(F32)
        if straight:
            outs[0][...] = value[:, :straight]
        if turned:
            outs[-1][...] = value[:, straight:].T

    specs, shapes = [], []
    if straight:
        specs.append(pl.BlockSpec((rows, straight), lambda i, place: (0, place[1] ^ i)))
        shapes.append(jax.ShapeDtypeStruct((rows, 2 * straight), F32))
    if turned:
        specs.append(pl.BlockSpec((turned, rows), lambda i, place: (place[1] ^ i, 0)))
        shapes.append(jax.ShapeDtypeStruct((2 * turned, rows), F32))
    return launch(
        join,
        [total, other],
        [
            pl.BlockSpec((1, rows, cols), lambda i, place: (place[1], 0, 0)),
            pl.BlockSpec((rows, cols), lambda i, place: (0, 0)),
        ],
        (2,),
        specs,
        shapes,
        "finish_weight",
        cost(1, 16 * rows * cols),
        prefetch=[place],
        tokens=tokens,
    )


def fill_other(place, both, other, tokens=()):
    tile, width = other.shape

    def kernel(place, value, out):
        out[0] = value[...]

    return launch(
        kernel,
        [other],
        [pl.BlockSpec((tile // 2, width), lambda i, place: (i, 0))],
        (2,),
        rows_at(tile // 2, width, False),
        jax.ShapeDtypeStruct(both.shape, BF16),
        "fill_other",
        cost(1, 4 * tile * width),
        prefetch=[place],
        tokens=tokens,
        held=[both],
    )


def per_device(
    block_input,
    first_norm_gain,
    first_norm_bias,
    second_norm_gain,
    second_norm_bias,
    query_key_value,
    query_key_value_bias,
    attention_dense,
    attention_dense_bias,
    expand_weight,
    expand_bias,
    contract_weight,
    contract_bias,
    document_starts,
    output_grad,
):
    seqs, tile, model_width = block_input.shape
    tiles = lax.axis_size("tp")
    groups = lax.axis_size("seq")
    core = lax.axis_index("branch")
    here = lax.axis_index("tp")
    first_core = core == 0
    length = tile * tiles
    rows_in_all = length * seqs
    share = query_key_value.shape[0]

    def by_core(mine, others):
        return jnp.where(first_core, mine, others), jnp.where(first_core, others, mine)

    def halves_of(value, axis):
        size = value.shape[axis] // 2
        return (
            lax.dynamic_slice_in_dim(value, core * size, size, axis),
            lax.dynamic_slice_in_dim(value, (1 - core) * size, size, axis),
        )

    place = jnp.stack([here, core]).astype(jnp.int32)

    input_halves = own_halves(place, block_input)
    near = {**gather_near(input_halves, 0), **gather_near(input_halves, 1)}

    def core_halves(weight, axis):
        mine, others = halves_of(weight, axis)
        return jnp.stack(by_core(mine, swap(others, "branch", 1)))

    def gather_seq(piece):
        return lax.all_gather(piece, "seq", axis=0)

    weight_pieces = [
        core_halves(query_key_value, 1),
        core_halves(expand_weight, 1),
        core_halves(attention_dense, 0),
        core_halves(contract_weight, 0),
    ]
    joined_weight, expand_full, dense_full, contract_full = map(gather_seq, weight_pieces)
    joined_bias = halves_of(query_key_value_bias, 0)[0].astype(F32)[None]
    hidden_bias = halves_of(expand_bias, 0)[0].astype(F32)[None]

    gain1 = first_norm_gain.astype(F32)[None]
    gain2 = second_norm_gain.astype(F32)[None]
    gains = (
        gain1,
        first_norm_bias.astype(F32)[None],
        gain2,
        second_norm_bias.astype(F32)[None],
    )
    tables = rotary_tables(place, document_starts, rows_in_all, weight_pieces)
    grad_halves = own_halves(place, output_grad, [tables[0]])
    grad_rows = place_piece(0, place, output_grad, rows_in_all, (), grad_halves)
    *normed, mark = norm_piece(
        0, place, block_input, rows_in_all, gains, (), [tables[0], grad_rows]
    )
    near = in_pieces(hold_all(near, mark), {})
    far = gather_far(near)
    for j in sorted(near):
        *normed, mark = norm_piece(
            j, place, with_other_core(near[j]), rows_in_all, gains, normed, []
        )
    heads_held = ()
    far_from = tiles
    if tiles == 4:
        heads_held = project(0, 3, normed[1], joined_weight, joined_bias, tables, ())
        far_from = 3
    for j in sorted(far):
        last_items = [hold(item, mark) for item in far[j]]
        *normed, mark = norm_piece(
            j, place, with_other_core(last_items), rows_in_all, gains, normed, heads_held[:1]
        )
    heads_held = project(
        far_from % tiles, tiles, normed[1], joined_weight, joined_bias, tables, heads_held
    )
    normal, first_normed, second_normed = normed
    queries, keys, values = heads_held

    first = gather_near([hold(item, *last_items) for item in grad_halves], 0)
    first = hold_all(first, queries)
    second = gather_near([hold(item, *first.values()) for item in grad_halves], 1)
    attended, attended_send, log_sums = attend(
        place, document_starts, queries, keys, values, [*first.values()]
    )
    attended_flat = attended.reshape(rows_in_all, -1)
    near = in_pieces(first, hold_all(second, log_sums))
    far = gather_far(near)
    activated, activated_send, slope = expand(
        second_normed, expand_full, hidden_bias, [item for j in near for item in near[j]]
    )
    near = {
        j: items + [hold(swap(item, "branch", 1), slope) for item in items]
        for j, items in near.items()
    }
    far = {j: [hold(item, slope) for item in items] for j, items in far.items()}
    arrived = [item for items in [*near.values(), *far.values()] for item in items]
    far = {j: with_other_core(items) for j, items in far.items()}
    for j, items in {**near, **far}.items():
        grad_rows = place_piece(j, place, items, rows_in_all, [grad_rows], [slope])

    def weight_grad(left, right):
        return lax.dot_general(left, right, CONTRACT_FIRST, preferred_element_type=F32).astype(BF16)

    def in_order(part):
        return part.reshape(2, groups, share, part.shape[1]).transpose(1, 0, 2, 3)

    def scatter(blocks):
        return lax.psum_scatter(blocks, "seq", scatter_dimension=0, tiled=False)

    def exchanged(own, send, *tokens):
        send = send.reshape(-1, send.shape[-1])
        return own.reshape(-1, own.shape[-1]), swap(hold(send, *tokens) if tokens else send, "branch", 1)

    def with_other_weight(weight):
        return weight, swap(weight, "branch", 1)

    contract_blocks = in_order(weight_grad(grad_rows, activated))
    contract_full = hold(contract_full, contract_blocks)
    pre_grad, pre_send, pre_sums = pre_grad_of(
        grad_rows, slope, contract_full, [contract_blocks]
    )
    contract_total = scatter(hold(contract_blocks, pre_sums))
    pre_pair = exchanged(pre_grad, pre_send)
    dense_full = hold(dense_full, pre_sums)
    attended_pair = exchanged(attended, attended_send, pre_sums)
    activated_pair = exchanged(activated, activated_send, pre_sums)
    contract_pair = with_other_weight(hold(contract_full, pre_sums))
    expand_blocks = in_order(weight_grad(second_normed, pre_grad))
    expand_total = scatter(expand_blocks)
    dense_pair = with_other_weight(dense_full)
    order = sorted(range(1, tiles), key=lambda j: (-bin(j).count("1"), j))
    outputs = TileSum()

    def output(j, *tokens):
        return output_piece(
            j, tiles, attended_pair, activated_pair, dense_pair, contract_pair, outputs, tokens
        )

    mark = expand_blocks
    operands = []
    for number, j in enumerate(order):
        if number and bin(order[number - 1]).count("1") > bin(j).count("1"):
            if not outputs.pieces.get(0) is None:
                operands += outputs.land(mark)
            else:
                attended_grad, dense_blocks = dense_back(
                    grad_rows, attended_flat, dense_full, [mark, *operands]
                )
                mark = output(0, attended_grad)
                operands = outputs.land(mark)
        mark = output(j, mark, *operands)
        operands = outputs.send() if outputs.complete(j) else []
    operands += outputs.send()
    landed = []
    joined_grad, joined_send, joined_sums = attend_back(
        place,
        document_starts,
        queries,
        keys,
        values,
        attended_grad.reshape(attended.shape),
        attended,
        log_sums,
        tables,
        [mark, *operands],
    )
    landed = outputs.land(joined_sums)
    joined_pair = exchanged(joined_grad, joined_send, *landed)
    joined_weight_pair = with_other_weight(joined_weight)
    expand_weight_pair = with_other_weight(expand_full)
    joined_grad = joined_pair[0]
    inputs = TileSum()
    sums = jnp.zeros((8, model_width), F32)
    mark = joined_sums
    wait = landed
    joined_blocks = None
    for number, j in enumerate(order + [0]):
        if number and j and bin(order[number - 1]).count("1") > bin(j).count("1"):
            if joined_blocks is None:
                part = weight_grad(hold(first_normed, mark, *wait), joined_grad)
                wait = inputs.land(part)
                joined_blocks = jnp.concatenate(
                    [in_order(hold(part, *wait)), dense_blocks], axis=3
                )
                joined_total = scatter(joined_blocks)
                mark = joined_blocks
            else:
                wait = inputs.land(mark)
        part = normed_grad_piece(
            j,
            tiles,
            joined_pair,
            pre_pair,
            joined_weight_pair,
            expand_weight_pair,
            normal,
            gain1,
            gain2,
            inputs,
            [mark, *wait],
        )
        sums = sums + part
        mark = part
        wait = inputs.send()
    landed = inputs.land(mark)

    biases = (
        attention_dense_bias.astype(F32)[None],
        contract_bias.astype(F32)[None],
    )

    def output_body(values, whole):
        return add_up(values) + whole[0][...] + whole[1][...]

    def input_body(values, whole):
        x, grad = values[0].astype(F32), values[1].astype(F32)
        total = add_up(values[2:])
        centred = x - jnp.mean(x, axis=-1, keepdims=True)
        rate = lax.rsqrt(jnp.mean(centred * centred, axis=-1, keepdims=True) + EPSILON)
        n = centred * rate
        middle = jnp.mean(total, axis=-1, keepdims=True)
        along = jnp.mean(total * n, axis=-1, keepdims=True)
        return grad + rate * (total - middle - n * along)

    def all_sum_beside(value, axis, others):
        size = lax.axis_size(axis)
        bit = 1
        while bit < size:
            arrived = swap(value, axis, bit)
            if others:
                arrived = hold(arrived, *others.pop(0)(value))
            value = value + arrived
            bit *= 2
        return value

    kept = {}

    def first_beside(value):
        kept["both"], kept["own"] = finish_tile(
            output_body,
            "finish_output",
            place,
            [block_input] + outputs.terms(),
            biases,
            tile,
            model_width,
            [value],
        )
        return [kept["own"]]

    def second_beside(value):
        kept["contract"] = pick_other(place, contract_total, [value])
        kept["expand"] = pick_other(place, expand_total, [kept["contract"]])
        (kept["contract_grad"],) = join_cores(place, contract_total, kept["contract"], 0, [value])
        (kept["expand_grad"],) = join_cores(
            place, expand_total, kept["expand"], expand_total.shape[2], [kept["contract_grad"]]
        )
        return [kept["expand_grad"], *landed]

    def third_beside(value):
        kept["output"] = fill_other(
            place, kept["both"], swap(kept["own"], "branch", 1), [value, kept["expand_grad"]]
        )
        return [kept["output"]]

    def fourth_beside(value):
        kept["input_both"], kept["input_own"] = finish_tile(
            input_body,
            "finish_input",
            place,
            [block_input, output_grad] + inputs.terms(),
            (),
            tile,
            model_width,
            [value],
        )
        return [kept["input_own"]]

    def fifth_beside(value):
        kept["joined"] = pick_other(place, joined_total, [value])
        return [kept["joined"]]

    others = [first_beside, second_beside, third_beside, fourth_beside, fifth_beside]
    joined_bias_part = jnp.sum(joined_sums, axis=0).reshape(-1)
    hidden_bias_part = pre_sums[0]
    grad_own = lax.dynamic_index_in_dim(output_grad, core, 0, False)
    small = jnp.concatenate(
        [
            sums[:4].reshape(-1),
            jnp.sum(grad_own.astype(F32), axis=0),
            joined_bias_part,
            hidden_bias_part,
        ]
    )
    everywhere = 5 * model_width
    small = all_sum_beside(hold(small, mark), "seq", others)
    per_core = small[everywhere:]
    both = jnp.stack(by_core(per_core, swap(per_core, "branch", 1)))
    query_key_value_bias_grad = both[:, : joined_bias_part.shape[0]].reshape(-1)
    expand_bias_grad = both[:, joined_bias_part.shape[0] :].reshape(-1)
    shared = all_sum_beside(small[:everywhere], "tp", others)
    shared = all_sum_beside(shared, "branch", others).reshape(5, model_width)
    while others:
        others.pop(0)(mark)
    contract_grad, expand_grad = kept["contract_grad"], kept["expand_grad"]
    block_output, joined_other = kept["output"], kept["joined"]
    input_grad = fill_other(
        place, kept["input_both"], swap(kept["input_own"], "branch", 1), [joined_other]
    )
    query_key_value_grad, dense_grad = join_cores(
        place, joined_total, joined_other, joined_weight.shape[3], [input_grad]
    )
    return (
        block_output,
        input_grad,
        shared[0],
        shared[1],
        shared[2],
        shared[3],
        query_key_value_grad,
        query_key_value_bias_grad,
        dense_grad,
        shared[4],
        expand_grad,
        expand_bias_grad,
        contract_grad,
        shared[4],
    )


def solution(mesh):
    in_specs = (
        P("seq", "tp", None),
        P(),
        P(),
        P(),
        P(),
        P(("branch", "seq"), "tp"),
        P("tp"),
        P("tp", ("branch", "seq")),
        P(),
        P(("branch", "seq"), "tp"),
        P("tp"),
        P("tp", ("branch", "seq")),
        P(),
        P("seq", None),
        P("seq", "tp", None),
    )
    out_specs = (
        P("seq", "tp", None),
        P("seq", "tp", None),
        P(),
        P(),
        P(),
        P(),
        P(("branch", "seq"), "tp"),
        P("tp"),
        P("tp", ("branch", "seq")),
        P(),
        P(("branch", "seq"), "tp"),
        P("tp"),
        P("tp", ("branch", "seq")),
        P(),
    )
    return jax.shard_map(
        per_device, mesh=mesh, in_specs=in_specs, out_specs=out_specs, check_vma=False
    )
```

```python
from functools import partial
import math

import jax
import jax.numpy as jnp
from jax import lax
from jax.experimental import pallas as pl
from jax.experimental.pallas import tpu as pltpu
from jax.sharding import PartitionSpec as P

HD = 128
ROT = 32


EPSILON = 1e-05
NEGATIVE = -1e30
ROPE_BASE = 10000.0
LOG2E = math.log2(math.e)
F32 = jnp.float32
BF16 = jnp.bfloat16
CONTRACT_LAST = (((1,), (1,)), ((), ()))
CONTRACT_FIRST = (((0,), (0,)), ((), ()))
VMEM_BYTES = 56 * 1024 * 1024
ANY = pl.BlockSpec(memory_space=pl.ANY)
HINT = 0.02


def cost(flops, moved, transcendentals=0):
    return pl.CostEstimate(
        flops=1 + int(flops * HINT), bytes_accessed=1 + int(moved * HINT), transcendentals=0
    )


def launch(
    kernel,
    operands,
    in_specs,
    grid,
    out_specs,
    out_shape,
    name,
    cost_estimate,
    prefetch=(),
    held=(),
    tokens=(),
    scratch_shapes=(),
):
    lead = len(prefetch) + len(operands)
    extra = len(held) + len(tokens)

    def body(*refs):
        kernel(*refs[:lead], *refs[lead + extra :])

    return pl.pallas_call(
        body,
        grid_spec=pltpu.PrefetchScalarGridSpec(
            num_scalar_prefetch=len(prefetch),
            grid=grid,
            in_specs=list(in_specs) + [ANY] * extra,
            out_specs=out_specs,
            scratch_shapes=list(scratch_shapes),
        ),
        out_shape=out_shape,
        input_output_aliases={lead + k: k for k in range(len(held))},
        compiler_params=pltpu.CompilerParams(
            dimension_semantics=("arbitrary",) * len(grid), vmem_limit_bytes=VMEM_BYTES
        ),
        cost_estimate=cost_estimate,
        name=name,
    )(*prefetch, *operands, *held, *tokens)


def hold(value, *tokens):
    def nothing(out):
        pass

    return launch(
        nothing,
        [],
        [],
        (1,),
        ANY,
        jax.ShapeDtypeStruct(value.shape, value.dtype),
        "hold",
        cost(1, 1),
        held=[value],
        tokens=tokens,
    )


def swap(value, axis, bit):
    size = lax.axis_size(axis)
    return lax.ppermute(value, axis, [(i, i ^ bit) for i in range(size)])


def onward(value, axis):
    size = lax.axis_size(axis)
    return lax.ppermute(value, axis, [(i, (i + 1) % size) for i in range(size)])


def bit_orders(size):
    bits = [1 << k for k in range(size.bit_length() - 1)]
    return (bits, bits[::-1])


def last_bit(number, order):
    return [bit for bit in order if number & bit][-1]


def gather_near(own, number):
    size = lax.axis_size("tp")
    bits = [1 << k for k in range(size.bit_length() - 1)]
    return {
        (bit, (n + number) % 2): swap(own[(n + number) % 2], "tp", bit)
        for n, bit in enumerate(bits)
    }


def hold_all(items, *tokens):
    return {key: hold(item, *tokens) for key, item in items.items()}


def in_pieces(first, second):
    items = {**first, **second}
    return {j: [items[j, 0], items[j, 1]] for j in sorted({j for j, _ in items})}


def gather_far(near):
    size = lax.axis_size("tp")
    pieces = dict(near)
    far = {}
    for j in sorted(range(1, size), key=lambda j: bin(j).count("1")):
        if j not in near:
            bits = [last_bit(j, order) for order in bit_orders(size)]
            far[j] = [swap(pieces[j ^ bit][q], "tp", bit) for q, bit in enumerate(bits)]
            pieces[j] = far[j]
    return far


def with_other_core(items):
    return items + [swap(item, "branch", 1) for item in items]


def add_up(items):
    total = items[0].astype(F32)
    for item in items[1:]:
        total = total + item.astype(F32)
    return total


class TileSum:
    def __init__(self):
        size = lax.axis_size("tp")
        self.orders = bit_orders(size)
        self.waiting = [(q, j) for j in range(1, size) for q in range(2)]
        self.expected = {(q, j): 0 for j in range(size) for q in range(2)}
        for q, j in self.waiting:
            self.expected[q, j ^ last_bit(j, self.orders[q])] += 1
        self.waiting.sort(key=lambda at: (-bin(at[1]).count("1"), at[1]))
        self.pieces = {}
        self.arrived = {}
        self.moving = []

    def splits(self, j):
        return j > 0 and len({last_bit(j, order) for order in self.orders}) > 1

    def extras(self, j):
        return [(q, item) for q in range(2) for item in self.arrived.get((q, j), [])]

    def complete(self, j):
        return all(len(self.arrived.get((q, j), [])) == self.expected[q, j] for q in range(2))

    def send(self, *tokens):
        operands = []
        for q, j in list(self.waiting):
            if j not in self.pieces or (q, j) not in self.waiting:
                continue
            bit = last_bit(j, self.orders[q])
            if self.splits(j):
                sides, operand = [q], self.pieces[j][q]
            else:
                sides, operand = [0, 1], self.pieces[j]
            for side in sides:
                self.waiting.remove((side, j))
            if tokens:
                operand = hold(operand, *tokens)
            self.moving.append((sides, j ^ bit, swap(operand, "tp", bit)))
            operands.append(operand)
        return operands

    def land(self, *tokens):
        items = []
        for sides, j, item in self.moving:
            item = hold(item, *tokens) if tokens else item
            items.append(item)
            if j == 0:
                self.arrived.setdefault(0, []).append(item)
                continue
            half = item.shape[0] // 2
            for side in sides:
                part = item[side * half : (side + 1) * half] if len(sides) > 1 else item
                self.arrived.setdefault((side, j), []).append(part)
        self.moving = []
        return items

    def terms(self):
        return [[(item, 0), (item, 1)] for item in [self.pieces[0]] + self.arrived[0]]


def finish_piece(total, column, extras, outs):
    half = total.shape[0] // 2
    width = total.shape[1]
    cols = slice(column, column + width)
    parts = [total[:half], total[half:]]
    for q, ref in extras:
        parts[q] = parts[q] + ref[:, cols].astype(F32)
    for q in range(2):
        if len(outs) > 1:
            outs[q][:, cols] = parts[q].astype(BF16)
        else:
            outs[0][q * half : (q + 1) * half, cols] = parts[q].astype(BF16)


def piece_specs(tile, share, steps, split):
    rows, count = (tile // 2, 2) if split else (tile, 1)
    return (
        [pl.BlockSpec((rows, share), lambda i: (0, i))] * count,
        [jax.ShapeDtypeStruct((rows, steps * share), BF16)] * count,
    )


def all_sum(value, axis):
    size = lax.axis_size(axis)
    bit = 1
    while bit < size:
        value = value + swap(value, axis, bit)
        bit *= 2
    return value


def rope(vectors, cosine, sine_up, sine_down):
    return (
        vectors * cosine
        + pltpu.roll(vectors, ROT // 2, 1) * sine_up
        + pltpu.roll(vectors, HD - ROT // 2, 1) * sine_down
    )


class Documents:
    def __init__(self, place, starts, seq_at, rows):
        self.row = place[1] ^ seq_at
        self.starts = starts
        self.rows = rows

    def begin(self, places):
        begin = jnp.zeros_like(places)
        for number in range(self.starts.shape[1]):
            start = self.starts[self.row, number]
            begin = jnp.where(places >= start, start, begin)
        return begin

    def first_key_block(self, block):
        return lax.div(self.begin(block * self.rows), jnp.int32(self.rows))

    def first_whole_key_block(self, block):
        begin = self.begin((block + 1) * self.rows - 1)
        return lax.div(begin + (self.rows - 1), jnp.int32(self.rows))

    def last_whole_query_block(self, block, blocks):
        last = block
        for number in range(1, blocks):
            after = jnp.minimum(block + number, blocks - 1)
            whole = self.begin((after + 1) * self.rows - 1) <= block * self.rows
            last = jnp.where(whole, jnp.maximum(last, after), last)
        return last

    def last_query_block(self, block, blocks):
        last = block
        for number in range(1, blocks):
            after = jnp.minimum(block + number, blocks - 1)
            last = jnp.where(self.first_key_block(after) <= block, jnp.maximum(last, after), last)
        return last


def table_kernel(place, starts, cosine, sine_up, sine_down):
    rows = cosine.shape[0]
    blocks = lax.axis_size("tp")
    step = pl.program_id(0)
    block, seq_at = lax.rem(step, blocks) ^ place[0], lax.div(step, blocks)
    places = block * rows + lax.broadcasted_iota(jnp.int32, (rows, 1), 0)
    begin = Documents(place, starts, seq_at, rows).begin(places)
    lane = lax.broadcasted_iota(jnp.int32, (1, HD), 1)
    half = ROT // 2
    number = jnp.where(lane < half, lane, lane - half).astype(F32)
    frequency = jnp.exp2(number * (-2.0 / ROT * math.log2(ROPE_BASE)))
    angles = (places - begin).astype(F32) * jnp.where(lane < ROT, frequency, 0.0)
    cosine[...] = jnp.cos(angles)
    sines = jnp.sin(angles)
    sine_up[...] = jnp.where((lane >= half) & (lane < ROT), sines, 0.0)
    sine_down[...] = jnp.where(lane < half, -sines, 0.0)


def rotary_tables(place, starts, rows, tokens):
    steps = 2 * lax.axis_size("tp")
    tile = rows // steps
    out = pl.BlockSpec((tile, HD), lambda i, *_: (i, 0))
    return launch(
        table_kernel,
        [],
        [],
        (steps,),
        [out] * 3,
        [jax.ShapeDtypeStruct((rows, HD), F32)] * 3,
        "rotary_tables",
        cost(rows * HD * 100, rows * HD * 48),
        prefetch=[place, starts],
        tokens=tokens,
    )


def half_of_piece(j):
    size = lax.axis_size("tp")
    return lambda i, *_: ((lax.div(i, 2) * size + j) * 2 + lax.rem(i, 2), 0)


def own_tile_specs(tile):
    _, rows, width = tile.shape

    def spec(h, q):
        return pl.BlockSpec((1, rows // 2, width), lambda i, place: (place[1] ^ h, q, 0))

    return [spec(h, q) for h in range(2) for q in range(2)]


def own_halves(place, tile, tokens=()):
    _, rows, width = tile.shape

    def kernel(place, first, second, out_first, out_second):
        out_first[...] = first[0]
        out_second[...] = second[0]

    shape = jax.ShapeDtypeStruct((rows // 2, width), BF16)
    return launch(
        kernel,
        [tile, tile],
        own_tile_specs(tile)[:2],
        (1,),
        [whole_spec(shape)] * 2,
        [shape, shape],
        "own_halves",
        cost(1, 4 * rows * width),
        prefetch=[place],
        tokens=tokens,
    )


def place_kernel(place, x0, x1, x2, x3, out):
    step = pl.program_id(0)
    for number, x_ref in enumerate((x0, x1, x2, x3)):

        @pl.when(step == number)
        def _(x_ref=x_ref):
            out[...] = x_ref[...].reshape(out.shape)


def place_piece(j, place, halves, rows_in_all, held, tokens=()):
    if j == 0:
        specs = own_tile_specs(halves)
        half, model_width = halves.shape[1] // 2, halves.shape[2]
        halves = [halves] * 4
    else:
        half, model_width = halves[0].shape
        specs = [whole_spec(item) for item in halves]
    return launch(
        place_kernel,
        halves,
        specs,
        (4,),
        pl.BlockSpec((half, model_width), half_of_piece(j)),
        jax.ShapeDtypeStruct((rows_in_all, model_width), BF16),
        "place_piece",
        cost(1, 4 * half * model_width * 4),
        prefetch=[place],
        held=held,
        tokens=tokens,
    )


def norm_kernel(place, x0, x1, x2, x3, gain1, shift1, gain2, shift2, *rest):
    normal, first, second, mark, scratch = rest[-5:]
    step = pl.program_id(0)
    mark[...] = jnp.zeros_like(mark)
    for number, x_ref in enumerate((x0, x1, x2, x3)):

        @pl.when(step == number)
        def _(x_ref=x_ref):
            scratch[...] = (x_ref[0] if len(x_ref.shape) == 3 else x_ref[...]).astype(F32)

    x = scratch[...]
    centred = x - jnp.mean(x, axis=-1, keepdims=True)
    variance = jnp.mean(centred * centred, axis=-1, keepdims=True)
    n = centred * lax.rsqrt(variance + EPSILON)
    normal[...] = n.astype(BF16)
    first[...] = (n * gain1[...] + shift1[...]).astype(BF16)
    second[...] = (n * gain2[...] + shift2[...]).astype(BF16)


def norm_piece(j, place, halves, rows_in_all, gains, held, tokens):
    if j == 0:
        specs = own_tile_specs(halves)
        half, model_width = halves.shape[1] // 2, halves.shape[2]
        halves = [halves] * 4
    else:
        half, model_width = halves[0].shape
        specs = [whole_spec(item) for item in halves]
    wide = pl.BlockSpec((half, model_width), half_of_piece(j))
    return launch(
        norm_kernel,
        halves + list(gains),
        specs + [whole_spec(item) for item in gains],
        (4,),
        [wide] * 3 + [pl.BlockSpec((8, HD), lambda i, *_: (0, 0))],
        [jax.ShapeDtypeStruct((rows_in_all, model_width), BF16)] * 3
        + [jax.ShapeDtypeStruct((8, HD), F32)],
        "norm_piece",
        cost(4 * half * model_width * 16, 4 * half * model_width * 16),
        prefetch=[place],
        held=held,
        tokens=tokens,
        scratch_shapes=[pltpu.VMEM((half, model_width), F32)],
    )


def chunks_of(weight):
    groups, cores = weight.shape[:2]
    return [(z, c, c * groups + z) for c in range(cores) for z in range(groups)]


def row_product(left, weight, share):
    total = None
    for z, c, at in chunks_of(weight):
        part = jnp.dot(
            left[:, at * share : (at + 1) * share], weight[z, c], preferred_element_type=F32
        )
        total = part if total is None else total + part
    return total


def column_back(left, weight, share):
    total = None
    for z, c, at in chunks_of(weight):
        part = lax.dot_general(
            left[:, at * share : (at + 1) * share],
            weight[z, c],
            CONTRACT_LAST,
            preferred_element_type=F32,
        )
        total = part if total is None else total + part
    return total


def whole_spec(array, prefetched=0):
    rank = array.ndim
    return pl.BlockSpec(array.shape, lambda *at: (0,) * rank)


def project_kernel(normed, weight, bias, cosine, sine_up, sine_down, queries, keys, values):
    joined = row_product(normed, weight, weight.shape[2]) + bias[...]
    tables = (cosine[...], sine_up[...], sine_down[...])
    for head in range(queries.shape[0]):
        at = head * 3 * HD
        queries[head, 0, 0] = rope(joined[:, at : at + HD], *tables).astype(BF16)
        keys[head, 0, 0] = rope(joined[:, at + HD : at + 2 * HD], *tables).astype(BF16)
        values[head, 0, 0] = joined[:, at + 2 * HD : at + 3 * HD].astype(BF16)


def project(first, last, normed, weight, bias, tables, held):
    rows, model_width = normed.shape
    joined_cols = weight.shape[3]
    heads = joined_cols // (3 * HD)
    size = lax.axis_size("tp")
    tile = rows // (2 * size)
    table = pl.BlockSpec((tile, HD), lambda s, i: (s * size + first + i, 0))
    share = (last - first) / size
    return launch(
        project_kernel,
        [normed, weight, bias] + list(tables),
        [
            pl.BlockSpec((tile, model_width), lambda s, i: (s * size + first + i, 0)),
            whole_spec(weight),
            whole_spec(bias),
            table,
            table,
            table,
        ],
        (2, last - first),
        [pl.BlockSpec((heads, 1, 1, tile, HD), lambda s, i: (0, s, first + i, 0, 0))] * 3,
        [jax.ShapeDtypeStruct((heads, 2, size, tile, HD), BF16)] * 3,
        "project",
        cost(
            2 * rows * share * model_width * joined_cols,
            2 * (rows * share * (model_width + joined_cols) + weight.size),
        ),
        held=held,
    )


def attend_kernel(place, starts, q_ref, k_ref, v_ref, out_ref, send_ref, lse_ref):
    block = pl.program_id(1)
    heads, rows = q_ref.shape[0], q_ref.shape[-2]
    here = place[0]
    documents = Documents(place, starts, pl.program_id(0), rows)
    low = documents.first_key_block(block)
    query_places = block * rows + lax.broadcasted_iota(jnp.int32, (rows, 1), 0)
    begin = documents.begin(query_places)
    factor = LOG2E / math.sqrt(HD)

    def step(masked, number, carry):
        key_places = number * rows + lax.broadcasted_iota(jnp.int32, (1, rows), 1)
        if masked:
            allowed = (key_places >= begin) & (key_places <= query_places)
        results = []
        for head in range(heads):
            top, total, mixed = carry[head]
            key = k_ref[head, 0, number ^ here]
            value = v_ref[head, 0, number ^ here]
            scores = lax.dot_general(
                q_ref[head, 0, 0], key, CONTRACT_LAST, preferred_element_type=F32
            )
            if masked:
                scores = jnp.where(allowed, scores, NEGATIVE)
            new_top = jnp.maximum(top, jnp.max(scores, axis=-1, keepdims=True))
            weights = jnp.exp2((scores - new_top) * factor)
            shrink = jnp.exp2((top - new_top) * factor)
            total = total * shrink + jnp.sum(weights, axis=-1, keepdims=True)
            mixed = mixed * shrink + jnp.dot(
                weights.astype(BF16), value, preferred_element_type=F32
            )
            results.append((new_top, total, mixed))
        return tuple(results)

    empty = (
        jnp.full((rows, 1), NEGATIVE, F32),
        jnp.zeros((rows, 1), F32),
        jnp.zeros((rows, HD), F32),
    )
    whole = jnp.minimum(jnp.maximum(documents.first_whole_key_block(block), low), block)
    results = lax.fori_loop(low, whole, partial(step, True), (empty,) * heads)
    results = lax.fori_loop(whole, block, partial(step, False), results)
    results = step(True, block, results)
    for head, (top, total, mixed) in enumerate(results):
        result = (mixed / total).astype(BF16)
        out_ref[0, 0, :, head * HD : (head + 1) * HD] = result
        send_ref[0, :, head * HD : (head + 1) * HD] = result
        log_sum = top * factor + jnp.log(total) * LOG2E
        lse_ref[head, 0, 0] = jnp.broadcast_to(log_sum, (rows, HD)).T[:1]


def attend(place, starts, queries, keys, values, tokens):
    heads, seqs, blocks, rows, _ = queries.shape
    one = pl.BlockSpec(
        (heads, 1, 1, rows, HD), lambda s, i, place, starts: (0, s, i ^ place[0], 0, 0)
    )
    full = pl.BlockSpec((heads, 1, blocks, rows, HD), lambda s, i, *_: (0, s, 0, 0, 0))
    pairs = heads * seqs * blocks * (blocks + 1) // 2
    return launch(
        attend_kernel,
        [queries, keys, values],
        [one, full, full],
        (seqs, blocks),
        [
            pl.BlockSpec(
                (1, 1, rows, heads * HD), lambda s, i, place, starts: (s, i ^ place[0], 0, 0)
            ),
            pl.BlockSpec(
                (1, rows, heads * HD), lambda s, i, place, starts: ((s * i) ^ place[0], 0, 0)
            ),
            pl.BlockSpec(
                (heads, 1, 1, 1, rows), lambda s, i, place, starts: (0, s, i ^ place[0], 0, 0)
            ),
        ],
        [
            jax.ShapeDtypeStruct((seqs, blocks, rows, heads * HD), BF16),
            jax.ShapeDtypeStruct((blocks, rows, heads * HD), BF16),
            jax.ShapeDtypeStruct((heads, seqs, blocks, 1, rows), F32),
        ],
        "attend",
        cost(pairs * 30 * rows * rows * HD, 4 * queries.size * 2),
        prefetch=[place, starts],
        tokens=tokens,
    )


def attend_back_kernel(
    place,
    starts,
    q_ref,
    k_ref,
    v_ref,
    grad_ref,
    out_ref,
    lse_ref,
    cosine,
    sine_up,
    sine_down,
    joined_ref,
    send_ref,
    sum_ref,
    query_grad,
    delta,
):
    block = pl.program_id(1)
    heads, blocks, rows = q_ref.shape[0], q_ref.shape[2], q_ref.shape[-2]
    here = place[0]
    documents = Documents(place, starts, pl.program_id(0), rows)
    high = documents.last_query_block(block, blocks)
    scaling = 1.0 / math.sqrt(HD)

    @pl.when(block == 0)
    def _():
        query_grad[...] = jnp.zeros_like(query_grad)

        def inner(j, carry):
            for head in range(heads):
                cols = slice(head * HD, (head + 1) * HD)
                product = grad_ref[0, j, :, cols].astype(F32) * out_ref[0, j, :, cols].astype(F32)
                delta[head, j] = jnp.sum(product.T, axis=0, keepdims=True)
            return carry

        lax.fori_loop(0, blocks, inner, 0)

    own = block ^ here
    key_places = block * rows + lax.broadcasted_iota(jnp.int32, (rows, 1), 0)

    def step(masked, number, carry):
        at = number ^ here
        if masked:
            query_places = number * rows + lax.broadcasted_iota(jnp.int32, (1, rows), 1)
            allowed = (key_places >= documents.begin(query_places)) & (
                key_places <= query_places
            )
        results = []
        for head in range(heads):
            key_grad, value_grad = carry[head]
            key = k_ref[head, 0, own]
            value = v_ref[head, 0, own]
            query = q_ref[head, 0, at]
            grad = grad_ref[0, at, :, head * HD : (head + 1) * HD]
            scores = lax.dot_general(key, query, CONTRACT_LAST, preferred_element_type=F32)
            weights = jnp.exp2(scores * (scaling * LOG2E) - lse_ref[head, 0, at])
            if masked:
                weights = jnp.where(allowed, weights, 0.0)
            weight_grad = lax.dot_general(value, grad, CONTRACT_LAST, preferred_element_type=F32)
            score_grad = (weights * (weight_grad - delta[head, at]) * scaling).astype(BF16)
            value_grad = value_grad + jnp.dot(
                weights.astype(BF16), grad, preferred_element_type=F32
            )
            key_grad = key_grad + jnp.dot(score_grad, query, preferred_element_type=F32)
            query_grad[head, at] = query_grad[head, at] + lax.dot_general(
                score_grad, key, CONTRACT_FIRST, preferred_element_type=F32
            )
            results.append((key_grad, value_grad))
        return tuple(results)

    empty = jnp.zeros((rows, HD), F32)
    whole = documents.last_whole_query_block(block, blocks)
    results = step(True, block, ((empty, empty),) * heads)
    results = lax.fori_loop(block + 1, whole + 1, partial(step, False), results)
    results = lax.fori_loop(whole + 1, high + 1, partial(step, True), results)
    tables = (cosine[0, own], -sine_up[0, own], -sine_down[0, own])
    for head, (key_grad, value_grad) in enumerate(results):
        at = head * 3 * HD
        joined_ref[0, own, :, at + HD : at + 2 * HD] = rope(key_grad, *tables).astype(BF16)
        joined_ref[0, own, :, at + 2 * HD : at + 3 * HD] = value_grad.astype(BF16)

    @pl.when(block == blocks - 1)
    def _():
        def inner(j, carry):
            tables = (cosine[0, j], -sine_up[0, j], -sine_down[0, j])
            for head in range(heads):
                at = head * 3 * HD
                joined_ref[0, j, :, at : at + HD] = rope(query_grad[head, j], *tables).astype(BF16)
            send_ref[j] = joined_ref[0, j]
            return carry + jnp.sum(joined_ref[0, j].astype(F32), axis=0, keepdims=True)

        sum_ref[0] = lax.fori_loop(0, blocks, inner, jnp.zeros((1, heads * 3 * HD), F32))


def attend_back(place, starts, queries, keys, values, grad, out, log_sums, tables, tokens):
    heads, seqs, blocks, rows, _ = queries.shape
    joined_cols = heads * 3 * HD
    head_spec = pl.BlockSpec((heads, 1, blocks, rows, HD), lambda s, i, *_: (0, s, 0, 0, 0))
    side = pl.BlockSpec((1, blocks, rows, heads * HD), lambda s, i, *_: (s, 0, 0, 0))
    table = pl.BlockSpec((1, blocks, rows, HD), lambda s, i, *_: (s, 0, 0, 0))
    pairs = heads * seqs * blocks * (blocks + 1) // 2
    return launch(
        attend_back_kernel,
        [queries, keys, values, grad, out, log_sums]
        + [item.reshape(seqs, blocks, rows, HD) for item in tables],
        [
            head_spec,
            head_spec,
            head_spec,
            side,
            side,
            pl.BlockSpec((heads, 1, blocks, 1, rows), lambda s, i, *_: (0, s, 0, 0, 0)),
            table,
            table,
            table,
        ],
        (seqs, blocks),
        [
            pl.BlockSpec((1, blocks, rows, joined_cols), lambda s, i, *_: (s, 0, 0, 0)),
            pl.BlockSpec((blocks, rows, joined_cols), lambda s, i, *_: (0, 0, 0)),
            pl.BlockSpec((1, 1, joined_cols), lambda s, i, *_: (s, 0, 0)),
        ],
        [
            jax.ShapeDtypeStruct((seqs, blocks, rows, joined_cols), BF16),
            jax.ShapeDtypeStruct((blocks, rows, joined_cols), BF16),
            jax.ShapeDtypeStruct((seqs, 1, joined_cols), F32),
        ],
        "attend_back",
        cost(pairs * 50 * rows * rows * HD, 12 * queries.size * 2),
        prefetch=[place, starts],
        tokens=tokens,
        scratch_shapes=[
            pltpu.VMEM((heads, blocks, rows, HD), F32),
            pltpu.VMEM((heads, blocks, 1, rows), F32),
        ],
    )


def expand_kernel(normed, weight, bias, activated, send, slope):
    pre = row_product(normed, weight, weight.shape[2]) + bias[...]
    share = 0.5 + 0.5 * lax.erf(pre * math.sqrt(0.5))
    density = jnp.exp2(pre * pre * (-0.5 * LOG2E)) * (1.0 / math.sqrt(2.0 * math.pi))
    result = (pre * share).astype(BF16)
    activated[...] = result
    send[...] = result
    slope[...] = (share + pre * density).astype(BF16)


def later_half(tile, width, steps):
    half = steps // 2
    return pl.BlockSpec((tile, width), lambda i: (jnp.maximum(i - half, 0), 0))


def expand(normed, weight, bias, tokens):
    rows, model_width = normed.shape
    cols = weight.shape[3]
    tile = 512
    steps = rows // tile
    out = pl.BlockSpec((tile, cols), lambda i: (i, 0))
    shape = jax.ShapeDtypeStruct((rows, cols), BF16)
    return launch(
        expand_kernel,
        [normed, weight, bias],
        [pl.BlockSpec((tile, model_width), lambda i: (i, 0)), whole_spec(weight), whole_spec(bias)],
        (steps,),
        [out, later_half(tile, cols, steps), out],
        [shape, jax.ShapeDtypeStruct((rows // 2, cols), BF16), shape],
        "expand",
        cost(
            2 * rows * model_width * cols,
            2 * (rows * model_width + weight.size + 2 * rows * cols),
        ),
        tokens=tokens,
    )


def by_columns(weight):
    groups = weight.shape[0] // 2
    return pl.BlockSpec(
        (2, 1) + weight.shape[2:], lambda i: (lax.rem(i, groups), lax.div(i, groups), 0, 0)
    )


def output_piece(j, pieces, attended, activated, dense, contract, sums, tokens):
    tile = attended[1].shape[0] // pieces
    groups, cores, _, share = dense[0].shape
    steps = groups * cores // 2
    lefts = [*attended, *activated]
    rights = [*dense, *contract]
    extras = sums.extras(j)

    def kernel(*refs):
        outs = refs[8 + len(extras) :]
        arrived = [(q, ref) for (q, _), ref in zip(extras, refs[8:])]
        for n in range(2):
            total = None
            for left, right in zip(refs[:4], refs[4:8]):
                part = jnp.dot(left[...], right[n, 0], preferred_element_type=F32)
                total = part if total is None else total + part
            finish_piece(total, n * share, arrived, outs)

    specs, shapes = piece_specs(tile, 2 * share, steps, sums.splits(j))
    result = launch(
        kernel,
        lefts + rights + [item for _, item in extras],
        [pl.BlockSpec((tile, item.shape[1]), lambda i: (j, 0)) for item in lefts]
        + [by_columns(item) for item in rights]
        + [pl.BlockSpec((tile // 2, 2 * share), lambda i: (0, i))] * len(extras),
        (steps,),
        specs,
        shapes,
        "output_piece",
        cost(4 * tile * sum(item.size for item in rights), 4 * sum(item.size for item in rights)),
        tokens=tokens,
    )
    sums.pieces[j] = result if sums.splits(j) else result[0]
    return result[0]


def dense_back_kernel(grad_ref, att_ref, dense, out, blocks, total):
    step = pl.program_id(0)
    share = dense.shape[3]

    @pl.when(step == 0)
    def _():
        total[...] = jnp.zeros_like(total)

    out[...] = column_back(grad_ref, dense, share).astype(BF16)
    total[...] += lax.dot_general(
        att_ref[...], grad_ref[...], CONTRACT_FIRST, preferred_element_type=F32
    )

    @pl.when(step == pl.num_programs(0) - 1)
    def _():
        for z, c, at in chunks_of(dense):
            blocks[z, c] = total[:, at * share : (at + 1) * share].T.astype(BF16)


def dense_back(grad, attended, dense, tokens):
    rows, width = grad.shape
    groups, cores, cols, share = dense.shape
    turned = jax.ShapeDtypeStruct((groups, cores, share, cols), BF16)
    tile = 512
    return launch(
        dense_back_kernel,
        [grad, attended, dense],
        [
            pl.BlockSpec((tile, width), lambda i: (i, 0)),
            pl.BlockSpec((tile, cols), lambda i: (i, 0)),
            whole_spec(dense),
        ],
        (rows // tile,),
        [pl.BlockSpec((tile, cols), lambda i: (i, 0)), whole_spec(turned)],
        [jax.ShapeDtypeStruct((rows, cols), BF16), turned],
        "dense_back",
        cost(4 * rows * dense.size, 2 * (rows * (width + cols) + dense.size)),
        tokens=tokens,
        scratch_shapes=[pltpu.VMEM((cols, width), F32)],
    )


def pre_grad_kernel(grad_ref, slope, contract, out, send, sums):
    @pl.when(pl.program_id(0) == 0)
    def _():
        sums[...] = jnp.zeros_like(sums)

    part = column_back(grad_ref, contract, contract.shape[3]) * slope[...].astype(F32)
    part = part.astype(BF16)
    out[...] = part
    send[...] = part
    sums[...] += jnp.sum(part.astype(F32), axis=0, keepdims=True)


def pre_grad_of(grad, slope, contract, tokens):
    rows, width = grad.shape
    cols = contract.shape[2]
    tile = 512
    steps = rows // tile
    return launch(
        pre_grad_kernel,
        [grad, slope, contract],
        [
            pl.BlockSpec((tile, width), lambda i: (i, 0)),
            pl.BlockSpec((tile, cols), lambda i: (i, 0)),
            whole_spec(contract),
        ],
        (steps,),
        [
            pl.BlockSpec((tile, cols), lambda i: (i, 0)),
            later_half(tile, cols, steps),
            pl.BlockSpec((1, cols), lambda i: (0, 0)),
        ],
        [
            jax.ShapeDtypeStruct((rows, cols), BF16),
            jax.ShapeDtypeStruct((rows // 2, cols), BF16),
            jax.ShapeDtypeStruct((1, cols), F32),
        ],
        "pre_grad",
        cost(2 * rows * contract.size, 2 * (rows * width + contract.size + 2 * rows * cols)),
        tokens=tokens,
    )


def normed_grad_piece(
    j, pieces, joined, pre, joined_weight, expand_weight, normal, gain1, gain2, sums, tokens
):
    tile = joined[1].shape[0] // pieces
    groups, cores, share, _ = joined_weight[0].shape
    steps = groups * cores // 2
    lefts = [*joined, *pre]
    rights = [*joined_weight, *expand_weight]
    extras = sums.extras(j)

    def kernel(*refs):
        normal, gain1, gain2 = refs[8:11]
        arrived = [(q, ref) for (q, _), ref in zip(extras, refs[11:])]
        *outs, along = refs[11 + len(extras) :]
        for n in range(2):

            def back(at):
                return lax.dot_general(
                    refs[at][...], refs[at + 4][n, 0], CONTRACT_LAST, preferred_element_type=F32
                )

            cols = slice(n * share, (n + 1) * share)
            first, second = back(0) + back(1), back(2) + back(3)
            rows = normal[:, cols].astype(F32)
            along[0:1, cols] = jnp.sum(first * rows, axis=0, keepdims=True)
            along[1:2, cols] = jnp.sum(first, axis=0, keepdims=True)
            along[2:3, cols] = jnp.sum(second * rows, axis=0, keepdims=True)
            along[3:4, cols] = jnp.sum(second, axis=0, keepdims=True)
            finish_piece(
                first * gain1[:, cols] + second * gain2[:, cols], n * share, arrived, outs
            )

    row = pl.BlockSpec((1, 2 * share), lambda i: (0, i))
    specs, shapes = piece_specs(tile, 2 * share, steps, sums.splits(j))
    *result, along = launch(
        kernel,
        lefts + rights + [normal, gain1, gain2] + [item for _, item in extras],
        [pl.BlockSpec((tile, item.shape[1]), lambda i: (j, 0)) for item in lefts]
        + [by_columns(item) for item in rights]
        + [pl.BlockSpec((tile, 2 * share), lambda i: (j, i)), row, row]
        + [pl.BlockSpec((tile // 2, 2 * share), lambda i: (0, i))] * len(extras),
        (steps,),
        specs + [pl.BlockSpec((8, 2 * share), lambda i: (0, i))],
        shapes + [jax.ShapeDtypeStruct((8, steps * 2 * share), F32)],
        "normed_grad_piece",
        cost(4 * tile * sum(item.size for item in rights), 4 * sum(item.size for item in rights)),
        tokens=tokens,
    )
    sums.pieces[j] = result if sums.splits(j) else result[0]
    return along


def rows_at(half, width, here):
    if here:
        return pl.BlockSpec((1, half, width), lambda i, place: (place[1], i, 0))
    return pl.BlockSpec((1, half, width), lambda i, place: (1 - place[1], i, 0))


def finish_tile(body, name, place, operands, whole, tile, width, tokens=()):
    half = tile // 2
    listed, specs, picks = [], [], []
    for pair in operands:
        if not isinstance(pair, list):
            picks.append((len(listed), False))
            listed.append(pair)
            specs.append(pl.BlockSpec((1, half, width), lambda i, place: (place[1], i, 0)))
        elif pair[0][0] is pair[1][0] and (pair[0][1], pair[1][1]) == (0, 1):
            picks.append((len(listed), False))
            listed.append(pair[0][0])
            specs.append(pl.BlockSpec((half, width), lambda i, place: (i, 0)))
        else:
            picks.append((len(listed), True))
            for item, at in pair:
                listed.append(item)
                specs.append(pl.BlockSpec((half, width), lambda i, place, at=at: (at, 0)))
    count = len(listed)

    def kernel(place, *refs):
        both, own = refs[count + len(whole) :]
        first = pl.program_id(0) == 0
        values = [
            jnp.where(first, refs[at][...], refs[at + 1][...])
            if pair
            else refs[at][...].reshape(half, width)
            for at, pair in picks
        ]
        result = body(values, refs[count : count + len(whole)]).astype(BF16)
        both[0] = result
        own[...] = result

    return launch(
        kernel,
        listed + list(whole),
        specs + [pl.BlockSpec(item.shape, lambda i, place: (0, 0)) for item in whole],
        (2,),
        [rows_at(half, width, True), pl.BlockSpec((half, width), lambda i, place: (i, 0))],
        [
            jax.ShapeDtypeStruct((2, tile, width), BF16),
            jax.ShapeDtypeStruct((tile, width), BF16),
        ],
        name,
        cost(20 * tile * width, 20 * tile * width),
        prefetch=[place],
        tokens=tokens,
    )


def pick_other(place, total, tokens):
    _, rows, cols = total.shape

    def pick(place, value, out):
        out[...] = value[0]

    other = launch(
        pick,
        [total],
        [pl.BlockSpec((1, rows, cols), lambda i, place: (1 - place[1], 0, 0))],
        (1,),
        pl.BlockSpec((rows, cols), lambda i, place: (0, 0)),
        jax.ShapeDtypeStruct((rows, cols), BF16),
        "pick_other",
        cost(1, 4 * rows * cols),
        prefetch=[place],
        tokens=tokens,
    )
    return swap(other, "branch", 1)


def join_cores(place, total, other, straight, tokens):
    _, rows, cols = total.shape
    turned = cols - straight

    def join(place, mine, others, *outs):
        value = jnp.where(pl.program_id(0) == 0, mine[0], others[...]).astype(F32)
        if straight:
            outs[0][...] = value[:, :straight]
        if turned:
            outs[-1][...] = value[:, straight:].T

    specs, shapes = [], []
    if straight:
        specs.append(pl.BlockSpec((rows, straight), lambda i, place: (0, place[1] ^ i)))
        shapes.append(jax.ShapeDtypeStruct((rows, 2 * straight), F32))
    if turned:
        specs.append(pl.BlockSpec((turned, rows), lambda i, place: (place[1] ^ i, 0)))
        shapes.append(jax.ShapeDtypeStruct((2 * turned, rows), F32))
    return launch(
        join,
        [total, other],
        [
            pl.BlockSpec((1, rows, cols), lambda i, place: (place[1], 0, 0)),
            pl.BlockSpec((rows, cols), lambda i, place: (0, 0)),
        ],
        (2,),
        specs,
        shapes,
        "finish_weight",
        cost(1, 16 * rows * cols),
        prefetch=[place],
        tokens=tokens,
    )


def fill_other(place, both, other, tokens=()):
    tile, width = other.shape

    def kernel(place, value, out):
        out[0] = value[...]

    return launch(
        kernel,
        [other],
        [pl.BlockSpec((tile // 2, width), lambda i, place: (i, 0))],
        (2,),
        rows_at(tile // 2, width, False),
        jax.ShapeDtypeStruct(both.shape, BF16),
        "fill_other",
        cost(1, 4 * tile * width),
        prefetch=[place],
        tokens=tokens,
        held=[both],
    )


def per_device(
    block_input,
    first_norm_gain,
    first_norm_bias,
    second_norm_gain,
    second_norm_bias,
    query_key_value,
    query_key_value_bias,
    attention_dense,
    attention_dense_bias,
    expand_weight,
    expand_bias,
    contract_weight,
    contract_bias,
    document_starts,
    output_grad,
):
    seqs, tile, model_width = block_input.shape
    tiles = lax.axis_size("tp")
    groups = lax.axis_size("seq")
    core = lax.axis_index("branch")
    here = lax.axis_index("tp")
    first_core = core == 0
    length = tile * tiles
    rows_in_all = length * seqs
    share = query_key_value.shape[0]

    def by_core(mine, others):
        return jnp.where(first_core, mine, others), jnp.where(first_core, others, mine)

    def halves_of(value, axis):
        size = value.shape[axis] // 2
        return (
            lax.dynamic_slice_in_dim(value, core * size, size, axis),
            lax.dynamic_slice_in_dim(value, (1 - core) * size, size, axis),
        )

    place = jnp.stack([here, core]).astype(jnp.int32)

    input_halves = own_halves(place, block_input)
    near = {**gather_near(input_halves, 0), **gather_near(input_halves, 1)}

    def core_halves(weight, axis):
        mine, others = halves_of(weight, axis)
        return jnp.stack(by_core(mine, swap(others, "branch", 1)))

    def gather_seq(piece):
        return lax.all_gather(piece, "seq", axis=0)

    weight_pieces = [
        core_halves(query_key_value, 1),
        core_halves(expand_weight, 1),
        core_halves(attention_dense, 0),
        core_halves(contract_weight, 0),
    ]
    joined_weight, expand_full, dense_full, contract_full = map(gather_seq, weight_pieces)
    joined_bias = halves_of(query_key_value_bias, 0)[0].astype(F32)[None]
    hidden_bias = halves_of(expand_bias, 0)[0].astype(F32)[None]

    gain1 = first_norm_gain.astype(F32)[None]
    gain2 = second_norm_gain.astype(F32)[None]
    gains = (
        gain1,
        first_norm_bias.astype(F32)[None],
        gain2,
        second_norm_bias.astype(F32)[None],
    )
    tables = rotary_tables(place, document_starts, rows_in_all, weight_pieces)
    grad_halves = own_halves(place, output_grad, [tables[0]])
    grad_rows = place_piece(0, place, output_grad, rows_in_all, (), grad_halves)
    *normed, mark = norm_piece(
        0, place, block_input, rows_in_all, gains, (), [tables[0], grad_rows]
    )
    near = in_pieces(hold_all(near, mark), {})
    far = gather_far(near)
    for j in sorted(near):
        *normed, mark = norm_piece(
            j, place, with_other_core(near[j]), rows_in_all, gains, normed, []
        )
    heads_held = ()
    far_from = tiles
    if tiles == 4:
        heads_held = project(0, 3, normed[1], joined_weight, joined_bias, tables, ())
        far_from = 3
    for j in sorted(far):
        last_items = [hold(item, mark) for item in far[j]]
        *normed, mark = norm_piece(
            j, place, with_other_core(last_items), rows_in_all, gains, normed, heads_held[:1]
        )
    heads_held = project(
        far_from % tiles, tiles, normed[1], joined_weight, joined_bias, tables, heads_held
    )
    normal, first_normed, second_normed = normed
    queries, keys, values = heads_held

    grad_halves = [hold(item, *last_items) for item in grad_halves]
    first = hold_all(gather_near(grad_halves, 0), queries)
    second = gather_near([hold(item, *first.values()) for item in grad_halves], 1)
    attended, attended_send, log_sums = attend(
        place, document_starts, queries, keys, values, [*first.values()]
    )
    attended_flat = attended.reshape(rows_in_all, -1)
    near = in_pieces(first, hold_all(second, log_sums))
    far = gather_far(near)
    activated, activated_send, slope = expand(
        second_normed, expand_full, hidden_bias, [item for j in near for item in near[j]]
    )
    near = {
        j: items + [hold(swap(item, "branch", 1), slope) for item in items]
        for j, items in near.items()
    }
    far = {j: [hold(item, slope) for item in items] for j, items in far.items()}
    arrived = [item for items in [*near.values(), *far.values()] for item in items]
    far = {j: with_other_core(items) for j, items in far.items()}
    for j, items in {**near, **far}.items():
        grad_rows = place_piece(j, place, items, rows_in_all, [grad_rows], [slope])

    def weight_grad(left, right):
        return lax.dot_general(left, right, CONTRACT_FIRST, preferred_element_type=F32).astype(BF16)

    def in_order(part):
        return part.reshape(2, groups, share, part.shape[1]).transpose(1, 0, 2, 3)

    def scatter(blocks):
        return lax.psum_scatter(blocks, "seq", scatter_dimension=0, tiled=False)

    def exchanged(own, send, *tokens):
        send = send.reshape(-1, send.shape[-1])
        return own.reshape(-1, own.shape[-1]), swap(hold(send, *tokens) if tokens else send, "branch", 1)

    def with_other_weight(weight):
        return weight, swap(weight, "branch", 1)

    contract_blocks = in_order(weight_grad(grad_rows, activated))
    contract_full = hold(contract_full, contract_blocks)
    pre_grad, pre_send, pre_sums = pre_grad_of(
        grad_rows, slope, contract_full, [contract_blocks]
    )
    contract_total = scatter(hold(contract_blocks, pre_sums))
    pre_pair = exchanged(pre_grad, pre_send)
    dense_full = hold(dense_full, pre_sums)
    attended_pair = exchanged(attended, attended_send, pre_sums)
    activated_pair = exchanged(activated, activated_send, pre_sums)
    contract_pair = with_other_weight(hold(contract_full, pre_sums))
    expand_blocks = in_order(weight_grad(second_normed, pre_grad))
    expand_total = scatter(expand_blocks)
    dense_pair = with_other_weight(dense_full)
    order = sorted(range(1, tiles), key=lambda j: (-bin(j).count("1"), j))
    outputs = TileSum()

    def output(j, *tokens):
        return output_piece(
            j, tiles, attended_pair, activated_pair, dense_pair, contract_pair, outputs, tokens
        )

    mark = expand_blocks
    operands = []
    for number, j in enumerate(order):
        if number and bin(order[number - 1]).count("1") > bin(j).count("1"):
            if not outputs.pieces.get(0) is None:
                operands += outputs.land(mark)
            else:
                attended_grad, dense_blocks = dense_back(
                    grad_rows, attended_flat, dense_full, [mark, *operands]
                )
                mark = output(0, attended_grad)
                operands = outputs.land(mark)
        mark = output(j, mark, *operands)
        operands = outputs.send() if outputs.complete(j) else []
    operands += outputs.send()
    landed = []
    joined_grad, joined_send, joined_sums = attend_back(
        place,
        document_starts,
        queries,
        keys,
        values,
        attended_grad.reshape(attended.shape),
        attended,
        log_sums,
        tables,
        [mark, *operands],
    )
    landed = outputs.land(joined_sums)
    joined_pair = exchanged(joined_grad, joined_send, *landed)
    joined_weight_pair = with_other_weight(joined_weight)
    expand_weight_pair = with_other_weight(expand_full)
    joined_grad = joined_pair[0]
    inputs = TileSum()
    sums = jnp.zeros((8, model_width), F32)
    mark = joined_sums
    wait = landed
    joined_blocks = None
    for number, j in enumerate(order + [0]):
        if number and j and bin(order[number - 1]).count("1") > bin(j).count("1"):
            if joined_blocks is None:
                part = weight_grad(hold(first_normed, mark, *wait), joined_grad)
                wait = inputs.land(part)
                joined_blocks = jnp.concatenate(
                    [in_order(hold(part, *wait)), dense_blocks], axis=3
                )
                joined_total = scatter(joined_blocks)
                mark = joined_blocks
            else:
                wait = inputs.land(mark)
        part = normed_grad_piece(
            j,
            tiles,
            joined_pair,
            pre_pair,
            joined_weight_pair,
            expand_weight_pair,
            normal,
            gain1,
            gain2,
            inputs,
            [mark, *wait],
        )
        sums = sums + part
        mark = part
        wait = inputs.send()
    landed = inputs.land(mark)

    biases = (
        attention_dense_bias.astype(F32)[None],
        contract_bias.astype(F32)[None],
    )

    def output_body(values, whole):
        return add_up(values) + whole[0][...] + whole[1][...]

    def input_body(values, whole):
        x, grad = values[0].astype(F32), values[1].astype(F32)
        total = add_up(values[2:])
        centred = x - jnp.mean(x, axis=-1, keepdims=True)
        rate = lax.rsqrt(jnp.mean(centred * centred, axis=-1, keepdims=True) + EPSILON)
        n = centred * rate
        middle = jnp.mean(total, axis=-1, keepdims=True)
        along = jnp.mean(total * n, axis=-1, keepdims=True)
        return grad + rate * (total - middle - n * along)

    def all_sum_beside(value, axis, others):
        size = lax.axis_size(axis)
        bit = 1
        while bit < size:
            arrived = swap(value, axis, bit)
            if others:
                arrived = hold(arrived, *others.pop(0)(value))
            value = value + arrived
            bit *= 2
        return value

    kept = {}

    def first_beside(value):
        kept["both"], kept["own"] = finish_tile(
            output_body,
            "finish_output",
            place,
            [block_input] + outputs.terms(),
            biases,
            tile,
            model_width,
            [value],
        )
        return [kept["own"]]

    def second_beside(value):
        kept["contract"] = pick_other(place, contract_total, [value])
        kept["expand"] = pick_other(place, expand_total, [kept["contract"]])
        (kept["contract_grad"],) = join_cores(place, contract_total, kept["contract"], 0, [value])
        (kept["expand_grad"],) = join_cores(
            place, expand_total, kept["expand"], expand_total.shape[2], [kept["contract_grad"]]
        )
        return [kept["expand_grad"], *landed]

    def third_beside(value):
        kept["input_both"], kept["input_own"] = finish_tile(
            input_body,
            "finish_input",
            place,
            [block_input, output_grad] + inputs.terms(),
            (),
            tile,
            model_width,
            [value],
        )
        kept["own_other"] = swap(hold(kept["own"], value), "branch", 1)
        return [kept["input_own"]]

    def fourth_beside(value):
        kept["output"] = fill_other(place, kept["both"], kept["own_other"], [value])
        return [kept["output"]]

    def fifth_beside(value):
        kept["joined"] = pick_other(place, joined_total, [value])
        return [kept["joined"]]

    others = [first_beside, second_beside, third_beside, fourth_beside, fifth_beside]
    joined_bias_part = jnp.sum(joined_sums, axis=0).reshape(-1)
    hidden_bias_part = pre_sums[0]
    grad_own = lax.dynamic_index_in_dim(output_grad, core, 0, False)
    small = jnp.concatenate(
        [
            sums[:4].reshape(-1),
            jnp.sum(grad_own.astype(F32), axis=0),
            joined_bias_part,
            hidden_bias_part,
        ]
    )
    everywhere = 5 * model_width
    small = all_sum_beside(hold(small, mark), "seq", others)
    per_core = small[everywhere:]
    both = jnp.stack(by_core(per_core, swap(per_core, "branch", 1)))
    query_key_value_bias_grad = both[:, : joined_bias_part.shape[0]].reshape(-1)
    expand_bias_grad = both[:, joined_bias_part.shape[0] :].reshape(-1)
    shared = all_sum_beside(small[:everywhere], "tp", others)
    shared = all_sum_beside(shared, "branch", others).reshape(5, model_width)
    while others:
        others.pop(0)(mark)
    contract_grad, expand_grad = kept["contract_grad"], kept["expand_grad"]
    block_output, joined_other = kept["output"], kept["joined"]
    input_grad = fill_other(
        place, kept["input_both"], swap(kept["input_own"], "branch", 1), [joined_other]
    )
    query_key_value_grad, dense_grad = join_cores(
        place, joined_total, joined_other, joined_weight.shape[3], [input_grad]
    )
    return (
        block_output,
        input_grad,
        shared[0],
        shared[1],
        shared[2],
        shared[3],
        query_key_value_grad,
        query_key_value_bias_grad,
        dense_grad,
        shared[4],
        expand_grad,
        expand_bias_grad,
        contract_grad,
        shared[4],
    )


def solution(mesh):
    in_specs = (
        P("seq", "tp", None),
        P(),
        P(),
        P(),
        P(),
        P(("branch", "seq"), "tp"),
        P("tp"),
        P("tp", ("branch", "seq")),
        P(),
        P(("branch", "seq"), "tp"),
        P("tp"),
        P("tp", ("branch", "seq")),
        P(),
        P("seq", None),
        P("seq", "tp", None),
    )
    out_specs = (
        P("seq", "tp", None),
        P("seq", "tp", None),
        P(),
        P(),
        P(),
        P(),
        P(("branch", "seq"), "tp"),
        P("tp"),
        P("tp", ("branch", "seq")),
        P(),
        P(("branch", "seq"), "tp"),
        P("tp"),
        P("tp", ("branch", "seq")),
        P(),
    )
    return jax.shard_map(
        per_device, mesh=mesh, in_specs=in_specs, out_specs=out_specs, check_vma=False
    )
```

```python
from functools import partial
import math

import jax
import jax.numpy as jnp
from jax import lax
from jax.experimental import pallas as pl
from jax.experimental.pallas import tpu as pltpu
from jax.sharding import PartitionSpec as P

HD = 128
ROT = 32


EPSILON = 1e-05
NEGATIVE = -1e30
ROPE_BASE = 10000.0
LOG2E = math.log2(math.e)
F32 = jnp.float32
BF16 = jnp.bfloat16
CONTRACT_LAST = (((1,), (1,)), ((), ()))
CONTRACT_FIRST = (((0,), (0,)), ((), ()))
VMEM_BYTES = 56 * 1024 * 1024
ANY = pl.BlockSpec(memory_space=pl.ANY)
HINT = 0.02


def cost(flops, moved, transcendentals=0):
    return pl.CostEstimate(
        flops=1 + int(flops * HINT), bytes_accessed=1 + int(moved * HINT), transcendentals=0
    )


def launch(
    kernel,
    operands,
    in_specs,
    grid,
    out_specs,
    out_shape,
    name,
    cost_estimate,
    prefetch=(),
    held=(),
    tokens=(),
    scratch_shapes=(),
):
    lead = len(prefetch) + len(operands)
    extra = len(held) + len(tokens)

    def body(*refs):
        kernel(*refs[:lead], *refs[lead + extra :])

    return pl.pallas_call(
        body,
        grid_spec=pltpu.PrefetchScalarGridSpec(
            num_scalar_prefetch=len(prefetch),
            grid=grid,
            in_specs=list(in_specs) + [ANY] * extra,
            out_specs=out_specs,
            scratch_shapes=list(scratch_shapes),
        ),
        out_shape=out_shape,
        input_output_aliases={lead + k: k for k in range(len(held))},
        compiler_params=pltpu.CompilerParams(
            dimension_semantics=("arbitrary",) * len(grid), vmem_limit_bytes=VMEM_BYTES
        ),
        cost_estimate=cost_estimate,
        name=name,
    )(*prefetch, *operands, *held, *tokens)


def hold(value, *tokens):
    def nothing(out):
        pass

    return launch(
        nothing,
        [],
        [],
        (1,),
        ANY,
        jax.ShapeDtypeStruct(value.shape, value.dtype),
        "hold",
        cost(1, 1),
        held=[value],
        tokens=tokens,
    )


def swap(value, axis, bit):
    size = lax.axis_size(axis)
    return lax.ppermute(value, axis, [(i, i ^ bit) for i in range(size)])


def onward(value, axis):
    size = lax.axis_size(axis)
    return lax.ppermute(value, axis, [(i, (i + 1) % size) for i in range(size)])


def bit_orders(size):
    bits = [1 << k for k in range(size.bit_length() - 1)]
    return (bits, bits[::-1])


def last_bit(number, order):
    return [bit for bit in order if number & bit][-1]


def gather_near(own, number):
    size = lax.axis_size("tp")
    bits = [1 << k for k in range(size.bit_length() - 1)]
    return {
        (bit, (n + number) % 2): swap(own[(n + number) % 2], "tp", bit)
        for n, bit in enumerate(bits)
    }


def hold_all(items, *tokens):
    return {key: hold(item, *tokens) for key, item in items.items()}


def in_pieces(first, second):
    items = {**first, **second}
    return {j: [items[j, 0], items[j, 1]] for j in sorted({j for j, _ in items})}


def gather_far(near):
    size = lax.axis_size("tp")
    pieces = dict(near)
    far = {}
    for j in sorted(range(1, size), key=lambda j: bin(j).count("1")):
        if j not in near:
            bits = [last_bit(j, order) for order in bit_orders(size)]
            far[j] = [swap(pieces[j ^ bit][q], "tp", bit) for q, bit in enumerate(bits)]
            pieces[j] = far[j]
    return far


def with_other_core(items):
    return items + [swap(item, "branch", 1) for item in items]


def add_up(items):
    total = items[0].astype(F32)
    for item in items[1:]:
        total = total + item.astype(F32)
    return total


class TileSum:
    def __init__(self):
        size = lax.axis_size("tp")
        self.orders = bit_orders(size)
        self.waiting = [(q, j) for j in range(1, size) for q in range(2)]
        self.expected = {(q, j): 0 for j in range(size) for q in range(2)}
        for q, j in self.waiting:
            self.expected[q, j ^ last_bit(j, self.orders[q])] += 1
        self.waiting.sort(key=lambda at: (-bin(at[1]).count("1"), at[1]))
        self.pieces = {}
        self.arrived = {}
        self.moving = []

    def splits(self, j):
        return j > 0 and len({last_bit(j, order) for order in self.orders}) > 1

    def extras(self, j):
        return [(q, item) for q in range(2) for item in self.arrived.get((q, j), [])]

    def complete(self, j):
        return all(len(self.arrived.get((q, j), [])) == self.expected[q, j] for q in range(2))

    def send(self, *tokens):
        operands = []
        for q, j in list(self.waiting):
            if j not in self.pieces or (q, j) not in self.waiting:
                continue
            bit = last_bit(j, self.orders[q])
            if self.splits(j):
                sides, operand = [q], self.pieces[j][q]
            else:
                sides, operand = [0, 1], self.pieces[j]
            for side in sides:
                self.waiting.remove((side, j))
            if tokens:
                operand = hold(operand, *tokens)
            self.moving.append((sides, j ^ bit, swap(operand, "tp", bit)))
            operands.append(operand)
        return operands

    def land(self, *tokens):
        items = []
        for sides, j, item in self.moving:
            item = hold(item, *tokens) if tokens else item
            items.append(item)
            if j == 0:
                self.arrived.setdefault(0, []).append(item)
                continue
            half = item.shape[0] // 2
            for side in sides:
                part = item[side * half : (side + 1) * half] if len(sides) > 1 else item
                self.arrived.setdefault((side, j), []).append(part)
        self.moving = []
        return items

    def terms(self):
        return [[(item, 0), (item, 1)] for item in [self.pieces[0]] + self.arrived[0]]


def finish_piece(total, column, extras, outs):
    half = total.shape[0] // 2
    width = total.shape[1]
    cols = slice(column, column + width)
    parts = [total[:half], total[half:]]
    for q, ref in extras:
        parts[q] = parts[q] + ref[:, cols].astype(F32)
    for q in range(2):
        if len(outs) > 1:
            outs[q][:, cols] = parts[q].astype(BF16)
        else:
            outs[0][q * half : (q + 1) * half, cols] = parts[q].astype(BF16)


def piece_specs(tile, share, steps, split):
    rows, count = (tile // 2, 2) if split else (tile, 1)
    return (
        [pl.BlockSpec((rows, share), lambda i: (0, i))] * count,
        [jax.ShapeDtypeStruct((rows, steps * share), BF16)] * count,
    )


def all_sum(value, axis):
    size = lax.axis_size(axis)
    bit = 1
    while bit < size:
        value = value + swap(value, axis, bit)
        bit *= 2
    return value


def rope(vectors, cosine, sine_up, sine_down):
    return (
        vectors * cosine
        + pltpu.roll(vectors, ROT // 2, 1) * sine_up
        + pltpu.roll(vectors, HD - ROT // 2, 1) * sine_down
    )


class Documents:
    def __init__(self, place, starts, seq_at, rows):
        self.row = place[1] ^ seq_at
        self.starts = starts
        self.rows = rows

    def begin(self, places):
        begin = jnp.zeros_like(places)
        for number in range(self.starts.shape[1]):
            start = self.starts[self.row, number]
            begin = jnp.where(places >= start, start, begin)
        return begin

    def first_key_block(self, block):
        return lax.div(self.begin(block * self.rows), jnp.int32(self.rows))

    def first_whole_key_block(self, block):
        begin = self.begin((block + 1) * self.rows - 1)
        return lax.div(begin + (self.rows - 1), jnp.int32(self.rows))

    def last_whole_query_block(self, block, blocks):
        last = block
        for number in range(1, blocks):
            after = jnp.minimum(block + number, blocks - 1)
            whole = self.begin((after + 1) * self.rows - 1) <= block * self.rows
            last = jnp.where(whole, jnp.maximum(last, after), last)
        return last

    def last_query_block(self, block, blocks):
        last = block
        for number in range(1, blocks):
            after = jnp.minimum(block + number, blocks - 1)
            last = jnp.where(self.first_key_block(after) <= block, jnp.maximum(last, after), last)
        return last


def table_kernel(place, starts, cosine, sine_up, sine_down):
    rows = cosine.shape[0]
    blocks = lax.axis_size("tp")
    step = pl.program_id(0)
    block, seq_at = lax.rem(step, blocks) ^ place[0], lax.div(step, blocks)
    places = block * rows + lax.broadcasted_iota(jnp.int32, (rows, 1), 0)
    begin = Documents(place, starts, seq_at, rows).begin(places)
    lane = lax.broadcasted_iota(jnp.int32, (1, HD), 1)
    half = ROT // 2
    number = jnp.where(lane < half, lane, lane - half).astype(F32)
    frequency = jnp.exp2(number * (-2.0 / ROT * math.log2(ROPE_BASE)))
    angles = (places - begin).astype(F32) * jnp.where(lane < ROT, frequency, 0.0)
    cosine[...] = jnp.cos(angles)
    sines = jnp.sin(angles)
    sine_up[...] = jnp.where((lane >= half) & (lane < ROT), sines, 0.0)
    sine_down[...] = jnp.where(lane < half, -sines, 0.0)


def rotary_tables(place, starts, rows, tokens):
    steps = 2 * lax.axis_size("tp")
    tile = rows // steps
    out = pl.BlockSpec((tile, HD), lambda i, *_: (i, 0))
    return launch(
        table_kernel,
        [],
        [],
        (steps,),
        [out] * 3,
        [jax.ShapeDtypeStruct((rows, HD), F32)] * 3,
        "rotary_tables",
        cost(rows * HD * 100, rows * HD * 48),
        prefetch=[place, starts],
        tokens=tokens,
    )


def rows_of_piece(j):
    size = lax.axis_size("tp")
    return lambda i, *_: (i * size + j, 0)


def own_tile_specs(tile):
    _, rows, width = tile.shape

    def spec(h, q):
        return pl.BlockSpec((1, rows // 2, width), lambda i, place: (place[1] ^ h, q, 0))

    return [spec(h, q) for h in range(2) for q in range(2)]


def own_halves(place, tile, tokens=()):
    _, rows, width = tile.shape

    def kernel(place, first, second, out_first, out_second):
        out_first[...] = first[0]
        out_second[...] = second[0]

    shape = jax.ShapeDtypeStruct((rows // 2, width), BF16)
    return launch(
        kernel,
        [tile, tile],
        own_tile_specs(tile)[:2],
        (1,),
        [whole_spec(shape)] * 2,
        [shape, shape],
        "own_halves",
        cost(1, 4 * rows * width),
        prefetch=[place],
        tokens=tokens,
    )


def take_rows(halves, target):
    half = target.shape[0] // 2
    step = pl.program_id(0)
    for number in range(2):

        @pl.when(step == number)
        def _(number=number):
            for q in range(2):
                rows = halves[2 * number + q][...].reshape(half, target.shape[1])
                target[q * half : (q + 1) * half] = rows


def place_piece(j, place, halves, rows_in_all, held, tokens=()):
    if j == 0:
        specs = own_tile_specs(halves)
        half, model_width = halves.shape[1] // 2, halves.shape[2]
        halves = [halves] * 4
    else:
        half, model_width = halves[0].shape
        specs = [whole_spec(item) for item in halves]

    def kernel(place, *refs):
        take_rows(refs[:4], refs[4])

    return launch(
        kernel,
        halves,
        specs,
        (2,),
        pl.BlockSpec((2 * half, model_width), rows_of_piece(j)),
        jax.ShapeDtypeStruct((rows_in_all, model_width), BF16),
        "place_piece",
        cost(1, 4 * half * model_width * 4),
        prefetch=[place],
        held=held,
        tokens=tokens,
    )


def norm_kernel(place, x0, x1, x2, x3, gain1, shift1, gain2, shift2, *rest):
    normal, first, second, mark, scratch = rest[-5:]
    mark[...] = jnp.zeros_like(mark)
    take_rows((x0, x1, x2, x3), scratch)
    x = scratch[...].astype(F32)
    centred = x - jnp.mean(x, axis=-1, keepdims=True)
    variance = jnp.mean(centred * centred, axis=-1, keepdims=True)
    n = centred * lax.rsqrt(variance + EPSILON)
    normal[...] = n.astype(BF16)
    first[...] = (n * gain1[...] + shift1[...]).astype(BF16)
    second[...] = (n * gain2[...] + shift2[...]).astype(BF16)


def norm_piece(j, place, halves, rows_in_all, gains, held, tokens):
    if j == 0:
        specs = own_tile_specs(halves)
        half, model_width = halves.shape[1] // 2, halves.shape[2]
        halves = [halves] * 4
    else:
        half, model_width = halves[0].shape
        specs = [whole_spec(item) for item in halves]
    wide = pl.BlockSpec((2 * half, model_width), rows_of_piece(j))
    return launch(
        norm_kernel,
        halves + list(gains),
        specs + [whole_spec(item) for item in gains],
        (2,),
        [wide] * 3 + [pl.BlockSpec((8, HD), lambda i, *_: (0, 0))],
        [jax.ShapeDtypeStruct((rows_in_all, model_width), BF16)] * 3
        + [jax.ShapeDtypeStruct((8, HD), F32)],
        "norm_piece",
        cost(4 * half * model_width * 16, 4 * half * model_width * 16),
        prefetch=[place],
        held=held,
        tokens=tokens,
        scratch_shapes=[pltpu.VMEM((2 * half, model_width), BF16)],
    )


def chunks_of(weight):
    groups, cores = weight.shape[:2]
    return [(z, c, c * groups + z) for c in range(cores) for z in range(groups)]


def row_product(left, weight, share):
    total = None
    for z, c, at in chunks_of(weight):
        part = jnp.dot(
            left[:, at * share : (at + 1) * share], weight[z, c], preferred_element_type=F32
        )
        total = part if total is None else total + part
    return total


def column_back(left, weight, share):
    total = None
    for z, c, at in chunks_of(weight):
        part = lax.dot_general(
            left[:, at * share : (at + 1) * share],
            weight[z, c],
            CONTRACT_LAST,
            preferred_element_type=F32,
        )
        total = part if total is None else total + part
    return total


def whole_spec(array, prefetched=0):
    rank = array.ndim
    return pl.BlockSpec(array.shape, lambda *at: (0,) * rank)


def project_kernel(normed, weight, bias, cosine, sine_up, sine_down, queries, keys, values):
    joined = row_product(normed, weight, weight.shape[2]) + bias[...]
    tables = (cosine[...], sine_up[...], sine_down[...])
    for head in range(queries.shape[0]):
        at = head * 3 * HD
        queries[head, 0, 0] = rope(joined[:, at : at + HD], *tables).astype(BF16)
        keys[head, 0, 0] = rope(joined[:, at + HD : at + 2 * HD], *tables).astype(BF16)
        values[head, 0, 0] = joined[:, at + 2 * HD : at + 3 * HD].astype(BF16)


def project(first, last, normed, weight, bias, tables, held):
    rows, model_width = normed.shape
    joined_cols = weight.shape[3]
    heads = joined_cols // (3 * HD)
    size = lax.axis_size("tp")
    tile = rows // (2 * size)
    table = pl.BlockSpec((tile, HD), lambda s, i: (s * size + first + i, 0))
    share = (last - first) / size
    return launch(
        project_kernel,
        [normed, weight, bias] + list(tables),
        [
            pl.BlockSpec((tile, model_width), lambda s, i: (s * size + first + i, 0)),
            whole_spec(weight),
            whole_spec(bias),
            table,
            table,
            table,
        ],
        (2, last - first),
        [pl.BlockSpec((heads, 1, 1, tile, HD), lambda s, i: (0, s, first + i, 0, 0))] * 3,
        [jax.ShapeDtypeStruct((heads, 2, size, tile, HD), BF16)] * 3,
        "project",
        cost(
            2 * rows * share * model_width * joined_cols,
            2 * (rows * share * (model_width + joined_cols) + weight.size),
        ),
        held=held,
    )


def attend_kernel(place, starts, q_ref, k_ref, v_ref, out_ref, send_ref, lse_ref):
    block = pl.program_id(1)
    heads, rows = q_ref.shape[0], q_ref.shape[-2]
    here = place[0]
    documents = Documents(place, starts, pl.program_id(0), rows)
    low = documents.first_key_block(block)
    query_places = block * rows + lax.broadcasted_iota(jnp.int32, (rows, 1), 0)
    begin = documents.begin(query_places)
    factor = LOG2E / math.sqrt(HD)

    def step(masked, number, carry):
        key_places = number * rows + lax.broadcasted_iota(jnp.int32, (1, rows), 1)
        if masked:
            allowed = (key_places >= begin) & (key_places <= query_places)
        results = []
        for head in range(heads):
            top, total, mixed = carry[head]
            key = k_ref[head, 0, number ^ here]
            value = v_ref[head, 0, number ^ here]
            scores = lax.dot_general(
                q_ref[head, 0, 0], key, CONTRACT_LAST, preferred_element_type=F32
            )
            if masked:
                scores = jnp.where(allowed, scores, NEGATIVE)
            new_top = jnp.maximum(top, jnp.max(scores, axis=-1, keepdims=True))
            weights = jnp.exp2((scores - new_top) * factor)
            shrink = jnp.exp2((top - new_top) * factor)
            total = total * shrink + jnp.sum(weights, axis=-1, keepdims=True)
            mixed = mixed * shrink + jnp.dot(
                weights.astype(BF16), value, preferred_element_type=F32
            )
            results.append((new_top, total, mixed))
        return tuple(results)

    empty = (
        jnp.full((rows, 1), NEGATIVE, F32),
        jnp.zeros((rows, 1), F32),
        jnp.zeros((rows, HD), F32),
    )
    whole = jnp.minimum(jnp.maximum(documents.first_whole_key_block(block), low), block)
    results = lax.fori_loop(low, whole, partial(step, True), (empty,) * heads)
    results = lax.fori_loop(whole, block, partial(step, False), results)
    results = step(True, block, results)
    for head, (top, total, mixed) in enumerate(results):
        result = (mixed / total).astype(BF16)
        out_ref[0, 0, :, head * HD : (head + 1) * HD] = result
        send_ref[0, :, head * HD : (head + 1) * HD] = result
        log_sum = top * factor + jnp.log(total) * LOG2E
        lse_ref[head, 0, 0] = jnp.broadcast_to(log_sum, (rows, HD)).T[:1]


def attend(place, starts, queries, keys, values, tokens):
    heads, seqs, blocks, rows, _ = queries.shape
    one = pl.BlockSpec(
        (heads, 1, 1, rows, HD), lambda s, i, place, starts: (0, s, i ^ place[0], 0, 0)
    )
    full = pl.BlockSpec((heads, 1, blocks, rows, HD), lambda s, i, *_: (0, s, 0, 0, 0))
    pairs = heads * seqs * blocks * (blocks + 1) // 2
    return launch(
        attend_kernel,
        [queries, keys, values],
        [one, full, full],
        (seqs, blocks),
        [
            pl.BlockSpec(
                (1, 1, rows, heads * HD), lambda s, i, place, starts: (s, i ^ place[0], 0, 0)
            ),
            pl.BlockSpec(
                (1, rows, heads * HD), lambda s, i, place, starts: ((s * i) ^ place[0], 0, 0)
            ),
            pl.BlockSpec(
                (heads, 1, 1, 1, rows), lambda s, i, place, starts: (0, s, i ^ place[0], 0, 0)
            ),
        ],
        [
            jax.ShapeDtypeStruct((seqs, blocks, rows, heads * HD), BF16),
            jax.ShapeDtypeStruct((blocks, rows, heads * HD), BF16),
            jax.ShapeDtypeStruct((heads, seqs, blocks, 1, rows), F32),
        ],
        "attend",
        cost(pairs * 30 * rows * rows * HD, 4 * queries.size * 2),
        prefetch=[place, starts],
        tokens=tokens,
    )


def attend_back_kernel(
    place,
    starts,
    q_ref,
    k_ref,
    v_ref,
    grad_ref,
    out_ref,
    lse_ref,
    cosine,
    sine_up,
    sine_down,
    joined_ref,
    send_ref,
    sum_ref,
    query_grad,
    delta,
):
    block = pl.program_id(1)
    heads, blocks, rows = q_ref.shape[0], q_ref.shape[2], q_ref.shape[-2]
    here = place[0]
    documents = Documents(place, starts, pl.program_id(0), rows)
    high = documents.last_query_block(block, blocks)
    scaling = 1.0 / math.sqrt(HD)

    @pl.when(block == 0)
    def _():
        query_grad[...] = jnp.zeros_like(query_grad)

        def inner(j, carry):
            for head in range(heads):
                cols = slice(head * HD, (head + 1) * HD)
                product = grad_ref[0, j, :, cols].astype(F32) * out_ref[0, j, :, cols].astype(F32)
                delta[head, j] = jnp.sum(product.T, axis=0, keepdims=True)
            return carry

        lax.fori_loop(0, blocks, inner, 0)

    own = block ^ here
    key_places = block * rows + lax.broadcasted_iota(jnp.int32, (rows, 1), 0)

    def step(masked, number, carry):
        at = number ^ here
        if masked:
            query_places = number * rows + lax.broadcasted_iota(jnp.int32, (1, rows), 1)
            allowed = (key_places >= documents.begin(query_places)) & (
                key_places <= query_places
            )
        results = []
        for head in range(heads):
            key_grad, value_grad = carry[head]
            key = k_ref[head, 0, own]
            value = v_ref[head, 0, own]
            query = q_ref[head, 0, at]
            grad = grad_ref[0, at, :, head * HD : (head + 1) * HD]
            scores = lax.dot_general(key, query, CONTRACT_LAST, preferred_element_type=F32)
            weights = jnp.exp2(scores * (scaling * LOG2E) - lse_ref[head, 0, at])
            if masked:
                weights = jnp.where(allowed, weights, 0.0)
            weight_grad = lax.dot_general(value, grad, CONTRACT_LAST, preferred_element_type=F32)
            score_grad = (weights * (weight_grad - delta[head, at]) * scaling).astype(BF16)
            value_grad = value_grad + jnp.dot(
                weights.astype(BF16), grad, preferred_element_type=F32
            )
            key_grad = key_grad + jnp.dot(score_grad, query, preferred_element_type=F32)
            query_grad[head, at] = query_grad[head, at] + lax.dot_general(
                score_grad, key, CONTRACT_FIRST, preferred_element_type=F32
            )
            results.append((key_grad, value_grad))
        return tuple(results)

    empty = jnp.zeros((rows, HD), F32)
    whole = documents.last_whole_query_block(block, blocks)
    results = step(True, block, ((empty, empty),) * heads)
    results = lax.fori_loop(block + 1, whole + 1, partial(step, False), results)
    results = lax.fori_loop(whole + 1, high + 1, partial(step, True), results)
    tables = (cosine[0, own], -sine_up[0, own], -sine_down[0, own])
    for head, (key_grad, value_grad) in enumerate(results):
        at = head * 3 * HD
        joined_ref[0, own, :, at + HD : at + 2 * HD] = rope(key_grad, *tables).astype(BF16)
        joined_ref[0, own, :, at + 2 * HD : at + 3 * HD] = value_grad.astype(BF16)

    @pl.when(block == blocks - 1)
    def _():
        def inner(j, carry):
            tables = (cosine[0, j], -sine_up[0, j], -sine_down[0, j])
            for head in range(heads):
                at = head * 3 * HD
                joined_ref[0, j, :, at : at + HD] = rope(query_grad[head, j], *tables).astype(BF16)
            send_ref[j] = joined_ref[0, j]
            return carry + jnp.sum(joined_ref[0, j].astype(F32), axis=0, keepdims=True)

        sum_ref[0] = lax.fori_loop(0, blocks, inner, jnp.zeros((1, heads * 3 * HD), F32))


def attend_back(place, starts, queries, keys, values, grad, out, log_sums, tables, tokens):
    heads, seqs, blocks, rows, _ = queries.shape
    joined_cols = heads * 3 * HD
    head_spec = pl.BlockSpec((heads, 1, blocks, rows, HD), lambda s, i, *_: (0, s, 0, 0, 0))
    side = pl.BlockSpec((1, blocks, rows, heads * HD), lambda s, i, *_: (s, 0, 0, 0))
    table = pl.BlockSpec((1, blocks, rows, HD), lambda s, i, *_: (s, 0, 0, 0))
    pairs = heads * seqs * blocks * (blocks + 1) // 2
    return launch(
        attend_back_kernel,
        [queries, keys, values, grad, out, log_sums]
        + [item.reshape(seqs, blocks, rows, HD) for item in tables],
        [
            head_spec,
            head_spec,
            head_spec,
            side,
            side,
            pl.BlockSpec((heads, 1, blocks, 1, rows), lambda s, i, *_: (0, s, 0, 0, 0)),
            table,
            table,
            table,
        ],
        (seqs, blocks),
        [
            pl.BlockSpec((1, blocks, rows, joined_cols), lambda s, i, *_: (s, 0, 0, 0)),
            pl.BlockSpec((blocks, rows, joined_cols), lambda s, i, *_: (0, 0, 0)),
            pl.BlockSpec((1, 1, joined_cols), lambda s, i, *_: (s, 0, 0)),
        ],
        [
            jax.ShapeDtypeStruct((seqs, blocks, rows, joined_cols), BF16),
            jax.ShapeDtypeStruct((blocks, rows, joined_cols), BF16),
            jax.ShapeDtypeStruct((seqs, 1, joined_cols), F32),
        ],
        "attend_back",
        cost(pairs * 50 * rows * rows * HD, 12 * queries.size * 2),
        prefetch=[place, starts],
        tokens=tokens,
        scratch_shapes=[
            pltpu.VMEM((heads, blocks, rows, HD), F32),
            pltpu.VMEM((heads, blocks, 1, rows), F32),
        ],
    )


def expand_kernel(normed, weight, bias, activated, send, slope):
    pre = row_product(normed, weight, weight.shape[2]) + bias[...]
    share = 0.5 + 0.5 * lax.erf(pre * math.sqrt(0.5))
    density = jnp.exp2(pre * pre * (-0.5 * LOG2E)) * (1.0 / math.sqrt(2.0 * math.pi))
    result = (pre * share).astype(BF16)
    activated[...] = result
    send[...] = result
    slope[...] = (share + pre * density).astype(BF16)


def later_half(tile, width, steps):
    half = steps // 2
    return pl.BlockSpec((tile, width), lambda i: (jnp.maximum(i - half, 0), 0))


def expand(normed, weight, bias, tokens):
    rows, model_width = normed.shape
    cols = weight.shape[3]
    tile = 512
    steps = rows // tile
    out = pl.BlockSpec((tile, cols), lambda i: (i, 0))
    shape = jax.ShapeDtypeStruct((rows, cols), BF16)
    return launch(
        expand_kernel,
        [normed, weight, bias],
        [pl.BlockSpec((tile, model_width), lambda i: (i, 0)), whole_spec(weight), whole_spec(bias)],
        (steps,),
        [out, later_half(tile, cols, steps), out],
        [shape, jax.ShapeDtypeStruct((rows // 2, cols), BF16), shape],
        "expand",
        cost(
            2 * rows * model_width * cols,
            2 * (rows * model_width + weight.size + 2 * rows * cols),
        ),
        tokens=tokens,
    )


def by_columns(weight):
    groups = weight.shape[0] // 2
    return pl.BlockSpec(
        (2, 1) + weight.shape[2:], lambda i: (lax.rem(i, groups), lax.div(i, groups), 0, 0)
    )


def output_piece(j, pieces, attended, activated, dense, contract, sums, tokens):
    tile = attended[1].shape[0] // pieces
    groups, cores, _, share = dense[0].shape
    steps = groups * cores // 2
    lefts = [*attended, *activated]
    rights = [*dense, *contract]
    extras = sums.extras(j)

    def kernel(*refs):
        outs = refs[8 + len(extras) :]
        arrived = [(q, ref) for (q, _), ref in zip(extras, refs[8:])]
        for n in range(2):
            total = None
            for left, right in zip(refs[:4], refs[4:8]):
                part = jnp.dot(left[...], right[n, 0], preferred_element_type=F32)
                total = part if total is None else total + part
            finish_piece(total, n * share, arrived, outs)

    specs, shapes = piece_specs(tile, 2 * share, steps, sums.splits(j))
    result = launch(
        kernel,
        lefts + rights + [item for _, item in extras],
        [pl.BlockSpec((tile, item.shape[1]), lambda i: (j, 0)) for item in lefts]
        + [by_columns(item) for item in rights]
        + [pl.BlockSpec((tile // 2, 2 * share), lambda i: (0, i))] * len(extras),
        (steps,),
        specs,
        shapes,
        "output_piece",
        cost(4 * tile * sum(item.size for item in rights), 4 * sum(item.size for item in rights)),
        tokens=tokens,
    )
    sums.pieces[j] = result if sums.splits(j) else result[0]
    return result[0]


def dense_back_kernel(grad_ref, att_ref, dense, out, blocks, total):
    step = pl.program_id(0)
    share = dense.shape[3]

    @pl.when(step == 0)
    def _():
        total[...] = jnp.zeros_like(total)

    out[...] = column_back(grad_ref, dense, share).astype(BF16)
    total[...] += lax.dot_general(
        att_ref[...], grad_ref[...], CONTRACT_FIRST, preferred_element_type=F32
    )

    @pl.when(step == pl.num_programs(0) - 1)
    def _():
        for z, c, at in chunks_of(dense):
            blocks[z, c] = total[:, at * share : (at + 1) * share].T.astype(BF16)


def dense_back(grad, attended, dense, tokens):
    rows, width = grad.shape
    groups, cores, cols, share = dense.shape
    turned = jax.ShapeDtypeStruct((groups, cores, share, cols), BF16)
    tile = 512
    return launch(
        dense_back_kernel,
        [grad, attended, dense],
        [
            pl.BlockSpec((tile, width), lambda i: (i, 0)),
            pl.BlockSpec((tile, cols), lambda i: (i, 0)),
            whole_spec(dense),
        ],
        (rows // tile,),
        [pl.BlockSpec((tile, cols), lambda i: (i, 0)), whole_spec(turned)],
        [jax.ShapeDtypeStruct((rows, cols), BF16), turned],
        "dense_back",
        cost(4 * rows * dense.size, 2 * (rows * (width + cols) + dense.size)),
        tokens=tokens,
        scratch_shapes=[pltpu.VMEM((cols, width), F32)],
    )


def pre_grad_kernel(grad_ref, slope, contract, out, send, sums):
    @pl.when(pl.program_id(0) == 0)
    def _():
        sums[...] = jnp.zeros_like(sums)

    part = column_back(grad_ref, contract, contract.shape[3]) * slope[...].astype(F32)
    part = part.astype(BF16)
    out[...] = part
    send[...] = part
    sums[...] += jnp.sum(part.astype(F32), axis=0, keepdims=True)


def pre_grad_of(grad, slope, contract, tokens):
    rows, width = grad.shape
    cols = contract.shape[2]
    tile = 512
    steps = rows // tile
    return launch(
        pre_grad_kernel,
        [grad, slope, contract],
        [
            pl.BlockSpec((tile, width), lambda i: (i, 0)),
            pl.BlockSpec((tile, cols), lambda i: (i, 0)),
            whole_spec(contract),
        ],
        (steps,),
        [
            pl.BlockSpec((tile, cols), lambda i: (i, 0)),
            later_half(tile, cols, steps),
            pl.BlockSpec((1, cols), lambda i: (0, 0)),
        ],
        [
            jax.ShapeDtypeStruct((rows, cols), BF16),
            jax.ShapeDtypeStruct((rows // 2, cols), BF16),
            jax.ShapeDtypeStruct((1, cols), F32),
        ],
        "pre_grad",
        cost(2 * rows * contract.size, 2 * (rows * width + contract.size + 2 * rows * cols)),
        tokens=tokens,
    )


def normed_grad_piece(
    j, pieces, joined, pre, joined_weight, expand_weight, normal, gain1, gain2, sums, tokens
):
    tile = joined[1].shape[0] // pieces
    groups, cores, share, _ = joined_weight[0].shape
    steps = groups * cores // 2
    lefts = [*joined, *pre]
    rights = [*joined_weight, *expand_weight]
    extras = sums.extras(j)

    def kernel(*refs):
        normal, gain1, gain2 = refs[8:11]
        arrived = [(q, ref) for (q, _), ref in zip(extras, refs[11:])]
        *outs, along = refs[11 + len(extras) :]
        for n in range(2):

            def back(at):
                return lax.dot_general(
                    refs[at][...], refs[at + 4][n, 0], CONTRACT_LAST, preferred_element_type=F32
                )

            cols = slice(n * share, (n + 1) * share)
            first, second = back(0) + back(1), back(2) + back(3)
            rows = normal[:, cols].astype(F32)
            along[0:1, cols] = jnp.sum(first * rows, axis=0, keepdims=True)
            along[1:2, cols] = jnp.sum(first, axis=0, keepdims=True)
            along[2:3, cols] = jnp.sum(second * rows, axis=0, keepdims=True)
            along[3:4, cols] = jnp.sum(second, axis=0, keepdims=True)
            finish_piece(
                first * gain1[:, cols] + second * gain2[:, cols], n * share, arrived, outs
            )

    row = pl.BlockSpec((1, 2 * share), lambda i: (0, i))
    specs, shapes = piece_specs(tile, 2 * share, steps, sums.splits(j))
    *result, along = launch(
        kernel,
        lefts + rights + [normal, gain1, gain2] + [item for _, item in extras],
        [pl.BlockSpec((tile, item.shape[1]), lambda i: (j, 0)) for item in lefts]
        + [by_columns(item) for item in rights]
        + [pl.BlockSpec((tile, 2 * share), lambda i: (j, i)), row, row]
        + [pl.BlockSpec((tile // 2, 2 * share), lambda i: (0, i))] * len(extras),
        (steps,),
        specs + [pl.BlockSpec((8, 2 * share), lambda i: (0, i))],
        shapes + [jax.ShapeDtypeStruct((8, steps * 2 * share), F32)],
        "normed_grad_piece",
        cost(4 * tile * sum(item.size for item in rights), 4 * sum(item.size for item in rights)),
        tokens=tokens,
    )
    sums.pieces[j] = result if sums.splits(j) else result[0]
    return along


def rows_at(half, width, here):
    if here:
        return pl.BlockSpec((1, half, width), lambda i, place: (place[1], i, 0))
    return pl.BlockSpec((1, half, width), lambda i, place: (1 - place[1], i, 0))


def finish_tile(body, name, place, operands, whole, tile, width, tokens=()):
    half = tile // 2
    listed, specs, picks = [], [], []
    for pair in operands:
        if not isinstance(pair, list):
            picks.append((len(listed), False))
            listed.append(pair)
            specs.append(pl.BlockSpec((1, half, width), lambda i, place: (place[1], i, 0)))
        elif pair[0][0] is pair[1][0] and (pair[0][1], pair[1][1]) == (0, 1):
            picks.append((len(listed), False))
            listed.append(pair[0][0])
            specs.append(pl.BlockSpec((half, width), lambda i, place: (i, 0)))
        else:
            picks.append((len(listed), True))
            for item, at in pair:
                listed.append(item)
                specs.append(pl.BlockSpec((half, width), lambda i, place, at=at: (at, 0)))
    count = len(listed)

    def kernel(place, *refs):
        both, own = refs[count + len(whole) :]
        first = pl.program_id(0) == 0
        values = [
            jnp.where(first, refs[at][...], refs[at + 1][...])
            if pair
            else refs[at][...].reshape(half, width)
            for at, pair in picks
        ]
        result = body(values, refs[count : count + len(whole)]).astype(BF16)
        both[0] = result
        own[...] = result

    return launch(
        kernel,
        listed + list(whole),
        specs + [pl.BlockSpec(item.shape, lambda i, place: (0, 0)) for item in whole],
        (2,),
        [rows_at(half, width, True), pl.BlockSpec((half, width), lambda i, place: (i, 0))],
        [
            jax.ShapeDtypeStruct((2, tile, width), BF16),
            jax.ShapeDtypeStruct((tile, width), BF16),
        ],
        name,
        cost(20 * tile * width, 20 * tile * width),
        prefetch=[place],
        tokens=tokens,
    )


def pick_other(place, total, tokens):
    _, rows, cols = total.shape

    def pick(place, value, out):
        out[...] = value[0]

    other = launch(
        pick,
        [total],
        [pl.BlockSpec((1, rows, cols), lambda i, place: (1 - place[1], 0, 0))],
        (1,),
        pl.BlockSpec((rows, cols), lambda i, place: (0, 0)),
        jax.ShapeDtypeStruct((rows, cols), BF16),
        "pick_other",
        cost(1, 4 * rows * cols),
        prefetch=[place],
        tokens=tokens,
    )
    return swap(other, "branch", 1)


def join_cores(place, total, other, straight, tokens):
    _, rows, cols = total.shape
    turned = cols - straight

    def join(place, mine, others, *outs):
        value = jnp.where(pl.program_id(0) == 0, mine[0], others[...]).astype(F32)
        if straight:
            outs[0][...] = value[:, :straight]
        if turned:
            outs[-1][...] = value[:, straight:].T

    specs, shapes = [], []
    if straight:
        specs.append(pl.BlockSpec((rows, straight), lambda i, place: (0, place[1] ^ i)))
        shapes.append(jax.ShapeDtypeStruct((rows, 2 * straight), F32))
    if turned:
        specs.append(pl.BlockSpec((turned, rows), lambda i, place: (place[1] ^ i, 0)))
        shapes.append(jax.ShapeDtypeStruct((2 * turned, rows), F32))
    return launch(
        join,
        [total, other],
        [
            pl.BlockSpec((1, rows, cols), lambda i, place: (place[1], 0, 0)),
            pl.BlockSpec((rows, cols), lambda i, place: (0, 0)),
        ],
        (2,),
        specs,
        shapes,
        "finish_weight",
        cost(1, 16 * rows * cols),
        prefetch=[place],
        tokens=tokens,
    )


def fill_other(place, both, other, tokens=()):
    tile, width = other.shape

    def kernel(place, value, out):
        out[0] = value[...]

    return launch(
        kernel,
        [other],
        [pl.BlockSpec((tile // 2, width), lambda i, place: (i, 0))],
        (2,),
        rows_at(tile // 2, width, False),
        jax.ShapeDtypeStruct(both.shape, BF16),
        "fill_other",
        cost(1, 4 * tile * width),
        prefetch=[place],
        tokens=tokens,
        held=[both],
    )


def per_device(
    block_input,
    first_norm_gain,
    first_norm_bias,
    second_norm_gain,
    second_norm_bias,
    query_key_value,
    query_key_value_bias,
    attention_dense,
    attention_dense_bias,
    expand_weight,
    expand_bias,
    contract_weight,
    contract_bias,
    document_starts,
    output_grad,
):
    seqs, tile, model_width = block_input.shape
    tiles = lax.axis_size("tp")
    groups = lax.axis_size("seq")
    core = lax.axis_index("branch")
    here = lax.axis_index("tp")
    first_core = core == 0
    length = tile * tiles
    rows_in_all = length * seqs
    share = query_key_value.shape[0]

    def by_core(mine, others):
        return jnp.where(first_core, mine, others), jnp.where(first_core, others, mine)

    def halves_of(value, axis):
        size = value.shape[axis] // 2
        return (
            lax.dynamic_slice_in_dim(value, core * size, size, axis),
            lax.dynamic_slice_in_dim(value, (1 - core) * size, size, axis),
        )

    place = jnp.stack([here, core]).astype(jnp.int32)

    input_halves = own_halves(place, block_input)
    near = {**gather_near(input_halves, 0), **gather_near(input_halves, 1)}

    def core_halves(weight, axis):
        mine, others = halves_of(weight, axis)
        return jnp.stack(by_core(mine, swap(others, "branch", 1)))

    def gather_seq(piece):
        return lax.all_gather(piece, "seq", axis=0)

    weight_pieces = [
        core_halves(query_key_value, 1),
        core_halves(expand_weight, 1),
        core_halves(attention_dense, 0),
        core_halves(contract_weight, 0),
    ]
    joined_weight, expand_full, dense_full, contract_full = map(gather_seq, weight_pieces)
    joined_bias = halves_of(query_key_value_bias, 0)[0].astype(F32)[None]
    hidden_bias = halves_of(expand_bias, 0)[0].astype(F32)[None]

    gain1 = first_norm_gain.astype(F32)[None]
    gain2 = second_norm_gain.astype(F32)[None]
    gains = (
        gain1,
        first_norm_bias.astype(F32)[None],
        gain2,
        second_norm_bias.astype(F32)[None],
    )
    tables = rotary_tables(place, document_starts, rows_in_all, weight_pieces)
    grad_halves = own_halves(place, output_grad, [tables[0]])
    grad_rows = place_piece(0, place, output_grad, rows_in_all, (), grad_halves)
    *normed, mark = norm_piece(
        0, place, block_input, rows_in_all, gains, (), [tables[0], grad_rows]
    )
    near = in_pieces(hold_all(near, mark), {})
    far = gather_far(near)
    for j in sorted(near):
        *normed, mark = norm_piece(
            j, place, with_other_core(near[j]), rows_in_all, gains, normed, []
        )
    heads_held = ()
    far_from = tiles
    if tiles == 4:
        heads_held = project(0, 3, normed[1], joined_weight, joined_bias, tables, ())
        far_from = 3
    for j in sorted(far):
        last_items = [hold(item, mark) for item in far[j]]
        *normed, mark = norm_piece(
            j, place, with_other_core(last_items), rows_in_all, gains, normed, heads_held[:1]
        )
    heads_held = project(
        far_from % tiles, tiles, normed[1], joined_weight, joined_bias, tables, heads_held
    )
    normal, first_normed, second_normed = normed
    queries, keys, values = heads_held

    grad_halves = [hold(item, *last_items) for item in grad_halves]
    first = hold_all(gather_near(grad_halves, 0), queries)
    second = gather_near([hold(item, *first.values()) for item in grad_halves], 1)
    attended, attended_send, log_sums = attend(
        place, document_starts, queries, keys, values, [*first.values()]
    )
    attended_flat = attended.reshape(rows_in_all, -1)
    near = in_pieces(first, hold_all(second, log_sums))
    far = gather_far(near)
    activated, activated_send, slope = expand(
        second_normed, expand_full, hidden_bias, [item for j in near for item in near[j]]
    )
    near = {
        j: items + [hold(swap(item, "branch", 1), slope) for item in items]
        for j, items in near.items()
    }
    far = {j: [hold(item, slope) for item in items] for j, items in far.items()}
    arrived = [item for items in [*near.values(), *far.values()] for item in items]
    far = {j: with_other_core(items) for j, items in far.items()}
    for j, items in {**near, **far}.items():
        grad_rows = place_piece(j, place, items, rows_in_all, [grad_rows], [slope])

    def weight_grad(left, right):
        return lax.dot_general(left, right, CONTRACT_FIRST, preferred_element_type=F32).astype(BF16)

    def in_order(part):
        return part.reshape(2, groups, share, part.shape[1]).transpose(1, 0, 2, 3)

    def scatter(blocks):
        return lax.psum_scatter(blocks, "seq", scatter_dimension=0, tiled=False)

    def exchanged(own, send, *tokens):
        send = send.reshape(-1, send.shape[-1])
        return own.reshape(-1, own.shape[-1]), swap(hold(send, *tokens) if tokens else send, "branch", 1)

    def with_other_weight(weight):
        return weight, swap(weight, "branch", 1)

    contract_blocks = in_order(weight_grad(grad_rows, activated))
    contract_full = hold(contract_full, contract_blocks)
    pre_grad, pre_send, pre_sums = pre_grad_of(
        grad_rows, slope, contract_full, [contract_blocks]
    )
    contract_total = scatter(hold(contract_blocks, pre_sums))
    pre_pair = exchanged(pre_grad, pre_send)
    dense_full = hold(dense_full, pre_sums)
    attended_pair = exchanged(attended, attended_send, pre_sums)
    activated_pair = exchanged(activated, activated_send, pre_sums)
    contract_pair = with_other_weight(hold(contract_full, pre_sums))
    expand_blocks = in_order(weight_grad(second_normed, pre_grad))
    expand_total = scatter(expand_blocks)
    dense_pair = with_other_weight(dense_full)
    order = sorted(range(1, tiles), key=lambda j: (-bin(j).count("1"), j))
    outputs = TileSum()

    def output(j, *tokens):
        return output_piece(
            j, tiles, attended_pair, activated_pair, dense_pair, contract_pair, outputs, tokens
        )

    mark = expand_blocks
    operands = []
    for number, j in enumerate(order):
        if number and bin(order[number - 1]).count("1") > bin(j).count("1"):
            if not outputs.pieces.get(0) is None:
                operands += outputs.land(mark)
            else:
                attended_grad, dense_blocks = dense_back(
                    grad_rows, attended_flat, dense_full, [mark, *operands]
                )
                mark = output(0, attended_grad)
                operands = outputs.land(mark)
        mark = output(j, mark, *operands)
        operands = outputs.send() if outputs.complete(j) else []
    operands += outputs.send()
    landed = []
    joined_grad, joined_send, joined_sums = attend_back(
        place,
        document_starts,
        queries,
        keys,
        values,
        attended_grad.reshape(attended.shape),
        attended,
        log_sums,
        tables,
        [mark, *operands],
    )
    landed = outputs.land(joined_sums)
    joined_pair = exchanged(joined_grad, joined_send, *landed)
    joined_weight_pair = with_other_weight(joined_weight)
    expand_weight_pair = with_other_weight(expand_full)
    joined_grad = joined_pair[0]
    inputs = TileSum()
    sums = jnp.zeros((8, model_width), F32)
    mark = joined_sums
    wait = landed
    joined_blocks = None
    for number, j in enumerate(order + [0]):
        if number and j and bin(order[number - 1]).count("1") > bin(j).count("1"):
            if joined_blocks is None:
                part = weight_grad(hold(first_normed, mark, *wait), joined_grad)
                wait = inputs.land(part)
                joined_blocks = jnp.concatenate(
                    [in_order(hold(part, *wait)), dense_blocks], axis=3
                )
                joined_total = scatter(joined_blocks)
                mark = joined_blocks
            else:
                wait = inputs.land(mark)
        part = normed_grad_piece(
            j,
            tiles,
            joined_pair,
            pre_pair,
            joined_weight_pair,
            expand_weight_pair,
            normal,
            gain1,
            gain2,
            inputs,
            [mark, *wait],
        )
        sums = sums + part
        mark = part
        wait = inputs.send()
    landed = inputs.land(mark)

    biases = (
        attention_dense_bias.astype(F32)[None],
        contract_bias.astype(F32)[None],
    )

    def output_body(values, whole):
        return add_up(values) + whole[0][...] + whole[1][...]

    def input_body(values, whole):
        x, grad = values[0].astype(F32), values[1].astype(F32)
        total = add_up(values[2:])
        centred = x - jnp.mean(x, axis=-1, keepdims=True)
        rate = lax.rsqrt(jnp.mean(centred * centred, axis=-1, keepdims=True) + EPSILON)
        n = centred * rate
        middle = jnp.mean(total, axis=-1, keepdims=True)
        along = jnp.mean(total * n, axis=-1, keepdims=True)
        return grad + rate * (total - middle - n * along)

    def all_sum_beside(value, axis, others):
        size = lax.axis_size(axis)
        bit = 1
        while bit < size:
            arrived = swap(value, axis, bit)
            if others:
                arrived = hold(arrived, *others.pop(0)(value))
            value = value + arrived
            bit *= 2
        return value

    kept = {}

    def first_beside(value):
        kept["both"], kept["own"] = finish_tile(
            output_body,
            "finish_output",
            place,
            [block_input] + outputs.terms(),
            biases,
            tile,
            model_width,
            [value],
        )
        return [kept["own"]]

    def second_beside(value):
        kept["contract"] = pick_other(place, contract_total, [value])
        kept["expand"] = pick_other(place, expand_total, [kept["contract"]])
        (kept["contract_grad"],) = join_cores(place, contract_total, kept["contract"], 0, [value])
        (kept["expand_grad"],) = join_cores(
            place, expand_total, kept["expand"], expand_total.shape[2], [kept["contract_grad"]]
        )
        return [kept["expand_grad"], *landed]

    def third_beside(value):
        kept["input_both"], kept["input_own"] = finish_tile(
            input_body,
            "finish_input",
            place,
            [block_input, output_grad] + inputs.terms(),
            (),
            tile,
            model_width,
            [value],
        )
        kept["own_other"] = swap(hold(kept["own"], value), "branch", 1)
        return [kept["input_own"]]

    def fourth_beside(value):
        kept["output"] = fill_other(place, kept["both"], kept["own_other"], [value])
        return [kept["output"]]

    def fifth_beside(value):
        kept["joined"] = pick_other(place, joined_total, [value])
        return [kept["joined"]]

    others = [first_beside, second_beside, third_beside, fourth_beside, fifth_beside]
    joined_bias_part = jnp.sum(joined_sums, axis=0).reshape(-1)
    hidden_bias_part = pre_sums[0]
    grad_own = lax.dynamic_index_in_dim(output_grad, core, 0, False)
    small = jnp.concatenate(
        [
            sums[:4].reshape(-1),
            jnp.sum(grad_own.astype(F32), axis=0),
            joined_bias_part,
            hidden_bias_part,
        ]
    )
    everywhere = 5 * model_width
    small = all_sum_beside(hold(small, mark), "seq", others)
    per_core = small[everywhere:]
    both = jnp.stack(by_core(per_core, swap(per_core, "branch", 1)))
    query_key_value_bias_grad = both[:, : joined_bias_part.shape[0]].reshape(-1)
    expand_bias_grad = both[:, joined_bias_part.shape[0] :].reshape(-1)
    shared = all_sum_beside(small[:everywhere], "tp", others)
    shared = all_sum_beside(shared, "branch", others).reshape(5, model_width)
    while others:
        others.pop(0)(mark)
    contract_grad, expand_grad = kept["contract_grad"], kept["expand_grad"]
    block_output, joined_other = kept["output"], kept["joined"]
    input_grad = fill_other(
        place, kept["input_both"], swap(kept["input_own"], "branch", 1), [joined_other]
    )
    query_key_value_grad, dense_grad = join_cores(
        place, joined_total, joined_other, joined_weight.shape[3], [input_grad]
    )
    return (
        block_output,
        input_grad,
        shared[0],
        shared[1],
        shared[2],
        shared[3],
        query_key_value_grad,
        query_key_value_bias_grad,
        dense_grad,
        shared[4],
        expand_grad,
        expand_bias_grad,
        contract_grad,
        shared[4],
    )


def solution(mesh):
    in_specs = (
        P("seq", "tp", None),
        P(),
        P(),
        P(),
        P(),
        P(("branch", "seq"), "tp"),
        P("tp"),
        P("tp", ("branch", "seq")),
        P(),
        P(("branch", "seq"), "tp"),
        P("tp"),
        P("tp", ("branch", "seq")),
        P(),
        P("seq", None),
        P("seq", "tp", None),
    )
    out_specs = (
        P("seq", "tp", None),
        P("seq", "tp", None),
        P(),
        P(),
        P(),
        P(),
        P(("branch", "seq"), "tp"),
        P("tp"),
        P("tp", ("branch", "seq")),
        P(),
        P(("branch", "seq"), "tp"),
        P("tp"),
        P("tp", ("branch", "seq")),
        P(),
    )
    return jax.shard_map(
        per_device, mesh=mesh, in_specs=in_specs, out_specs=out_specs, check_vma=False
    )
```

```python
from functools import partial
import math

import jax
import jax.numpy as jnp
from jax import lax
from jax.experimental import pallas as pl
from jax.experimental.pallas import tpu as pltpu
from jax.sharding import PartitionSpec as P

HD = 128
ROT = 32


EPSILON = 1e-05
NEGATIVE = -1e30
ROPE_BASE = 10000.0
LOG2E = math.log2(math.e)
F32 = jnp.float32
BF16 = jnp.bfloat16
CONTRACT_LAST = (((1,), (1,)), ((), ()))
CONTRACT_FIRST = (((0,), (0,)), ((), ()))
VMEM_BYTES = 56 * 1024 * 1024
ANY = pl.BlockSpec(memory_space=pl.ANY)
HINT = 0.02


def cost(flops, moved, transcendentals=0):
    return pl.CostEstimate(
        flops=1 + int(flops * HINT), bytes_accessed=1 + int(moved * HINT), transcendentals=0
    )


def launch(
    kernel,
    operands,
    in_specs,
    grid,
    out_specs,
    out_shape,
    name,
    cost_estimate,
    prefetch=(),
    held=(),
    tokens=(),
    scratch_shapes=(),
):
    lead = len(prefetch) + len(operands)
    extra = len(held) + len(tokens)

    def body(*refs):
        kernel(*refs[:lead], *refs[lead + extra :])

    return pl.pallas_call(
        body,
        grid_spec=pltpu.PrefetchScalarGridSpec(
            num_scalar_prefetch=len(prefetch),
            grid=grid,
            in_specs=list(in_specs) + [ANY] * extra,
            out_specs=out_specs,
            scratch_shapes=list(scratch_shapes),
        ),
        out_shape=out_shape,
        input_output_aliases={lead + k: k for k in range(len(held))},
        compiler_params=pltpu.CompilerParams(
            dimension_semantics=("arbitrary",) * len(grid), vmem_limit_bytes=VMEM_BYTES
        ),
        cost_estimate=cost_estimate,
        name=name,
    )(*prefetch, *operands, *held, *tokens)


def hold(value, *tokens):
    def nothing(out):
        pass

    return launch(
        nothing,
        [],
        [],
        (1,),
        ANY,
        jax.ShapeDtypeStruct(value.shape, value.dtype),
        "hold",
        cost(1, 1),
        held=[value],
        tokens=tokens,
    )


def swap(value, axis, bit):
    size = lax.axis_size(axis)
    return lax.ppermute(value, axis, [(i, i ^ bit) for i in range(size)])


def onward(value, axis):
    size = lax.axis_size(axis)
    return lax.ppermute(value, axis, [(i, (i + 1) % size) for i in range(size)])


def bit_orders(size):
    bits = [1 << k for k in range(size.bit_length() - 1)]
    return (bits, bits[::-1])


def last_bit(number, order):
    return [bit for bit in order if number & bit][-1]


def gather_near(own, number):
    size = lax.axis_size("tp")
    bits = [1 << k for k in range(size.bit_length() - 1)]
    return {
        (bit, (n + number) % 2): swap(own[(n + number) % 2], "tp", bit)
        for n, bit in enumerate(bits)
    }


def hold_all(items, *tokens):
    return {key: hold(item, *tokens) for key, item in items.items()}


def in_pieces(first, second):
    items = {**first, **second}
    return {j: [items[j, 0], items[j, 1]] for j in sorted({j for j, _ in items})}


def gather_far(near):
    size = lax.axis_size("tp")
    pieces = dict(near)
    far = {}
    for j in sorted(range(1, size), key=lambda j: bin(j).count("1")):
        if j not in near:
            bits = [last_bit(j, order) for order in bit_orders(size)]
            far[j] = [swap(pieces[j ^ bit][q], "tp", bit) for q, bit in enumerate(bits)]
            pieces[j] = far[j]
    return far


def with_other_core(items):
    return items + [swap(item, "branch", 1) for item in items]


def add_up(items):
    total = items[0].astype(F32)
    for item in items[1:]:
        total = total + item.astype(F32)
    return total


class TileSum:
    def __init__(self):
        size = lax.axis_size("tp")
        self.orders = bit_orders(size)
        self.waiting = [(q, j) for j in range(1, size) for q in range(2)]
        self.expected = {(q, j): 0 for j in range(size) for q in range(2)}
        for q, j in self.waiting:
            self.expected[q, j ^ last_bit(j, self.orders[q])] += 1
        self.waiting.sort(key=lambda at: (-bin(at[1]).count("1"), at[1]))
        self.pieces = {}
        self.arrived = {}
        self.moving = []

    def splits(self, j):
        return j > 0 and len({last_bit(j, order) for order in self.orders}) > 1

    def extras(self, j):
        return [(q, item) for q in range(2) for item in self.arrived.get((q, j), [])]

    def complete(self, j):
        return all(len(self.arrived.get((q, j), [])) == self.expected[q, j] for q in range(2))

    def send(self, *tokens):
        operands = []
        for q, j in list(self.waiting):
            if j not in self.pieces or (q, j) not in self.waiting:
                continue
            bit = last_bit(j, self.orders[q])
            if self.splits(j):
                sides, operand = [q], self.pieces[j][q]
            else:
                sides, operand = [0, 1], self.pieces[j]
            for side in sides:
                self.waiting.remove((side, j))
            if tokens:
                operand = hold(operand, *tokens)
            self.moving.append((sides, j ^ bit, swap(operand, "tp", bit)))
            operands.append(operand)
        return operands

    def land(self, *tokens):
        items = []
        for sides, j, item in self.moving:
            item = hold(item, *tokens) if tokens else item
            items.append(item)
            if j == 0:
                self.arrived.setdefault(0, []).append(item)
                continue
            half = item.shape[0] // 2
            for side in sides:
                part = item[side * half : (side + 1) * half] if len(sides) > 1 else item
                self.arrived.setdefault((side, j), []).append(part)
        self.moving = []
        return items

    def terms(self):
        return [[(item, 0), (item, 1)] for item in [self.pieces[0]] + self.arrived[0]]


def finish_piece(total, column, extras, outs):
    half = total.shape[0] // 2
    width = total.shape[1]
    cols = slice(column, column + width)
    parts = [total[:half], total[half:]]
    for q, ref in extras:
        parts[q] = parts[q] + ref[:, cols].astype(F32)
    for q in range(2):
        if len(outs) > 1:
            outs[q][:, cols] = parts[q].astype(BF16)
        else:
            outs[0][q * half : (q + 1) * half, cols] = parts[q].astype(BF16)


def piece_specs(tile, share, steps, split):
    rows, count = (tile // 2, 2) if split else (tile, 1)
    return (
        [pl.BlockSpec((rows, share), lambda i: (0, i))] * count,
        [jax.ShapeDtypeStruct((rows, steps * share), BF16)] * count,
    )


def all_sum(value, axis):
    size = lax.axis_size(axis)
    bit = 1
    while bit < size:
        value = value + swap(value, axis, bit)
        bit *= 2
    return value


def rope(vectors, cosine, sine_up, sine_down):
    return (
        vectors * cosine
        + pltpu.roll(vectors, ROT // 2, 1) * sine_up
        + pltpu.roll(vectors, HD - ROT // 2, 1) * sine_down
    )


class Documents:
    def __init__(self, place, starts, seq_at, rows):
        self.row = place[1] ^ seq_at
        self.starts = starts
        self.rows = rows

    def begin(self, places):
        begin = jnp.zeros_like(places)
        for number in range(self.starts.shape[1]):
            start = self.starts[self.row, number]
            begin = jnp.where(places >= start, start, begin)
        return begin

    def first_key_block(self, block):
        return lax.div(self.begin(block * self.rows), jnp.int32(self.rows))

    def first_whole_key_block(self, block):
        begin = self.begin((block + 1) * self.rows - 1)
        return lax.div(begin + (self.rows - 1), jnp.int32(self.rows))

    def last_whole_query_block(self, block, blocks):
        last = block
        for number in range(1, blocks):
            after = jnp.minimum(block + number, blocks - 1)
            whole = self.begin((after + 1) * self.rows - 1) <= block * self.rows
            last = jnp.where(whole, jnp.maximum(last, after), last)
        return last

    def last_query_block(self, block, blocks):
        last = block
        for number in range(1, blocks):
            after = jnp.minimum(block + number, blocks - 1)
            last = jnp.where(self.first_key_block(after) <= block, jnp.maximum(last, after), last)
        return last


def table_kernel(place, starts, cosine, sine_up, sine_down):
    rows = cosine.shape[0]
    blocks = lax.axis_size("tp")
    step = pl.program_id(0)
    block, seq_at = lax.rem(step, blocks) ^ place[0], lax.div(step, blocks)
    places = block * rows + lax.broadcasted_iota(jnp.int32, (rows, 1), 0)
    begin = Documents(place, starts, seq_at, rows).begin(places)
    lane = lax.broadcasted_iota(jnp.int32, (1, HD), 1)
    half = ROT // 2
    number = jnp.where(lane < half, lane, lane - half).astype(F32)
    frequency = jnp.exp2(number * (-2.0 / ROT * math.log2(ROPE_BASE)))
    angles = (places - begin).astype(F32) * jnp.where(lane < ROT, frequency, 0.0)
    cosine[...] = jnp.cos(angles)
    sines = jnp.sin(angles)
    sine_up[...] = jnp.where((lane >= half) & (lane < ROT), sines, 0.0)
    sine_down[...] = jnp.where(lane < half, -sines, 0.0)


def rotary_tables(place, starts, rows, tokens):
    steps = 2 * lax.axis_size("tp")
    tile = rows // steps
    out = pl.BlockSpec((tile, HD), lambda i, *_: (i, 0))
    return launch(
        table_kernel,
        [],
        [],
        (steps,),
        [out] * 3,
        [jax.ShapeDtypeStruct((rows, HD), F32)] * 3,
        "rotary_tables",
        cost(rows * HD * 100, rows * HD * 48),
        prefetch=[place, starts],
        tokens=tokens,
    )


def rows_of_piece(j):
    size = lax.axis_size("tp")
    return lambda i, *_: (i * size + j, 0)


def own_tile_specs(tile):
    _, rows, width = tile.shape

    def spec(h, q):
        return pl.BlockSpec((1, rows // 2, width), lambda i, place: (place[1] ^ h, q, 0))

    return [spec(h, q) for h in range(2) for q in range(2)]


def own_halves(place, tile, tokens=()):
    _, rows, width = tile.shape

    def kernel(place, first, second, out_first, out_second):
        out_first[...] = first[0]
        out_second[...] = second[0]

    shape = jax.ShapeDtypeStruct((rows // 2, width), BF16)
    return launch(
        kernel,
        [tile, tile],
        own_tile_specs(tile)[:2],
        (1,),
        [whole_spec(shape)] * 2,
        [shape, shape],
        "own_halves",
        cost(1, 4 * rows * width),
        prefetch=[place],
        tokens=tokens,
    )


def take_rows(halves, target):
    half = target.shape[0] // 2
    step = pl.program_id(0)
    for number in range(2):

        @pl.when(step == number)
        def _(number=number):
            for q in range(2):
                rows = halves[2 * number + q][...].reshape(half, target.shape[1])
                target[q * half : (q + 1) * half] = rows


def place_piece(j, place, halves, rows_in_all, held, tokens=()):
    if j == 0:
        specs = own_tile_specs(halves)
        half, model_width = halves.shape[1] // 2, halves.shape[2]
        halves = [halves] * 4
    else:
        half, model_width = halves[0].shape
        specs = [whole_spec(item) for item in halves]

    def kernel(place, *refs):
        take_rows(refs[:4], refs[4])

    return launch(
        kernel,
        halves,
        specs,
        (2,),
        pl.BlockSpec((2 * half, model_width), rows_of_piece(j)),
        jax.ShapeDtypeStruct((rows_in_all, model_width), BF16),
        "place_piece",
        cost(1, 4 * half * model_width * 4),
        prefetch=[place],
        held=held,
        tokens=tokens,
    )


def norm_kernel(place, x0, x1, x2, x3, gain1, shift1, gain2, shift2, *rest):
    normal, first, second, mark, scratch = rest[-5:]
    mark[...] = jnp.zeros_like(mark)
    take_rows((x0, x1, x2, x3), scratch)
    x = scratch[...].astype(F32)
    centred = x - jnp.mean(x, axis=-1, keepdims=True)
    variance = jnp.mean(centred * centred, axis=-1, keepdims=True)
    n = centred * lax.rsqrt(variance + EPSILON)
    normal[...] = n.astype(BF16)
    first[...] = (n * gain1[...] + shift1[...]).astype(BF16)
    second[...] = (n * gain2[...] + shift2[...]).astype(BF16)


def norm_piece(j, place, halves, rows_in_all, gains, held, tokens):
    if j == 0:
        specs = own_tile_specs(halves)
        half, model_width = halves.shape[1] // 2, halves.shape[2]
        halves = [halves] * 4
    else:
        half, model_width = halves[0].shape
        specs = [whole_spec(item) for item in halves]
    wide = pl.BlockSpec((2 * half, model_width), rows_of_piece(j))
    return launch(
        norm_kernel,
        halves + list(gains),
        specs + [whole_spec(item) for item in gains],
        (2,),
        [wide] * 3 + [pl.BlockSpec((8, HD), lambda i, *_: (0, 0))],
        [jax.ShapeDtypeStruct((rows_in_all, model_width), BF16)] * 3
        + [jax.ShapeDtypeStruct((8, HD), F32)],
        "norm_piece",
        cost(4 * half * model_width * 16, 4 * half * model_width * 16),
        prefetch=[place],
        held=held,
        tokens=tokens,
        scratch_shapes=[pltpu.VMEM((2 * half, model_width), BF16)],
    )


def chunks_of(weight):
    groups, cores = weight.shape[:2]
    return [(z, c, c * groups + z) for c in range(cores) for z in range(groups)]


def row_product(left, weight, share):
    total = None
    for z, c, at in chunks_of(weight):
        part = jnp.dot(
            left[:, at * share : (at + 1) * share], weight[z, c], preferred_element_type=F32
        )
        total = part if total is None else total + part
    return total


def column_back(left, weight, share):
    total = None
    for z, c, at in chunks_of(weight):
        part = lax.dot_general(
            left[:, at * share : (at + 1) * share],
            weight[z, c],
            CONTRACT_LAST,
            preferred_element_type=F32,
        )
        total = part if total is None else total + part
    return total


def whole_spec(array, prefetched=0):
    rank = array.ndim
    return pl.BlockSpec(array.shape, lambda *at: (0,) * rank)


def project_kernel(normed, weight, bias, cosine, sine_up, sine_down, queries, keys, values):
    joined = row_product(normed, weight, weight.shape[2]) + bias[...]
    tables = (cosine[...], sine_up[...], sine_down[...])
    for head in range(queries.shape[0]):
        at = head * 3 * HD
        queries[head, 0, 0] = rope(joined[:, at : at + HD], *tables).astype(BF16)
        keys[head, 0, 0] = rope(joined[:, at + HD : at + 2 * HD], *tables).astype(BF16)
        values[head, 0, 0] = joined[:, at + 2 * HD : at + 3 * HD].astype(BF16)


def project(first, last, normed, weight, bias, tables, held):
    rows, model_width = normed.shape
    joined_cols = weight.shape[3]
    heads = joined_cols // (3 * HD)
    size = lax.axis_size("tp")
    tile = rows // (2 * size)
    table = pl.BlockSpec((tile, HD), lambda s, i: (s * size + first + i, 0))
    share = (last - first) / size
    return launch(
        project_kernel,
        [normed, weight, bias] + list(tables),
        [
            pl.BlockSpec((tile, model_width), lambda s, i: (s * size + first + i, 0)),
            whole_spec(weight),
            whole_spec(bias),
            table,
            table,
            table,
        ],
        (2, last - first),
        [pl.BlockSpec((heads, 1, 1, tile, HD), lambda s, i: (0, s, first + i, 0, 0))] * 3,
        [jax.ShapeDtypeStruct((heads, 2, size, tile, HD), BF16)] * 3,
        "project",
        cost(
            2 * rows * share * model_width * joined_cols,
            2 * (rows * share * (model_width + joined_cols) + weight.size),
        ),
        held=held,
    )


def attend_kernel(place, starts, q_ref, k_ref, v_ref, out_ref, send_ref, lse_ref):
    block = pl.program_id(1)
    heads, rows = q_ref.shape[0], q_ref.shape[-2]
    here = place[0]
    documents = Documents(place, starts, pl.program_id(0), rows)
    low = documents.first_key_block(block)
    query_places = block * rows + lax.broadcasted_iota(jnp.int32, (rows, 1), 0)
    begin = documents.begin(query_places)
    factor = LOG2E / math.sqrt(HD)

    def step(masked, number, carry):
        key_places = number * rows + lax.broadcasted_iota(jnp.int32, (1, rows), 1)
        if masked:
            allowed = (key_places >= begin) & (key_places <= query_places)
        results = []
        for head in range(heads):
            top, total, mixed = carry[head]
            key = k_ref[head, 0, number ^ here]
            value = v_ref[head, 0, number ^ here]
            scores = lax.dot_general(
                q_ref[head, 0, 0], key, CONTRACT_LAST, preferred_element_type=F32
            )
            if masked:
                scores = jnp.where(allowed, scores, NEGATIVE)
            new_top = jnp.maximum(top, jnp.max(scores, axis=-1, keepdims=True))
            weights = jnp.exp2((scores - new_top) * factor)
            shrink = jnp.exp2((top - new_top) * factor)
            total = total * shrink + jnp.sum(weights, axis=-1, keepdims=True)
            mixed = mixed * shrink + jnp.dot(
                weights.astype(BF16), value, preferred_element_type=F32
            )
            results.append((new_top, total, mixed))
        return tuple(results)

    empty = (
        jnp.full((rows, 1), NEGATIVE, F32),
        jnp.zeros((rows, 1), F32),
        jnp.zeros((rows, HD), F32),
    )
    whole = jnp.minimum(jnp.maximum(documents.first_whole_key_block(block), low), block)
    results = lax.fori_loop(low, whole, partial(step, True), (empty,) * heads)
    results = lax.fori_loop(whole, block, partial(step, False), results)
    results = step(True, block, results)
    for head, (top, total, mixed) in enumerate(results):
        result = (mixed / total).astype(BF16)
        out_ref[0, 0, :, head * HD : (head + 1) * HD] = result
        send_ref[0, :, head * HD : (head + 1) * HD] = result
        log_sum = top * factor + jnp.log(total) * LOG2E
        lse_ref[head, 0, 0] = jnp.broadcast_to(log_sum, (rows, HD)).T[:1]


def attend(place, starts, queries, keys, values, tokens):
    heads, seqs, blocks, rows, _ = queries.shape
    one = pl.BlockSpec(
        (heads, 1, 1, rows, HD), lambda s, i, place, starts: (0, s, i ^ place[0], 0, 0)
    )
    full = pl.BlockSpec((heads, 1, blocks, rows, HD), lambda s, i, *_: (0, s, 0, 0, 0))
    pairs = heads * seqs * blocks * (blocks + 1) // 2
    return launch(
        attend_kernel,
        [queries, keys, values],
        [one, full, full],
        (seqs, blocks),
        [
            pl.BlockSpec(
                (1, 1, rows, heads * HD), lambda s, i, place, starts: (s, i ^ place[0], 0, 0)
            ),
            pl.BlockSpec(
                (1, rows, heads * HD), lambda s, i, place, starts: ((s * i) ^ place[0], 0, 0)
            ),
            pl.BlockSpec(
                (heads, 1, 1, 1, rows), lambda s, i, place, starts: (0, s, i ^ place[0], 0, 0)
            ),
        ],
        [
            jax.ShapeDtypeStruct((seqs, blocks, rows, heads * HD), BF16),
            jax.ShapeDtypeStruct((blocks, rows, heads * HD), BF16),
            jax.ShapeDtypeStruct((heads, seqs, blocks, 1, rows), F32),
        ],
        "attend",
        cost(pairs * 30 * rows * rows * HD, 4 * queries.size * 2),
        prefetch=[place, starts],
        tokens=tokens,
    )


def attend_back_kernel(
    place,
    starts,
    q_ref,
    k_ref,
    v_ref,
    grad_ref,
    out_ref,
    lse_ref,
    cosine,
    sine_up,
    sine_down,
    joined_ref,
    send_ref,
    sum_ref,
    query_grad,
    delta,
):
    block = pl.program_id(1)
    heads, blocks, rows = q_ref.shape[0], q_ref.shape[2], q_ref.shape[-2]
    here = place[0]
    documents = Documents(place, starts, pl.program_id(0), rows)
    high = documents.last_query_block(block, blocks)
    scaling = 1.0 / math.sqrt(HD)

    @pl.when(block == 0)
    def _():
        query_grad[...] = jnp.zeros_like(query_grad)

        def inner(j, carry):
            for head in range(heads):
                cols = slice(head * HD, (head + 1) * HD)
                product = grad_ref[0, j, :, cols].astype(F32) * out_ref[0, j, :, cols].astype(F32)
                delta[head, j] = jnp.sum(product.T, axis=0, keepdims=True)
            return carry

        lax.fori_loop(0, blocks, inner, 0)

    own = block ^ here
    key_places = block * rows + lax.broadcasted_iota(jnp.int32, (rows, 1), 0)

    def step(masked, number, carry):
        at = number ^ here
        if masked:
            query_places = number * rows + lax.broadcasted_iota(jnp.int32, (1, rows), 1)
            allowed = (key_places >= documents.begin(query_places)) & (
                key_places <= query_places
            )
        results = []
        for head in range(heads):
            key_grad, value_grad = carry[head]
            key = k_ref[head, 0, own]
            value = v_ref[head, 0, own]
            query = q_ref[head, 0, at]
            grad = grad_ref[0, at, :, head * HD : (head + 1) * HD]
            scores = lax.dot_general(key, query, CONTRACT_LAST, preferred_element_type=F32)
            weights = jnp.exp2(scores * (scaling * LOG2E) - lse_ref[head, 0, at])
            if masked:
                weights = jnp.where(allowed, weights, 0.0)
            weight_grad = lax.dot_general(value, grad, CONTRACT_LAST, preferred_element_type=F32)
            score_grad = (weights * (weight_grad - delta[head, at]) * scaling).astype(BF16)
            value_grad = value_grad + jnp.dot(
                weights.astype(BF16), grad, preferred_element_type=F32
            )
            key_grad = key_grad + jnp.dot(score_grad, query, preferred_element_type=F32)
            query_grad[head, at] = query_grad[head, at] + lax.dot_general(
                score_grad, key, CONTRACT_FIRST, preferred_element_type=F32
            )
            results.append((key_grad, value_grad))
        return tuple(results)

    empty = jnp.zeros((rows, HD), F32)
    whole = documents.last_whole_query_block(block, blocks)
    results = step(True, block, ((empty, empty),) * heads)
    results = lax.fori_loop(block + 1, whole + 1, partial(step, False), results)
    results = lax.fori_loop(whole + 1, high + 1, partial(step, True), results)
    tables = (cosine[0, own], -sine_up[0, own], -sine_down[0, own])
    for head, (key_grad, value_grad) in enumerate(results):
        at = head * 3 * HD
        joined_ref[0, own, :, at + HD : at + 2 * HD] = rope(key_grad, *tables).astype(BF16)
        joined_ref[0, own, :, at + 2 * HD : at + 3 * HD] = value_grad.astype(BF16)

    @pl.when(block == blocks - 1)
    def _():
        def inner(j, carry):
            tables = (cosine[0, j], -sine_up[0, j], -sine_down[0, j])
            for head in range(heads):
                at = head * 3 * HD
                joined_ref[0, j, :, at : at + HD] = rope(query_grad[head, j], *tables).astype(BF16)
            @pl.when(pl.program_id(0) == 1)
            def _():
                send_ref[j] = joined_ref[0, j]

            return carry + jnp.sum(joined_ref[0, j].astype(F32), axis=0, keepdims=True)

        sum_ref[0] = lax.fori_loop(0, blocks, inner, jnp.zeros((1, heads * 3 * HD), F32))


def attend_back(place, starts, queries, keys, values, grad, out, log_sums, tables, tokens):
    heads, seqs, blocks, rows, _ = queries.shape
    joined_cols = heads * 3 * HD
    head_spec = pl.BlockSpec((heads, 1, blocks, rows, HD), lambda s, i, *_: (0, s, 0, 0, 0))
    side = pl.BlockSpec((1, blocks, rows, heads * HD), lambda s, i, *_: (s, 0, 0, 0))
    table = pl.BlockSpec((1, blocks, rows, HD), lambda s, i, *_: (s, 0, 0, 0))
    pairs = heads * seqs * blocks * (blocks + 1) // 2
    return launch(
        attend_back_kernel,
        [queries, keys, values, grad, out, log_sums]
        + [item.reshape(seqs, blocks, rows, HD) for item in tables],
        [
            head_spec,
            head_spec,
            head_spec,
            side,
            side,
            pl.BlockSpec((heads, 1, blocks, 1, rows), lambda s, i, *_: (0, s, 0, 0, 0)),
            table,
            table,
            table,
        ],
        (seqs, blocks),
        [
            pl.BlockSpec((1, blocks, rows, joined_cols), lambda s, i, *_: (s, 0, 0, 0)),
            pl.BlockSpec((blocks, rows, joined_cols), lambda s, i, *_: (0, 0, 0)),
            pl.BlockSpec((1, 1, joined_cols), lambda s, i, *_: (s, 0, 0)),
        ],
        [
            jax.ShapeDtypeStruct((seqs, blocks, rows, joined_cols), BF16),
            jax.ShapeDtypeStruct((blocks, rows, joined_cols), BF16),
            jax.ShapeDtypeStruct((seqs, 1, joined_cols), F32),
        ],
        "attend_back",
        cost(pairs * 50 * rows * rows * HD, 12 * queries.size * 2),
        prefetch=[place, starts],
        tokens=tokens,
        scratch_shapes=[
            pltpu.VMEM((heads, blocks, rows, HD), F32),
            pltpu.VMEM((heads, blocks, 1, rows), F32),
        ],
    )


def expand_kernel(normed, weight, bias, activated, send, slope):
    pre = row_product(normed, weight, weight.shape[2]) + bias[...]
    share = 0.5 + 0.5 * lax.erf(pre * math.sqrt(0.5))
    density = jnp.exp2(pre * pre * (-0.5 * LOG2E)) * (1.0 / math.sqrt(2.0 * math.pi))
    result = (pre * share).astype(BF16)
    activated[...] = result
    send[...] = result
    slope[...] = (share + pre * density).astype(BF16)


def later_half(tile, width, steps):
    half = steps // 2
    return pl.BlockSpec((tile, width), lambda i: (jnp.maximum(i - half, 0), 0))


def expand(normed, weight, bias, tokens):
    rows, model_width = normed.shape
    cols = weight.shape[3]
    tile = 512
    steps = rows // tile
    out = pl.BlockSpec((tile, cols), lambda i: (i, 0))
    shape = jax.ShapeDtypeStruct((rows, cols), BF16)
    return launch(
        expand_kernel,
        [normed, weight, bias],
        [pl.BlockSpec((tile, model_width), lambda i: (i, 0)), whole_spec(weight), whole_spec(bias)],
        (steps,),
        [out, later_half(tile, cols, steps), out],
        [shape, jax.ShapeDtypeStruct((rows // 2, cols), BF16), shape],
        "expand",
        cost(
            2 * rows * model_width * cols,
            2 * (rows * model_width + weight.size + 2 * rows * cols),
        ),
        tokens=tokens,
    )


def by_columns(weight):
    groups = weight.shape[0] // 2
    return pl.BlockSpec(
        (2, 1) + weight.shape[2:], lambda i: (lax.rem(i, groups), lax.div(i, groups), 0, 0)
    )


def output_piece(j, pieces, attended, activated, dense, contract, sums, tokens):
    tile = attended[1].shape[0] // pieces
    groups, cores, _, share = dense[0].shape
    steps = groups * cores // 2
    lefts = [*attended, *activated]
    rights = [*dense, *contract]
    extras = sums.extras(j)

    def kernel(*refs):
        outs = refs[8 + len(extras) :]
        arrived = [(q, ref) for (q, _), ref in zip(extras, refs[8:])]
        for n in range(2):
            total = None
            for left, right in zip(refs[:4], refs[4:8]):
                part = jnp.dot(left[...], right[n, 0], preferred_element_type=F32)
                total = part if total is None else total + part
            finish_piece(total, n * share, arrived, outs)

    specs, shapes = piece_specs(tile, 2 * share, steps, sums.splits(j))
    result = launch(
        kernel,
        lefts + rights + [item for _, item in extras],
        [pl.BlockSpec((tile, item.shape[1]), lambda i: (j, 0)) for item in lefts]
        + [by_columns(item) for item in rights]
        + [pl.BlockSpec((tile // 2, 2 * share), lambda i: (0, i))] * len(extras),
        (steps,),
        specs,
        shapes,
        "output_piece",
        cost(4 * tile * sum(item.size for item in rights), 4 * sum(item.size for item in rights)),
        tokens=tokens,
    )
    sums.pieces[j] = result if sums.splits(j) else result[0]
    return result[0]


def dense_back_kernel(grad_ref, att_ref, dense, out, blocks, total):
    step = pl.program_id(0)
    share = dense.shape[3]

    @pl.when(step == 0)
    def _():
        total[...] = jnp.zeros_like(total)

    out[...] = column_back(grad_ref, dense, share).astype(BF16)
    total[...] += lax.dot_general(
        att_ref[...], grad_ref[...], CONTRACT_FIRST, preferred_element_type=F32
    )

    @pl.when(step == pl.num_programs(0) - 1)
    def _():
        for z, c, at in chunks_of(dense):
            blocks[z, c] = total[:, at * share : (at + 1) * share].T.astype(BF16)


def dense_back(grad, attended, dense, tokens):
    rows, width = grad.shape
    groups, cores, cols, share = dense.shape
    turned = jax.ShapeDtypeStruct((groups, cores, share, cols), BF16)
    tile = 512
    return launch(
        dense_back_kernel,
        [grad, attended, dense],
        [
            pl.BlockSpec((tile, width), lambda i: (i, 0)),
            pl.BlockSpec((tile, cols), lambda i: (i, 0)),
            whole_spec(dense),
        ],
        (rows // tile,),
        [pl.BlockSpec((tile, cols), lambda i: (i, 0)), whole_spec(turned)],
        [jax.ShapeDtypeStruct((rows, cols), BF16), turned],
        "dense_back",
        cost(4 * rows * dense.size, 2 * (rows * (width + cols) + dense.size)),
        tokens=tokens,
        scratch_shapes=[pltpu.VMEM((cols, width), F32)],
    )


def pre_grad_kernel(grad_ref, slope, contract, out, send, sums):
    @pl.when(pl.program_id(0) == 0)
    def _():
        sums[...] = jnp.zeros_like(sums)

    part = column_back(grad_ref, contract, contract.shape[3]) * slope[...].astype(F32)
    part = part.astype(BF16)
    out[...] = part
    send[...] = part
    sums[...] += jnp.sum(part.astype(F32), axis=0, keepdims=True)


def pre_grad_of(grad, slope, contract, tokens):
    rows, width = grad.shape
    cols = contract.shape[2]
    tile = 512
    steps = rows // tile
    return launch(
        pre_grad_kernel,
        [grad, slope, contract],
        [
            pl.BlockSpec((tile, width), lambda i: (i, 0)),
            pl.BlockSpec((tile, cols), lambda i: (i, 0)),
            whole_spec(contract),
        ],
        (steps,),
        [
            pl.BlockSpec((tile, cols), lambda i: (i, 0)),
            later_half(tile, cols, steps),
            pl.BlockSpec((1, cols), lambda i: (0, 0)),
        ],
        [
            jax.ShapeDtypeStruct((rows, cols), BF16),
            jax.ShapeDtypeStruct((rows // 2, cols), BF16),
            jax.ShapeDtypeStruct((1, cols), F32),
        ],
        "pre_grad",
        cost(2 * rows * contract.size, 2 * (rows * width + contract.size + 2 * rows * cols)),
        tokens=tokens,
    )


def normed_grad_piece(
    j, pieces, joined, pre, joined_weight, expand_weight, normal, gain1, gain2, sums, tokens
):
    tile = joined[1].shape[0] // pieces
    groups, cores, share, _ = joined_weight[0].shape
    steps = groups * cores // 2
    lefts = [*joined, *pre]
    rights = [*joined_weight, *expand_weight]
    extras = sums.extras(j)

    def kernel(*refs):
        normal, gain1, gain2 = refs[8:11]
        arrived = [(q, ref) for (q, _), ref in zip(extras, refs[11:])]
        *outs, along = refs[11 + len(extras) :]
        for n in range(2):

            def back(at):
                return lax.dot_general(
                    refs[at][...], refs[at + 4][n, 0], CONTRACT_LAST, preferred_element_type=F32
                )

            cols = slice(n * share, (n + 1) * share)
            first, second = back(0) + back(1), back(2) + back(3)
            rows = normal[:, cols].astype(F32)
            along[0:1, cols] = jnp.sum(first * rows, axis=0, keepdims=True)
            along[1:2, cols] = jnp.sum(first, axis=0, keepdims=True)
            along[2:3, cols] = jnp.sum(second * rows, axis=0, keepdims=True)
            along[3:4, cols] = jnp.sum(second, axis=0, keepdims=True)
            finish_piece(
                first * gain1[:, cols] + second * gain2[:, cols], n * share, arrived, outs
            )

    row = pl.BlockSpec((1, 2 * share), lambda i: (0, i))
    specs, shapes = piece_specs(tile, 2 * share, steps, sums.splits(j))
    *result, along = launch(
        kernel,
        lefts + rights + [normal, gain1, gain2] + [item for _, item in extras],
        [pl.BlockSpec((tile, item.shape[1]), lambda i: (j, 0)) for item in lefts]
        + [by_columns(item) for item in rights]
        + [pl.BlockSpec((tile, 2 * share), lambda i: (j, i)), row, row]
        + [pl.BlockSpec((tile // 2, 2 * share), lambda i: (0, i))] * len(extras),
        (steps,),
        specs + [pl.BlockSpec((8, 2 * share), lambda i: (0, i))],
        shapes + [jax.ShapeDtypeStruct((8, steps * 2 * share), F32)],
        "normed_grad_piece",
        cost(4 * tile * sum(item.size for item in rights), 4 * sum(item.size for item in rights)),
        tokens=tokens,
    )
    sums.pieces[j] = result if sums.splits(j) else result[0]
    return along


def rows_at(half, width, here):
    if here:
        return pl.BlockSpec((1, half, width), lambda i, place: (place[1], i, 0))
    return pl.BlockSpec((1, half, width), lambda i, place: (1 - place[1], i, 0))


def finish_tile(body, name, place, operands, whole, tile, width, tokens=()):
    half = tile // 2
    listed, specs, picks = [], [], []
    for pair in operands:
        if not isinstance(pair, list):
            picks.append((len(listed), False))
            listed.append(pair)
            specs.append(pl.BlockSpec((1, half, width), lambda i, place: (place[1], i, 0)))
        elif pair[0][0] is pair[1][0] and (pair[0][1], pair[1][1]) == (0, 1):
            picks.append((len(listed), False))
            listed.append(pair[0][0])
            specs.append(pl.BlockSpec((half, width), lambda i, place: (i, 0)))
        else:
            picks.append((len(listed), True))
            for item, at in pair:
                listed.append(item)
                specs.append(pl.BlockSpec((half, width), lambda i, place, at=at: (at, 0)))
    count = len(listed)

    def kernel(place, *refs):
        both, own = refs[count + len(whole) :]
        first = pl.program_id(0) == 0
        values = [
            jnp.where(first, refs[at][...], refs[at + 1][...])
            if pair
            else refs[at][...].reshape(half, width)
            for at, pair in picks
        ]
        result = body(values, refs[count : count + len(whole)]).astype(BF16)
        both[0] = result
        own[...] = result

    return launch(
        kernel,
        listed + list(whole),
        specs + [pl.BlockSpec(item.shape, lambda i, place: (0, 0)) for item in whole],
        (2,),
        [rows_at(half, width, True), pl.BlockSpec((half, width), lambda i, place: (i, 0))],
        [
            jax.ShapeDtypeStruct((2, tile, width), BF16),
            jax.ShapeDtypeStruct((tile, width), BF16),
        ],
        name,
        cost(20 * tile * width, 20 * tile * width),
        prefetch=[place],
        tokens=tokens,
    )


def pick_other(place, total, tokens):
    _, rows, cols = total.shape

    def pick(place, value, out):
        out[...] = value[0]

    other = launch(
        pick,
        [total],
        [pl.BlockSpec((1, rows, cols), lambda i, place: (1 - place[1], 0, 0))],
        (1,),
        pl.BlockSpec((rows, cols), lambda i, place: (0, 0)),
        jax.ShapeDtypeStruct((rows, cols), BF16),
        "pick_other",
        cost(1, 4 * rows * cols),
        prefetch=[place],
        tokens=tokens,
    )
    return swap(other, "branch", 1)


def join_cores(place, total, other, straight, tokens):
    _, rows, cols = total.shape
    turned = cols - straight

    def join(place, mine, others, *outs):
        value = jnp.where(pl.program_id(0) == 0, mine[0], others[...]).astype(F32)
        if straight:
            outs[0][...] = value[:, :straight]
        if turned:
            outs[-1][...] = value[:, straight:].T

    specs, shapes = [], []
    if straight:
        specs.append(pl.BlockSpec((rows, straight), lambda i, place: (0, place[1] ^ i)))
        shapes.append(jax.ShapeDtypeStruct((rows, 2 * straight), F32))
    if turned:
        specs.append(pl.BlockSpec((turned, rows), lambda i, place: (place[1] ^ i, 0)))
        shapes.append(jax.ShapeDtypeStruct((2 * turned, rows), F32))
    return launch(
        join,
        [total, other],
        [
            pl.BlockSpec((1, rows, cols), lambda i, place: (place[1], 0, 0)),
            pl.BlockSpec((rows, cols), lambda i, place: (0, 0)),
        ],
        (2,),
        specs,
        shapes,
        "finish_weight",
        cost(1, 16 * rows * cols),
        prefetch=[place],
        tokens=tokens,
    )


def fill_other(place, both, other, tokens=()):
    tile, width = other.shape

    def kernel(place, value, out):
        out[0] = value[...]

    return launch(
        kernel,
        [other],
        [pl.BlockSpec((tile // 2, width), lambda i, place: (i, 0))],
        (2,),
        rows_at(tile // 2, width, False),
        jax.ShapeDtypeStruct(both.shape, BF16),
        "fill_other",
        cost(1, 4 * tile * width),
        prefetch=[place],
        tokens=tokens,
        held=[both],
    )


def per_device(
    block_input,
    first_norm_gain,
    first_norm_bias,
    second_norm_gain,
    second_norm_bias,
    query_key_value,
    query_key_value_bias,
    attention_dense,
    attention_dense_bias,
    expand_weight,
    expand_bias,
    contract_weight,
    contract_bias,
    document_starts,
    output_grad,
):
    seqs, tile, model_width = block_input.shape
    tiles = lax.axis_size("tp")
    groups = lax.axis_size("seq")
    core = lax.axis_index("branch")
    here = lax.axis_index("tp")
    first_core = core == 0
    length = tile * tiles
    rows_in_all = length * seqs
    share = query_key_value.shape[0]

    def by_core(mine, others):
        return jnp.where(first_core, mine, others), jnp.where(first_core, others, mine)

    def halves_of(value, axis):
        size = value.shape[axis] // 2
        return (
            lax.dynamic_slice_in_dim(value, core * size, size, axis),
            lax.dynamic_slice_in_dim(value, (1 - core) * size, size, axis),
        )

    place = jnp.stack([here, core]).astype(jnp.int32)

    input_halves = own_halves(place, block_input)
    near = {**gather_near(input_halves, 0), **gather_near(input_halves, 1)}

    def core_halves(weight, axis):
        mine, others = halves_of(weight, axis)
        return jnp.stack(by_core(mine, swap(others, "branch", 1)))

    def gather_seq(piece):
        return lax.all_gather(piece, "seq", axis=0)

    weight_pieces = [
        core_halves(query_key_value, 1),
        core_halves(expand_weight, 1),
        core_halves(attention_dense, 0),
        core_halves(contract_weight, 0),
    ]
    joined_weight, expand_full, dense_full, contract_full = map(gather_seq, weight_pieces)
    joined_bias = halves_of(query_key_value_bias, 0)[0].astype(F32)[None]
    hidden_bias = halves_of(expand_bias, 0)[0].astype(F32)[None]

    gain1 = first_norm_gain.astype(F32)[None]
    gain2 = second_norm_gain.astype(F32)[None]
    gains = (
        gain1,
        first_norm_bias.astype(F32)[None],
        gain2,
        second_norm_bias.astype(F32)[None],
    )
    tables = rotary_tables(place, document_starts, rows_in_all, weight_pieces)
    grad_halves = own_halves(place, output_grad, [tables[0]])
    grad_rows = place_piece(0, place, output_grad, rows_in_all, (), grad_halves)
    *normed, mark = norm_piece(
        0, place, block_input, rows_in_all, gains, (), [tables[0], grad_rows]
    )
    grad_own = lax.dynamic_index_in_dim(output_grad, core, 0, False)
    grad_sum = jnp.sum(grad_own.astype(F32), axis=0)
    near = in_pieces(hold_all(near, mark), {})
    far = gather_far(near)
    for j in sorted(near):
        *normed, mark = norm_piece(
            j, place, with_other_core(near[j]), rows_in_all, gains, normed, [grad_sum]
        )
    heads_held = ()
    far_from = tiles
    if tiles == 4:
        heads_held = project(0, 3, normed[1], joined_weight, joined_bias, tables, ())
        far_from = 3
    for j in sorted(far):
        last_items = [hold(item, mark) for item in far[j]]
        *normed, mark = norm_piece(
            j, place, with_other_core(last_items), rows_in_all, gains, normed, heads_held[:1]
        )
    heads_held = project(
        far_from % tiles, tiles, normed[1], joined_weight, joined_bias, tables, heads_held
    )
    normal, first_normed, second_normed = normed
    queries, keys, values = heads_held

    grad_halves = [hold(item, *last_items) for item in grad_halves]
    first = hold_all(gather_near(grad_halves, 0), queries)
    second = gather_near([hold(item, *first.values()) for item in grad_halves], 1)
    attended, attended_send, log_sums = attend(
        place, document_starts, queries, keys, values, [*first.values()]
    )
    attended_flat = attended.reshape(rows_in_all, -1)
    near = in_pieces(first, hold_all(second, log_sums))
    far = gather_far(near)
    activated, activated_send, slope = expand(
        second_normed, expand_full, hidden_bias, [item for j in near for item in near[j]]
    )
    near = {
        j: items + [hold(swap(item, "branch", 1), slope) for item in items]
        for j, items in near.items()
    }
    far = {j: [hold(item, slope) for item in items] for j, items in far.items()}
    arrived = [item for items in [*near.values(), *far.values()] for item in items]
    far = {j: with_other_core(items) for j, items in far.items()}
    for j, items in {**near, **far}.items():
        grad_rows = place_piece(j, place, items, rows_in_all, [grad_rows], [slope])

    def weight_grad(left, right):
        return lax.dot_general(left, right, CONTRACT_FIRST, preferred_element_type=F32).astype(BF16)

    def in_order(part):
        return part.reshape(2, groups, share, part.shape[1]).transpose(1, 0, 2, 3)

    def scatter(blocks):
        return lax.psum_scatter(blocks, "seq", scatter_dimension=0, tiled=False)

    def exchanged(own, send, *tokens):
        send = send.reshape(-1, send.shape[-1])
        return own.reshape(-1, own.shape[-1]), swap(hold(send, *tokens) if tokens else send, "branch", 1)

    def with_other_weight(weight):
        return weight, swap(weight, "branch", 1)

    contract_blocks = in_order(weight_grad(grad_rows, activated))
    contract_full = hold(contract_full, contract_blocks)
    pre_grad, pre_send, pre_sums = pre_grad_of(
        grad_rows, slope, contract_full, [contract_blocks]
    )
    contract_total = scatter(hold(contract_blocks, pre_sums))
    pre_pair = exchanged(pre_grad, pre_send)
    dense_full = hold(dense_full, pre_sums)
    attended_pair = exchanged(attended, attended_send, pre_sums)
    activated_pair = exchanged(activated, activated_send, pre_sums)
    contract_pair = with_other_weight(hold(contract_full, pre_sums))
    expand_blocks = in_order(weight_grad(second_normed, pre_grad))
    expand_total = scatter(expand_blocks)
    dense_pair = with_other_weight(dense_full)
    order = sorted(range(1, tiles), key=lambda j: (-bin(j).count("1"), j))
    outputs = TileSum()

    def output(j, *tokens):
        return output_piece(
            j, tiles, attended_pair, activated_pair, dense_pair, contract_pair, outputs, tokens
        )

    mark = expand_blocks
    operands = []
    for number, j in enumerate(order):
        if number and bin(order[number - 1]).count("1") > bin(j).count("1"):
            if not outputs.pieces.get(0) is None:
                operands += outputs.land(mark)
            else:
                attended_grad, dense_blocks = dense_back(
                    grad_rows, attended_flat, dense_full, [mark, *operands]
                )
                mark = output(0, attended_grad)
                operands = outputs.land(mark)
        mark = output(j, mark, *operands)
        operands = outputs.send() if outputs.complete(j) else []
    operands += outputs.send()
    landed = []
    joined_grad, joined_send, joined_sums = attend_back(
        place,
        document_starts,
        queries,
        keys,
        values,
        attended_grad.reshape(attended.shape),
        attended,
        log_sums,
        tables,
        [mark, *operands],
    )
    landed = outputs.land(joined_sums)
    joined_pair = exchanged(joined_grad, joined_send, *landed)
    joined_weight_pair = with_other_weight(joined_weight)
    expand_weight_pair = with_other_weight(expand_full)
    joined_grad = joined_pair[0]
    contract_other = pick_other(place, contract_total, [joined_sums])
    (contract_grad,) = join_cores(place, contract_total, contract_other, 0, [joined_sums])
    inputs = TileSum()
    sums = jnp.zeros((8, model_width), F32)
    mark = joined_sums
    wait = [*landed, contract_grad]
    joined_blocks = None
    for number, j in enumerate(order + [0]):
        if number and j and bin(order[number - 1]).count("1") > bin(j).count("1"):
            if joined_blocks is None:
                part = weight_grad(hold(first_normed, mark, *wait), joined_grad)
                wait = inputs.land(part)
                joined_blocks = jnp.concatenate(
                    [in_order(hold(part, *wait)), dense_blocks], axis=3
                )
                joined_total = scatter(joined_blocks)
                mark = joined_blocks
            else:
                wait = inputs.land(mark)
        part = normed_grad_piece(
            j,
            tiles,
            joined_pair,
            pre_pair,
            joined_weight_pair,
            expand_weight_pair,
            normal,
            gain1,
            gain2,
            inputs,
            [mark, *wait],
        )
        sums = sums + part
        mark = part
        wait = inputs.send()
    landed = inputs.land(mark)

    biases = (
        attention_dense_bias.astype(F32)[None],
        contract_bias.astype(F32)[None],
    )

    def output_body(values, whole):
        return add_up(values) + whole[0][...] + whole[1][...]

    def input_body(values, whole):
        x, grad = values[0].astype(F32), values[1].astype(F32)
        total = add_up(values[2:])
        centred = x - jnp.mean(x, axis=-1, keepdims=True)
        rate = lax.rsqrt(jnp.mean(centred * centred, axis=-1, keepdims=True) + EPSILON)
        n = centred * rate
        middle = jnp.mean(total, axis=-1, keepdims=True)
        along = jnp.mean(total * n, axis=-1, keepdims=True)
        return grad + rate * (total - middle - n * along)

    def all_sum_beside(value, axis, others):
        size = lax.axis_size(axis)
        bit = 1
        while bit < size:
            arrived = swap(value, axis, bit)
            if others:
                arrived = hold(arrived, *others.pop(0)(value))
            value = value + arrived
            bit *= 2
        return value

    kept = {}

    def first_beside(value):
        kept["both"], kept["own"] = finish_tile(
            output_body,
            "finish_output",
            place,
            [block_input] + outputs.terms(),
            biases,
            tile,
            model_width,
            [value],
        )
        return [kept["own"]]

    def second_beside(value):
        kept["expand"] = pick_other(place, expand_total, [value])
        (kept["expand_grad"],) = join_cores(
            place, expand_total, kept["expand"], expand_total.shape[2], [value]
        )
        return [kept["expand_grad"], *landed]

    def third_beside(value):
        kept["input_both"], kept["input_own"] = finish_tile(
            input_body,
            "finish_input",
            place,
            [block_input, output_grad] + inputs.terms(),
            (),
            tile,
            model_width,
            [value],
        )
        kept["own_other"] = swap(hold(kept["own"], value), "branch", 1)
        return [kept["input_own"]]

    def fourth_beside(value):
        kept["output"] = fill_other(place, kept["both"], kept["own_other"], [value])
        return [kept["output"]]

    def fifth_beside(value):
        kept["joined"] = pick_other(place, joined_total, [value])
        return [kept["joined"]]

    others = [first_beside, second_beside, third_beside, fourth_beside, fifth_beside]
    joined_bias_part = jnp.sum(joined_sums, axis=0).reshape(-1)
    hidden_bias_part = pre_sums[0]
    small = jnp.concatenate(
        [
            sums[:4].reshape(-1),
            grad_sum,
            joined_bias_part,
            hidden_bias_part,
        ]
    )
    everywhere = 5 * model_width
    small = all_sum_beside(hold(small, mark), "seq", others)
    per_core = small[everywhere:]
    both = jnp.stack(by_core(per_core, swap(per_core, "branch", 1)))
    query_key_value_bias_grad = both[:, : joined_bias_part.shape[0]].reshape(-1)
    expand_bias_grad = both[:, joined_bias_part.shape[0] :].reshape(-1)
    shared = all_sum_beside(small[:everywhere], "tp", others)
    shared = all_sum_beside(shared, "branch", others).reshape(5, model_width)
    while others:
        others.pop(0)(mark)
    expand_grad = kept["expand_grad"]
    block_output, joined_other = kept["output"], kept["joined"]
    input_grad = fill_other(
        place, kept["input_both"], swap(kept["input_own"], "branch", 1), [joined_other]
    )
    query_key_value_grad, dense_grad = join_cores(
        place, joined_total, joined_other, joined_weight.shape[3], [input_grad]
    )
    return (
        block_output,
        input_grad,
        shared[0],
        shared[1],
        shared[2],
        shared[3],
        query_key_value_grad,
        query_key_value_bias_grad,
        dense_grad,
        shared[4],
        expand_grad,
        expand_bias_grad,
        contract_grad,
        shared[4],
    )


def solution(mesh):
    in_specs = (
        P("seq", "tp", None),
        P(),
        P(),
        P(),
        P(),
        P(("branch", "seq"), "tp"),
        P("tp"),
        P("tp", ("branch", "seq")),
        P(),
        P(("branch", "seq"), "tp"),
        P("tp"),
        P("tp", ("branch", "seq")),
        P(),
        P("seq", None),
        P("seq", "tp", None),
    )
    out_specs = (
        P("seq", "tp", None),
        P("seq", "tp", None),
        P(),
        P(),
        P(),
        P(),
        P(("branch", "seq"), "tp"),
        P("tp"),
        P("tp", ("branch", "seq")),
        P(),
        P(("branch", "seq"), "tp"),
        P("tp"),
        P("tp", ("branch", "seq")),
        P(),
    )
    return jax.shard_map(
        per_device, mesh=mesh, in_specs=in_specs, out_specs=out_specs, check_vma=False
    )
```
